32 devices in a mesh: dp: 8 (over y, x, core), mp: 4 (over z).
Axes of the slice: x: 2, y: 2, z: 4, core: 2. Of those that a mesh axis runs over, the one named last changes fastest.
Arguments:
- cells: bfloat16 [16, 1024, 1024], P('dp', 'mp'), may hold values from -6 to 6
- lengths: int32 [16], P('dp'), may hold values from 256 to 1024, as said below
- query_matrix: bfloat16 [1024, 1024], P(None, 'mp'), may hold values from -0.1875 to 0.1875
- key_matrix: bfloat16 [1024, 1024], P(None, 'mp'), may hold values from -0.1875 to 0.1875
- value_matrix: bfloat16 [1024, 1024], P(None, 'mp'), may hold values from -0.1875 to 0.1875
- query_bias: float32 [1024], P('mp'), may hold values from -3 to 3
- value_bias: float32 [1024], P('mp'), may hold values from -3 to 3
- output_matrix: bfloat16 [1024, 1024], P('mp'), may hold values from -1.5 to 1.5
- b_out: float32 [1024], replicated, may hold values from -2 to 2
- gain_one: float32 [1024], replicated, may hold values from 0.5 to 1.5
- shift_one: float32 [1024], replicated, may hold values from -2 to 2
- gain_two: float32 [1024], replicated, may hold values from 0.5 to 1.5
- shift_two: float32 [1024], replicated, may hold values from -2 to 2
- expand_weight: bfloat16 [1024, 4096], P(None, 'mp'), may hold values from -0.1875 to 0.1875
- expand_bias: float32 [4096], P('mp'), may hold values from -3 to 3
- contract_weight: bfloat16 [4096, 1024], P('mp'), may hold values from -0.09375 to 0.09375
- b_down: float32 [1024], replicated, may hold values from -2 to 2
- grad_out: bfloat16 [16, 1024, 1024], P('dp', 'mp'), may hold values from -6 to 6
Outputs:
- out_cells: bfloat16 [16, 1024, 1024], P('dp', 'mp')
- grad_cells: float32 [16, 1024, 1024], P('dp', 'mp')
- grad_w_query: float32 [1024, 1024], P('dp', 'mp')
- grad_w_key: float32 [1024, 1024], P('dp', 'mp')
- grad_w_value: float32 [1024, 1024], P('dp', 'mp')
- grad_b_query: float32 [1024], P(('mp', 'dp'))
- grad_b_value: float32 [1024], P(('mp', 'dp'))
- grad_w_out: float32 [1024, 1024], P('mp', 'dp')
- grad_b_out: float32 [1024], P(('dp', 'mp'))
- grad_gain_one: float32 [1024], P(('dp', 'mp'))
- grad_shift_one: float32 [1024], P(('dp', 'mp'))
- grad_gain_two: float32 [1024], P(('dp', 'mp'))
- grad_shift_two: float32 [1024], P(('dp', 'mp'))
- grad_w_up: float32 [1024, 4096], P('dp', 'mp')
- grad_b_up: float32 [4096], P(('mp', 'dp'))
- grad_w_down: float32 [4096, 1024], P('mp', 'dp')
- grad_b_down: float32 [1024], P(('dp', 'mp'))
The draws below stay inside these ranges and needn't reach their ends.
Inputs may be any that keep to these rules, and one draw needn't show every extreme that they name: `lengths`: among the 2 slides of each index of dp, one, drawn from the seed, has exactly 1024 cells.
All inputs are finite; a program needn't handle non-finite values.
Results may differ from the reference program's by a relative error of at most 0.019.
Values may be sent and summed in bfloat16 or wider, within the bound.
A program may use at most 192 MiB of HBM per device.

```python
import math
from functools import partial
import jax
import jax.numpy as jnp
from jax import lax

MODEL_WIDTH_SIZE = 1024
H = 16
HD = 64
FF = 4096
SLIDE_CELLS = 1024
SLIDES_DEV = 2
SLIDES = 16


def draw_lengths(key, part):
    key = jax.random.fold_in(key, 7)
    first_key, second_key = jax.random.split(key)
    base_lengths = jax.random.randint(first_key, (SLIDES,), SLIDE_CELLS // 4, SLIDE_CELLS + 1)
    chosen = jax.random.randint(second_key, (SLIDES // SLIDES_DEV,), 0, SLIDES_DEV)
    slot_index = jnp.arange(SLIDES) % SLIDES_DEV
    full_slot = jnp.repeat(chosen, SLIDES_DEV, total_repeat_length=SLIDES)
    return jnp.where(slot_index == full_slot, SLIDE_CELLS, base_lengths).astype(jnp.int32)


def strengthened(array, key, source, target, blocks, factor):
    owner, partner = [(jnp.arange(array.shape[position]) // (array.shape[position] // blocks)).reshape([-1 if axis == position else 1 for axis in range(array.ndim)]) for position in (source, target)]
    chosen = jax.random.permutation(key, blocks)[partner]
    strong = (owner == chosen) | (owner == (partner + blocks // 2) % blocks)
    return jnp.where(strong, factor * array, array)


def steps_of(rng, shape, cuts, low, largest):
    def one(dim, parts):
        steps = jax.random.uniform(jax.random.fold_in(jax.random.fold_in(rng, 6), dim), (parts,), jnp.float32, low / len(cuts), largest / len(cuts))
        return jnp.repeat(jnp.exp(steps), shape[dim] // parts).reshape((-1,) + (1,) * (len(shape) - dim - 1))

    factor_of = one(*cuts[0])
    for cut in cuts[1:]:
        factor_of = factor_of * one(*cut)
    return factor_of


def noise(stream_key, shape, scale, most, shards=(), dtype=jnp.bfloat16):
    factor_of = steps_of(stream_key, shape, shards, -0.22, 0.18) if shards else 1.0
    values = jax.random.normal(stream_key, shape, jnp.float32) * scale * factor_of
    return jnp.minimum(jnp.maximum(values, -most), most).astype(dtype)


def noise_with(rng, dims, width, limit, cuts, heavy, held_as=jnp.bfloat16):
    drawn = width * jax.random.normal(rng, dims, jnp.float32)
    if cuts:
        drawn = drawn * steps_of(rng, dims, cuts, -0.22, 0.18)
    return jnp.clip(strengthened(drawn, jax.random.fold_in(rng, 3), *heavy), -limit, limit).astype(held_as)


def setup_inputs(seed: int = 0) -> dict:
    splits = jax.random.split(jax.random.key(seed), 19)
    cells = noise(splits[0], (SLIDES, SLIDE_CELLS, MODEL_WIDTH_SIZE), 1.0, 6.0, ((0, 8), (1, 4)))
    lengths = draw_lengths(jax.random.fold_in(splits[18], 71), 0)
    query_matrix = noise(splits[2], (MODEL_WIDTH_SIZE, MODEL_WIDTH_SIZE), MODEL_WIDTH_SIZE ** -0.5, 0.1875, ((1, 4),))
    key_matrix = noise(splits[3], (MODEL_WIDTH_SIZE, MODEL_WIDTH_SIZE), MODEL_WIDTH_SIZE ** -0.5, 0.1875, ((1, 4),))
    value_matrix = noise(splits[4], (MODEL_WIDTH_SIZE, MODEL_WIDTH_SIZE), MODEL_WIDTH_SIZE ** -0.5, 0.1875, ((1, 4),))
    query_bias = noise(splits[5], (MODEL_WIDTH_SIZE,), 0.5, 3.0, ((0, 4),), jnp.float32)
    value_bias = noise(splits[6], (MODEL_WIDTH_SIZE,), 0.5, 3.0, ((0, 4),), jnp.float32)
    output_matrix = noise(splits[7], (MODEL_WIDTH_SIZE, MODEL_WIDTH_SIZE), (MODEL_WIDTH_SIZE // 64) ** -0.5, 1.5, ((0, 4),))
    b_out = noise(splits[8], (MODEL_WIDTH_SIZE,), 0.3, 2.0, (), jnp.float32)
    gain_one = jnp.clip(1.0 + 0.1 * jax.random.normal(splits[9], (MODEL_WIDTH_SIZE,), jnp.float32), 0.5, 1.5)
    shift_one = noise(splits[10], (MODEL_WIDTH_SIZE,), 0.3, 2.0, (), jnp.float32)
    gain_two = jnp.clip(1.0 + 0.1 * jax.random.normal(splits[11], (MODEL_WIDTH_SIZE,), jnp.float32), 0.5, 1.5)
    shift_two = noise(splits[12], (MODEL_WIDTH_SIZE,), 0.3, 2.0, (), jnp.float32)
    expand_weight = noise(splits[13], (MODEL_WIDTH_SIZE, FF), MODEL_WIDTH_SIZE ** -0.5, 0.1875, ((1, 4),))
    expand_bias = noise(splits[14], (FF,), 0.5, 3.0, ((0, 4),), jnp.float32)
    contract_weight = noise(splits[15], (FF, MODEL_WIDTH_SIZE), FF ** -0.5, 0.09375, ((0, 4),))
    b_down = noise(splits[16], (MODEL_WIDTH_SIZE,), 0.3, 2.0, (), jnp.float32)
    grad_out = noise_with(splits[17], (SLIDES, SLIDE_CELLS, MODEL_WIDTH_SIZE), 1.0, 6.0, ((0, 8), (1, 4)), (0, 2, 8, 2.0))
    return {"cells": cells, "lengths": lengths, "query_matrix": query_matrix, "key_matrix": key_matrix, "value_matrix": value_matrix, "query_bias": query_bias, "value_bias": value_bias, "output_matrix": output_matrix, "b_out": b_out, "gain_one": gain_one, "shift_one": shift_one, "gain_two": gain_two, "shift_two": shift_two, "expand_weight": expand_weight, "expand_bias": expand_bias, "contract_weight": contract_weight, "b_down": b_down, "grad_out": grad_out}


@jax.custom_vjp
def reduced_dtype(v):
    return lax.optimization_barrier(v.astype(jnp.bfloat16)).astype(jnp.float32)

@jax.custom_vjp
def reduced_backward(v):
    return v

def low_keep(v):
    return (reduced_dtype(v), None)

def low_pass(kept, grad):
    return (grad,)

def back_keep(v):
    return (v, None)

def back_low(kept, grad):
    return (reduced_dtype(grad),)
reduced_dtype.defvjp(low_keep, low_pass)
reduced_backward.defvjp(back_keep, back_low)
epsilon = 1e-05
top_precision = lax.Precision.HIGHEST

def layer_norm(values, norm_gain, norm_shift):
    center = values - lax.optimization_barrier(jnp.mean(values, -1, keepdims=True))
    inverse = lax.rsqrt(lax.optimization_barrier(jnp.mean(center * center, -1, keepdims=True)) + epsilon)
    return center * inverse * norm_gain + norm_shift

def attend_slide(packed):
    query_rows, key_inputs, value_inputs, allowed = packed
    scores = reduced_backward(jnp.einsum('qhd,khd->hqk', query_rows, key_inputs, precision=top_precision) * HD ** (-0.5))
    scores = jnp.where(allowed[None, None, :], scores, -1e+30)
    soft_rows = reduced_dtype(jax.nn.softmax(scores, axis=-1))
    return reduced_dtype(reduced_backward(jnp.einsum('hqk,khd->qhd', soft_rows, value_inputs, precision=top_precision)))

def forward(lengths_block, params, cells_block):
    query_matrix, key_matrix, value_matrix, query_bias, value_bias, output_matrix, b_out, gain_one, shift_one, gain_two, shift_two, expand_weight, expand_bias, contract_weight, b_down = params
    number_slides = cells_block.shape[0]
    allowed = jnp.arange(SLIDE_CELLS)[None, :] < lengths_block[:, None]
    first_rows = reduced_dtype(layer_norm(cells_block, gain_one, shift_one))
    query_rows = reduced_dtype(reduced_backward(jnp.einsum('ujg,gm->ujm', first_rows, query_matrix, precision=top_precision) + query_bias))
    key_inputs = reduced_dtype(reduced_backward(jnp.einsum('ujg,gm->ujm', first_rows, key_matrix, precision=top_precision)))
    value_inputs = reduced_dtype(reduced_backward(jnp.einsum('ujg,gm->ujm', first_rows, value_matrix, precision=top_precision) + value_bias))
    head_shape = (number_slides, SLIDE_CELLS, H, HD)
    blended_heads = lax.map(jax.checkpoint(attend_slide), (query_rows.reshape(head_shape), key_inputs.reshape(head_shape), value_inputs.reshape(head_shape), allowed))
    attention_total = reduced_backward(jnp.einsum('tbk,kf->tbf', blended_heads.reshape(number_slides, SLIDE_CELLS, MODEL_WIDTH_SIZE), output_matrix, precision=top_precision))
    middle = cells_block + attention_total + b_out
    second_rows = reduced_dtype(layer_norm(middle, gain_two, shift_two))
    expanded_rows = reduced_backward(jnp.einsum('uwz,zo->uwo', second_rows, expand_weight, precision=top_precision) + expand_bias)
    hidden_activated = reduced_dtype(jax.nn.gelu(expanded_rows, approximate=False))
    contract_total = reduced_backward(jnp.einsum('ptm,mz->ptz', hidden_activated, contract_weight, precision=top_precision))
    keep_rows = allowed.astype(jnp.float32)[:, :, None]
    return keep_rows * (middle + contract_total + b_down)

def reference(cells, lengths, query_matrix, key_matrix, value_matrix, query_bias, value_bias, output_matrix, b_out, gain_one, shift_one, gain_two, shift_two, expand_weight, expand_bias, contract_weight, b_down, grad_out):
    params = tuple((weight_arg.astype(jnp.float32) for weight_arg in (query_matrix, key_matrix, value_matrix, query_bias, value_bias, output_matrix, b_out, gain_one, shift_one, gain_two, shift_two, expand_weight, expand_bias, contract_weight, b_down)))
    group = math.gcd(SLIDES, 4)
    step_count = SLIDES // group
    cells_blocks = cells.astype(jnp.float32).reshape(step_count, group, SLIDE_CELLS, MODEL_WIDTH_SIZE)
    grad_blocks = grad_out.astype(jnp.float32).reshape(step_count, group, SLIDE_CELLS, MODEL_WIDTH_SIZE)
    length_blocks = lengths.reshape(step_count, group)

    def one_step(carry, block):
        cells_block, grad_block, lengths_block = block
        result, pullback = jax.vjp(partial(forward, lengths_block), params, cells_block)
        d_params, d_cells = pullback(grad_block)
        carry = jax.tree.map(jnp.add, carry, d_params)
        return (carry, (result.astype(jnp.bfloat16), d_cells))
    zeros = jax.tree.map(jnp.zeros_like, params)
    totals, (out_blocks, dcell_blocks) = lax.scan(one_step, zeros, (cells_blocks, grad_blocks, length_blocks))
    return (out_blocks.reshape(SLIDES, SLIDE_CELLS, MODEL_WIDTH_SIZE), dcell_blocks.reshape(SLIDES, SLIDE_CELLS, MODEL_WIDTH_SIZE), totals[0], totals[1], totals[2], totals[3], totals[4], totals[5], totals[6], totals[7], totals[8], totals[9], totals[10], totals[11], totals[12], totals[13], totals[14])
```

```python
import jax
import jax.numpy as jnp
from jax import lax
from jax.sharding import PartitionSpec as P

HD = 64
EPS = 1e-05
BF = jnp.bfloat16
F32 = jnp.float32


def dot(a, b, ca, cb):
    return lax.dot_general(a, b, (((ca,), (cb,)), ((), ())), preferred_element_type=F32)


def cross(x, bit):
    n = lax.axis_size("dp")
    return lax.ppermute(x, "dp", [(i, i ^ (1 << bit)) for i in range(n)])


def shift(x, by):
    n = lax.axis_size("mp")
    return lax.ppermute(x, "mp", [(i, (i + by) % n) for i in range(n)])


def moves(n_dp, n_mp, slots):
    per = n_mp // slots
    turns = []
    for t in range(slots):
        pairs = []
        for d in range(n_dp):
            for m in range(n_mp):
                s = (t + m) % slots
                base, c = d - d % per, d % per
                target = (base + m // slots, c * slots + s)
                pairs.append((d * n_mp + m, target[0] * n_mp + target[1]))
        turns.append(pairs)
    return turns


def plane_bits(n_dp, flip):
    bits = list(range(1, n_dp.bit_length() - 1))
    return bits[::-1] if flip else bits


def gather(piece, flip):
    n_dp, n_mp = lax.axis_size("dp"), lax.axis_size("mp")
    stack = jnp.stack([shift(piece, n_mp - r) for r in range(1, n_mp)])
    held = {0: stack}
    for bit in plane_bits(n_dp, flip) + [0]:
        held.update({i ^ (1 << bit): cross(v, bit) for i, v in list(held.items())})
    return held


def assemble(held, own, d):
    n = len(held)
    stack = jnp.stack([held[i] for i in range(n)])
    order = jnp.arange(n) ^ d
    placed = jnp.take(stack, order, axis=0)
    placed = jnp.moveaxis(placed, 0, 1).reshape((stack.shape[1], -1, stack.shape[-1]))
    return [own] + [placed[r] for r in range(placed.shape[0])]


def scatter(blocks, flip):
    n_dp = lax.axis_size("dp")
    for bit in plane_bits(n_dp, flip):
        keep = sorted(i for i in blocks if not i >> bit & 1)
        got = cross(jnp.stack([blocks[i ^ (1 << bit)] for i in keep]), bit)
        blocks = {
            i: (blocks[i].astype(F32) + got[k].astype(F32)).astype(blocks[i].dtype)
            for k, i in enumerate(keep)
        }
    return blocks[0]


def layer_norm(v, gain, bias):
    center = v - jnp.mean(v, -1, keepdims=True)
    inverse = lax.rsqrt(jnp.mean(center * center, -1, keepdims=True) + EPS)
    unit = center * inverse
    return unit * gain + bias, unit, inverse


def norm_back(up, unit, inverse, gain):
    u = up * gain
    return inverse * (
        u - jnp.mean(u, -1, keepdims=True) - unit * jnp.mean(u * unit, -1, keepdims=True)
    )


def gelu_pair(v):
    cumulative = 0.5 * (1.0 + lax.erf(v * 0.7071067811865476))
    density = jnp.exp(-0.5 * v * v) * 0.3989422804014327
    return v * cumulative, cumulative + v * density


def attend(q, k, v, allowed):
    heads = q.shape[1] // HD
    qh = q.reshape(-1, heads, HD)
    kh = k.reshape(-1, heads, HD)
    vh = v.reshape(-1, heads, HD)
    s = jnp.einsum("qhd,khd->hqk", qh, kh, preferred_element_type=F32) * HD**-0.5
    s = jnp.where(allowed[None, None, :], s, -1e30)
    e = jnp.exp(s - jnp.max(s, -1, keepdims=True))
    p = (e / jnp.sum(e, -1, keepdims=True)).astype(BF)
    mixed = jnp.einsum("hqk,khd->qhd", p, vh, preferred_element_type=F32)
    return mixed.astype(BF).reshape(q.shape), p


def attend_back(q, k, v, p, mixed, dm):
    heads = q.shape[1] // HD
    qh = q.reshape(-1, heads, HD)
    kh = k.reshape(-1, heads, HD)
    vh = v.reshape(-1, heads, HD)
    dh = dm.reshape(-1, heads, HD)
    pf = p.astype(F32)
    dp = jnp.einsum("qhd,khd->hqk", dh, vh, preferred_element_type=F32)
    total = jnp.sum(dp * pf, -1, keepdims=True)
    ds = (pf * (dp - total)).astype(BF)
    dv = jnp.einsum("hqk,qhd->khd", p, dh, preferred_element_type=F32)
    dq = jnp.einsum("hqk,khd->qhd", ds, kh, preferred_element_type=F32) * HD**-0.5
    dk = jnp.einsum("hqk,qhd->khd", ds, qh, preferred_element_type=F32) * HD**-0.5
    return (
        dq.astype(BF).reshape(q.shape),
        dk.astype(BF).reshape(k.shape),
        dv.astype(BF).reshape(k.shape),
    )


def body(
    cells,
    lengths,
    query_matrix,
    key_matrix,
    value_matrix,
    query_bias,
    value_bias,
    output_matrix,
    b_out,
    gain_one,
    shift_one,
    gain_two,
    shift_two,
    expand_weight,
    expand_bias,
    contract_weight,
    b_down,
    grad_out,
):
    slots, rows, width = cells.shape
    n_dp, n_mp = lax.axis_size("dp"), lax.axis_size("mp")
    d, z = lax.axis_index("dp"), lax.axis_index("mp")
    per = n_mp // slots
    core = d % per
    tokens = slots * rows
    part = width // n_dp
    hw = query_matrix.shape[1]
    turns = moves(n_dp, n_mp, slots)

    def bring(x):
        got = [
            lax.ppermute(
                lax.dynamic_index_in_dim(x, (t + z) % slots, 0, False), ("dp", "mp"), turns[t]
            )
            for t in range(slots)
        ]
        even = z % slots == 0
        return jnp.concatenate(
            [jnp.where(even, got[0], got[1]), jnp.where(even, got[1], got[0])], 0
        )

    def give_back(x):
        x = x.reshape(slots, rows, width)
        got = [
            lax.ppermute(
                lax.dynamic_index_in_dim(x, (t + z) % slots, 0, False),
                ("dp", "mp"),
                [(b, a) for a, b in turns[t]],
            )
            for t in range(slots)
        ]
        even = z % slots == 0
        return jnp.stack(
            [jnp.where(even, got[0], got[1]), jnp.where(even, got[1], got[0])], 0
        )

    mine = bring(cells)
    attn_own = jnp.concatenate(
        [query_matrix, key_matrix, value_matrix, output_matrix.T], 1
    )
    first = d * part

    def piece_of(w):
        return lax.dynamic_slice_in_dim(w, first, part, 0)

    half = attn_own.shape[1] // 2
    a_piece = piece_of(attn_own)
    a_left = gather(a_piece[:, :half], False)
    a_right = gather(a_piece[:, half:], True)
    u_held = gather(piece_of(expand_weight), False)
    d_held = gather(piece_of(contract_weight), True)
    grad_rows = bring(grad_out)
    small = jnp.concatenate([query_bias, value_bias, expand_bias])
    small = [small] + [shift(small, n_mp - r) for r in range(1, n_mp)]
    both = cross(lengths, 0)
    length_all = jnp.where(core == 0, jnp.concatenate([lengths, both]), jnp.concatenate([both, lengths]))
    length = lax.dynamic_index_in_dim(length_all, z, 0, False)

    attn_w = [
        jnp.concatenate([a, b], 1)
        for a, b in zip(
            assemble(a_left, attn_own[:, :half], d), assemble(a_right, attn_own[:, half:], d)
        )
    ]
    up_w = assemble(u_held, expand_weight, d)
    down_w = assemble(d_held, contract_weight, d)

    position = core * tokens + jnp.arange(tokens)
    keep = (position < length).astype(F32)[:, None]
    sib_position = (per - 1 - core) * tokens + jnp.arange(tokens)
    allowed = jnp.concatenate([position, sib_position]) < length

    x = mine.astype(F32)
    rows_one, unit_one, inv_one = layer_norm(x, gain_one, shift_one)
    rows_one = rows_one.astype(BF)
    kept = []
    attention = jnp.zeros((tokens, width), F32)
    for r in range(n_mp):
        w = attn_w[r]
        q = (dot(rows_one, w[:, :hw], 1, 0) + small[r][:hw]).astype(BF)
        k = dot(rows_one, w[:, hw : 2 * hw], 1, 0).astype(BF)
        v = (dot(rows_one, w[:, 2 * hw : 3 * hw], 1, 0) + small[r][hw : 2 * hw]).astype(BF)
        k = jnp.concatenate([k, cross(k, 0)], 0)
        v = jnp.concatenate([v, cross(v, 0)], 0)
        mixed, p = attend(q, k, v, allowed)
        kept.append((q, k, v, mixed, p))
        attention = attention + dot(mixed, w[:, 3 * hw :], 1, 1)
    middle = x + attention + b_out
    rows_two, unit_two, inv_two = layer_norm(middle, gain_two, shift_two)
    rows_two = rows_two.astype(BF)
    g = keep * grad_rows.astype(F32)
    gz = g.astype(BF)

    order = jnp.arange(0, n_dp, 2) ^ d

    def chosen(v):
        return jnp.take(v.reshape(v.shape[0], n_dp, part), order, axis=1).reshape(v.shape[0], -1)

    def other(v):
        return jnp.take(v.reshape(v.shape[0], n_dp, part), order ^ 1, axis=1).reshape(v.shape[0], -1)

    def both_cores(v):
        return jnp.concatenate([chosen(v), cross(other(v), 0)], 0)

    def weight_grad(left, right, flip):
        right = jnp.concatenate([right, cross(right, 0)], 0)
        return weight_grad_all(left, right, flip)

    def weight_grad_all(left, right, flip):
        got = dot(left, right, 0, 0).astype(BF).reshape(-1, part, right.shape[1])
        return scatter({2 * i: got[i] for i in range(got.shape[0])}, flip)

    def finish(pieces):
        total = pieces[0].astype(F32)
        for r in range(1, n_mp):
            total = total + shift(pieces[r], r).astype(F32)
        return total

    two_both = both_cores(rows_two)
    gz_both = both_cores(gz)
    result = middle + b_down
    e2 = jnp.zeros((tokens, width), F32)
    up_parts, down_parts, b_up = [], [], []
    for r in range(n_mp):
        upper = dot(rows_two, up_w[r], 1, 0) + small[r][2 * hw :]
        hidden, slope = gelu_pair(upper)
        hidden = hidden.astype(BF)
        result = result + dot(hidden, down_w[r], 1, 0)
        d_upper = (dot(gz, down_w[r], 1, 1) * slope).astype(BF)
        e2 = e2 + dot(d_upper, up_w[r], 1, 1)
        up_parts.append(weight_grad(two_both, d_upper, False))
        down_parts.append(weight_grad(gz_both, hidden, True))
        b_up.append(jnp.sum(d_upper.astype(F32), 0))
    out_cells = give_back((keep * result).astype(BF))
    grad_up = finish(up_parts)
    grad_down = finish(down_parts).T

    d_middle = g + norm_back(e2, unit_two, inv_two, gain_two)
    gm = d_middle.astype(BF)
    gm_both = both_cores(gm)
    one_both = both_cores(rows_one)
    e1 = jnp.zeros((tokens, width), F32)
    a_parts, b_q, b_v = [], [], []
    for r in range(n_mp):
        q, k, v, mixed, p = kept[r]
        w = attn_w[r]
        d_mixed = dot(gm, w[:, 3 * hw :], 1, 0).astype(BF)
        dq, dk, dv = attend_back(q, k, v, p, mixed, d_mixed)
        dk_all = (dk.astype(F32) + jnp.roll(cross(dk, 0), tokens, 0).astype(F32)).astype(BF)
        dv_all = (dv.astype(F32) + jnp.roll(cross(dv, 0), tokens, 0).astype(F32)).astype(BF)
        dq_all = jnp.concatenate([dq, cross(dq, 0)], 0)
        e1 = (
            e1
            + dot(dq, w[:, :hw], 1, 1)
            + dot(dk_all[:tokens], w[:, hw : 2 * hw], 1, 1)
            + dot(dv_all[:tokens], w[:, 2 * hw : 3 * hw], 1, 1)
        )
        b_q.append(jnp.sum(dq.astype(F32), 0))
        b_v.append(jnp.sum(dv_all[:tokens].astype(F32), 0))
        qkv_part = weight_grad_all(one_both, jnp.concatenate([dq_all, dk_all, dv_all], 1), r % 2 == 1)
        o_part = weight_grad(gm_both, mixed, r % 2 == 0)
        a_parts.append(jnp.concatenate([qkv_part, o_part], 1))
    d_cells = d_middle + norm_back(e1, unit_one, inv_one, gain_one)
    grad_cells = give_back(d_cells.astype(BF)).astype(F32)
    grad_attn = finish(a_parts)

    split_mp = [jnp.stack(b_q).reshape(n_mp, n_dp, -1), jnp.stack(b_v).reshape(n_mp, n_dp, -1), jnp.stack(b_up).reshape(n_mp, n_dp, -1)]
    sums = [
        jnp.sum(d_middle, 0),
        jnp.sum(e1 * unit_one, 0),
        jnp.sum(e1, 0),
        jnp.sum(e2 * unit_two, 0),
        jnp.sum(e2, 0),
        jnp.sum(g, 0),
    ]
    split_dp = [jnp.roll(jnp.swapaxes(s.reshape(n_dp, n_mp, -1), 0, 1), -z, 0) for s in sums]
    packed = jnp.concatenate(split_mp + split_dp, 2)
    packed = jnp.take(packed, jnp.arange(n_dp) ^ d, axis=1)
    packed = packed[:, 0::2] + cross(packed[:, 1::2], 0)
    packed = scatter({2 * i: packed[:, i] for i in range(packed.shape[1])}, False)
    vec = packed[0]
    for r in range(1, n_mp):
        vec = vec + shift(packed[r], r)
    nq = split_mp[0].shape[2]
    nu = split_mp[2].shape[2]
    ns = split_dp[0].shape[2]
    vq, vv, vu = vec[:nq], vec[nq : 2 * nq], vec[2 * nq : 2 * nq + nu]
    rest = [vec[2 * nq + nu + i * ns : 2 * nq + nu + (i + 1) * ns] for i in range(6)]
    return (
        out_cells,
        grad_cells,
        grad_attn[:, :hw],
        grad_attn[:, hw : 2 * hw],
        grad_attn[:, 2 * hw : 3 * hw],
        vq,
        vv,
        grad_attn[:, 3 * hw :].T,
        rest[0],
        rest[1],
        rest[2],
        rest[3],
        rest[4],
        grad_up,
        vu,
        grad_down,
        rest[5],
    )


def solution(mesh):
    return jax.shard_map(
        body,
        mesh=mesh,
        in_specs=(
            P("dp", "mp", None),
            P("dp"),
            P(None, "mp"),
            P(None, "mp"),
            P(None, "mp"),
            P("mp"),
            P("mp"),
            P("mp", None),
            P(),
            P(),
            P(),
            P(),
            P(),
            P(None, "mp"),
            P("mp"),
            P("mp", None),
            P(),
            P("dp", "mp", None),
        ),
        out_specs=(
            P("dp", "mp", None),
            P("dp", "mp", None),
            P("dp", "mp"),
            P("dp", "mp"),
            P("dp", "mp"),
            P(("mp", "dp")),
            P(("mp", "dp")),
            P("mp", "dp"),
            P(("dp", "mp")),
            P(("dp", "mp")),
            P(("dp", "mp")),
            P(("dp", "mp")),
            P(("dp", "mp")),
            P("dp", "mp"),
            P(("mp", "dp")),
            P("mp", "dp"),
            P(("dp", "mp")),
        ),
        check_vma=False,
    )
```

```python
import jax
import jax.numpy as jnp
from jax import lax
from jax.experimental import pallas as pl
from jax.experimental.pallas import tpu as pltpu
from jax.sharding import PartitionSpec as P

HD = 64
EPS = 1e-05
BF = jnp.bfloat16
F32 = jnp.float32
MESH = pl.DeviceIdType.MESH
T = 512
PART = 128


def dot(a, b, ca, cb):
    return lax.dot_general(a, b, (((ca,), (cb,)), ((), ())), preferred_element_type=F32)


def cross(x, bit):
    n = lax.axis_size("dp")
    return lax.ppermute(x, "dp", [(i, i ^ (1 << bit)) for i in range(n)])


def shift(x, by):
    n = lax.axis_size("mp")
    return lax.ppermute(x, "mp", [(i, (i + by) % n) for i in range(n)])


def moves(n_dp, n_mp, slots):
    per = n_mp // slots
    turns = []
    for t in range(slots):
        pairs = []
        for d in range(n_dp):
            for m in range(n_mp):
                s = (t + m) % slots
                base, c = d - d % per, d % per
                target = (base + m // slots, c * slots + s)
                pairs.append((d * n_mp + m, target[0] * n_mp + target[1]))
        turns.append(pairs)
    return turns


def plane_bits(n_dp, flip):
    bits = list(range(1, n_dp.bit_length() - 1))
    return bits[::-1] if flip else bits


def gather(piece, flip):
    n_dp, n_mp = lax.axis_size("dp"), lax.axis_size("mp")
    stack = jnp.stack([shift(piece, n_mp - r) for r in range(1, n_mp)])
    held = {0: stack}
    for bit in plane_bits(n_dp, flip) + [0]:
        held.update({i ^ (1 << bit): cross(v, bit) for i, v in list(held.items())})
    return held


def assemble(held, own, d):
    n = len(held)
    stack = jnp.stack([held[i] for i in range(n)])
    order = jnp.arange(n) ^ d
    placed = jnp.take(stack, order, axis=0)
    placed = jnp.moveaxis(placed, 0, 1).reshape((stack.shape[1], -1, stack.shape[-1]))
    return [own] + [placed[r] for r in range(placed.shape[0])]


def scatter(blocks, flip):
    n_dp = lax.axis_size("dp")
    for bit in plane_bits(n_dp, flip):
        keep = sorted(i for i in blocks if not i >> bit & 1)
        got = cross(jnp.stack([blocks[i ^ (1 << bit)] for i in keep]), bit)
        blocks = {
            i: (blocks[i].astype(F32) + got[k].astype(F32)).astype(blocks[i].dtype)
            for k, i in enumerate(keep)
        }
    return blocks[0]


def layer_norm(v, gain, bias):
    center = v - jnp.mean(v, -1, keepdims=True)
    inverse = lax.rsqrt(jnp.mean(center * center, -1, keepdims=True) + EPS)
    unit = center * inverse
    return unit * gain + bias, unit, inverse


def norm_back(up, unit, inverse, gain):
    u = up * gain
    return inverse * (
        u - jnp.mean(u, -1, keepdims=True) - unit * jnp.mean(u * unit, -1, keepdims=True)
    )


def gelu_pair(v):
    cumulative = 0.5 * (1.0 + lax.erf(v * 0.7071067811865476))
    density = jnp.exp(-0.5 * v * v) * 0.3989422804014327
    return v * cumulative, cumulative + v * density


def attend(q, k, v, allowed):
    heads = q.shape[1] // HD
    qh = q.reshape(-1, heads, HD)
    kh = k.reshape(-1, heads, HD)
    vh = v.reshape(-1, heads, HD)
    s = jnp.einsum("qhd,khd->hqk", qh, kh, preferred_element_type=F32) * HD**-0.5
    s = jnp.where(allowed[None, None, :], s, -1e30)
    e = jnp.exp(s - jnp.max(s, -1, keepdims=True))
    p = (e / jnp.sum(e, -1, keepdims=True)).astype(BF)
    mixed = jnp.einsum("hqk,khd->qhd", p, vh, preferred_element_type=F32)
    return mixed.astype(BF).reshape(q.shape), p


def attend_back(q, k, v, p, mixed, dm):
    heads = q.shape[1] // HD
    qh = q.reshape(-1, heads, HD)
    kh = k.reshape(-1, heads, HD)
    vh = v.reshape(-1, heads, HD)
    dh = dm.reshape(-1, heads, HD)
    pf = p.astype(F32)
    dp = jnp.einsum("qhd,khd->hqk", dh, vh, preferred_element_type=F32)
    total = jnp.sum(dp * pf, -1, keepdims=True)
    ds = (pf * (dp - total)).astype(BF)
    dv = jnp.einsum("hqk,qhd->khd", p, dh, preferred_element_type=F32)
    dq = jnp.einsum("hqk,khd->qhd", ds, kh, preferred_element_type=F32) * HD**-0.5
    dk = jnp.einsum("hqk,qhd->khd", ds, qh, preferred_element_type=F32) * HD**-0.5
    return (
        dq.astype(BF).reshape(q.shape),
        dk.astype(BF).reshape(k.shape),
        dv.astype(BF).reshape(k.shape),
    )


def plain_body(
    cells,
    lengths,
    query_matrix,
    key_matrix,
    value_matrix,
    query_bias,
    value_bias,
    output_matrix,
    b_out,
    gain_one,
    shift_one,
    gain_two,
    shift_two,
    expand_weight,
    expand_bias,
    contract_weight,
    b_down,
    grad_out,
):
    slots, rows, width = cells.shape
    n_dp, n_mp = lax.axis_size("dp"), lax.axis_size("mp")
    d, z = lax.axis_index("dp"), lax.axis_index("mp")
    per = n_mp // slots
    core = d % per
    tokens = slots * rows
    part = width // n_dp
    hw = query_matrix.shape[1]
    turns = moves(n_dp, n_mp, slots)

    def bring(x):
        got = [
            lax.ppermute(
                lax.dynamic_index_in_dim(x, (t + z) % slots, 0, False), ("dp", "mp"), turns[t]
            )
            for t in range(slots)
        ]
        even = z % slots == 0
        return jnp.concatenate(
            [jnp.where(even, got[0], got[1]), jnp.where(even, got[1], got[0])], 0
        )

    def give_back(x):
        x = x.reshape(slots, rows, width)
        got = [
            lax.ppermute(
                lax.dynamic_index_in_dim(x, (t + z) % slots, 0, False),
                ("dp", "mp"),
                [(b, a) for a, b in turns[t]],
            )
            for t in range(slots)
        ]
        even = z % slots == 0
        return jnp.stack(
            [jnp.where(even, got[0], got[1]), jnp.where(even, got[1], got[0])], 0
        )

    mine = bring(cells)
    attn_own = jnp.concatenate(
        [query_matrix, key_matrix, value_matrix, output_matrix.T], 1
    )
    first = d * part

    def piece_of(w):
        return lax.dynamic_slice_in_dim(w, first, part, 0)

    half = attn_own.shape[1] // 2
    a_piece = piece_of(attn_own)
    a_left = gather(a_piece[:, :half], False)
    a_right = gather(a_piece[:, half:], True)
    u_held = gather(piece_of(expand_weight), False)
    d_held = gather(piece_of(contract_weight), True)
    grad_rows = bring(grad_out)
    small = jnp.concatenate([query_bias, value_bias, expand_bias])
    small = [small] + [shift(small, n_mp - r) for r in range(1, n_mp)]
    both = cross(lengths, 0)
    length_all = jnp.where(core == 0, jnp.concatenate([lengths, both]), jnp.concatenate([both, lengths]))
    length = lax.dynamic_index_in_dim(length_all, z, 0, False)

    attn_w = [
        jnp.concatenate([a, b], 1)
        for a, b in zip(
            assemble(a_left, attn_own[:, :half], d), assemble(a_right, attn_own[:, half:], d)
        )
    ]
    up_w = assemble(u_held, expand_weight, d)
    down_w = assemble(d_held, contract_weight, d)

    position = core * tokens + jnp.arange(tokens)
    keep = (position < length).astype(F32)[:, None]
    sib_position = (per - 1 - core) * tokens + jnp.arange(tokens)
    allowed = jnp.concatenate([position, sib_position]) < length

    x = mine.astype(F32)
    rows_one, unit_one, inv_one = layer_norm(x, gain_one, shift_one)
    rows_one = rows_one.astype(BF)
    kept = []
    attention = jnp.zeros((tokens, width), F32)
    for r in range(n_mp):
        w = attn_w[r]
        q = (dot(rows_one, w[:, :hw], 1, 0) + small[r][:hw]).astype(BF)
        k = dot(rows_one, w[:, hw : 2 * hw], 1, 0).astype(BF)
        v = (dot(rows_one, w[:, 2 * hw : 3 * hw], 1, 0) + small[r][hw : 2 * hw]).astype(BF)
        k = jnp.concatenate([k, cross(k, 0)], 0)
        v = jnp.concatenate([v, cross(v, 0)], 0)
        mixed, p = attend(q, k, v, allowed)
        kept.append((q, k, v, mixed, p))
        attention = attention + dot(mixed, w[:, 3 * hw :], 1, 1)
    middle = x + attention + b_out
    rows_two, unit_two, inv_two = layer_norm(middle, gain_two, shift_two)
    rows_two = rows_two.astype(BF)
    g = keep * grad_rows.astype(F32)
    gz = g.astype(BF)

    order = jnp.arange(0, n_dp, 2) ^ d

    def chosen(v):
        return jnp.take(v.reshape(v.shape[0], n_dp, part), order, axis=1).reshape(v.shape[0], -1)

    def other(v):
        return jnp.take(v.reshape(v.shape[0], n_dp, part), order ^ 1, axis=1).reshape(v.shape[0], -1)

    def both_cores(v):
        return jnp.concatenate([chosen(v), cross(other(v), 0)], 0)

    def weight_grad(left, right, flip):
        right = jnp.concatenate([right, cross(right, 0)], 0)
        return weight_grad_all(left, right, flip)

    def weight_grad_all(left, right, flip):
        got = dot(left, right, 0, 0).astype(BF).reshape(-1, part, right.shape[1])
        return scatter({2 * i: got[i] for i in range(got.shape[0])}, flip)

    def finish(pieces):
        total = pieces[0].astype(F32)
        for r in range(1, n_mp):
            total = total + shift(pieces[r], r).astype(F32)
        return total

    two_both = both_cores(rows_two)
    gz_both = both_cores(gz)
    result = middle + b_down
    e2 = jnp.zeros((tokens, width), F32)
    up_parts, down_parts, b_up = [], [], []
    for r in range(n_mp):
        upper = dot(rows_two, up_w[r], 1, 0) + small[r][2 * hw :]
        hidden, slope = gelu_pair(upper)
        hidden = hidden.astype(BF)
        result = result + dot(hidden, down_w[r], 1, 0)
        d_upper = (dot(gz, down_w[r], 1, 1) * slope).astype(BF)
        e2 = e2 + dot(d_upper, up_w[r], 1, 1)
        up_parts.append(weight_grad(two_both, d_upper, False))
        down_parts.append(weight_grad(gz_both, hidden, True))
        b_up.append(jnp.sum(d_upper.astype(F32), 0))
    out_cells = give_back((keep * result).astype(BF))
    grad_up = finish(up_parts)
    grad_down = finish(down_parts).T

    d_middle = g + norm_back(e2, unit_two, inv_two, gain_two)
    gm = d_middle.astype(BF)
    gm_both = both_cores(gm)
    one_both = both_cores(rows_one)
    e1 = jnp.zeros((tokens, width), F32)
    a_parts, b_q, b_v = [], [], []
    for r in range(n_mp):
        q, k, v, mixed, p = kept[r]
        w = attn_w[r]
        d_mixed = dot(gm, w[:, 3 * hw :], 1, 0).astype(BF)
        dq, dk, dv = attend_back(q, k, v, p, mixed, d_mixed)
        dk_all = (dk.astype(F32) + jnp.roll(cross(dk, 0), tokens, 0).astype(F32)).astype(BF)
        dv_all = (dv.astype(F32) + jnp.roll(cross(dv, 0), tokens, 0).astype(F32)).astype(BF)
        dq_all = jnp.concatenate([dq, cross(dq, 0)], 0)
        e1 = (
            e1
            + dot(dq, w[:, :hw], 1, 1)
            + dot(dk_all[:tokens], w[:, hw : 2 * hw], 1, 1)
            + dot(dv_all[:tokens], w[:, 2 * hw : 3 * hw], 1, 1)
        )
        b_q.append(jnp.sum(dq.astype(F32), 0))
        b_v.append(jnp.sum(dv_all[:tokens].astype(F32), 0))
        qkv_part = weight_grad_all(one_both, jnp.concatenate([dq_all, dk_all, dv_all], 1), r % 2 == 1)
        o_part = weight_grad(gm_both, mixed, r % 2 == 0)
        a_parts.append(jnp.concatenate([qkv_part, o_part], 1))
    d_cells = d_middle + norm_back(e1, unit_one, inv_one, gain_one)
    grad_cells = give_back(d_cells.astype(BF)).astype(F32)
    grad_attn = finish(a_parts)

    split_mp = [jnp.stack(b_q).reshape(n_mp, n_dp, -1), jnp.stack(b_v).reshape(n_mp, n_dp, -1), jnp.stack(b_up).reshape(n_mp, n_dp, -1)]
    sums = [
        jnp.sum(d_middle, 0),
        jnp.sum(e1 * unit_one, 0),
        jnp.sum(e1, 0),
        jnp.sum(e2 * unit_two, 0),
        jnp.sum(e2, 0),
        jnp.sum(g, 0),
    ]
    split_dp = [jnp.roll(jnp.swapaxes(s.reshape(n_dp, n_mp, -1), 0, 1), -z, 0) for s in sums]
    packed = jnp.concatenate(split_mp + split_dp, 2)
    packed = jnp.take(packed, jnp.arange(n_dp) ^ d, axis=1)
    packed = packed[:, 0::2] + cross(packed[:, 1::2], 0)
    packed = scatter({2 * i: packed[:, i] for i in range(packed.shape[1])}, False)
    vec = packed[0]
    for r in range(1, n_mp):
        vec = vec + shift(packed[r], r)
    nq = split_mp[0].shape[2]
    nu = split_mp[2].shape[2]
    ns = split_dp[0].shape[2]
    vq, vv, vu = vec[:nq], vec[nq : 2 * nq], vec[2 * nq : 2 * nq + nu]
    rest = [vec[2 * nq + nu + i * ns : 2 * nq + nu + (i + 1) * ns] for i in range(6)]
    return (
        out_cells,
        grad_cells,
        grad_attn[:, :hw],
        grad_attn[:, hw : 2 * hw],
        grad_attn[:, 2 * hw : 3 * hw],
        vq,
        vv,
        grad_attn[:, 3 * hw :].T,
        rest[0],
        rest[1],
        rest[2],
        rest[3],
        rest[4],
        grad_up,
        vu,
        grad_down,
        rest[5],
    )


def dg(a, b, ca, cb):
    return lax.dot_general(a, b, (((ca,), (cb,)), ((), ())), preferred_element_type=F32)


def lane_block(start, size=128):
    return pl.ds(pl.multiple_of(start, size), size)


class Place:
    def __init__(self):
        self.d, self.z = lax.axis_index("dp"), lax.axis_index("mp")
        self.bit = [lax.rem(self.d // (1 << b), 2) for b in range(3)]
        self.core = self.bit[0]
        self.base = self.d - self.core

    def across(self, i):
        v = self.d
        for b in range(3):
            if i >> b & 1:
                v = v + (1 << b) * (1 - 2 * self.bit[b])
        return v

    def rows(self, i):
        return lane_block(self.across(i) * PART, PART)

    def greet(self):
        barrier = pltpu.get_barrier_semaphore()
        for step in range(1, 4):
            for c in range(2):
                pl.semaphore_signal(
                    barrier,
                    inc=1,
                    device_id=(self.base + c, lax.rem(self.z + step, 4)),
                    device_id_type=MESH,
                )
        for i in (1, 2, 4):
            pl.semaphore_signal(barrier, inc=1, device_id=(self.across(i), self.z), device_id_type=MESH)
        pl.semaphore_wait(barrier, 9)


def remote(src, dst, send, recv, device):
    return pltpu.make_async_remote_copy(
        src_ref=src, dst_ref=dst, send_sem=send, recv_sem=recv, device_id=device, device_id_type=MESH
    )


class Unit:
    def __init__(self, place, own, at, parts, zsend, zrecv, send, recv, flip):
        self.p, self.own, self.at, self.parts = place, own, at, parts
        self.zsend, self.zrecv, self.send, self.recv = zsend, zrecv, send, recv
        self.first, self.second = (4, 2) if flip else (2, 4)

    def along(self, k, slot_from, slot_to, right):
        p = self.p
        device = (p.d, p.z + 1 if right else p.z - 1)
        return [
            remote(
                self.own(q) if slot_from is None else self.at(slot_from, 0, q),
                self.at(slot_to, 0, q),
                self.zsend.at[k, q],
                self.zrecv.at[slot_to - 1, q],
                device,
            )
            for q in range(self.parts)
        ]

    def steps(self):
        z = self.p.z
        inner = jnp.logical_and(z >= 1, z <= 2)
        return [
            (z <= 2, (0, None, 3, True)),
            (z >= 1, (1, None, 1, False)),
            (inner, (2, 3, 2, True)),
            (inner, (3, 1, 2, False)),
            (z == 1, (4, 2, 3, False)),
            (z == 2, (5, 2, 1, True)),
        ]

    def go(self, k):
        cond, what = self.steps()[k]

        @pl.when(cond)
        def _():
            for c in self.along(*what):
                c.start()

    def start(self):
        self.go(0)
        self.go(1)

    def landed(self, slot):
        for q in range(self.parts):
            here = self.at(slot, 0, q)
            remote(here, here, self.zsend.at[0, q], self.zrecv.at[slot - 1, q], (self.p.across(1), self.p.z)).wait_recv()

    def xy(self, slot, k, i, bit):
        here = self.at(slot, i, None)
        return remote(
            here,
            here,
            self.send.at[slot - 1, k],
            self.recv.at[slot - 1, i ^ bit],
            (self.p.across(bit), self.p.z),
        )

    def arrived(self, slot, i):
        here = self.at(slot, i, None)
        remote(here, here, self.send.at[slot - 1, 0], self.recv.at[slot - 1, i], (self.p.across(1), self.p.z)).wait_recv()

    def one(self, slot):
        self.xy(slot, 0, 0, self.first).start()

    def z_one(self):
        z = self.p.z

        @pl.when(z >= 1)
        def _():
            self.landed(3)

        self.go(2)

        @pl.when(z <= 2)
        def _():
            self.landed(1)

        self.go(3)

        @pl.when(z >= 1)
        def _():
            self.one(3)

        @pl.when(z <= 2)
        def _():
            self.one(1)

    def z_two(self):
        self.landed(2)
        self.go(4)
        self.go(5)
        self.one(2)

    def z_three(self):
        z = self.p.z

        @pl.when(z == 0)
        def _():
            self.landed(3)
            self.one(3)

        @pl.when(z == 3)
        def _():
            self.landed(1)
            self.one(1)

    def two(self, slot):
        self.arrived(slot, self.first)
        self.xy(slot, 1, 0, self.second).start()
        self.xy(slot, 2, self.first, self.second).start()

    def three(self, slot):
        self.arrived(slot, self.second)
        self.arrived(slot, self.first + self.second)
        for k, i in enumerate((0, 2, 4, 6)):
            self.xy(slot, 3 + k, i, 1).start()

    def whole(self, slot):
        for i in (1, 3, 5, 7):
            self.arrived(slot, i)

    def finish(self):
        for k in range(6):
            cond, what = self.steps()[k]

            @pl.when(cond)
            def _(what=what):
                for c in self.along(*what):
                    c.wait_send()

        for slot in (1, 2, 3):
            self.xy(slot, 0, 0, self.first).wait_send()
            self.xy(slot, 1, 0, self.second).wait_send()
            self.xy(slot, 2, self.first, self.second).wait_send()
            for k, i in enumerate((0, 2, 4, 6)):
                self.xy(slot, 3 + k, i, 1).wait_send()


def bring_copies(p, src, dst, sends, recvs, here):
    for s in range(2):
        target = (p.base + p.z // 2, 2 * p.core + s)
        half = lax.rem(p.z, 2)
        rows = lane_block(half * 256, 256)
        same = jnp.logical_and(p.core == p.z // 2, p.z == 2 * p.core + s)

        @pl.when(same)
        def _():
            pltpu.make_async_copy(src.at[s], dst.at[rows], here).start()

        @pl.when(jnp.logical_not(same))
        def _():
            remote(src.at[s], dst.at[rows], sends.at[s], recvs.at[half], target).start()


def bring_wait(p, dst, recvs, here):
    for half in range(2):
        block = dst.at[pl.ds(half * 256, 256)]
        same = jnp.logical_and(p.core == p.z // 2, lax.rem(p.z, 2) == half)

        @pl.when(same)
        def _():
            pltpu.make_async_copy(block, block, here).wait()

        @pl.when(jnp.logical_not(same))
        def _():
            remote(block, block, recvs.at[half], recvs.at[half], (p.across(1), p.z)).wait_recv()


def bring_sent(p, src, sends):
    for s in range(2):
        same = jnp.logical_and(p.core == p.z // 2, p.z == 2 * p.core + s)

        @pl.when(jnp.logical_not(same))
        def _():
            remote(src.at[s], src.at[s], sends.at[s], sends.at[s], (p.across(1), p.z)).wait_send()


def norm_stats(x):
    center = x - jnp.mean(x, -1, keepdims=True)
    inverse = lax.rsqrt(jnp.mean(center * center, -1, keepdims=True) + EPS)
    return center * inverse, inverse


def each_rows(size, total, f):
    def step(i, carry):
        f(pl.ds(pl.multiple_of(i * size, size), size))
        return carry

    lax.fori_loop(0, total // size, step, 0)


def chosen_both(p, t_ref, both_ref, sends, recvs):
    copies = []
    for k, i in enumerate((0, 2, 4, 6)):
        block = pl.ds(k * PART, PART)
        both_ref[block, 0:T] = t_ref[p.rows(i), :]
        copies.append(
            remote(
                t_ref.at[p.rows(i ^ 1)],
                both_ref.at[block, T : 2 * T],
                sends.at[k],
                recvs.at[k],
                (p.across(1), p.z),
            )
        )
    for c in copies:
        c.start()
    return copies


def forward_kernel(
    cells, grad, len_own, wq, wk, wv, wo, up, down, small_own, b_out, gain1, shift1, gain2, shift2, b_down,
    x_out, rows1_out, q_out, k_out, v_out, mix_out, e_out, r_out, wa_out, wo_out, wu, wd, res_out, dm_out, gu_out, gd_out, vec_out,
    xv, gv, rows1, wav, wov, qv, kv, vv, mix, eb, rv, bias, vt, ot, middle, rows2, tt, xb, gb, acc, e2,
    uv, dv, ho, du, hs, ds, gus, gds, len_sib, small1, small2, small3,
    a_zs, a_zr, a_s, a_r, o_zs, o_zr, o_s, o_r, u_zs, u_zr, u_s, u_r, d_zs, d_zr, d_s, d_r,
    act_s, act_r, sm_s, sm_r, kv_s, kv_r, both_s, both_r, hd_s, hd_r, credit, loc, load, store,
):
    p = Place()
    small = [small_own, small1, small2, small3]
    sibling = (p.across(1), p.z)

    ws = (wq, wk, wv)
    own_rows = p.rows(0)

    def a_at(slot, i, part):
        if part is None:
            return wav.at[slot, p.rows(i)]
        return wav.at[slot, p.rows(i), pl.ds(part * 256, 256)]

    unit_a = Unit(p, lambda q: ws[q].at[own_rows], a_at, 3, a_zs, a_zr, a_s, a_r, False)
    unit_o = Unit(
        p,
        lambda q: wo.at[:, own_rows],
        lambda slot, i, q: wov.at[pl.ds(slot * 256, 256), p.rows(i)],
        1, o_zs, o_zr, o_s, o_r, True,
    )
    unit_u = Unit(p, lambda q: up.at[own_rows], lambda slot, i, q: wu.at[slot - 1, p.rows(i)], 1, u_zs, u_zr, u_s, u_r, False)
    unit_d = Unit(p, lambda q: down.at[own_rows], lambda slot, i, q: wd.at[slot - 1, p.rows(i)], 1, d_zs, d_zr, d_s, d_r, True)

    own_loads = [pltpu.make_async_copy(w, wav.at[0, :, pl.ds(k * 256, 256)], loc.at[k]) for k, w in enumerate(ws)]
    own_loads.append(pltpu.make_async_copy(wo, wov.at[pl.ds(0, 256)], loc.at[3]))
    for c in own_loads:
        c.start()
    first_loads = [pltpu.make_async_copy(up, uv.at[0], load.at[0, 0]), pltpu.make_async_copy(down, dv.at[0], load.at[1, 0])]
    for c in first_loads:
        c.start()

    p.greet()
    unit_a.start()
    bring_copies(p, cells, xv, act_s.at[0], act_r.at[0], loc.at[4])
    small_copies = []
    for r in (1, 2, 3):
        small_copies.append(remote(small_own, small[r], sm_s.at[r], sm_r.at[r], (p.d, lax.rem(p.z + 4 - r, 4))))
    small_copies.append(remote(len_own, len_sib, sm_s.at[0], sm_r.at[0], sibling))
    for c in small_copies:
        c.start()
    unit_a.z_one()
    unit_a.z_two()
    unit_a.z_three()
    unit_o.start()
    unit_u.start()
    for slot in (1, 3, 2):
        unit_a.two(slot)

    bring_wait(p, xv, act_r.at[0], loc.at[4])
    bring_copies(p, grad, gv, act_s.at[1], act_r.at[1], loc.at[5])
    unit_d.start()

    def first_norm(rows):
        unit, _ = norm_stats(xv[rows, :].astype(F32))
        rows1[rows, :] = (unit * gain1[...] + shift1[...]).astype(BF)

    each_rows(128, T, first_norm)
    outs = [pltpu.make_async_copy(xv, x_out, store.at[0]), pltpu.make_async_copy(rows1, rows1_out, store.at[1])]
    for c in outs:
        c.start()
    for slot in (1, 3, 2):
        unit_a.three(slot)
    unit_o.z_one()
    unit_o.z_two()
    unit_o.z_three()
    unit_u.z_one()

    small_copies[3].wait_recv()
    slot_row = lax.rem(p.z, 2)
    near = jnp.where(p.z // 2 == p.core, 1.0, 0.0)
    length = near * len_own[pl.ds(slot_row, 1), :] + (1.0 - near) * len_sib[pl.ds(slot_row, 1), :]
    length = length[:, :1]
    lane = lax.broadcasted_iota(jnp.int32, (1, 128), 1)
    key = lax.broadcasted_iota(jnp.int32, (2 * T, 128), 0)
    key = jnp.where(key < T, key + p.core * T, key - T + (1 - p.core) * T)
    barred = jnp.where(key.astype(F32) < length, 0.0, -1e30)
    bias[0] = jnp.where(lane == 64, barred, 0.0).astype(BF)
    bias[1] = jnp.where(lane == 0, barred, 0.0).astype(BF)

    def kept(rows_start, size):
        row = lax.broadcasted_iota(jnp.int32, (size, 1), 0) + rows_start + p.core * T
        return row.astype(F32) < length

    for c in own_loads:
        c.wait()
    for r in (1, 2, 3):
        small_copies[r - 1].wait_recv()

    kv_copies = []

    def project(r):
        b = small[r]
        x = rows1[...]
        qv[r] = (dg(x, wav[r, :, 0:256], 1, 0) + b[:, 0:256]).astype(BF)
        kv[r, 0:T, :] = dg(x, wav[r, :, 256:512], 1, 0).astype(BF)
        vv[r, 0:T, :] = (dg(x, wav[r, :, 512:768], 1, 0) + b[:, 256:512]).astype(BF)
        cs = [
            remote(ref.at[r, pl.ds(0, T)], ref.at[r, pl.ds(T, T)], kv_s.at[r, n], kv_r.at[r, n], sibling)
            for n, ref in enumerate((kv, vv))
        ]
        for c in cs:
            c.start()
        kv_copies.append(cs)

    def e_copy(head, slot):
        return pltpu.make_async_copy(eb.at[slot], e_out.at[head], store.at[2 + slot])

    def attend(r):
        for c in kv_copies[r]:
            c.wait_recv()
        vt[...] = jnp.transpose(vv[r], (1, 0))

        def pair(j, carry):
            cols = lane_block(j * 128)
            kp = kv[r, :, cols]
            qp = qv[r, :, cols] * BF(HD**-0.5)
            for h in range(2):
                mine = (lane < 64) if h == 0 else (lane >= 64)
                one = lane == (64 if h == 0 else 0)
                ka = jnp.where(mine, kp, bias[h])
                qa = jnp.where(mine, qp, jnp.where(one, BF(1), BF(0)))
                s = dg(ka, qa, 1, 1)
                e = jnp.exp(s - jnp.max(s, 0, keepdims=True))
                inv = 1.0 / jnp.sum(e, 0, keepdims=True)
                head = r * 4 + 2 * j + h
                if r == 0:
                    @pl.when(j > 0)
                    def _():
                        e_copy(head - 2, h).wait()
                else:
                    e_copy(head - 2, h).wait()
                eb[h] = e.astype(BF)
                e_copy(head, h).start()
                feats = pl.ds(pl.multiple_of(j * 128 + h * 64, 64), 64)
                ot[feats, :] = (dg(vt[feats, :], eb[h], 1, 0) * inv).astype(BF)
                rv[head] = inv
            return carry

        lax.fori_loop(0, 2, pair, 0)
        mix[:, r * 256 : (r + 1) * 256] = jnp.transpose(ot[...], (1, 0))

    project(0)
    unit_u.z_two()
    for slot in (1, 2, 3):
        unit_a.whole(slot)
    project(1)
    unit_u.z_three()
    for slot in (1, 3, 2):
        unit_o.two(slot)
    attend(0)
    unit_d.z_one()
    project(2)
    project(3)
    for slot in (1, 3, 2):
        unit_o.three(slot)
        unit_u.two(slot)
    unit_d.z_two()
    unit_d.z_three()
    attend(1)
    for slot in (1, 3, 2):
        unit_u.three(slot)
        unit_d.two(slot)
    attend(2)
    for slot in (1, 3, 2):
        unit_d.three(slot)
        unit_o.whole(slot)
    attend(3)
    for h in range(2):
        e_copy(14 + h, h).wait()

    outs += [
        pltpu.make_async_copy(wav, wa_out, store.at[4]),
        pltpu.make_async_copy(wov, wo_out, store.at[5]),
        pltpu.make_async_copy(qv, q_out, store.at[6]),
        pltpu.make_async_copy(kv, k_out, store.at[7]),
        pltpu.make_async_copy(vv, v_out, store.at[8]),
        pltpu.make_async_copy(mix, mix_out, store.at[9]),
        pltpu.make_async_copy(rv, r_out, store.at[10]),
    ]
    for c in outs[2:]:
        c.start()

    for n in range(2):
        cols = pl.ds(n * 512, 512)
        middle[:, cols] = dg(mix[...], wov[:, cols], 1, 0)

    def second_norm(rows):
        m = middle[rows, :] + xv[rows, :].astype(F32) + b_out[...]
        middle[rows, :] = m
        unit, _ = norm_stats(m)
        rows2[rows, :] = (unit * gain2[...] + shift2[...]).astype(BF)
        acc[rows, :] = m + b_down[...]

    each_rows(128, T, second_norm)
    tt[...] = jnp.transpose(rows2[...], (1, 0))
    both = chosen_both(p, tt, xb, both_s.at[0], both_r.at[0])
    bring_wait(p, gv, act_r.at[1], loc.at[5])

    def mask_grad(i, carry):
        rows = pl.ds(pl.multiple_of(i * 128, 128), 128)
        gv[rows, :] = jnp.where(kept(i * 128, 128), gv[rows, :].astype(F32), 0.0).astype(BF)
        return carry

    lax.fori_loop(0, T // 128, mask_grad, 0)
    for c in both:
        c.wait_send()
    tt[...] = jnp.transpose(gv[...], (1, 0))
    both2 = chosen_both(p, tt, gb, both_s.at[1], both_r.at[1])

    order = (0, 1, 3, 2)

    def load_copies(n):
        r = order[n]
        return [
            pltpu.make_async_copy(wu.at[r - 1], uv.at[n % 2], load.at[0, n % 2]),
            pltpu.make_async_copy(wd.at[r - 1], dv.at[n % 2], load.at[1, n % 2]),
        ]

    def hidden(n):
        r, slot = order[n], n % 2
        for k in range(2):
            c = pl.ds(k * 512, 512)
            upper = dg(rows2[...], uv[slot, :, c], 1, 0) + small[r][:, 512 + k * 512 : 1024 + k * 512]
            act, slope = gelu_pair(upper)
            ho[slot, :, c] = act.astype(BF)
            d_up = (dg(gv[...], dv[slot, c, :], 1, 1) * slope).astype(BF)
            du[slot, :, c] = d_up
            vec_out[r : r + 1, c] = jnp.sum(d_up.astype(F32), 0, keepdims=True)
        if n >= 2:
            pl.semaphore_wait(credit, 1)
        cs = [
            remote(ho.at[slot], hs.at[slot], hd_s.at[0, slot], hd_r.at[0, slot], sibling),
            remote(du.at[slot], ds.at[slot], hd_s.at[1, slot], hd_r.at[1, slot], sibling),
        ]
        for c in cs:
            c.start()
        for k in range(2):
            c = pl.ds(k * 512, 512)
            acc[:, c] = acc[:, c] + dg(ho[slot], dv[slot, :, c], 1, 0)
            new = dg(du[slot], uv[slot, c, :], 1, 1)
            e2[:, c] = new if n == 0 else e2[:, c] + new
        return cs

    g_stores = [None, None]

    def weight_grads(n, cs):
        r, slot = order[n], n % 2
        for c in cs:
            c.wait_recv()
        if n >= 1:
            for c in g_stores:
                c.wait()
        gus[...] = (dg(xb[:, 0:T], du[slot], 1, 0) + dg(xb[:, T : 2 * T], ds[slot], 1, 0)).astype(BF)
        gds[...] = (dg(gb[:, 0:T], ho[slot], 1, 0) + dg(gb[:, T : 2 * T], hs[slot], 1, 0)).astype(BF)
        if n < 2:
            pl.semaphore_signal(credit, inc=1, device_id=sibling, device_id_type=MESH)
        g_stores[0] = pltpu.make_async_copy(gus, gu_out.at[r], store.at[11])
        g_stores[1] = pltpu.make_async_copy(gds, gd_out.at[r], store.at[12])
        for c in g_stores:
            c.start()
        for c in cs:
            c.wait_send()

    for c in first_loads:
        c.wait()
    held = [hidden(0)]
    for n in range(1, 4):
        unit_u.whole(order[n])
        unit_d.whole(order[n])
        cs = load_copies(n)
        for c in cs:
            c.start()
        if n == 1:
            for c in both + both2:
                c.wait_recv()
        if n >= 2:
            weight_grads(n - 2, held[n - 2])
        for c in cs:
            c.wait()
        held.append(hidden(n))
    weight_grads(2, held[2])
    weight_grads(3, held[3])

    vec_out[4:16, :] = jnp.zeros((12, width_of(vec_out)), F32)

    def last(i, carry):
        rows = pl.ds(pl.multiple_of(i * 128, 128), 128)
        res = jnp.where(kept(i * 128, 128), acc[rows, :], 0.0)
        rows2[rows, :] = res.astype(BF)
        unit, inverse = norm_stats(middle[rows, :])
        e = e2[rows, :]
        g = gv[rows, :].astype(F32)
        u = e * gain2[...]
        d_mid = g + inverse * (u - jnp.mean(u, -1, keepdims=True) - unit * jnp.mean(u * unit, -1, keepdims=True))
        middle[rows, :] = d_mid
        for k, v in enumerate((d_mid, e * unit, e, g)):
            vec_out[4 + k : 5 + k, :] += jnp.sum(v, 0, keepdims=True)
        return carry

    lax.fori_loop(0, T // 128, last, 0)
    ends = [pltpu.make_async_copy(rows2, res_out, store.at[13]), pltpu.make_async_copy(middle, dm_out, store.at[14])]
    for c in ends:
        c.start()
    for c in ends + outs + g_stores:
        c.wait()
    for c in both2 + small_copies:
        c.wait_send()
    for cs in kv_copies:
        for c in cs:
            c.wait_send()
    for unit in (unit_a, unit_o, unit_u, unit_d):
        unit.finish()
    bring_sent(p, cells, act_s.at[0])
    bring_sent(p, grad, act_s.at[1])


def width_of(ref):
    return ref.shape[-1]

def forward(*args):
    s = jax.ShapeDtypeStruct
    outs = [
        (T, 1024), (T, 1024), (4, T, 256), (4, 2 * T, 256), (4, 2 * T, 256), (T, 1024), (16, 2 * T, T), (16, 1, T),
        (4, 1024, 768), (1024, 1024), (3, 1024, 1024), (3, 1024, 1024), (T, 1024), (T, 1024), (4, T, 1024), (4, T, 1024), (16, 1024),
    ]
    wide = (7, 13, 16)
    hbm, fast = pl.BlockSpec(memory_space=pltpu.HBM), pl.BlockSpec(memory_space=pltpu.VMEM)
    b, f, dma = (lambda *x: pltpu.VMEM(x, BF)), (lambda *x: pltpu.VMEM(x, F32)), (lambda *x: pltpu.SemaphoreType.DMA(x))
    sems = []
    for parts in (3, 1, 1, 1):
        sems += [dma(6, parts), dma(3, parts), dma(3, 7), dma(3, 8)]
    return pl.pallas_call(
        forward_kernel,
        out_shape=[s(o, F32 if n in wide else BF) for n, o in enumerate(outs)],
        in_specs=[hbm, hbm, fast] + [hbm] * 6 + [fast] * 7,
        out_specs=[hbm] * 16 + [fast],
        scratch_shapes=[
            b(T, 1024), b(T, 1024), b(T, 1024), b(4, 1024, 768), b(1024, 1024), b(4, T, 256), b(4, 2 * T, 256), b(4, 2 * T, 256),
            b(T, 1024), b(2, 2 * T, T), f(16, 1, T), b(2, 2 * T, 128), b(256, 2 * T), b(256, T), f(T, 1024), b(T, 1024),
            b(1024, T), b(T, 2 * T), b(T, 2 * T), f(T, 1024), f(T, 1024),
            b(2, 1024, 1024), b(2, 1024, 1024), b(2, T, 1024), b(2, T, 1024), b(2, T, 1024), b(2, T, 1024), b(T, 1024), b(T, 1024),
            f(8, 128), f(1, 1536), f(1, 1536), f(1, 1536),
        ]
        + sems
        + [dma(2, 2), dma(2, 2), dma(4), dma(4), dma(4, 2), dma(4, 2), dma(2, 4), dma(2, 4), dma(2, 2), dma(2, 2),
           pltpu.SemaphoreType.REGULAR, dma(6), dma(2, 2), dma(15)],
        compiler_params=pltpu.CompilerParams(collective_id=0, has_side_effects=True, vmem_limit_bytes=62 * 2**20),
    )(*args)


def body(*args):
    if lax.axis_size("dp") == 8 and lax.axis_size("mp") == 4:
        return fused_body(*args)
    return plain_body(*args)


def fused_body(
    cells,
    lengths,
    query_matrix,
    key_matrix,
    value_matrix,
    query_bias,
    value_bias,
    output_matrix,
    b_out,
    gain_one,
    shift_one,
    gain_two,
    shift_two,
    expand_weight,
    expand_bias,
    contract_weight,
    b_down,
    grad_out,
):
    slots, rows, width = cells.shape
    n_dp, n_mp = lax.axis_size("dp"), lax.axis_size("mp")
    d, z = lax.axis_index("dp"), lax.axis_index("mp")
    per = n_mp // slots
    core = d % per
    tokens = slots * rows
    part = width // n_dp
    hw = query_matrix.shape[1]
    turns = moves(n_dp, n_mp, slots)

    def bring(x):
        got = [
            lax.ppermute(
                lax.dynamic_index_in_dim(x, (t + z) % slots, 0, False), ("dp", "mp"), turns[t]
            )
            for t in range(slots)
        ]
        even = z % slots == 0
        return jnp.concatenate(
            [jnp.where(even, got[0], got[1]), jnp.where(even, got[1], got[0])], 0
        )

    def give_back(x):
        x = x.reshape(slots, rows, width)
        got = [
            lax.ppermute(
                lax.dynamic_index_in_dim(x, (t + z) % slots, 0, False),
                ("dp", "mp"),
                [(b, a) for a, b in turns[t]],
            )
            for t in range(slots)
        ]
        even = z % slots == 0
        return jnp.stack(
            [jnp.where(even, got[0], got[1]), jnp.where(even, got[1], got[0])], 0
        )

    row = lambda v: v.reshape(1, -1)
    small = row(jnp.concatenate([query_bias, value_bias, expand_bias]))
    len_own = jnp.pad(jnp.broadcast_to(lengths.astype(F32)[:, None], (slots, 128)), ((0, 8 - slots), (0, 0)))
    (x, rows_one, q_all, k_all, v_all, mixed_all, e_all, r_all, wa, wo, _, _, res, d_middle, gu, gd, vec) = forward(
        cells, grad_out, len_own, query_matrix, key_matrix, value_matrix, output_matrix, expand_weight, contract_weight,
        small, row(b_out), row(gain_one), row(shift_one), row(gain_two), row(shift_two), row(b_down),
    )
    _, unit_one, inv_one = layer_norm(x.astype(F32), gain_one, shift_one)

    order = jnp.arange(0, n_dp, 2) ^ d

    def chosen(v):
        return jnp.take(v.reshape(v.shape[0], n_dp, part), order, axis=1).reshape(v.shape[0], -1)

    def other(v):
        return jnp.take(v.reshape(v.shape[0], n_dp, part), order ^ 1, axis=1).reshape(v.shape[0], -1)

    def both_cores(v):
        return jnp.concatenate([chosen(v), cross(other(v), 0)], 0)

    def weight_grad(left, right, flip):
        right = jnp.concatenate([right, cross(right, 0)], 0)
        return weight_grad_all(left, right, flip)

    def weight_grad_all(left, right, flip):
        got = dot(left, right, 0, 0).astype(BF).reshape(-1, part, right.shape[1])
        return scatter({2 * i: got[i] for i in range(got.shape[0])}, flip)

    def finish(pieces):
        total = pieces[0].astype(F32)
        for r in range(1, n_mp):
            total = total + shift(pieces[r], r).astype(F32)
        return total

    def plane(block, flip):
        got = block.reshape(-1, part, block.shape[-1])
        return scatter({2 * i: got[i] for i in range(got.shape[0])}, flip)

    up_parts = [plane(gu[r], False) for r in range(n_mp)]
    down_parts = [plane(gd[r], True) for r in range(n_mp)]
    b_up = [vec[r] for r in range(n_mp)]
    out_cells = give_back(res)
    grad_up = finish(up_parts)
    grad_down = finish(down_parts).T
    gm = d_middle.astype(BF)
    gm_both = both_cores(gm)
    one_both = both_cores(rows_one)
    e1 = jnp.zeros((tokens, width), F32)
    a_parts, b_q, b_v = [], [], []
    for r in range(n_mp):
        q, k, v, mixed = q_all[r], k_all[r], v_all[r], mixed_all[:, r * hw : (r + 1) * hw]
        heads = hw // HD
        p = jnp.swapaxes(e_all[r * heads : (r + 1) * heads].astype(F32) * r_all[r * heads : (r + 1) * heads], 1, 2).astype(BF)
        w = wa[r]
        d_mixed = dot(gm, wo[r * hw : (r + 1) * hw], 1, 1).astype(BF)
        dq, dk, dv = attend_back(q, k, v, p, mixed, d_mixed)
        dk_all = (dk.astype(F32) + jnp.roll(cross(dk, 0), tokens, 0).astype(F32)).astype(BF)
        dv_all = (dv.astype(F32) + jnp.roll(cross(dv, 0), tokens, 0).astype(F32)).astype(BF)
        dq_all = jnp.concatenate([dq, cross(dq, 0)], 0)
        e1 = (
            e1
            + dot(dq, w[:, :hw], 1, 1)
            + dot(dk_all[:tokens], w[:, hw : 2 * hw], 1, 1)
            + dot(dv_all[:tokens], w[:, 2 * hw : 3 * hw], 1, 1)
        )
        b_q.append(jnp.sum(dq.astype(F32), 0))
        b_v.append(jnp.sum(dv_all[:tokens].astype(F32), 0))
        qkv_part = weight_grad_all(one_both, jnp.concatenate([dq_all, dk_all, dv_all], 1), r % 2 == 1)
        o_part = weight_grad(gm_both, mixed, r % 2 == 0)
        a_parts.append(jnp.concatenate([qkv_part, o_part], 1))
    d_cells = d_middle + norm_back(e1, unit_one, inv_one, gain_one)
    grad_cells = give_back(d_cells.astype(BF)).astype(F32)
    grad_attn = finish(a_parts)

    split_mp = [jnp.stack(b_q).reshape(n_mp, n_dp, -1), jnp.stack(b_v).reshape(n_mp, n_dp, -1), jnp.stack(b_up).reshape(n_mp, n_dp, -1)]
    sums = [
        vec[4],
        jnp.sum(e1 * unit_one, 0),
        jnp.sum(e1, 0),
        vec[5],
        vec[6],
        vec[7],
    ]
    split_dp = [jnp.roll(jnp.swapaxes(s.reshape(n_dp, n_mp, -1), 0, 1), -z, 0) for s in sums]
    packed = jnp.concatenate(split_mp + split_dp, 2)
    packed = jnp.take(packed, jnp.arange(n_dp) ^ d, axis=1)
    packed = packed[:, 0::2] + cross(packed[:, 1::2], 0)
    packed = scatter({2 * i: packed[:, i] for i in range(packed.shape[1])}, False)
    vec = packed[0]
    for r in range(1, n_mp):
        vec = vec + shift(packed[r], r)
    nq = split_mp[0].shape[2]
    nu = split_mp[2].shape[2]
    ns = split_dp[0].shape[2]
    vq, vv, vu = vec[:nq], vec[nq : 2 * nq], vec[2 * nq : 2 * nq + nu]
    rest = [vec[2 * nq + nu + i * ns : 2 * nq + nu + (i + 1) * ns] for i in range(6)]
    return (
        out_cells,
        grad_cells,
        grad_attn[:, :hw],
        grad_attn[:, hw : 2 * hw],
        grad_attn[:, 2 * hw : 3 * hw],
        vq,
        vv,
        grad_attn[:, 3 * hw :].T,
        rest[0],
        rest[1],
        rest[2],
        rest[3],
        rest[4],
        grad_up,
        vu,
        grad_down,
        rest[5],
    )


def solution(mesh):
    return jax.shard_map(
        body,
        mesh=mesh,
        in_specs=(
            P("dp", "mp", None),
            P("dp"),
            P(None, "mp"),
            P(None, "mp"),
            P(None, "mp"),
            P("mp"),
            P("mp"),
            P("mp", None),
            P(),
            P(),
            P(),
            P(),
            P(),
            P(None, "mp"),
            P("mp"),
            P("mp", None),
            P(),
            P("dp", "mp", None),
        ),
        out_specs=(
            P("dp", "mp", None),
            P("dp", "mp", None),
            P("dp", "mp"),
            P("dp", "mp"),
            P("dp", "mp"),
            P(("mp", "dp")),
            P(("mp", "dp")),
            P("mp", "dp"),
            P(("dp", "mp")),
            P(("dp", "mp")),
            P(("dp", "mp")),
            P(("dp", "mp")),
            P(("dp", "mp")),
            P("dp", "mp"),
            P(("mp", "dp")),
            P("mp", "dp"),
            P(("dp", "mp")),
        ),
        check_vma=False,
    )
```

```python
import jax
import jax.numpy as jnp
from jax import lax
from jax.experimental import pallas as pl
from jax.experimental.pallas import tpu as pltpu
from jax.sharding import PartitionSpec as P

HD = 64
EPS = 1e-05
BF = jnp.bfloat16
F32 = jnp.float32
MESH = pl.DeviceIdType.MESH
T = 512
PART = 128


def dot(a, b, ca, cb):
    return lax.dot_general(a, b, (((ca,), (cb,)), ((), ())), preferred_element_type=F32)


def cross(x, bit):
    n = lax.axis_size("dp")
    return lax.ppermute(x, "dp", [(i, i ^ (1 << bit)) for i in range(n)])


def shift(x, by):
    n = lax.axis_size("mp")
    return lax.ppermute(x, "mp", [(i, (i + by) % n) for i in range(n)])


def moves(n_dp, n_mp, slots):
    per = n_mp // slots
    turns = []
    for t in range(slots):
        pairs = []
        for d in range(n_dp):
            for m in range(n_mp):
                s = (t + m) % slots
                base, c = d - d % per, d % per
                target = (base + m // slots, c * slots + s)
                pairs.append((d * n_mp + m, target[0] * n_mp + target[1]))
        turns.append(pairs)
    return turns


def plane_bits(n_dp, flip):
    bits = list(range(1, n_dp.bit_length() - 1))
    return bits[::-1] if flip else bits


def gather(piece, flip):
    n_dp, n_mp = lax.axis_size("dp"), lax.axis_size("mp")
    stack = jnp.stack([shift(piece, n_mp - r) for r in range(1, n_mp)])
    held = {0: stack}
    for bit in plane_bits(n_dp, flip) + [0]:
        held.update({i ^ (1 << bit): cross(v, bit) for i, v in list(held.items())})
    return held


def assemble(held, own, d):
    n = len(held)
    stack = jnp.stack([held[i] for i in range(n)])
    order = jnp.arange(n) ^ d
    placed = jnp.take(stack, order, axis=0)
    placed = jnp.moveaxis(placed, 0, 1).reshape((stack.shape[1], -1, stack.shape[-1]))
    return [own] + [placed[r] for r in range(placed.shape[0])]


def scatter(blocks, flip):
    n_dp = lax.axis_size("dp")
    for bit in plane_bits(n_dp, flip):
        keep = sorted(i for i in blocks if not i >> bit & 1)
        got = cross(jnp.stack([blocks[i ^ (1 << bit)] for i in keep]), bit)
        blocks = {
            i: (blocks[i].astype(F32) + got[k].astype(F32)).astype(blocks[i].dtype)
            for k, i in enumerate(keep)
        }
    return blocks[0]


def layer_norm(v, gain, bias):
    center = v - jnp.mean(v, -1, keepdims=True)
    inverse = lax.rsqrt(jnp.mean(center * center, -1, keepdims=True) + EPS)
    unit = center * inverse
    return unit * gain + bias, unit, inverse


def norm_back(up, unit, inverse, gain):
    u = up * gain
    return inverse * (
        u - jnp.mean(u, -1, keepdims=True) - unit * jnp.mean(u * unit, -1, keepdims=True)
    )


def gelu_pair(v):
    cumulative = 0.5 * (1.0 + lax.erf(v * 0.7071067811865476))
    density = jnp.exp(-0.5 * v * v) * 0.3989422804014327
    return v * cumulative, cumulative + v * density


def attend(q, k, v, allowed):
    heads = q.shape[1] // HD
    qh = q.reshape(-1, heads, HD)
    kh = k.reshape(-1, heads, HD)
    vh = v.reshape(-1, heads, HD)
    s = jnp.einsum("qhd,khd->hqk", qh, kh, preferred_element_type=F32) * HD**-0.5
    s = jnp.where(allowed[None, None, :], s, -1e30)
    e = jnp.exp(s - jnp.max(s, -1, keepdims=True))
    p = (e / jnp.sum(e, -1, keepdims=True)).astype(BF)
    mixed = jnp.einsum("hqk,khd->qhd", p, vh, preferred_element_type=F32)
    return mixed.astype(BF).reshape(q.shape), p


def attend_back(q, k, v, p, mixed, dm):
    heads = q.shape[1] // HD
    qh = q.reshape(-1, heads, HD)
    kh = k.reshape(-1, heads, HD)
    vh = v.reshape(-1, heads, HD)
    dh = dm.reshape(-1, heads, HD)
    pf = p.astype(F32)
    dp = jnp.einsum("qhd,khd->hqk", dh, vh, preferred_element_type=F32)
    total = jnp.sum(dp * pf, -1, keepdims=True)
    ds = (pf * (dp - total)).astype(BF)
    dv = jnp.einsum("hqk,qhd->khd", p, dh, preferred_element_type=F32)
    dq = jnp.einsum("hqk,khd->qhd", ds, kh, preferred_element_type=F32) * HD**-0.5
    dk = jnp.einsum("hqk,qhd->khd", ds, qh, preferred_element_type=F32) * HD**-0.5
    return (
        dq.astype(BF).reshape(q.shape),
        dk.astype(BF).reshape(k.shape),
        dv.astype(BF).reshape(k.shape),
    )


def plain_body(
    cells,
    lengths,
    query_matrix,
    key_matrix,
    value_matrix,
    query_bias,
    value_bias,
    output_matrix,
    b_out,
    gain_one,
    shift_one,
    gain_two,
    shift_two,
    expand_weight,
    expand_bias,
    contract_weight,
    b_down,
    grad_out,
):
    slots, rows, width = cells.shape
    n_dp, n_mp = lax.axis_size("dp"), lax.axis_size("mp")
    d, z = lax.axis_index("dp"), lax.axis_index("mp")
    per = n_mp // slots
    core = d % per
    tokens = slots * rows
    part = width // n_dp
    hw = query_matrix.shape[1]
    turns = moves(n_dp, n_mp, slots)

    def bring(x):
        got = [
            lax.ppermute(
                lax.dynamic_index_in_dim(x, (t + z) % slots, 0, False), ("dp", "mp"), turns[t]
            )
            for t in range(slots)
        ]
        even = z % slots == 0
        return jnp.concatenate(
            [jnp.where(even, got[0], got[1]), jnp.where(even, got[1], got[0])], 0
        )

    def give_back(x):
        x = x.reshape(slots, rows, width)
        got = [
            lax.ppermute(
                lax.dynamic_index_in_dim(x, (t + z) % slots, 0, False),
                ("dp", "mp"),
                [(b, a) for a, b in turns[t]],
            )
            for t in range(slots)
        ]
        even = z % slots == 0
        return jnp.stack(
            [jnp.where(even, got[0], got[1]), jnp.where(even, got[1], got[0])], 0
        )

    mine = bring(cells)
    attn_own = jnp.concatenate(
        [query_matrix, key_matrix, value_matrix, output_matrix.T], 1
    )
    first = d * part

    def piece_of(w):
        return lax.dynamic_slice_in_dim(w, first, part, 0)

    half = attn_own.shape[1] // 2
    a_piece = piece_of(attn_own)
    a_left = gather(a_piece[:, :half], False)
    a_right = gather(a_piece[:, half:], True)
    u_held = gather(piece_of(expand_weight), False)
    d_held = gather(piece_of(contract_weight), True)
    grad_rows = bring(grad_out)
    small = jnp.concatenate([query_bias, value_bias, expand_bias])
    small = [small] + [shift(small, n_mp - r) for r in range(1, n_mp)]
    both = cross(lengths, 0)
    length_all = jnp.where(core == 0, jnp.concatenate([lengths, both]), jnp.concatenate([both, lengths]))
    length = lax.dynamic_index_in_dim(length_all, z, 0, False)

    attn_w = [
        jnp.concatenate([a, b], 1)
        for a, b in zip(
            assemble(a_left, attn_own[:, :half], d), assemble(a_right, attn_own[:, half:], d)
        )
    ]
    up_w = assemble(u_held, expand_weight, d)
    down_w = assemble(d_held, contract_weight, d)

    position = core * tokens + jnp.arange(tokens)
    keep = (position < length).astype(F32)[:, None]
    sib_position = (per - 1 - core) * tokens + jnp.arange(tokens)
    allowed = jnp.concatenate([position, sib_position]) < length

    x = mine.astype(F32)
    rows_one, unit_one, inv_one = layer_norm(x, gain_one, shift_one)
    rows_one = rows_one.astype(BF)
    kept = []
    attention = jnp.zeros((tokens, width), F32)
    for r in range(n_mp):
        w = attn_w[r]
        q = (dot(rows_one, w[:, :hw], 1, 0) + small[r][:hw]).astype(BF)
        k = dot(rows_one, w[:, hw : 2 * hw], 1, 0).astype(BF)
        v = (dot(rows_one, w[:, 2 * hw : 3 * hw], 1, 0) + small[r][hw : 2 * hw]).astype(BF)
        k = jnp.concatenate([k, cross(k, 0)], 0)
        v = jnp.concatenate([v, cross(v, 0)], 0)
        mixed, p = attend(q, k, v, allowed)
        kept.append((q, k, v, mixed, p))
        attention = attention + dot(mixed, w[:, 3 * hw :], 1, 1)
    middle = x + attention + b_out
    rows_two, unit_two, inv_two = layer_norm(middle, gain_two, shift_two)
    rows_two = rows_two.astype(BF)
    g = keep * grad_rows.astype(F32)
    gz = g.astype(BF)

    order = jnp.arange(0, n_dp, 2) ^ d

    def chosen(v):
        return jnp.take(v.reshape(v.shape[0], n_dp, part), order, axis=1).reshape(v.shape[0], -1)

    def other(v):
        return jnp.take(v.reshape(v.shape[0], n_dp, part), order ^ 1, axis=1).reshape(v.shape[0], -1)

    def both_cores(v):
        return jnp.concatenate([chosen(v), cross(other(v), 0)], 0)

    def weight_grad(left, right, flip):
        right = jnp.concatenate([right, cross(right, 0)], 0)
        return weight_grad_all(left, right, flip)

    def weight_grad_all(left, right, flip):
        got = dot(left, right, 0, 0).astype(BF).reshape(-1, part, right.shape[1])
        return scatter({2 * i: got[i] for i in range(got.shape[0])}, flip)

    def finish(pieces):
        total = pieces[0].astype(F32)
        for r in range(1, n_mp):
            total = total + shift(pieces[r], r).astype(F32)
        return total

    two_both = both_cores(rows_two)
    gz_both = both_cores(gz)
    result = middle + b_down
    e2 = jnp.zeros((tokens, width), F32)
    up_parts, down_parts, b_up = [], [], []
    for r in range(n_mp):
        upper = dot(rows_two, up_w[r], 1, 0) + small[r][2 * hw :]
        hidden, slope = gelu_pair(upper)
        hidden = hidden.astype(BF)
        result = result + dot(hidden, down_w[r], 1, 0)
        d_upper = (dot(gz, down_w[r], 1, 1) * slope).astype(BF)
        e2 = e2 + dot(d_upper, up_w[r], 1, 1)
        up_parts.append(weight_grad(two_both, d_upper, False))
        down_parts.append(weight_grad(gz_both, hidden, True))
        b_up.append(jnp.sum(d_upper.astype(F32), 0))
    out_cells = give_back((keep * result).astype(BF))
    grad_up = finish(up_parts)
    grad_down = finish(down_parts).T

    d_middle = g + norm_back(e2, unit_two, inv_two, gain_two)
    gm = d_middle.astype(BF)
    gm_both = both_cores(gm)
    one_both = both_cores(rows_one)
    e1 = jnp.zeros((tokens, width), F32)
    a_parts, b_q, b_v = [], [], []
    for r in range(n_mp):
        q, k, v, mixed, p = kept[r]
        w = attn_w[r]
        d_mixed = dot(gm, w[:, 3 * hw :], 1, 0).astype(BF)
        dq, dk, dv = attend_back(q, k, v, p, mixed, d_mixed)
        dk_all = (dk.astype(F32) + jnp.roll(cross(dk, 0), tokens, 0).astype(F32)).astype(BF)
        dv_all = (dv.astype(F32) + jnp.roll(cross(dv, 0), tokens, 0).astype(F32)).astype(BF)
        dq_all = jnp.concatenate([dq, cross(dq, 0)], 0)
        e1 = (
            e1
            + dot(dq, w[:, :hw], 1, 1)
            + dot(dk_all[:tokens], w[:, hw : 2 * hw], 1, 1)
            + dot(dv_all[:tokens], w[:, 2 * hw : 3 * hw], 1, 1)
        )
        b_q.append(jnp.sum(dq.astype(F32), 0))
        b_v.append(jnp.sum(dv_all[:tokens].astype(F32), 0))
        qkv_part = weight_grad_all(one_both, jnp.concatenate([dq_all, dk_all, dv_all], 1), r % 2 == 1)
        o_part = weight_grad(gm_both, mixed, r % 2 == 0)
        a_parts.append(jnp.concatenate([qkv_part, o_part], 1))
    d_cells = d_middle + norm_back(e1, unit_one, inv_one, gain_one)
    grad_cells = give_back(d_cells.astype(BF)).astype(F32)
    grad_attn = finish(a_parts)

    split_mp = [jnp.stack(b_q).reshape(n_mp, n_dp, -1), jnp.stack(b_v).reshape(n_mp, n_dp, -1), jnp.stack(b_up).reshape(n_mp, n_dp, -1)]
    sums = [
        jnp.sum(d_middle, 0),
        jnp.sum(e1 * unit_one, 0),
        jnp.sum(e1, 0),
        jnp.sum(e2 * unit_two, 0),
        jnp.sum(e2, 0),
        jnp.sum(g, 0),
    ]
    split_dp = [jnp.roll(jnp.swapaxes(s.reshape(n_dp, n_mp, -1), 0, 1), -z, 0) for s in sums]
    packed = jnp.concatenate(split_mp + split_dp, 2)
    packed = jnp.take(packed, jnp.arange(n_dp) ^ d, axis=1)
    packed = packed[:, 0::2] + cross(packed[:, 1::2], 0)
    packed = scatter({2 * i: packed[:, i] for i in range(packed.shape[1])}, False)
    vec = packed[0]
    for r in range(1, n_mp):
        vec = vec + shift(packed[r], r)
    nq = split_mp[0].shape[2]
    nu = split_mp[2].shape[2]
    ns = split_dp[0].shape[2]
    vq, vv, vu = vec[:nq], vec[nq : 2 * nq], vec[2 * nq : 2 * nq + nu]
    rest = [vec[2 * nq + nu + i * ns : 2 * nq + nu + (i + 1) * ns] for i in range(6)]
    return (
        out_cells,
        grad_cells,
        grad_attn[:, :hw],
        grad_attn[:, hw : 2 * hw],
        grad_attn[:, 2 * hw : 3 * hw],
        vq,
        vv,
        grad_attn[:, 3 * hw :].T,
        rest[0],
        rest[1],
        rest[2],
        rest[3],
        rest[4],
        grad_up,
        vu,
        grad_down,
        rest[5],
    )


def dg(a, b, ca, cb):
    return lax.dot_general(a, b, (((ca,), (cb,)), ((), ())), preferred_element_type=F32)


def lane_block(start, size=128):
    return pl.ds(pl.multiple_of(start, size), size)


class Place:
    def __init__(self):
        self.d, self.z = lax.axis_index("dp"), lax.axis_index("mp")
        self.bit = [lax.rem(self.d // (1 << b), 2) for b in range(3)]
        self.core = self.bit[0]
        self.base = self.d - self.core

    def across(self, i):
        v = self.d
        for b in range(3):
            if i >> b & 1:
                v = v + (1 << b) * (1 - 2 * self.bit[b])
        return v

    def rows(self, i):
        return lane_block(self.across(i) * PART, PART)

    def greet(self):
        barrier = pltpu.get_barrier_semaphore()
        for step in range(1, 4):
            for c in range(2):
                pl.semaphore_signal(
                    barrier,
                    inc=1,
                    device_id=(self.base + c, lax.rem(self.z + step, 4)),
                    device_id_type=MESH,
                )
        for i in (1, 2, 4):
            pl.semaphore_signal(barrier, inc=1, device_id=(self.across(i), self.z), device_id_type=MESH)
        pl.semaphore_wait(barrier, 9)


def remote(src, dst, send, recv, device):
    return pltpu.make_async_remote_copy(
        src_ref=src, dst_ref=dst, send_sem=send, recv_sem=recv, device_id=device, device_id_type=MESH
    )


class Unit:
    def __init__(self, place, own, at, parts, zsend, zrecv, send, recv, flip):
        self.p, self.own, self.at, self.parts = place, own, at, parts
        self.zsend, self.zrecv, self.send, self.recv = zsend, zrecv, send, recv
        self.first, self.second = (4, 2) if flip else (2, 4)

    def along(self, k, slot_from, slot_to, right):
        p = self.p
        device = (p.d, p.z + 1 if right else p.z - 1)
        return [
            remote(
                self.own(q) if slot_from is None else self.at(slot_from, 0, q),
                self.at(slot_to, 0, q),
                self.zsend.at[k, q],
                self.zrecv.at[slot_to - 1, q],
                device,
            )
            for q in range(self.parts)
        ]

    def steps(self):
        z = self.p.z
        inner = jnp.logical_and(z >= 1, z <= 2)
        return [
            (z <= 2, (0, None, 3, True)),
            (z >= 1, (1, None, 1, False)),
            (inner, (2, 3, 2, True)),
            (inner, (3, 1, 2, False)),
            (z == 1, (4, 2, 3, False)),
            (z == 2, (5, 2, 1, True)),
        ]

    def go(self, k):
        cond, what = self.steps()[k]

        @pl.when(cond)
        def _():
            for c in self.along(*what):
                c.start()

    def start(self):
        self.go(0)
        self.go(1)

    def landed(self, slot):
        for q in range(self.parts):
            here = self.at(slot, 0, q)
            remote(here, here, self.zsend.at[0, q], self.zrecv.at[slot - 1, q], (self.p.across(1), self.p.z)).wait_recv()

    def xy(self, slot, k, i, bit):
        here = self.at(slot, i, None)
        return remote(
            here,
            here,
            self.send.at[slot - 1, k],
            self.recv.at[slot - 1, i ^ bit],
            (self.p.across(bit), self.p.z),
        )

    def arrived(self, slot, i):
        here = self.at(slot, i, None)
        remote(here, here, self.send.at[slot - 1, 0], self.recv.at[slot - 1, i], (self.p.across(1), self.p.z)).wait_recv()

    def one(self, slot):
        self.xy(slot, 0, 0, self.first).start()

    def z_one(self):
        z = self.p.z

        @pl.when(z >= 1)
        def _():
            self.landed(3)

        self.go(2)

        @pl.when(z <= 2)
        def _():
            self.landed(1)

        self.go(3)

        @pl.when(z >= 1)
        def _():
            self.one(3)

        @pl.when(z <= 2)
        def _():
            self.one(1)

    def z_two(self):
        self.landed(2)
        self.go(4)
        self.go(5)
        self.one(2)

    def z_three(self):
        z = self.p.z

        @pl.when(z == 0)
        def _():
            self.landed(3)
            self.one(3)

        @pl.when(z == 3)
        def _():
            self.landed(1)
            self.one(1)

    def two(self, slot):
        self.arrived(slot, self.first)
        self.xy(slot, 1, 0, self.second).start()
        self.xy(slot, 2, self.first, self.second).start()

    def three(self, slot):
        self.arrived(slot, self.second)
        self.arrived(slot, self.first + self.second)
        for k, i in enumerate((0, 2, 4, 6)):
            self.xy(slot, 3 + k, i, 1).start()

    def whole(self, slot):
        for i in (1, 3, 5, 7):
            self.arrived(slot, i)

    def finish(self):
        for k in range(6):
            cond, what = self.steps()[k]

            @pl.when(cond)
            def _(what=what):
                for c in self.along(*what):
                    c.wait_send()

        for slot in (1, 2, 3):
            self.xy(slot, 0, 0, self.first).wait_send()
            self.xy(slot, 1, 0, self.second).wait_send()
            self.xy(slot, 2, self.first, self.second).wait_send()
            for k, i in enumerate((0, 2, 4, 6)):
                self.xy(slot, 3 + k, i, 1).wait_send()


def bring_copies(p, src, dst, sends, recvs, here):
    for s in range(2):
        target = (p.base + p.z // 2, 2 * p.core + s)
        half = lax.rem(p.z, 2)
        rows = lane_block(half * 256, 256)
        same = jnp.logical_and(p.core == p.z // 2, p.z == 2 * p.core + s)

        @pl.when(same)
        def _():
            pltpu.make_async_copy(src.at[s], dst.at[rows], here).start()

        @pl.when(jnp.logical_not(same))
        def _():
            remote(src.at[s], dst.at[rows], sends.at[s], recvs.at[half], target).start()


def bring_wait(p, dst, recvs, here):
    for half in range(2):
        block = dst.at[pl.ds(half * 256, 256)]
        same = jnp.logical_and(p.core == p.z // 2, lax.rem(p.z, 2) == half)

        @pl.when(same)
        def _():
            pltpu.make_async_copy(block, block, here).wait()

        @pl.when(jnp.logical_not(same))
        def _():
            remote(block, block, recvs.at[half], recvs.at[half], (p.across(1), p.z)).wait_recv()


def bring_sent(p, src, sends):
    for s in range(2):
        same = jnp.logical_and(p.core == p.z // 2, p.z == 2 * p.core + s)

        @pl.when(jnp.logical_not(same))
        def _():
            remote(src.at[s], src.at[s], sends.at[s], sends.at[s], (p.across(1), p.z)).wait_send()


def norm_stats(x):
    center = x - jnp.mean(x, -1, keepdims=True)
    inverse = lax.rsqrt(jnp.mean(center * center, -1, keepdims=True) + EPS)
    return center * inverse, inverse


def each_rows(size, total, f):
    def step(i, carry):
        f(pl.ds(pl.multiple_of(i * size, size), size))
        return carry

    lax.fori_loop(0, total // size, step, 0)


def chosen_both(p, t_ref, both_ref, sends, recvs):
    copies = []
    for k, i in enumerate((0, 2, 4, 6)):
        block = pl.ds(k * PART, PART)
        both_ref[block, 0:T] = t_ref[p.rows(i), :]
        copies.append(
            remote(
                t_ref.at[p.rows(i ^ 1)],
                both_ref.at[block, T : 2 * T],
                sends.at[k],
                recvs.at[k],
                (p.across(1), p.z),
            )
        )
    for c in copies:
        c.start()
    return copies


def forward_kernel(
    cells, grad, len_own, wq, wk, wv, wo, up, down, small_own, b_out, gain1, shift1, gain2, shift2, b_down,
    x_out, rows1_out, q_out, k_out, v_out, mix_out, e_out, r_out, wa_out, wo_out, wu, wd, res_out, dm_out, gu_out, gd_out, vec_out,
    xv, gv, rows1, wav, wov, qv, kv, vv, mix, eb, rv, bias, vt, ot, middle, rows2, tt, xb, gb, acc, e2,
    uv, dv, ho, du, hs, ds, gus, gds, len_sib, small1, small2, small3,
    a_zs, a_zr, a_s, a_r, o_zs, o_zr, o_s, o_r, u_zs, u_zr, u_s, u_r, d_zs, d_zr, d_s, d_r,
    act_s, act_r, sm_s, sm_r, kv_s, kv_r, both_s, both_r, hd_s, hd_r, credit, loc, load, store,
):
    p = Place()
    small = [small_own, small1, small2, small3]
    sibling = (p.across(1), p.z)

    ws = (wq, wk, wv)
    own_rows = p.rows(0)

    def a_at(slot, i, part):
        if part is None:
            return wav.at[slot, p.rows(i)]
        return wav.at[slot, p.rows(i), pl.ds(part * 256, 256)]

    unit_a = Unit(p, lambda q: ws[q].at[own_rows], a_at, 3, a_zs, a_zr, a_s, a_r, False)
    unit_o = Unit(
        p,
        lambda q: wo.at[:, own_rows],
        lambda slot, i, q: wov.at[pl.ds(slot * 256, 256), p.rows(i)],
        1, o_zs, o_zr, o_s, o_r, True,
    )
    unit_u = Unit(p, lambda q: up.at[own_rows], lambda slot, i, q: wu.at[slot - 1, p.rows(i)], 1, u_zs, u_zr, u_s, u_r, False)
    unit_d = Unit(p, lambda q: down.at[own_rows], lambda slot, i, q: wd.at[slot - 1, p.rows(i)], 1, d_zs, d_zr, d_s, d_r, True)

    own_loads = [pltpu.make_async_copy(w, wav.at[0, :, pl.ds(k * 256, 256)], loc.at[k]) for k, w in enumerate(ws)]
    own_loads.append(pltpu.make_async_copy(wo, wov.at[pl.ds(0, 256)], loc.at[3]))
    for c in own_loads:
        c.start()
    first_loads = [pltpu.make_async_copy(up, uv.at[0], load.at[0, 0]), pltpu.make_async_copy(down, dv.at[0], load.at[1, 0])]
    for c in first_loads:
        c.start()

    p.greet()
    unit_a.start()
    bring_copies(p, cells, xv, act_s.at[0], act_r.at[0], loc.at[4])
    small_copies = []
    for r in (1, 2, 3):
        small_copies.append(remote(small_own, small[r], sm_s.at[r], sm_r.at[r], (p.d, lax.rem(p.z + 4 - r, 4))))
    small_copies.append(remote(len_own, len_sib, sm_s.at[0], sm_r.at[0], sibling))
    for c in small_copies:
        c.start()
    unit_a.z_one()
    unit_a.z_two()
    unit_a.z_three()
    unit_o.start()
    unit_u.start()
    for slot in (1, 3, 2):
        unit_a.two(slot)

    bring_wait(p, xv, act_r.at[0], loc.at[4])
    bring_copies(p, grad, gv, act_s.at[1], act_r.at[1], loc.at[5])
    unit_d.start()

    def first_norm(rows):
        unit, _ = norm_stats(xv[rows, :].astype(F32))
        rows1[rows, :] = (unit * gain1[...] + shift1[...]).astype(BF)

    each_rows(128, T, first_norm)
    outs = [pltpu.make_async_copy(xv, x_out, store.at[0]), pltpu.make_async_copy(rows1, rows1_out, store.at[1])]
    for c in outs:
        c.start()
    for slot in (1, 3, 2):
        unit_a.three(slot)
    unit_o.z_one()
    unit_o.z_two()
    unit_o.z_three()
    unit_u.z_one()

    small_copies[3].wait_recv()
    slot_row = lax.rem(p.z, 2)
    near = jnp.where(p.z // 2 == p.core, 1.0, 0.0)
    length = near * len_own[pl.ds(slot_row, 1), :] + (1.0 - near) * len_sib[pl.ds(slot_row, 1), :]
    length = length[:, :1]
    lane = lax.broadcasted_iota(jnp.int32, (1, 128), 1)
    key = lax.broadcasted_iota(jnp.int32, (2 * T, 128), 0)
    key = jnp.where(key < T, key + p.core * T, key - T + (1 - p.core) * T)
    barred = jnp.where(key.astype(F32) < length, 0.0, -1e30)
    bias[0] = jnp.where(lane == 64, barred, 0.0).astype(BF)
    bias[1] = jnp.where(lane == 0, barred, 0.0).astype(BF)

    def kept(rows_start, size):
        row = lax.broadcasted_iota(jnp.int32, (size, 1), 0) + rows_start + p.core * T
        return row.astype(F32) < length

    for c in own_loads:
        c.wait()
    for r in (1, 2, 3):
        small_copies[r - 1].wait_recv()

    kv_copies = []

    def project(r):
        b = small[r]
        x = rows1[...]
        qv[r] = (dg(x, wav[r, :, 0:256], 1, 0) + b[:, 0:256]).astype(BF)
        kv[r, 0:T, :] = dg(x, wav[r, :, 256:512], 1, 0).astype(BF)
        vv[r, 0:T, :] = (dg(x, wav[r, :, 512:768], 1, 0) + b[:, 256:512]).astype(BF)
        cs = [
            remote(ref.at[r, pl.ds(0, T)], ref.at[r, pl.ds(T, T)], kv_s.at[r, n], kv_r.at[r, n], sibling)
            for n, ref in enumerate((kv, vv))
        ]
        for c in cs:
            c.start()
        kv_copies.append(cs)

    def e_copy(head, slot):
        return pltpu.make_async_copy(eb.at[slot], e_out.at[head], store.at[2 + slot])

    def attend(r):
        for c in kv_copies[r]:
            c.wait_recv()
        vt[...] = jnp.transpose(vv[r], (1, 0))

        def pair(j, carry):
            cols = lane_block(j * 128)
            kp = kv[r, :, cols]
            qp = qv[r, :, cols] * BF(HD**-0.5)
            for h in range(2):
                mine = (lane < 64) if h == 0 else (lane >= 64)
                one = lane == (64 if h == 0 else 0)
                ka = jnp.where(mine, kp, bias[h])
                qa = jnp.where(mine, qp, jnp.where(one, BF(1), BF(0)))
                s = dg(ka, qa, 1, 1)
                e = jnp.exp(s - jnp.max(s, 0, keepdims=True))
                inv = 1.0 / jnp.sum(e, 0, keepdims=True)
                head = r * 4 + 2 * j + h
                if r == 0:
                    @pl.when(j > 0)
                    def _():
                        e_copy(head - 2, h).wait()
                else:
                    e_copy(head - 2, h).wait()
                eb[h] = e.astype(BF)
                e_copy(head, h).start()
                feats = pl.ds(pl.multiple_of(j * 128 + h * 64, 64), 64)
                ot[feats, :] = (dg(vt[feats, :], eb[h], 1, 0) * inv).astype(BF)
                rv[head] = inv
            return carry

        lax.fori_loop(0, 2, pair, 0)
        mix[:, r * 256 : (r + 1) * 256] = jnp.transpose(ot[...], (1, 0))

    project(0)
    unit_u.z_two()
    for slot in (1, 2, 3):
        unit_a.whole(slot)
    project(1)
    unit_u.z_three()
    for slot in (1, 3, 2):
        unit_o.two(slot)
    attend(0)
    unit_d.z_one()
    project(2)
    project(3)
    for slot in (1, 3, 2):
        unit_o.three(slot)
        unit_u.two(slot)
    unit_d.z_two()
    unit_d.z_three()
    attend(1)
    for slot in (1, 3, 2):
        unit_u.three(slot)
        unit_d.two(slot)
    attend(2)
    for slot in (1, 3, 2):
        unit_d.three(slot)
        unit_o.whole(slot)
    attend(3)
    for h in range(2):
        e_copy(14 + h, h).wait()

    outs += [
        pltpu.make_async_copy(wav, wa_out, store.at[4]),
        pltpu.make_async_copy(wov, wo_out, store.at[5]),
        pltpu.make_async_copy(qv, q_out, store.at[6]),
        pltpu.make_async_copy(kv, k_out, store.at[7]),
        pltpu.make_async_copy(vv, v_out, store.at[8]),
        pltpu.make_async_copy(mix, mix_out, store.at[9]),
        pltpu.make_async_copy(rv, r_out, store.at[10]),
    ]
    for c in outs[2:]:
        c.start()

    for n in range(2):
        cols = pl.ds(n * 512, 512)
        middle[:, cols] = dg(mix[...], wov[:, cols], 1, 0)

    def second_norm(rows):
        m = middle[rows, :] + xv[rows, :].astype(F32) + b_out[...]
        middle[rows, :] = m
        unit, _ = norm_stats(m)
        rows2[rows, :] = (unit * gain2[...] + shift2[...]).astype(BF)
        acc[rows, :] = m + b_down[...]

    each_rows(128, T, second_norm)
    tt[...] = jnp.transpose(rows2[...], (1, 0))
    both = chosen_both(p, tt, xb, both_s.at[0], both_r.at[0])
    bring_wait(p, gv, act_r.at[1], loc.at[5])

    def mask_grad(i, carry):
        rows = pl.ds(pl.multiple_of(i * 128, 128), 128)
        gv[rows, :] = jnp.where(kept(i * 128, 128), gv[rows, :].astype(F32), 0.0).astype(BF)
        return carry

    lax.fori_loop(0, T // 128, mask_grad, 0)
    for c in both:
        c.wait_send()
    tt[...] = jnp.transpose(gv[...], (1, 0))
    both2 = chosen_both(p, tt, gb, both_s.at[1], both_r.at[1])

    order = (0, 1, 3, 2)

    def load_copies(n):
        r = order[n]
        return [
            pltpu.make_async_copy(wu.at[r - 1], uv.at[n % 2], load.at[0, n % 2]),
            pltpu.make_async_copy(wd.at[r - 1], dv.at[n % 2], load.at[1, n % 2]),
        ]

    def hidden(n):
        r, slot = order[n], n % 2
        for k in range(2):
            c = pl.ds(k * 512, 512)
            upper = dg(rows2[...], uv[slot, :, c], 1, 0) + small[r][:, 512 + k * 512 : 1024 + k * 512]
            act, slope = gelu_pair(upper)
            ho[slot, :, c] = act.astype(BF)
            d_up = (dg(gv[...], dv[slot, c, :], 1, 1) * slope).astype(BF)
            du[slot, :, c] = d_up
            vec_out[r : r + 1, c] = jnp.sum(d_up.astype(F32), 0, keepdims=True)
        if n >= 2:
            pl.semaphore_wait(credit, 1)
        cs = [
            remote(ho.at[slot], hs.at[slot], hd_s.at[0, slot], hd_r.at[0, slot], sibling),
            remote(du.at[slot], ds.at[slot], hd_s.at[1, slot], hd_r.at[1, slot], sibling),
        ]
        for c in cs:
            c.start()
        for k in range(2):
            c = pl.ds(k * 512, 512)
            acc[:, c] = acc[:, c] + dg(ho[slot], dv[slot, :, c], 1, 0)
            new = dg(du[slot], uv[slot, c, :], 1, 1)
            e2[:, c] = new if n == 0 else e2[:, c] + new
        return cs

    g_stores = [None, None]

    def weight_grads(n, cs):
        r, slot = order[n], n % 2
        for c in cs:
            c.wait_recv()
        if n >= 1:
            for c in g_stores:
                c.wait()
        gus[...] = (dg(xb[:, 0:T], du[slot], 1, 0) + dg(xb[:, T : 2 * T], ds[slot], 1, 0)).astype(BF)
        gds[...] = (dg(gb[:, 0:T], ho[slot], 1, 0) + dg(gb[:, T : 2 * T], hs[slot], 1, 0)).astype(BF)
        if n < 2:
            pl.semaphore_signal(credit, inc=1, device_id=sibling, device_id_type=MESH)
        g_stores[0] = pltpu.make_async_copy(gus, gu_out.at[r], store.at[11])
        g_stores[1] = pltpu.make_async_copy(gds, gd_out.at[r], store.at[12])
        for c in g_stores:
            c.start()
        for c in cs:
            c.wait_send()

    for c in first_loads:
        c.wait()
    held = [hidden(0)]
    for n in range(1, 4):
        unit_u.whole(order[n])
        unit_d.whole(order[n])
        cs = load_copies(n)
        for c in cs:
            c.start()
        if n == 1:
            for c in both + both2:
                c.wait_recv()
        if n >= 2:
            weight_grads(n - 2, held[n - 2])
        for c in cs:
            c.wait()
        held.append(hidden(n))
    weight_grads(2, held[2])
    weight_grads(3, held[3])

    vec_out[4:16, :] = jnp.zeros((12, width_of(vec_out)), F32)

    def last(i, carry):
        rows = pl.ds(pl.multiple_of(i * 128, 128), 128)
        res = jnp.where(kept(i * 128, 128), acc[rows, :], 0.0)
        rows2[rows, :] = res.astype(BF)
        unit, inverse = norm_stats(middle[rows, :])
        e = e2[rows, :]
        g = gv[rows, :].astype(F32)
        u = e * gain2[...]
        d_mid = g + inverse * (u - jnp.mean(u, -1, keepdims=True) - unit * jnp.mean(u * unit, -1, keepdims=True))
        middle[rows, :] = d_mid
        for k, v in enumerate((d_mid, e * unit, e, g)):
            vec_out[4 + k : 5 + k, :] += jnp.sum(v, 0, keepdims=True)
        return carry

    lax.fori_loop(0, T // 128, last, 0)
    ends = [pltpu.make_async_copy(rows2, res_out, store.at[13]), pltpu.make_async_copy(middle, dm_out, store.at[14])]
    for c in ends:
        c.start()
    for c in ends + outs + g_stores:
        c.wait()
    for c in both2 + small_copies:
        c.wait_send()
    for cs in kv_copies:
        for c in cs:
            c.wait_send()
    for unit in (unit_a, unit_o, unit_u, unit_d):
        unit.finish()
    bring_sent(p, cells, act_s.at[0])
    bring_sent(p, grad, act_s.at[1])


def width_of(ref):
    return ref.shape[-1]

def return_copies(p, src, dst, sends, recvs, here):
    slot = lax.rem(p.z, 2)
    for h in range(2):
        rows = src.at[pl.ds(h * 256, 256)]
        same = jnp.logical_and(p.core == p.z // 2, p.z == 2 * p.core + h)

        @pl.when(same)
        def _():
            pltpu.make_async_copy(rows, dst.at[slot], here).start()

        @pl.when(jnp.logical_not(same))
        def _():
            remote(rows, dst.at[slot], sends.at[h], recvs.at[slot], (p.base + p.z // 2, 2 * p.core + h)).start()


def return_wait(p, dst, recvs, here):
    for s in range(2):
        same = jnp.logical_and(p.core == p.z // 2, p.z == 2 * p.core + s)

        @pl.when(same)
        def _():
            pltpu.make_async_copy(dst.at[s], dst.at[s], here).wait()

        @pl.when(jnp.logical_not(same))
        def _():
            remote(dst.at[s], dst.at[s], recvs.at[s], recvs.at[s], (p.across(1), p.z)).wait_recv()


def return_sent(p, src, sends):
    for h in range(2):
        rows = src.at[pl.ds(h * 256, 256)]
        same = jnp.logical_and(p.core == p.z // 2, p.z == 2 * p.core + h)

        @pl.when(jnp.logical_not(same))
        def _():
            remote(rows, rows, sends.at[h], sends.at[h], (p.across(1), p.z)).wait_send()


class Chain:
    def __init__(self, p, r, block, keep0, keep1, land1, land2, land3, send, recv, zsend, zrecv, flip):
        first, second = (4, 2) if flip else (2, 4)
        self.r, self.keep0, self.keep1, self.land1, self.land2 = r, keep0, keep1, land1, land2
        near = (p.across(first), p.z)
        self.one = [remote(block(first + k * second), land1.at[k], send.at[k], recv.at[k], near) for k in range(2)]
        self.two = remote(keep1, land2, send.at[2], recv.at[2], (p.across(second), p.z))
        self.three = None
        if r:
            self.three = remote(keep0, land3, zsend, zrecv, (p.d, lax.rem(p.z + r, 4)))

    def start(self):
        for c in self.one:
            c.start()

    def middle(self):
        for c in self.one:
            c.wait_recv()
        self.keep1[...] = (self.keep1[...].astype(F32) + self.land1[1].astype(F32)).astype(BF)
        self.two.start()

    def total(self):
        return self.keep0[...].astype(F32) + self.land1[0].astype(F32) + self.land2[...].astype(F32)

    def end(self):
        self.two.wait_recv()
        if self.r:
            self.keep0[...] = self.total().astype(BF)
            self.three.start()

    def sent(self):
        for c in self.one + [self.two] + ([self.three] if self.r else []):
            c.wait_send()


class Vectors:
    def __init__(self, p, acc, land, zland, send, recv, zsend, zrecv):
        self.acc, self.land, self.zland = acc, land, zland
        self.steps = [
            remote(acc, land.at[b], send.at[b], recv.at[b], (p.across(1 << b), p.z)) for b in range(3)
        ]
        self.along = [
            remote(acc, zland.at[r - 1], zsend.at[r - 1], zrecv.at[r - 1], (p.d, lax.rem(p.z + r, 4)))
            for r in (1, 2, 3)
        ]

    def start(self, b):
        self.steps[b].start()

    def take(self, b):
        self.steps[b].wait()
        self.acc[...] = self.acc[...] + self.land[b]

    def z_start(self):
        for c in self.along:
            c.start()

    def z_wait(self):
        for c in self.along:
            c.wait()


def backward_kernel(
    x_in, rows1_in, q_in, k_in, v_in, mix_in, e_in, r_in, wa_in, wo_in, res_in, dm_in, gu_in, gd_in, vec_in, gain1,
    out_cells, grad_cells, gq_out, gk_out, gv_out, go_out, gup_out, gdown_out, early_out, late_out,
    land1, land2, land3, udk, ga, wav, wov, qv, kv, vv, mix, mixs, dm, e1, gmb, r1b, tt, gm, xv, rows1, eb, rv, xs, xr, da, gcl,
    kt, mixt, dmt_all, dqt, early, late, eland, lland, ezland, lzland,
    ch_s, ch_r, z_s, z_r, res_s, res_r, gc_s, gc_r, both_s, both_r, x_s, x_r, mix_s, mix_r, ev_s, ev_r, ez_s, ez_r,
    lv_s, lv_r, lz_s, lz_r, credit, here, load, eload, store,
):
    p = Place()
    sibling = (p.across(1), p.z)
    order = (0, 1, 3, 2)

    loads = {}
    for n, (name, src, dst) in enumerate(
        (
            ("dm", dm_in, dm), ("wo", wo_in, wov), ("rows1", rows1_in, rows1), ("mix", mix_in, mix), ("r", r_in, rv),
            ("q", q_in, qv), ("k", k_in, kv), ("v", v_in, vv), ("x", x_in, xv),
        )
    ):
        loads[name] = pltpu.make_async_copy(src, dst, load.at[n])
        loads[name].start()

    def wa_load(n):
        return pltpu.make_async_copy(wa_in.at[order[n]], wav.at[n % 2], load.at[9 + n % 2])

    def e_load(head, slot):
        return pltpu.make_async_copy(e_in.at[head], eb.at[slot], eload.at[slot])

    e_load(0, 0).start()
    e_load(1, 1).start()
    wa_load(0).start()

    p.greet()
    return_copies(p, res_in, out_cells, res_s, res_r, here.at[0])
    mix_copy = remote(mix_in, mixs, mix_s, mix_r, sibling)
    mix_copy.start()

    chains = {}
    keep_loads = []
    for n, r in enumerate(order):
        for u, src in enumerate((gu_in, gd_in)):
            flip = u == 1
            second = 2 if flip else 4
            j = u * 4 + r
            blocks = lambda i, src=src, r=r: src.at[r, pl.ds(i // 2 * PART, PART)]
            for k, i in enumerate((0, second)):
                c = pltpu.make_async_copy(blocks(i), udk.at[j, k], load.at[11 + j])
                c.start()
            keep_loads.append(pltpu.make_async_copy(udk.at[j], udk.at[j], load.at[11 + j]))
            chains[u, n] = Chain(
                p, r, blocks, udk.at[j, 0], udk.at[j, 1], land1.at[j], land2.at[j], land3.at[u, max(r, 1) - 1],
                ch_s.at[j], ch_r.at[j], z_s.at[u, max(r, 1) - 1], z_r.at[u, max(r, 1) - 1], flip,
            )
            chains[u, n].start()
    for n, r in enumerate(order):
        j = 8 + r
        flip = n % 2 == 1
        second = 2 if flip else 4
        chains[2, n] = Chain(
            p, r, lambda i, r=r: ga.at[r, pl.ds(i // 2 * PART, PART)], ga.at[r, pl.ds(0, PART)], ga.at[r, pl.ds(second // 2 * PART, PART)],
            land1.at[j], land2.at[j], land3.at[2, max(r, 1) - 1], ch_s.at[j], ch_r.at[j],
            z_s.at[2, max(r, 1) - 1], z_r.at[2, max(r, 1) - 1], flip,
        )

    early[...] = vec_in[0:8, :]
    ev = Vectors(p, early, eland, ezland, ev_s, ev_r, ez_s, ez_r)
    ev.start(0)
    late[...] = jnp.zeros((8, 1024), F32)

    loads["rows1"].wait()
    tt[...] = jnp.transpose(rows1[...], (1, 0))
    both = chosen_both(p, tt, r1b, both_s.at[0], both_r.at[0])
    loads["dm"].wait()

    def cast(rows):
        gm[rows, :] = dm[rows, :].astype(BF)

    each_rows(128, T, cast)
    for name in ("wo", "mix", "r", "q", "k", "v"):
        loads[name].wait()
    lane = lax.broadcasted_iota(jnp.int32, (1, 128), 1)

    def attend_back(n):
        r, slot = order[n], n % 2
        cols_r = pl.ds(r * 256, 256)
        kt[...] = jnp.transpose(kv[r], (1, 0))
        mixt[...] = jnp.transpose(mix[:, cols_r], (1, 0))
        dmt_all[...] = dg(wov[cols_r, :], gm[...], 1, 1).astype(BF)
        if n >= 2:
            for c in [x_copies[n - 2]]:
                c.wait_send()

        def pair(j, carry):
            cols = lane_block(j * 128)
            kp = kv[r, :, cols]
            vp = vv[r, :, cols]
            qp = qv[r, :, cols] * BF(HD**-0.5)
            dk = jnp.zeros((2 * T, 128), F32)
            d_v = jnp.zeros((2 * T, 128), F32)
            for h in range(2):
                head = r * 4 + 2 * j + h
                feats = pl.ds(pl.multiple_of(j * 128 + h * 64, 64), 64)
                mine = (lane < 64) if h == 0 else (lane >= 64)
                dmt = (dmt_all[feats, :].astype(F32) * rv[head]).astype(BF)
                delta = jnp.sum(dmt.astype(F32) * mixt[feats, :].astype(F32), 0, keepdims=True)
                zero = jnp.zeros((64, T), BF)
                dmt2 = jnp.concatenate([dmt, zero] if h == 0 else [zero, dmt], 0)
                dma = jnp.transpose(dmt2, (1, 0))
                dp = dg(vp, dmt2, 1, 0)
                e_load(head, h).wait()
                ds = (eb[h].astype(F32) * (dp - delta)).astype(BF)
                qa = jnp.where(mine, qp, BF(0))
                d_v = d_v + dg(eb[h], dma, 1, 0)
                if n < 3:
                    nxt = jnp.where(j == 0, head + 2, order[n + 1] * 4 + h)
                    e_load(nxt, h).start()
                else:
                    @pl.when(j == 0)
                    def _():
                        e_load(head + 2, h).start()
                dk = dk + dg(ds, qa, 1, 0)
                dqt[feats, :] = (dg(kt[feats, :], ds, 1, 0) * HD**-0.5).astype(BF)
            xs[slot, T : 3 * T, cols] = dk.astype(BF)
            xs[slot, 3 * T : 5 * T, cols] = d_v.astype(BF)
            return carry

        lax.fori_loop(0, 2, pair, 0)
        xs[slot, 0:T, :] = jnp.transpose(dqt[...], (1, 0))
        if n >= 2:
            pl.semaphore_wait(credit, 1)
        c = remote(xs.at[slot], xr.at[slot], x_s.at[slot], x_r.at[slot], sibling)
        c.start()
        return c

    x_copies = []

    def gather_up(n):
        r, slot = order[n], n % 2
        x_copies[n].wait_recv()
        da[0:T, 0:256] = xs[slot, 0:T, :]
        da[T : 2 * T, 0:256] = xr[slot, 0:T, :]
        for k in range(2):
            base = T + 2 * T * k
            cols = pl.ds(256 * (k + 1), 256)
            da[0:T, cols] = (
                xs[slot, base : base + T, :].astype(F32) + xr[slot, base + T : base + 2 * T, :].astype(F32)
            ).astype(BF)
            da[T : 2 * T, cols] = (
                xs[slot, base + T : base + 2 * T, :].astype(F32) + xr[slot, base : base + T, :].astype(F32)
            ).astype(BF)
        if n < 2:
            pl.semaphore_signal(credit, inc=1, device_id=sibling, device_id_type=MESH)
        ga[r, :, 0:768] = dg(r1b[...], da[...], 1, 0).astype(BF)
        cols_r = pl.ds(r * 256, 256)
        ga[r, :, 768:1024] = (dg(gmb[:, 0:T], mix[:, cols_r], 1, 0) + dg(gmb[:, T : 2 * T], mixs[:, cols_r], 1, 0)).astype(BF)
        chains[2, n].start()
        wa_load(n).wait()
        if n + 1 < 4:
            wa_load(n + 1).start()
        new = dg(da[0:T, :], wav[slot], 1, 1)
        e1[...] = new if n == 0 else e1[...] + new
        late[2:3, r * 256 : (r + 1) * 256] = jnp.sum(da[0:T, 0:256].astype(F32), 0, keepdims=True)
        late[3:4, r * 256 : (r + 1) * 256] = jnp.sum(da[0:T, 512:768].astype(F32), 0, keepdims=True)

    x_copies.append(attend_back(0))
    for c in both:
        c.wait_send()
    tt[...] = jnp.transpose(gm[...], (1, 0))
    both2 = chosen_both(p, tt, gmb, both_s.at[1], both_r.at[1])
    ev.take(0)
    ev.start(1)
    for c in keep_loads:
        c.wait()
    for u in range(2):
        chains[u, 0].middle()
    x_copies.append(attend_back(1))
    ev.take(1)
    ev.start(2)
    for u in range(2):
        chains[u, 0].end()
        chains[u, 1].middle()
    for c in both + both2:
        c.wait_recv()
    mix_copy.wait_recv()
    gather_up(0)
    x_copies.append(attend_back(2))
    ev.take(2)
    ev.z_start()
    for u in range(2):
        chains[u, 1].end()
        chains[u, 2].middle()
    gather_up(1)
    x_copies.append(attend_back(3))
    for u in range(2):
        chains[u, 2].end()
        chains[u, 3].middle()
    gather_up(2)
    gather_up(3)

    loads["x"].wait()

    def first_back(i, carry):
        rows = pl.ds(pl.multiple_of(i * 128, 128), 128)
        unit, inverse = norm_stats(xv[rows, :].astype(F32))
        e = e1[rows, :]
        u = e * gain1[...]
        d = dm[rows, :] + inverse * (u - jnp.mean(u, -1, keepdims=True) - unit * jnp.mean(u * unit, -1, keepdims=True))
        gm[rows, :] = d.astype(BF)
        for k, v in enumerate((e * unit, e)):
            late[k : k + 1, :] += jnp.sum(v, 0, keepdims=True)
        return carry

    lax.fori_loop(0, T // 128, first_back, 0)
    return_copies(p, gm, gcl, gc_s, gc_r, here.at[1])
    lv = Vectors(p, late, lland, lzland, lv_s, lv_r, lz_s, lz_r)
    lv.start(0)
    chains[2, 0].middle()
    for u in range(2):
        chains[u, 3].end()
    chains[2, 1].middle()
    lv.take(0)
    lv.start(1)
    chains[2, 0].end()
    chains[2, 2].middle()
    chains[2, 1].end()
    lv.take(1)
    lv.start(2)
    chains[2, 3].middle()
    chains[2, 2].end()
    lv.take(2)
    lv.z_start()

    def final(u):
        for r in (1, 2, 3):
            chains[u, order.index(r)].three.wait_recv()
        total = chains[u, 0].total()
        for r in (1, 2, 3):
            total = total + land3[u, r - 1].astype(F32)
        return total

    gup_out[...] = final(0)
    gdown_out[...] = jnp.transpose(final(1), (1, 0))
    ev.z_wait()
    shard = early[0:1, :]
    for r in (1, 2, 3):
        shard = shard + ezland[r - 1, r : r + 1, :]
    early_out[...] = early[...] + ezland[0] + ezland[1] + ezland[2]
    early_out[0:1, :] = shard
    chains[2, 3].end()

    return_wait(p, gcl, gc_r, here.at[1])
    for s in range(2):
        dm[pl.ds(s * 256, 256), :] = gcl[s].astype(F32)
    ends = [pltpu.make_async_copy(dm.at[pl.ds(s * 256, 256)], grad_cells.at[s], store.at[s]) for s in range(2)]
    for c in ends:
        c.start()
    lv.z_wait()
    late_out[...] = late[...] + lzland[0] + lzland[1] + lzland[2]
    for k in (2, 3):
        shard = late[k : k + 1, 0:256]
        for r in (1, 2, 3):
            shard = shard + lzland[r - 1, k : k + 1, r * 256 : (r + 1) * 256]
        late_out[k : k + 1, 0:256] = shard
    total = final(2)
    gq_out[...] = total[:, 0:256]
    gk_out[...] = total[:, 256:512]
    gv_out[...] = total[:, 512:768]
    go_out[...] = jnp.transpose(total[:, 768:1024], (1, 0))

    return_wait(p, out_cells, res_r, here.at[0])
    for c in ends:
        c.wait()
    for c in both2 + [mix_copy, x_copies[2], x_copies[3]]:
        c.wait_send()
    for c in chains.values():
        c.sent()
    return_sent(p, res_in, res_s)
    return_sent(p, gm, gc_s)


def backward(*args):
    s = jax.ShapeDtypeStruct
    hbm, fast = pl.BlockSpec(memory_space=pltpu.HBM), pl.BlockSpec(memory_space=pltpu.VMEM)
    b, f, dma = (lambda *x: pltpu.VMEM(x, BF)), (lambda *x: pltpu.VMEM(x, F32)), (lambda *x: pltpu.SemaphoreType.DMA(x))
    return pl.pallas_call(
        backward_kernel,
        out_shape=[
            s((2, 256, 1024), BF), s((2, 256, 1024), F32), s((PART, 256), F32), s((PART, 256), F32), s((PART, 256), F32),
            s((256, PART), F32), s((PART, 1024), F32), s((1024, PART), F32), s((8, 1024), F32), s((8, 1024), F32),
        ],
        in_specs=[hbm] * 14 + [fast] * 2,
        out_specs=[hbm] * 2 + [fast] * 8,
        scratch_shapes=[
            b(12, 2, PART, 1024), b(12, PART, 1024), b(3, 3, PART, 1024), b(8, 2, PART, 1024), b(4, 4 * PART, 1024), b(2, 1024, 768),
            b(1024, 1024), b(4, T, 256), b(4, 2 * T, 256), b(4, 2 * T, 256), b(T, 1024), b(T, 1024), f(T, 1024), f(T, 1024),
            b(T, 2 * T), b(T, 2 * T), b(1024, T), b(T, 1024), b(T, 1024), b(T, 1024), b(2, 2 * T, T), f(16, 1, T),
            b(2, 5 * T, 256), b(2, 5 * T, 256), b(2 * T, 768), b(2, 256, 1024),
            b(256, 2 * T), b(256, T), b(256, T), b(256, T), f(8, 1024), f(8, 1024), f(3, 8, 1024), f(3, 8, 1024), f(3, 8, 1024), f(3, 8, 1024),
            dma(12, 3), dma(12, 3), dma(3, 3), dma(3, 3), dma(2), dma(2), dma(2), dma(2), dma(2, 4), dma(2, 4), dma(2), dma(2),
            pltpu.SemaphoreType.DMA, pltpu.SemaphoreType.DMA, dma(3), dma(3), dma(3), dma(3), dma(3), dma(3), dma(3), dma(3),
            pltpu.SemaphoreType.REGULAR, dma(2), dma(19), dma(2), dma(2),
        ],
        compiler_params=pltpu.CompilerParams(collective_id=1, has_side_effects=True, vmem_limit_bytes=63 * 2**20),
    )(*args)


def forward(*args):
    s = jax.ShapeDtypeStruct
    outs = [
        (T, 1024), (T, 1024), (4, T, 256), (4, 2 * T, 256), (4, 2 * T, 256), (T, 1024), (16, 2 * T, T), (16, 1, T),
        (4, 1024, 768), (1024, 1024), (3, 1024, 1024), (3, 1024, 1024), (T, 1024), (T, 1024), (4, T, 1024), (4, T, 1024), (16, 1024),
    ]
    wide = (7, 13, 16)
    hbm, fast = pl.BlockSpec(memory_space=pltpu.HBM), pl.BlockSpec(memory_space=pltpu.VMEM)
    b, f, dma = (lambda *x: pltpu.VMEM(x, BF)), (lambda *x: pltpu.VMEM(x, F32)), (lambda *x: pltpu.SemaphoreType.DMA(x))
    sems = []
    for parts in (3, 1, 1, 1):
        sems += [dma(6, parts), dma(3, parts), dma(3, 7), dma(3, 8)]
    return pl.pallas_call(
        forward_kernel,
        out_shape=[s(o, F32 if n in wide else BF) for n, o in enumerate(outs)],
        in_specs=[hbm, hbm, fast] + [hbm] * 6 + [fast] * 7,
        out_specs=[hbm] * 16 + [fast],
        scratch_shapes=[
            b(T, 1024), b(T, 1024), b(T, 1024), b(4, 1024, 768), b(1024, 1024), b(4, T, 256), b(4, 2 * T, 256), b(4, 2 * T, 256),
            b(T, 1024), b(2, 2 * T, T), f(16, 1, T), b(2, 2 * T, 128), b(256, 2 * T), b(256, T), f(T, 1024), b(T, 1024),
            b(1024, T), b(T, 2 * T), b(T, 2 * T), f(T, 1024), f(T, 1024),
            b(2, 1024, 1024), b(2, 1024, 1024), b(2, T, 1024), b(2, T, 1024), b(2, T, 1024), b(2, T, 1024), b(T, 1024), b(T, 1024),
            f(8, 128), f(1, 1536), f(1, 1536), f(1, 1536),
        ]
        + sems
        + [dma(2, 2), dma(2, 2), dma(4), dma(4), dma(4, 2), dma(4, 2), dma(2, 4), dma(2, 4), dma(2, 2), dma(2, 2),
           pltpu.SemaphoreType.REGULAR, dma(6), dma(2, 2), dma(15)],
        compiler_params=pltpu.CompilerParams(collective_id=0, has_side_effects=True, vmem_limit_bytes=62 * 2**20),
    )(*args)


def body(*args):
    if lax.axis_size("dp") == 8 and lax.axis_size("mp") == 4:
        return fused_body(*args)
    return plain_body(*args)


def fused_body(
    cells,
    lengths,
    query_matrix,
    key_matrix,
    value_matrix,
    query_bias,
    value_bias,
    output_matrix,
    b_out,
    gain_one,
    shift_one,
    gain_two,
    shift_two,
    expand_weight,
    expand_bias,
    contract_weight,
    b_down,
    grad_out,
):
    slots = cells.shape[0]
    n_dp, n_mp = lax.axis_size("dp"), lax.axis_size("mp")
    d, z = lax.axis_index("dp"), lax.axis_index("mp")
    row = lambda v: v.reshape(1, -1)
    small = row(jnp.concatenate([query_bias, value_bias, expand_bias]))
    len_own = jnp.pad(jnp.broadcast_to(lengths.astype(F32)[:, None], (slots, 128)), ((0, 8 - slots), (0, 0)))
    (x, rows_one, q_all, k_all, v_all, mixed_all, e_all, r_all, wa, wo, _, _, res, d_middle, gu, gd, vec) = forward(
        cells, grad_out, len_own, query_matrix, key_matrix, value_matrix, output_matrix, expand_weight, contract_weight,
        small, row(b_out), row(gain_one), row(shift_one), row(gain_two), row(shift_two), row(b_down),
    )
    out_cells, grad_cells, gq, gk, gv, go, gup, gdown, early, late = backward(
        x, rows_one, q_all, k_all, v_all, mixed_all, e_all, r_all, wa, wo, res, d_middle, gu, gd, vec, row(gain_one)
    )
    cut = lambda v, at, size: lax.dynamic_slice_in_dim(v, at * size, size, 0)
    width, hw = cells.shape[2], query_matrix.shape[1]
    at, size = d * n_mp + z, width // (n_dp * n_mp)
    return (
        out_cells,
        grad_cells,
        gq,
        gk,
        gv,
        cut(late[2], d, hw // n_dp),
        cut(late[3], d, hw // n_dp),
        go,
        cut(early[4], at, size),
        cut(late[0], at, size),
        cut(late[1], at, size),
        cut(early[5], at, size),
        cut(early[6], at, size),
        gup,
        cut(early[0], d, expand_weight.shape[1] // n_dp),
        gdown,
        cut(early[7], at, size),
    )


def solution(mesh):
    return jax.shard_map(
        body,
        mesh=mesh,
        in_specs=(
            P("dp", "mp", None),
            P("dp"),
            P(None, "mp"),
            P(None, "mp"),
            P(None, "mp"),
            P("mp"),
            P("mp"),
            P("mp", None),
            P(),
            P(),
            P(),
            P(),
            P(),
            P(None, "mp"),
            P("mp"),
            P("mp", None),
            P(),
            P("dp", "mp", None),
        ),
        out_specs=(
            P("dp", "mp", None),
            P("dp", "mp", None),
            P("dp", "mp"),
            P("dp", "mp"),
            P("dp", "mp"),
            P(("mp", "dp")),
            P(("mp", "dp")),
            P("mp", "dp"),
            P(("dp", "mp")),
            P(("dp", "mp")),
            P(("dp", "mp")),
            P(("dp", "mp")),
            P(("dp", "mp")),
            P("dp", "mp"),
            P(("mp", "dp")),
            P("mp", "dp"),
            P(("dp", "mp")),
        ),
        check_vma=False,
    )
```

```python
import jax
import jax.numpy as jnp
from jax import lax
from jax.experimental import pallas as pl
from jax.experimental.pallas import tpu as pltpu
from jax.sharding import PartitionSpec as P

HD = 64
EPS = 1e-05
BF = jnp.bfloat16
F32 = jnp.float32
MESH = pl.DeviceIdType.MESH
T = 512
PART = 128


def dot(a, b, ca, cb):
    return lax.dot_general(a, b, (((ca,), (cb,)), ((), ())), preferred_element_type=F32)


def cross(x, bit):
    n = lax.axis_size("dp")
    return lax.ppermute(x, "dp", [(i, i ^ (1 << bit)) for i in range(n)])


def shift(x, by):
    n = lax.axis_size("mp")
    return lax.ppermute(x, "mp", [(i, (i + by) % n) for i in range(n)])


def moves(n_dp, n_mp, slots):
    per = n_mp // slots
    turns = []
    for t in range(slots):
        pairs = []
        for d in range(n_dp):
            for m in range(n_mp):
                s = (t + m) % slots
                base, c = d - d % per, d % per
                target = (base + m // slots, c * slots + s)
                pairs.append((d * n_mp + m, target[0] * n_mp + target[1]))
        turns.append(pairs)
    return turns


def plane_bits(n_dp, flip):
    bits = list(range(1, n_dp.bit_length() - 1))
    return bits[::-1] if flip else bits


def gather(piece, flip):
    n_dp, n_mp = lax.axis_size("dp"), lax.axis_size("mp")
    stack = jnp.stack([shift(piece, n_mp - r) for r in range(1, n_mp)])
    held = {0: stack}
    for bit in plane_bits(n_dp, flip) + [0]:
        held.update({i ^ (1 << bit): cross(v, bit) for i, v in list(held.items())})
    return held


def assemble(held, own, d):
    n = len(held)
    stack = jnp.stack([held[i] for i in range(n)])
    order = jnp.arange(n) ^ d
    placed = jnp.take(stack, order, axis=0)
    placed = jnp.moveaxis(placed, 0, 1).reshape((stack.shape[1], -1, stack.shape[-1]))
    return [own] + [placed[r] for r in range(placed.shape[0])]


def scatter(blocks, flip):
    n_dp = lax.axis_size("dp")
    for bit in plane_bits(n_dp, flip):
        keep = sorted(i for i in blocks if not i >> bit & 1)
        got = cross(jnp.stack([blocks[i ^ (1 << bit)] for i in keep]), bit)
        blocks = {
            i: (blocks[i].astype(F32) + got[k].astype(F32)).astype(blocks[i].dtype)
            for k, i in enumerate(keep)
        }
    return blocks[0]


def layer_norm(v, gain, bias):
    center = v - jnp.mean(v, -1, keepdims=True)
    inverse = lax.rsqrt(jnp.mean(center * center, -1, keepdims=True) + EPS)
    unit = center * inverse
    return unit * gain + bias, unit, inverse


def norm_back(up, unit, inverse, gain):
    u = up * gain
    return inverse * (
        u - jnp.mean(u, -1, keepdims=True) - unit * jnp.mean(u * unit, -1, keepdims=True)
    )


def gelu_pair(v):
    cumulative = 0.5 * (1.0 + lax.erf(v * 0.7071067811865476))
    density = jnp.exp(-0.5 * v * v) * 0.3989422804014327
    return v * cumulative, cumulative + v * density


def attend(q, k, v, allowed):
    heads = q.shape[1] // HD
    qh = q.reshape(-1, heads, HD)
    kh = k.reshape(-1, heads, HD)
    vh = v.reshape(-1, heads, HD)
    s = jnp.einsum("qhd,khd->hqk", qh, kh, preferred_element_type=F32) * HD**-0.5
    s = jnp.where(allowed[None, None, :], s, -1e30)
    e = jnp.exp(s - jnp.max(s, -1, keepdims=True))
    p = (e / jnp.sum(e, -1, keepdims=True)).astype(BF)
    mixed = jnp.einsum("hqk,khd->qhd", p, vh, preferred_element_type=F32)
    return mixed.astype(BF).reshape(q.shape), p


def attend_back(q, k, v, p, mixed, dm):
    heads = q.shape[1] // HD
    qh = q.reshape(-1, heads, HD)
    kh = k.reshape(-1, heads, HD)
    vh = v.reshape(-1, heads, HD)
    dh = dm.reshape(-1, heads, HD)
    pf = p.astype(F32)
    dp = jnp.einsum("qhd,khd->hqk", dh, vh, preferred_element_type=F32)
    total = jnp.sum(dp * pf, -1, keepdims=True)
    ds = (pf * (dp - total)).astype(BF)
    dv = jnp.einsum("hqk,qhd->khd", p, dh, preferred_element_type=F32)
    dq = jnp.einsum("hqk,khd->qhd", ds, kh, preferred_element_type=F32) * HD**-0.5
    dk = jnp.einsum("hqk,qhd->khd", ds, qh, preferred_element_type=F32) * HD**-0.5
    return (
        dq.astype(BF).reshape(q.shape),
        dk.astype(BF).reshape(k.shape),
        dv.astype(BF).reshape(k.shape),
    )


def plain_body(
    cells,
    lengths,
    query_matrix,
    key_matrix,
    value_matrix,
    query_bias,
    value_bias,
    output_matrix,
    b_out,
    gain_one,
    shift_one,
    gain_two,
    shift_two,
    expand_weight,
    expand_bias,
    contract_weight,
    b_down,
    grad_out,
):
    slots, rows, width = cells.shape
    n_dp, n_mp = lax.axis_size("dp"), lax.axis_size("mp")
    d, z = lax.axis_index("dp"), lax.axis_index("mp")
    per = n_mp // slots
    core = d % per
    tokens = slots * rows
    part = width // n_dp
    hw = query_matrix.shape[1]
    turns = moves(n_dp, n_mp, slots)

    def bring(x):
        got = [
            lax.ppermute(
                lax.dynamic_index_in_dim(x, (t + z) % slots, 0, False), ("dp", "mp"), turns[t]
            )
            for t in range(slots)
        ]
        even = z % slots == 0
        return jnp.concatenate(
            [jnp.where(even, got[0], got[1]), jnp.where(even, got[1], got[0])], 0
        )

    def give_back(x):
        x = x.reshape(slots, rows, width)
        got = [
            lax.ppermute(
                lax.dynamic_index_in_dim(x, (t + z) % slots, 0, False),
                ("dp", "mp"),
                [(b, a) for a, b in turns[t]],
            )
            for t in range(slots)
        ]
        even = z % slots == 0
        return jnp.stack(
            [jnp.where(even, got[0], got[1]), jnp.where(even, got[1], got[0])], 0
        )

    mine = bring(cells)
    attn_own = jnp.concatenate(
        [query_matrix, key_matrix, value_matrix, output_matrix.T], 1
    )
    first = d * part

    def piece_of(w):
        return lax.dynamic_slice_in_dim(w, first, part, 0)

    half = attn_own.shape[1] // 2
    a_piece = piece_of(attn_own)
    a_left = gather(a_piece[:, :half], False)
    a_right = gather(a_piece[:, half:], True)
    u_held = gather(piece_of(expand_weight), False)
    d_held = gather(piece_of(contract_weight), True)
    grad_rows = bring(grad_out)
    small = jnp.concatenate([query_bias, value_bias, expand_bias])
    small = [small] + [shift(small, n_mp - r) for r in range(1, n_mp)]
    both = cross(lengths, 0)
    length_all = jnp.where(core == 0, jnp.concatenate([lengths, both]), jnp.concatenate([both, lengths]))
    length = lax.dynamic_index_in_dim(length_all, z, 0, False)

    attn_w = [
        jnp.concatenate([a, b], 1)
        for a, b in zip(
            assemble(a_left, attn_own[:, :half], d), assemble(a_right, attn_own[:, half:], d)
        )
    ]
    up_w = assemble(u_held, expand_weight, d)
    down_w = assemble(d_held, contract_weight, d)

    position = core * tokens + jnp.arange(tokens)
    keep = (position < length).astype(F32)[:, None]
    sib_position = (per - 1 - core) * tokens + jnp.arange(tokens)
    allowed = jnp.concatenate([position, sib_position]) < length

    x = mine.astype(F32)
    rows_one, unit_one, inv_one = layer_norm(x, gain_one, shift_one)
    rows_one = rows_one.astype(BF)
    kept = []
    attention = jnp.zeros((tokens, width), F32)
    for r in range(n_mp):
        w = attn_w[r]
        q = (dot(rows_one, w[:, :hw], 1, 0) + small[r][:hw]).astype(BF)
        k = dot(rows_one, w[:, hw : 2 * hw], 1, 0).astype(BF)
        v = (dot(rows_one, w[:, 2 * hw : 3 * hw], 1, 0) + small[r][hw : 2 * hw]).astype(BF)
        k = jnp.concatenate([k, cross(k, 0)], 0)
        v = jnp.concatenate([v, cross(v, 0)], 0)
        mixed, p = attend(q, k, v, allowed)
        kept.append((q, k, v, mixed, p))
        attention = attention + dot(mixed, w[:, 3 * hw :], 1, 1)
    middle = x + attention + b_out
    rows_two, unit_two, inv_two = layer_norm(middle, gain_two, shift_two)
    rows_two = rows_two.astype(BF)
    g = keep * grad_rows.astype(F32)
    gz = g.astype(BF)

    order = jnp.arange(0, n_dp, 2) ^ d

    def chosen(v):
        return jnp.take(v.reshape(v.shape[0], n_dp, part), order, axis=1).reshape(v.shape[0], -1)

    def other(v):
        return jnp.take(v.reshape(v.shape[0], n_dp, part), order ^ 1, axis=1).reshape(v.shape[0], -1)

    def both_cores(v):
        return jnp.concatenate([chosen(v), cross(other(v), 0)], 0)

    def weight_grad(left, right, flip):
        right = jnp.concatenate([right, cross(right, 0)], 0)
        return weight_grad_all(left, right, flip)

    def weight_grad_all(left, right, flip):
        got = dot(left, right, 0, 0).astype(BF).reshape(-1, part, right.shape[1])
        return scatter({2 * i: got[i] for i in range(got.shape[0])}, flip)

    def finish(pieces):
        total = pieces[0].astype(F32)
        for r in range(1, n_mp):
            total = total + shift(pieces[r], r).astype(F32)
        return total

    two_both = both_cores(rows_two)
    gz_both = both_cores(gz)
    result = middle + b_down
    e2 = jnp.zeros((tokens, width), F32)
    up_parts, down_parts, b_up = [], [], []
    for r in range(n_mp):
        upper = dot(rows_two, up_w[r], 1, 0) + small[r][2 * hw :]
        hidden, slope = gelu_pair(upper)
        hidden = hidden.astype(BF)
        result = result + dot(hidden, down_w[r], 1, 0)
        d_upper = (dot(gz, down_w[r], 1, 1) * slope).astype(BF)
        e2 = e2 + dot(d_upper, up_w[r], 1, 1)
        up_parts.append(weight_grad(two_both, d_upper, False))
        down_parts.append(weight_grad(gz_both, hidden, True))
        b_up.append(jnp.sum(d_upper.astype(F32), 0))
    out_cells = give_back((keep * result).astype(BF))
    grad_up = finish(up_parts)
    grad_down = finish(down_parts).T

    d_middle = g + norm_back(e2, unit_two, inv_two, gain_two)
    gm = d_middle.astype(BF)
    gm_both = both_cores(gm)
    one_both = both_cores(rows_one)
    e1 = jnp.zeros((tokens, width), F32)
    a_parts, b_q, b_v = [], [], []
    for r in range(n_mp):
        q, k, v, mixed, p = kept[r]
        w = attn_w[r]
        d_mixed = dot(gm, w[:, 3 * hw :], 1, 0).astype(BF)
        dq, dk, dv = attend_back(q, k, v, p, mixed, d_mixed)
        dk_all = (dk.astype(F32) + jnp.roll(cross(dk, 0), tokens, 0).astype(F32)).astype(BF)
        dv_all = (dv.astype(F32) + jnp.roll(cross(dv, 0), tokens, 0).astype(F32)).astype(BF)
        dq_all = jnp.concatenate([dq, cross(dq, 0)], 0)
        e1 = (
            e1
            + dot(dq, w[:, :hw], 1, 1)
            + dot(dk_all[:tokens], w[:, hw : 2 * hw], 1, 1)
            + dot(dv_all[:tokens], w[:, 2 * hw : 3 * hw], 1, 1)
        )
        b_q.append(jnp.sum(dq.astype(F32), 0))
        b_v.append(jnp.sum(dv_all[:tokens].astype(F32), 0))
        qkv_part = weight_grad_all(one_both, jnp.concatenate([dq_all, dk_all, dv_all], 1), r % 2 == 1)
        o_part = weight_grad(gm_both, mixed, r % 2 == 0)
        a_parts.append(jnp.concatenate([qkv_part, o_part], 1))
    d_cells = d_middle + norm_back(e1, unit_one, inv_one, gain_one)
    grad_cells = give_back(d_cells.astype(BF)).astype(F32)
    grad_attn = finish(a_parts)

    split_mp = [jnp.stack(b_q).reshape(n_mp, n_dp, -1), jnp.stack(b_v).reshape(n_mp, n_dp, -1), jnp.stack(b_up).reshape(n_mp, n_dp, -1)]
    sums = [
        jnp.sum(d_middle, 0),
        jnp.sum(e1 * unit_one, 0),
        jnp.sum(e1, 0),
        jnp.sum(e2 * unit_two, 0),
        jnp.sum(e2, 0),
        jnp.sum(g, 0),
    ]
    split_dp = [jnp.roll(jnp.swapaxes(s.reshape(n_dp, n_mp, -1), 0, 1), -z, 0) for s in sums]
    packed = jnp.concatenate(split_mp + split_dp, 2)
    packed = jnp.take(packed, jnp.arange(n_dp) ^ d, axis=1)
    packed = packed[:, 0::2] + cross(packed[:, 1::2], 0)
    packed = scatter({2 * i: packed[:, i] for i in range(packed.shape[1])}, False)
    vec = packed[0]
    for r in range(1, n_mp):
        vec = vec + shift(packed[r], r)
    nq = split_mp[0].shape[2]
    nu = split_mp[2].shape[2]
    ns = split_dp[0].shape[2]
    vq, vv, vu = vec[:nq], vec[nq : 2 * nq], vec[2 * nq : 2 * nq + nu]
    rest = [vec[2 * nq + nu + i * ns : 2 * nq + nu + (i + 1) * ns] for i in range(6)]
    return (
        out_cells,
        grad_cells,
        grad_attn[:, :hw],
        grad_attn[:, hw : 2 * hw],
        grad_attn[:, 2 * hw : 3 * hw],
        vq,
        vv,
        grad_attn[:, 3 * hw :].T,
        rest[0],
        rest[1],
        rest[2],
        rest[3],
        rest[4],
        grad_up,
        vu,
        grad_down,
        rest[5],
    )


def dg(a, b, ca, cb):
    return lax.dot_general(a, b, (((ca,), (cb,)), ((), ())), preferred_element_type=F32)


def lane_block(start, size=128):
    return pl.ds(pl.multiple_of(start, size), size)


class Place:
    def __init__(self):
        self.d, self.z = lax.axis_index("dp"), lax.axis_index("mp")
        self.bit = [lax.rem(self.d // (1 << b), 2) for b in range(3)]
        self.core = self.bit[0]
        self.base = self.d - self.core

    def across(self, i):
        v = self.d
        for b in range(3):
            if i >> b & 1:
                v = v + (1 << b) * (1 - 2 * self.bit[b])
        return v

    def rows(self, i):
        return lane_block(self.across(i) * PART, PART)

    def greet(self):
        barrier = pltpu.get_barrier_semaphore()
        for step in range(1, 4):
            for c in range(2):
                pl.semaphore_signal(
                    barrier,
                    inc=1,
                    device_id=(self.base + c, lax.rem(self.z + step, 4)),
                    device_id_type=MESH,
                )
        for i in (1, 2, 4):
            pl.semaphore_signal(barrier, inc=1, device_id=(self.across(i), self.z), device_id_type=MESH)
        pl.semaphore_wait(barrier, 9)


def remote(src, dst, send, recv, device):
    return pltpu.make_async_remote_copy(
        src_ref=src, dst_ref=dst, send_sem=send, recv_sem=recv, device_id=device, device_id_type=MESH
    )


class Unit:
    def __init__(self, place, own, at, parts, zsend, zrecv, send, recv, flip, slots):
        self.p, self.own, self.at, self.parts = place, own, at, parts
        self.zsend, self.zrecv, self.send, self.recv = zsend, zrecv, send, recv
        self.flip, self.slots = flip, slots

    def bits(self, n):
        return (4, 2) if (n % 2 == 1) == self.flip else (2, 4)

    def copy(self, k, slot_from, slot_to, device):
        return [
            remote(
                self.own(q) if slot_from is None else self.at(slot_from, 0, q),
                self.at(slot_to, 0, q),
                self.zsend.at[k, q],
                self.zrecv.at[slot_to - 1, q],
                device,
            )
            for q in range(self.parts)
        ]

    def direct(self, k):
        return self.copy(k - 1, None, k, (self.p.d, lax.rem(self.p.z + 4 - k, 4)))

    def along(self, k, slot_from, slot_to, right):
        return self.copy(k, slot_from, slot_to, (self.p.d, self.p.z + 1 if right else self.p.z - 1))

    def steps(self):
        z = self.p.z
        inner = jnp.logical_and(z >= 1, z <= 2)
        return [
            (z <= 2, (0, None, 3, True)),
            (z >= 1, (1, None, 1, False)),
            (inner, (2, 3, 2, True)),
            (inner, (3, 1, 2, False)),
            (z == 1, (4, 2, 3, False)),
            (z == 2, (5, 2, 1, True)),
        ]

    def go(self, k):
        cond, what = self.steps()[k]

        @pl.when(cond)
        def _():
            for c in self.along(*what):
                c.start()

    def start(self):
        self.go(0)
        self.go(1)

    def start_direct(self):
        for k in (1, 3, 2):
            for c in self.direct(k):
                c.start()

    def landed(self, slot):
        for q in range(self.parts):
            here = self.at(slot, 0, q)
            remote(here, here, self.zsend.at[0, q], self.zrecv.at[slot - 1, q], (self.p.across(1), self.p.z)).wait_recv()

    def xy(self, n, k, i, bit):
        slot = self.slots[n]
        here = self.at(slot, i, None)
        return remote(
            here,
            here,
            self.send.at[slot - 1, k],
            self.recv.at[slot - 1, i ^ bit],
            (self.p.across(bit), self.p.z),
        )

    def arrived(self, n, i):
        slot = self.slots[n]
        here = self.at(slot, i, None)
        remote(here, here, self.send.at[slot - 1, 0], self.recv.at[slot - 1, i], (self.p.across(1), self.p.z)).wait_recv()

    def one(self, n):
        self.xy(n, 0, 0, self.bits(n)[0]).start()

    def take(self, n):
        self.landed(self.slots[n])
        self.one(n)

    def hop_one(self):
        self.landed(self.slots[0])
        self.go(3)
        self.one(0)

        @pl.when(jnp.logical_and(self.p.z >= 1, self.p.z <= 2))
        def _():
            self.landed(self.slots[1])
            for c in self.along(*self.steps()[2][1]):
                c.start()
            self.one(1)

    def hop_two(self):
        inner = jnp.logical_and(self.p.z >= 1, self.p.z <= 2)

        @pl.when(inner)
        def _():
            self.landed(self.slots[2])

        self.go(4)
        self.go(5)

        @pl.when(inner)
        def _():
            self.one(2)

        @pl.when(jnp.logical_not(inner))
        def _():
            self.take(1)

    def hop_three(self):
        @pl.when(jnp.logical_not(jnp.logical_and(self.p.z >= 1, self.p.z <= 2)))
        def _():
            self.take(2)

    def two(self, n):
        first, second = self.bits(n)
        self.arrived(n, first)
        self.xy(n, 1, 0, second).start()
        self.xy(n, 2, first, second).start()

    def three(self, n):
        first, second = self.bits(n)
        self.arrived(n, second)
        self.arrived(n, 6)
        for k, i in enumerate((0, 2, 4, 6)):
            self.xy(n, 3 + k, i, 1).start()

    def whole(self, n):
        for i in (1, 3, 5, 7):
            self.arrived(n, i)

    def finish(self, direct):
        if direct:
            for k in (1, 2, 3):
                for c in self.direct(k):
                    c.wait_send()
        else:
            for cond, what in self.steps():

                @pl.when(cond)
                def _(what=what):
                    for c in self.along(*what):
                        c.wait_send()

        for n in range(3):
            first, second = self.bits(n)
            self.xy(n, 0, 0, first).wait_send()
            self.xy(n, 1, 0, second).wait_send()
            self.xy(n, 2, first, second).wait_send()
            for k, i in enumerate((0, 2, 4, 6)):
                self.xy(n, 3 + k, i, 1).wait_send()


def bring_copies(p, src, dst, sends, recvs, here, which=(0, 1)):
    for s in which:
        target = (p.base + p.z // 2, 2 * p.core + s)
        half = lax.rem(p.z, 2)
        rows = lane_block(half * 256, 256)
        same = jnp.logical_and(p.core == p.z // 2, p.z == 2 * p.core + s)

        @pl.when(same)
        def _():
            pltpu.make_async_copy(src.at[s], dst.at[rows], here).start()

        @pl.when(jnp.logical_not(same))
        def _():
            remote(src.at[s], dst.at[rows], sends.at[s], recvs.at[half], target).start()


def bring_wait(p, dst, recvs, here):
    for half in range(2):
        block = dst.at[pl.ds(half * 256, 256)]
        same = jnp.logical_and(p.core == p.z // 2, lax.rem(p.z, 2) == half)

        @pl.when(same)
        def _():
            pltpu.make_async_copy(block, block, here).wait()

        @pl.when(jnp.logical_not(same))
        def _():
            remote(block, block, recvs.at[half], recvs.at[half], (p.across(1), p.z)).wait_recv()


def bring_sent(p, src, sends):
    for s in range(2):
        same = jnp.logical_and(p.core == p.z // 2, p.z == 2 * p.core + s)

        @pl.when(jnp.logical_not(same))
        def _():
            remote(src.at[s], src.at[s], sends.at[s], sends.at[s], (p.across(1), p.z)).wait_send()


def norm_stats(x):
    center = x - jnp.mean(x, -1, keepdims=True)
    inverse = lax.rsqrt(jnp.mean(center * center, -1, keepdims=True) + EPS)
    return center * inverse, inverse


def each_rows(size, total, f):
    def step(i, carry):
        f(pl.ds(pl.multiple_of(i * size, size), size))
        return carry

    lax.fori_loop(0, total // size, step, 0)


def chosen_both(p, t_ref, both_ref, sends, recvs):
    copies = []
    for k, i in enumerate((0, 2, 4, 6)):
        block = pl.ds(k * PART, PART)
        both_ref[block, 0:T] = t_ref[p.rows(i), :]
        copies.append(
            remote(
                t_ref.at[p.rows(i ^ 1)],
                both_ref.at[block, T : 2 * T],
                sends.at[k],
                recvs.at[k],
                (p.across(1), p.z),
            )
        )
    for c in copies:
        c.start()
    return copies


def forward_kernel(
    cells, grad, len_own, wq, wk, wv, wo, up, down, small_own, b_out, gain1, shift1, gain2, shift2, b_down,
    x_out, rows1_out, q_out, k_out, v_out, mix_out, e_out, r_out, wa_out, wo_out, wu, wd, res_out, dm_out, gu_out, gd_out, vec_out, bup_out,
    xv, gv, rows1, wav, wov, qv, kv, vv, mix, eb, rv, bias, vt, ot, middle, rows2, tt, xb, gb, acc, e2,
    uv, dv, ho, du, hs, ds, slope_v, gus, gds, len_sib, small,
    a_zs, a_zr, a_s, a_r, o_zs, o_zr, o_s, o_r, u_zs, u_zr, u_s, u_r, d_zs, d_zr, d_s, d_r,
    act_s, act_r, sm_s, sm_r, kv_s, kv_r, both_s, both_r, hd_s, hd_r, credit, loc, load, store,
):
    p = Place()
    sibling = (p.across(1), p.z)

    ws = (wq, wk, wv)
    own_rows = p.rows(0)

    def a_at(slot, i, part):
        if part is None:
            return wav.at[slot, p.rows(i)]
        return wav.at[slot, p.rows(i), pl.ds(part * 256, 256)]

    fixed = (1, 3, 2)
    inner = jnp.logical_and(p.z >= 1, p.z <= 2)
    by_arrival = (
        jnp.where(p.z <= 2, 1, 3),
        jnp.where(inner, 3, 2),
        jnp.where(inner, 2, jnp.where(p.z == 0, 3, 1)),
    )
    unit_a = Unit(p, lambda q: ws[q].at[own_rows], a_at, 3, a_zs, a_zr, a_s, a_r, True, fixed)
    unit_o = Unit(
        p,
        lambda q: wo.at[:, own_rows],
        lambda slot, i, q: wov.at[pl.ds(slot * 256, 256), p.rows(i)],
        1, o_zs, o_zr, o_s, o_r, False, fixed,
    )
    unit_u = Unit(
        p, lambda q: up.at[own_rows], lambda slot, i, q: wu.at[slot - 1, p.rows(i)], 1, u_zs, u_zr, u_s, u_r, False, by_arrival
    )
    unit_d = Unit(
        p, lambda q: down.at[own_rows], lambda slot, i, q: wd.at[slot - 1, p.rows(i)], 1, d_zs, d_zr, d_s, d_r, True, by_arrival
    )

    own_loads = [pltpu.make_async_copy(w, wav.at[0, :, pl.ds(k * 256, 256)], loc.at[k]) for k, w in enumerate(ws)]
    own_loads.append(pltpu.make_async_copy(wo, wov.at[pl.ds(0, 256)], loc.at[3]))
    for c in own_loads:
        c.start()
    first_loads = [pltpu.make_async_copy(up, uv.at[0], load.at[0, 0]), pltpu.make_async_copy(down, dv.at[0], load.at[1, 0])]
    for c in first_loads:
        c.start()

    p.greet()
    unit_a.start_direct()
    bring_copies(p, cells, xv, act_s.at[0], act_r.at[0], loc.at[4])
    small_copies = []
    for r in (1, 2, 3):
        small_copies.append(remote(small_own, small.at[r], sm_s.at[r], sm_r.at[r], (p.d, lax.rem(p.z + 4 - r, 4))))
    small_copies.append(remote(len_own, len_sib, sm_s.at[0], sm_r.at[0], sibling))
    for c in small_copies:
        c.start()
    small[0] = small_own[...]
    unit_o.start_direct()
    unit_u.start()
    unit_d.start()
    for n in range(3):
        unit_a.take(n)
    for n in range(3):
        unit_a.two(n)

    small_copies[3].wait_recv()
    slot_row = lax.rem(p.z, 2)
    near = jnp.where(p.z // 2 == p.core, 1.0, 0.0)
    length = near * len_own[pl.ds(slot_row, 1), :] + (1.0 - near) * len_sib[pl.ds(slot_row, 1), :]
    length = length[:, :1]
    lane = lax.broadcasted_iota(jnp.int32, (1, 128), 1)
    key = lax.broadcasted_iota(jnp.int32, (2 * T, 128), 0)
    key = jnp.where(key < T, key + p.core * T, key - T + (1 - p.core) * T)
    barred = jnp.where(key.astype(F32) < length, 0.0, -1e30)
    bias[0] = jnp.where(lane == 64, barred, 0.0).astype(BF)
    bias[1] = jnp.where(lane == 0, barred, 0.0).astype(BF)

    def kept(rows_start, size):
        row = lax.broadcasted_iota(jnp.int32, (size, 1), 0) + rows_start + p.core * T
        return row.astype(F32) < length

    for n in range(3):
        unit_a.three(n)

    bring_wait(p, xv, act_r.at[0], loc.at[4])

    def first_norm(rows):
        unit, _ = norm_stats(xv[rows, :].astype(F32))
        rows1[rows, :] = (unit * gain1[...] + shift1[...]).astype(BF)

    each_rows(128, T, first_norm)
    outs = [pltpu.make_async_copy(xv, x_out, store.at[0]), pltpu.make_async_copy(rows1, rows1_out, store.at[1])]
    for c in outs:
        c.start()
    for c in own_loads:
        c.wait()
    for r in (1, 2, 3):
        small_copies[r - 1].wait_recv()

    kv_copies = []

    def project(r):
        b = small.at[r]
        x = rows1[...]
        qv[r] = (dg(x, wav[r, :, 0:256], 1, 0) + b[:, 0:256]).astype(BF)
        kv[r, 0:T, :] = dg(x, wav[r, :, 256:512], 1, 0).astype(BF)
        vv[r, 0:T, :] = (dg(x, wav[r, :, 512:768], 1, 0) + b[:, 256:512]).astype(BF)
        cs = [
            remote(ref.at[r, pl.ds(0, T)], ref.at[r, pl.ds(T, T)], kv_s.at[r, n], kv_r.at[r, n], sibling)
            for n, ref in enumerate((kv, vv))
        ]
        for c in cs:
            c.start()
        kv_copies.append(cs)

    def e_copy(head, slot):
        return pltpu.make_async_copy(eb.at[slot], e_out.at[head], store.at[2 + slot])

    def attend(r):
        for c in kv_copies[r]:
            c.wait_recv()
        vt[...] = jnp.transpose(vv[r], (1, 0))

        def pair(j, carry):
            cols = lane_block(j * 128)
            kp = kv[r, :, cols]
            qp = qv[r, :, cols] * BF(HD**-0.5)
            for h in range(2):
                mine = (lane < 64) if h == 0 else (lane >= 64)
                one = lane == (64 if h == 0 else 0)
                ka = jnp.where(mine, kp, bias[h])
                qa = jnp.where(mine, qp, jnp.where(one, BF(1), BF(0)))
                s = dg(ka, qa, 1, 1)
                e = jnp.exp(s - jnp.max(s, 0, keepdims=True))
                inv = 1.0 / jnp.sum(e, 0, keepdims=True)
                head = r * 4 + 2 * j + h
                if r == 0:
                    @pl.when(j > 0)
                    def _():
                        e_copy(head - 2, h).wait()
                else:
                    e_copy(head - 2, h).wait()
                eb[h] = e.astype(BF)
                e_copy(head, h).start()
                feats = pl.ds(pl.multiple_of(j * 128 + h * 64, 64), 64)
                ot[feats, :] = (dg(vt[feats, :], eb[h], 1, 0) * inv).astype(BF)
                rv[head] = inv
            return carry

        lax.fori_loop(0, 2, pair, 0)
        mix[:, r * 256 : (r + 1) * 256] = jnp.transpose(ot[...], (1, 0))

    project(0)
    for n in range(3):
        unit_a.whole(n)
    for r in (1, 2, 3):
        project(r)
    attend(0)
    for n in range(3):
        unit_o.take(n)
    unit_u.hop_one()
    unit_d.hop_one()
    bring_copies(p, grad, gv, act_s.at[1], act_r.at[1], loc.at[5], (0,))
    attend(1)
    for n in range(3):
        unit_o.two(n)
    unit_u.two(0)
    unit_d.two(0)
    attend(2)
    for n in range(3):
        unit_o.three(n)
    unit_u.hop_two()
    unit_d.hop_two()
    bring_copies(p, grad, gv, act_s.at[1], act_r.at[1], loc.at[5], (1,))
    unit_u.three(0)
    unit_d.three(0)
    attend(3)
    unit_u.hop_three()
    unit_d.hop_three()
    unit_u.two(1)
    unit_d.two(1)
    for n in range(3):
        unit_o.whole(n)
    for h in range(2):
        e_copy(14 + h, h).wait()

    outs += [
        pltpu.make_async_copy(wav, wa_out, store.at[4]),
        pltpu.make_async_copy(wov, wo_out, store.at[5]),
        pltpu.make_async_copy(qv, q_out, store.at[6]),
        pltpu.make_async_copy(kv, k_out, store.at[7]),
        pltpu.make_async_copy(vv, v_out, store.at[8]),
        pltpu.make_async_copy(mix, mix_out, store.at[9]),
        pltpu.make_async_copy(rv, r_out, store.at[10]),
    ]
    for c in outs[2:]:
        c.start()

    for n in range(2):
        cols = pl.ds(n * 512, 512)
        middle[:, cols] = dg(mix[...], wov[:, cols], 1, 0)

    def second_norm(rows):
        m = middle[rows, :] + xv[rows, :].astype(F32) + b_out[...]
        middle[rows, :] = m
        unit, _ = norm_stats(m)
        rows2[rows, :] = (unit * gain2[...] + shift2[...]).astype(BF)
        acc[rows, :] = m + b_down[...]

    each_rows(128, T, second_norm)
    tt[...] = jnp.transpose(rows2[...], (1, 0))
    both = chosen_both(p, tt, xb, both_s.at[0], both_r.at[0])

    def mask_grad(i, carry):
        rows = pl.ds(pl.multiple_of(i * 128, 128), 128)
        gv[rows, :] = jnp.where(kept(i * 128, 128), gv[rows, :].astype(F32), 0.0).astype(BF)
        return carry

    order = (0,) + by_arrival

    def load_copies(n):
        r = order[n]
        return [
            pltpu.make_async_copy(wu.at[r - 1], uv.at[n % 2], load.at[0, n % 2]),
            pltpu.make_async_copy(wd.at[r - 1], dv.at[n % 2], load.at[1, n % 2]),
        ]

    def hidden(n):
        r, slot = order[n], n % 2
        for k in range(2):
            c = pl.ds(k * 512, 512)
            upper = dg(rows2[...], uv[slot, :, c], 1, 0) + small[r, :, pl.ds(512 + k * 512, 512)]
            act, slope = gelu_pair(upper)
            ho[slot, :, c] = act.astype(BF)
            slope_v[slot, :, c] = slope
        if n >= 2:
            pl.semaphore_wait(credit, 1)
        copy = remote(ho.at[slot], hs.at[slot], hd_s.at[0, slot], hd_r.at[0, slot], sibling)
        copy.start()
        for k in range(2):
            c = pl.ds(k * 512, 512)
            acc[:, c] = acc[:, c] + dg(ho[slot], dv[slot, :, c], 1, 0)
        return copy

    def hidden_back(n):
        r, slot = order[n], n % 2
        for k in range(2):
            c = pl.ds(k * 512, 512)
            d_up = (dg(gv[...], dv[slot, c, :], 1, 1) * slope_v[slot, :, c]).astype(BF)
            du[slot, :, c] = d_up
            bup_out[r, :, c] = jnp.sum(d_up.astype(F32), 0, keepdims=True)
        copy = remote(du.at[slot], ds.at[slot], hd_s.at[1, slot], hd_r.at[1, slot], sibling)
        copy.start()
        for k in range(2):
            c = pl.ds(k * 512, 512)
            new = dg(du[slot], uv[slot, c, :], 1, 1)
            e2[:, c] = new if n == 0 else e2[:, c] + new
        return copy

    g_stores = [None, None]

    def weight_grads(n, cs):
        r, slot = order[n], n % 2
        for c in cs:
            c.wait_recv()
        if n >= 1:
            for c in g_stores:
                c.wait()
        gus[...] = (dg(xb[:, 0:T], du[slot], 1, 0) + dg(xb[:, T : 2 * T], ds[slot], 1, 0)).astype(BF)
        gds[...] = (dg(gb[:, 0:T], ho[slot], 1, 0) + dg(gb[:, T : 2 * T], hs[slot], 1, 0)).astype(BF)
        if n < 2:
            pl.semaphore_signal(credit, inc=1, device_id=sibling, device_id_type=MESH)
        g_stores[0] = pltpu.make_async_copy(gus, gu_out.at[r], store.at[11])
        g_stores[1] = pltpu.make_async_copy(gds, gd_out.at[r], store.at[12])
        for c in g_stores:
            c.start()
        for c in cs:
            c.wait_send()

    for c in first_loads:
        c.wait()
    held = [[hidden(0)]]
    unit_u.three(1)
    unit_d.three(1)
    unit_u.two(2)
    unit_d.two(2)
    unit_u.whole(0)
    unit_d.whole(0)
    loads = load_copies(1)
    for c in loads:
        c.start()
    for c in both:
        c.wait_send()
    for c in loads:
        c.wait()
    held.append([hidden(1)])
    unit_u.three(2)
    unit_d.three(2)
    bring_wait(p, gv, act_r.at[1], loc.at[5])
    lax.fori_loop(0, T // 128, mask_grad, 0)
    tt[...] = jnp.transpose(gv[...], (1, 0))
    both2 = chosen_both(p, tt, gb, both_s.at[1], both_r.at[1])
    held[0].append(hidden_back(0))
    unit_u.whole(1)
    unit_d.whole(1)
    loads = load_copies(2)
    for c in loads:
        c.start()
    held[1].append(hidden_back(1))
    for c in both + both2:
        c.wait_recv()
    weight_grads(0, held[0])
    for c in loads:
        c.wait()
    held.append([hidden(2)])
    unit_u.whole(2)
    unit_d.whole(2)
    loads = load_copies(3)
    for c in loads:
        c.start()
    held[2].append(hidden_back(2))
    weight_grads(1, held[1])
    for c in loads:
        c.wait()
    held.append([hidden(3)])
    held[3].append(hidden_back(3))
    weight_grads(2, held[2])
    weight_grads(3, held[3])

    vec_out[...] = jnp.zeros(vec_out.shape, F32)

    def last(i, carry):
        rows = pl.ds(pl.multiple_of(i * 128, 128), 128)
        res = jnp.where(kept(i * 128, 128), acc[rows, :], 0.0)
        rows2[rows, :] = res.astype(BF)
        unit, inverse = norm_stats(middle[rows, :])
        e = e2[rows, :]
        g = gv[rows, :].astype(F32)
        u = e * gain2[...]
        d_mid = g + inverse * (u - jnp.mean(u, -1, keepdims=True) - unit * jnp.mean(u * unit, -1, keepdims=True))
        middle[rows, :] = d_mid
        for k, v in enumerate((d_mid, e * unit, e, g)):
            vec_out[4 + k : 5 + k, :] += jnp.sum(v, 0, keepdims=True)
        return carry

    lax.fori_loop(0, T // 128, last, 0)
    ends = [pltpu.make_async_copy(rows2, res_out, store.at[13]), pltpu.make_async_copy(middle, dm_out, store.at[14])]
    for c in ends:
        c.start()
    for c in ends + outs + g_stores:
        c.wait()
    for c in both2 + small_copies:
        c.wait_send()
    for cs in kv_copies:
        for c in cs:
            c.wait_send()
    for unit in (unit_a, unit_o, unit_u, unit_d):
        unit.finish(unit is unit_a or unit is unit_o)
    bring_sent(p, cells, act_s.at[0])
    bring_sent(p, grad, act_s.at[1])


def return_copies(p, src, dst, sends, recvs, here):
    slot = lax.rem(p.z, 2)
    for h in range(2):
        rows = src.at[pl.ds(h * 256, 256)]
        same = jnp.logical_and(p.core == p.z // 2, p.z == 2 * p.core + h)

        @pl.when(same)
        def _():
            pltpu.make_async_copy(rows, dst.at[slot], here).start()

        @pl.when(jnp.logical_not(same))
        def _():
            remote(rows, dst.at[slot], sends.at[h], recvs.at[slot], (p.base + p.z // 2, 2 * p.core + h)).start()


def return_wait(p, dst, recvs, here):
    for s in range(2):
        same = jnp.logical_and(p.core == p.z // 2, p.z == 2 * p.core + s)

        @pl.when(same)
        def _():
            pltpu.make_async_copy(dst.at[s], dst.at[s], here).wait()

        @pl.when(jnp.logical_not(same))
        def _():
            remote(dst.at[s], dst.at[s], recvs.at[s], recvs.at[s], (p.across(1), p.z)).wait_recv()


def return_sent(p, src, sends):
    for h in range(2):
        rows = src.at[pl.ds(h * 256, 256)]
        same = jnp.logical_and(p.core == p.z // 2, p.z == 2 * p.core + h)

        @pl.when(jnp.logical_not(same))
        def _():
            remote(rows, rows, sends.at[h], sends.at[h], (p.across(1), p.z)).wait_send()


class Chain:
    def __init__(self, p, r, block, keep0, keep1, land1, land2, land3, send, recv, zsend, zrecv, flip):
        first, second = (4, 2) if flip else (2, 4)
        self.r, self.keep0, self.keep1, self.land1, self.land2 = r, keep0, keep1, land1, land2
        near = (p.across(first), p.z)
        self.one = [remote(block(first + k * second), land1.at[k], send.at[k], recv.at[k], near) for k in range(2)]
        self.two = remote(keep1, land2, send.at[2], recv.at[2], (p.across(second), p.z))
        self.three = None
        if r:
            self.three = remote(keep0, land3, zsend, zrecv, (p.d, lax.rem(p.z + r, 4)))

    def start(self):
        for c in self.one:
            c.start()

    def middle(self):
        for c in self.one:
            c.wait_recv()
        self.keep1[...] = (self.keep1[...].astype(F32) + self.land1[1].astype(F32)).astype(BF)
        self.two.start()

    def total(self):
        return self.keep0[...].astype(F32) + self.land1[0].astype(F32) + self.land2[...].astype(F32)

    def end(self):
        self.two.wait_recv()
        if self.r:
            self.keep0[...] = self.total().astype(BF)
            self.three.start()

    def sent(self):
        for c in self.one + [self.two] + ([self.three] if self.r else []):
            c.wait_send()


class Vectors:
    def __init__(self, p, acc, land, zland, send, recv, zsend, zrecv):
        self.acc, self.land, self.zland = acc, land, zland
        self.steps = [
            remote(acc, land.at[b], send.at[b], recv.at[b], (p.across(1 << b), p.z)) for b in range(3)
        ]
        self.along = [
            remote(acc, zland.at[r - 1], zsend.at[r - 1], zrecv.at[r - 1], (p.d, lax.rem(p.z + r, 4)))
            for r in (1, 2, 3)
        ]

    def start(self, b):
        self.steps[b].start()

    def take(self, b):
        self.steps[b].wait()
        self.acc[...] = self.acc[...] + self.land[b]

    def z_start(self):
        for c in self.along:
            c.start()

    def z_wait(self):
        for c in self.along:
            c.wait()


def backward_kernel(
    x_in, rows1_in, q_in, k_in, v_in, mix_in, e_in, r_in, wa_in, wo_in, res_in, dm_in, gu_in, gd_in, vec_in, bup_in, gain1,
    out_cells, grad_cells, gq_out, gk_out, gv_out, go_out, gup_out, gdown_out, early_out, late_out,
    land1, land2, land3, land1a, land2a, land3a, udk, ga, wav, wov, qv, kv, vv, mix, mixs, dm, e1, gmb, r1b, tt, gm, xv, rows1, eb, rv, xs, xr, da, gcl,
    kt, mixt, dmt_all, dqt, early, late, eland, lland, ezland, lzland,
    ch_s, ch_r, z_s, z_r, res_s, res_r, gc_s, gc_r, both_s, both_r, x_s, x_r, mix_s, mix_r, ev_s, ev_r, ez_s, ez_r,
    lv_s, lv_r, lz_s, lz_r, credit, here, load, eload, store,
):
    p = Place()
    sibling = (p.across(1), p.z)
    order = (1, 3, 2, 0)

    loads = {}
    for n, (name, src, dst) in enumerate(
        (
            ("dm", dm_in, dm), ("wo", wo_in, wov), ("rows1", rows1_in, rows1), ("mix", mix_in, mix), ("r", r_in, rv),
            ("q", q_in, qv), ("k", k_in, kv), ("v", v_in, vv), ("x", x_in, xv),
        )
    ):
        loads[name] = pltpu.make_async_copy(src, dst, load.at[n])
        loads[name].start()

    def wa_load(n):
        return pltpu.make_async_copy(wa_in.at[order[n]], wav.at[n % 2], load.at[9 + n % 2])

    def e_load(head, slot):
        return pltpu.make_async_copy(e_in.at[head], eb.at[slot], eload.at[slot])

    for h in range(2):
        e_load(order[0] * 4 + h, h).start()
    wa_load(0).start()

    p.greet()
    return_copies(p, res_in, out_cells, res_s, res_r, here.at[0])
    mix_copy = remote(mix_in, mixs, mix_s, mix_r, sibling)
    mix_copy.start()

    chains = {}
    keep_loads = []
    for n, r in enumerate(order):
        for u, src in enumerate((gu_in, gd_in)):
            flip = u == 1
            second = 2 if flip else 4
            j = u * 4 + r
            blocks = lambda i, src=src, r=r: src.at[r, pl.ds(i // 2 * PART, PART)]
            for k, i in enumerate((0, second)):
                c = pltpu.make_async_copy(blocks(i), udk.at[j, k], load.at[11 + j])
                c.start()
            keep_loads.append(pltpu.make_async_copy(udk.at[j], udk.at[j], load.at[11 + j]))
            chains[u, n] = Chain(
                p, r, blocks, udk.at[j, 0], udk.at[j, 1], land1.at[j], land2.at[j], land3.at[u, max(r, 1) - 1],
                ch_s.at[j], ch_r.at[j], z_s.at[u, max(r, 1) - 1], z_r.at[u, max(r, 1) - 1], flip,
            )
    for n, r in enumerate(order):
        for half in range(2):
            second = 2 if half else 4
            blocks = lambda i, r=r, half=half: ga.at[r, half, pl.ds(i // 2 * PART, PART)]
            chains[2 + half, n] = Chain(
                p, r, blocks, blocks(0), blocks(second), land1a.at[r, half], land2a.at[r, half], land3a.at[half, max(r, 1) - 1],
                ch_s.at[8 + 2 * r + half], ch_r.at[8 + 2 * r + half], z_s.at[2 + half, max(r, 1) - 1], z_r.at[2 + half, max(r, 1) - 1],
                half == 1,
            )

    def start(kind, n):
        for u in (0, 1) if kind == "f" else (2, 3):
            chains[u, n].start()

    def middle(kind, n):
        for u in (0, 1) if kind == "f" else (2, 3):
            chains[u, n].middle()

    def end(kind, n):
        for u in (0, 1) if kind == "f" else (2, 3):
            chains[u, n].end()

    start("f", 0)
    start("f", 1)

    early[...] = vec_in[0:8, :]
    for r in range(4):
        early[r : r + 1, :] = bup_in[r]
    ev = Vectors(p, early, eland, ezland, ev_s, ev_r, ez_s, ez_r)
    ev.start(0)
    late[...] = jnp.zeros((8, 1024), F32)

    loads["rows1"].wait()
    tt[...] = jnp.transpose(rows1[...], (1, 0))
    both = chosen_both(p, tt, r1b, both_s.at[0], both_r.at[0])
    loads["dm"].wait()

    def cast(rows):
        gm[rows, :] = dm[rows, :].astype(BF)

    each_rows(128, T, cast)
    for name in ("wo", "mix", "r", "q", "k", "v"):
        loads[name].wait()
    lane = lax.broadcasted_iota(jnp.int32, (1, 128), 1)

    def attend_back(n):
        r, slot = order[n], n % 2
        cols_r = pl.ds(r * 256, 256)
        kt[...] = jnp.transpose(kv[r], (1, 0))
        mixt[...] = jnp.transpose(mix[:, cols_r], (1, 0))
        dmt_all[...] = dg(wov[cols_r, :], gm[...], 1, 1).astype(BF)
        if n >= 2:
            for c in [x_copies[n - 2]]:
                c.wait_send()

        def pair(j, carry):
            cols = lane_block(j * 128)
            kp = kv[r, :, cols]
            vp = vv[r, :, cols]
            qp = qv[r, :, cols] * BF(HD**-0.5)
            dk = jnp.zeros((2 * T, 128), F32)
            d_v = jnp.zeros((2 * T, 128), F32)
            for h in range(2):
                head = r * 4 + 2 * j + h
                feats = pl.ds(pl.multiple_of(j * 128 + h * 64, 64), 64)
                mine = (lane < 64) if h == 0 else (lane >= 64)
                dmt = (dmt_all[feats, :].astype(F32) * rv[head]).astype(BF)
                delta = jnp.sum(dmt.astype(F32) * mixt[feats, :].astype(F32), 0, keepdims=True)
                zero = jnp.zeros((64, T), BF)
                dmt2 = jnp.concatenate([dmt, zero] if h == 0 else [zero, dmt], 0)
                dma = jnp.transpose(dmt2, (1, 0))
                dp = dg(vp, dmt2, 1, 0)
                e_load(head, h).wait()
                ds = (eb[h].astype(F32) * (dp - delta)).astype(BF)
                qa = jnp.where(mine, qp, BF(0))
                d_v = d_v + dg(eb[h], dma, 1, 0)
                if n < 3:
                    nxt = jnp.where(j == 0, head + 2, order[n + 1] * 4 + h)
                    e_load(nxt, h).start()
                else:
                    @pl.when(j == 0)
                    def _():
                        e_load(head + 2, h).start()
                dk = dk + dg(ds, qa, 1, 0)
                dqt[feats, :] = (dg(kt[feats, :], ds, 1, 0) * HD**-0.5).astype(BF)
            xs[slot, T : 3 * T, cols] = dk.astype(BF)
            xs[slot, 3 * T : 5 * T, cols] = d_v.astype(BF)
            return carry

        lax.fori_loop(0, 2, pair, 0)
        xs[slot, 0:T, :] = jnp.transpose(dqt[...], (1, 0))
        if n >= 2:
            pl.semaphore_wait(credit, 1)
        c = remote(xs.at[slot], xr.at[slot], x_s.at[slot], x_r.at[slot], sibling)
        c.start()
        return c

    x_copies = []

    def gather_up(n):
        r, slot = order[n], n % 2
        x_copies[n].wait_recv()
        da[0:T, 0:256] = xs[slot, 0:T, :]
        da[T : 2 * T, 0:256] = xr[slot, 0:T, :]
        for k in range(2):
            base = T + 2 * T * k
            cols = pl.ds(256 * (k + 1), 256)
            da[0:T, cols] = (
                xs[slot, base : base + T, :].astype(F32) + xr[slot, base + T : base + 2 * T, :].astype(F32)
            ).astype(BF)
            da[T : 2 * T, cols] = (
                xs[slot, base + T : base + 2 * T, :].astype(F32) + xr[slot, base : base + T, :].astype(F32)
            ).astype(BF)
        if n < 2:
            pl.semaphore_signal(credit, inc=1, device_id=sibling, device_id_type=MESH)
        ga[r, 0] = dg(r1b[...], da[:, 0:512], 1, 0).astype(BF)
        ga[r, 1, :, 0:256] = dg(r1b[...], da[:, 512:768], 1, 0).astype(BF)
        cols_r = pl.ds(r * 256, 256)
        ga[r, 1, :, 256:512] = (dg(gmb[:, 0:T], mix[:, cols_r], 1, 0) + dg(gmb[:, T : 2 * T], mixs[:, cols_r], 1, 0)).astype(BF)
        wa_load(n).wait()
        if n + 1 < 4:
            wa_load(n + 1).start()
        new = dg(da[0:T, :], wav[slot], 1, 1)
        e1[...] = new if n == 0 else e1[...] + new
        late[2:3, r * 256 : (r + 1) * 256] = jnp.sum(da[0:T, 0:256].astype(F32), 0, keepdims=True)
        late[3:4, r * 256 : (r + 1) * 256] = jnp.sum(da[0:T, 512:768].astype(F32), 0, keepdims=True)

    x_copies.append(attend_back(0))
    for c in both:
        c.wait_send()
    tt[...] = jnp.transpose(gm[...], (1, 0))
    both2 = chosen_both(p, tt, gmb, both_s.at[1], both_r.at[1])
    for c in keep_loads:
        c.wait()
    middle("f", 0)
    start("f", 2)
    ev.take(0)
    ev.start(1)
    x_copies.append(attend_back(1))
    middle("f", 1)
    for c in both + both2:
        c.wait_recv()
    mix_copy.wait_recv()
    gather_up(0)
    start("a", 0)
    end("f", 0)
    x_copies.append(attend_back(2))
    middle("f", 2)
    ev.take(1)
    ev.start(2)
    gather_up(1)
    start("a", 1)
    end("f", 1)
    x_copies.append(attend_back(3))
    middle("a", 0)
    start("f", 3)
    gather_up(2)
    end("f", 2)
    middle("a", 1)
    start("a", 2)
    gather_up(3)
    ev.take(2)
    ev.z_start()
    end("a", 0)

    loads["x"].wait()

    def first_back(i, carry):
        rows = pl.ds(pl.multiple_of(i * 128, 128), 128)
        unit, inverse = norm_stats(xv[rows, :].astype(F32))
        e = e1[rows, :]
        u = e * gain1[...]
        d = dm[rows, :] + inverse * (u - jnp.mean(u, -1, keepdims=True) - unit * jnp.mean(u * unit, -1, keepdims=True))
        gm[rows, :] = d.astype(BF)
        for k, v in enumerate((e * unit, e)):
            late[k : k + 1, :] += jnp.sum(v, 0, keepdims=True)
        return carry

    lax.fori_loop(0, T // 128, first_back, 0)
    return_copies(p, gm, gcl, gc_s, gc_r, here.at[1])
    lv = Vectors(p, late, lland, lzland, lv_s, lv_r, lz_s, lz_r)
    lv.start(0)
    middle("f", 3)
    start("a", 3)
    end("a", 1)
    middle("a", 2)
    lv.take(0)
    lv.start(1)
    end("f", 3)
    middle("a", 3)
    end("a", 2)
    lv.take(1)
    lv.start(2)

    def final(u, land):
        for r in (1, 2, 3):
            chains[u, order.index(r)].three.wait_recv()
        total = chains[u, 3].total()
        for r in (1, 2, 3):
            total = total + land[r - 1].astype(F32)
        return total

    gup_out[...] = final(0, land3.at[0])
    gdown_out[...] = jnp.transpose(final(1, land3.at[1]), (1, 0))
    lv.take(2)
    lv.z_start()
    ev.z_wait()
    shard = early[0:1, :]
    for r in (1, 2, 3):
        shard = shard + ezland[r - 1, r : r + 1, :]
    early_out[...] = early[...] + ezland[0] + ezland[1] + ezland[2]
    early_out[0:1, :] = shard
    end("a", 3)

    return_wait(p, gcl, gc_r, here.at[1])
    for s in range(2):
        dm[pl.ds(s * 256, 256), :] = gcl[s].astype(F32)
    ends = [pltpu.make_async_copy(dm.at[pl.ds(s * 256, 256)], grad_cells.at[s], store.at[s]) for s in range(2)]
    for c in ends:
        c.start()
    lv.z_wait()
    late_out[...] = late[...] + lzland[0] + lzland[1] + lzland[2]
    for k in (2, 3):
        shard = late[k : k + 1, 0:256]
        for r in (1, 2, 3):
            shard = shard + lzland[r - 1, k : k + 1, r * 256 : (r + 1) * 256]
        late_out[k : k + 1, 0:256] = shard
    total = final(2, land3a.at[0])
    gq_out[...] = total[:, 0:256]
    gk_out[...] = total[:, 256:512]
    total = final(3, land3a.at[1])
    gv_out[...] = total[:, 0:256]
    go_out[...] = jnp.transpose(total[:, 256:512], (1, 0))

    return_wait(p, out_cells, res_r, here.at[0])
    for c in ends:
        c.wait()
    for c in both2 + [mix_copy, x_copies[2], x_copies[3]]:
        c.wait_send()
    for c in chains.values():
        c.sent()
    return_sent(p, res_in, res_s)
    return_sent(p, gm, gc_s)


def backward(*args):
    s = jax.ShapeDtypeStruct
    hbm, fast = pl.BlockSpec(memory_space=pltpu.HBM), pl.BlockSpec(memory_space=pltpu.VMEM)
    b, f, dma = (lambda *x: pltpu.VMEM(x, BF)), (lambda *x: pltpu.VMEM(x, F32)), (lambda *x: pltpu.SemaphoreType.DMA(x))
    return pl.pallas_call(
        backward_kernel,
        out_shape=[
            s((2, 256, 1024), BF), s((2, 256, 1024), F32), s((PART, 256), F32), s((PART, 256), F32), s((PART, 256), F32),
            s((256, PART), F32), s((PART, 1024), F32), s((1024, PART), F32), s((8, 1024), F32), s((8, 1024), F32),
        ],
        in_specs=[hbm] * 14 + [fast] * 3,
        out_specs=[hbm] * 2 + [fast] * 8,
        scratch_shapes=[
            b(8, 2, PART, 1024), b(8, PART, 1024), b(2, 3, PART, 1024), b(4, 2, 2, PART, 512), b(4, 2, PART, 512), b(2, 3, PART, 512),
            b(8, 2, PART, 1024), b(4, 2, 4 * PART, 512), b(2, 1024, 768),
            b(1024, 1024), b(4, T, 256), b(4, 2 * T, 256), b(4, 2 * T, 256), b(T, 1024), b(T, 1024), f(T, 1024), f(T, 1024),
            b(T, 2 * T), b(T, 2 * T), b(1024, T), b(T, 1024), b(T, 1024), b(T, 1024), b(2, 2 * T, T), f(16, 1, T),
            b(2, 5 * T, 256), b(2, 5 * T, 256), b(2 * T, 768), b(2, 256, 1024),
            b(256, 2 * T), b(256, T), b(256, T), b(256, T), f(8, 1024), f(8, 1024), f(3, 8, 1024), f(3, 8, 1024), f(3, 8, 1024), f(3, 8, 1024),
            dma(16, 3), dma(16, 3), dma(4, 3), dma(4, 3), dma(2), dma(2), dma(2), dma(2), dma(2, 4), dma(2, 4), dma(2), dma(2),
            pltpu.SemaphoreType.DMA, pltpu.SemaphoreType.DMA, dma(3), dma(3), dma(3), dma(3), dma(3), dma(3), dma(3), dma(3),
            pltpu.SemaphoreType.REGULAR, dma(2), dma(19), dma(2), dma(2),
        ],
        compiler_params=pltpu.CompilerParams(collective_id=1, has_side_effects=True, vmem_limit_bytes=63 * 2**20),
    )(*args)


def forward(*args):
    s = jax.ShapeDtypeStruct
    outs = [
        (T, 1024), (T, 1024), (4, T, 256), (4, 2 * T, 256), (4, 2 * T, 256), (T, 1024), (16, 2 * T, T), (16, 1, T),
        (4, 1024, 768), (1024, 1024), (3, 1024, 1024), (3, 1024, 1024), (T, 1024), (T, 1024), (4, T, 1024), (4, T, 1024), (16, 1024), (4, 1, 1024),
    ]
    wide = (7, 13, 16, 17)
    hbm, fast = pl.BlockSpec(memory_space=pltpu.HBM), pl.BlockSpec(memory_space=pltpu.VMEM)
    b, f, dma = (lambda *x: pltpu.VMEM(x, BF)), (lambda *x: pltpu.VMEM(x, F32)), (lambda *x: pltpu.SemaphoreType.DMA(x))
    sems = []
    for parts in (3, 1, 1, 1):
        sems += [dma(6, parts), dma(3, parts), dma(3, 7), dma(3, 8)]
    return pl.pallas_call(
        forward_kernel,
        out_shape=[s(o, F32 if n in wide else BF) for n, o in enumerate(outs)],
        in_specs=[hbm, hbm, fast] + [hbm] * 6 + [fast] * 7,
        out_specs=[hbm] * 16 + [fast] * 2,
        scratch_shapes=[
            b(T, 1024), b(T, 1024), b(T, 1024), b(4, 1024, 768), b(1024, 1024), b(4, T, 256), b(4, 2 * T, 256), b(4, 2 * T, 256),
            b(T, 1024), b(2, 2 * T, T), f(16, 1, T), b(2, 2 * T, 128), b(256, 2 * T), b(256, T), f(T, 1024), b(T, 1024),
            b(1024, T), b(T, 2 * T), b(T, 2 * T), f(T, 1024), f(T, 1024),
            b(2, 1024, 1024), b(2, 1024, 1024), b(2, T, 1024), b(2, T, 1024), b(2, T, 1024), b(2, T, 1024), f(2, T, 1024), b(T, 1024), b(T, 1024),
            f(8, 128), f(4, 1, 1536),
        ]
        + sems
        + [dma(2, 2), dma(2, 2), dma(4), dma(4), dma(4, 2), dma(4, 2), dma(2, 4), dma(2, 4), dma(2, 2), dma(2, 2),
           pltpu.SemaphoreType.REGULAR, dma(6), dma(2, 2), dma(15)],
        compiler_params=pltpu.CompilerParams(collective_id=0, has_side_effects=True, vmem_limit_bytes=62 * 2**20),
    )(*args)


def body(*args):
    if lax.axis_size("dp") == 8 and lax.axis_size("mp") == 4:
        return fused_body(*args)
    return plain_body(*args)


def fused_body(
    cells,
    lengths,
    query_matrix,
    key_matrix,
    value_matrix,
    query_bias,
    value_bias,
    output_matrix,
    b_out,
    gain_one,
    shift_one,
    gain_two,
    shift_two,
    expand_weight,
    expand_bias,
    contract_weight,
    b_down,
    grad_out,
):
    slots = cells.shape[0]
    n_dp, n_mp = lax.axis_size("dp"), lax.axis_size("mp")
    d, z = lax.axis_index("dp"), lax.axis_index("mp")
    row = lambda v: v.reshape(1, -1)
    small = row(jnp.concatenate([query_bias, value_bias, expand_bias]))
    len_own = jnp.pad(jnp.broadcast_to(lengths.astype(F32)[:, None], (slots, 128)), ((0, 8 - slots), (0, 0)))
    (x, rows_one, q_all, k_all, v_all, mixed_all, e_all, r_all, wa, wo, _, _, res, d_middle, gu, gd, vec, bup) = forward(
        cells, grad_out, len_own, query_matrix, key_matrix, value_matrix, output_matrix, expand_weight, contract_weight,
        small, row(b_out), row(gain_one), row(shift_one), row(gain_two), row(shift_two), row(b_down),
    )
    out_cells, grad_cells, gq, gk, gv, go, gup, gdown, early, late = backward(
        x, rows_one, q_all, k_all, v_all, mixed_all, e_all, r_all, wa, wo, res, d_middle, gu, gd, vec, bup, row(gain_one)
    )
    cut = lambda v, at, size: lax.dynamic_slice_in_dim(v, at * size, size, 0)
    width, hw = cells.shape[2], query_matrix.shape[1]
    at, size = d * n_mp + z, width // (n_dp * n_mp)
    return (
        out_cells,
        grad_cells,
        gq,
        gk,
        gv,
        cut(late[2], d, hw // n_dp),
        cut(late[3], d, hw // n_dp),
        go,
        cut(early[4], at, size),
        cut(late[0], at, size),
        cut(late[1], at, size),
        cut(early[5], at, size),
        cut(early[6], at, size),
        gup,
        cut(early[0], d, expand_weight.shape[1] // n_dp),
        gdown,
        cut(early[7], at, size),
    )


def solution(mesh):
    return jax.shard_map(
        body,
        mesh=mesh,
        in_specs=(
            P("dp", "mp", None),
            P("dp"),
            P(None, "mp"),
            P(None, "mp"),
            P(None, "mp"),
            P("mp"),
            P("mp"),
            P("mp", None),
            P(),
            P(),
            P(),
            P(),
            P(),
            P(None, "mp"),
            P("mp"),
            P("mp", None),
            P(),
            P("dp", "mp", None),
        ),
        out_specs=(
            P("dp", "mp", None),
            P("dp", "mp", None),
            P("dp", "mp"),
            P("dp", "mp"),
            P("dp", "mp"),
            P(("mp", "dp")),
            P(("mp", "dp")),
            P("mp", "dp"),
            P(("dp", "mp")),
            P(("dp", "mp")),
            P(("dp", "mp")),
            P(("dp", "mp")),
            P(("dp", "mp")),
            P("dp", "mp"),
            P(("mp", "dp")),
            P("mp", "dp"),
            P(("dp", "mp")),
        ),
        check_vma=False,
    )
```

```python
import jax
import jax.numpy as jnp
from jax import lax
from jax.experimental import pallas as pl
from jax.experimental.pallas import tpu as pltpu
from jax.sharding import PartitionSpec as P

HD = 64
EPS = 1e-05
BF = jnp.bfloat16
F32 = jnp.float32
MESH = pl.DeviceIdType.MESH
T = 512
PART = 128


def dot(a, b, ca, cb):
    return lax.dot_general(a, b, (((ca,), (cb,)), ((), ())), preferred_element_type=F32)


def cross(x, bit):
    n = lax.axis_size("dp")
    return lax.ppermute(x, "dp", [(i, i ^ (1 << bit)) for i in range(n)])


def shift(x, by):
    n = lax.axis_size("mp")
    return lax.ppermute(x, "mp", [(i, (i + by) % n) for i in range(n)])


def moves(n_dp, n_mp, slots):
    per = n_mp // slots
    turns = []
    for t in range(slots):
        pairs = []
        for d in range(n_dp):
            for m in range(n_mp):
                s = (t + m) % slots
                base, c = d - d % per, d % per
                target = (base + m // slots, c * slots + s)
                pairs.append((d * n_mp + m, target[0] * n_mp + target[1]))
        turns.append(pairs)
    return turns


def plane_bits(n_dp, flip):
    bits = list(range(1, n_dp.bit_length() - 1))
    return bits[::-1] if flip else bits


def gather(piece, flip):
    n_dp, n_mp = lax.axis_size("dp"), lax.axis_size("mp")
    stack = jnp.stack([shift(piece, n_mp - r) for r in range(1, n_mp)])
    held = {0: stack}
    for bit in plane_bits(n_dp, flip) + [0]:
        held.update({i ^ (1 << bit): cross(v, bit) for i, v in list(held.items())})
    return held


def assemble(held, own, d):
    n = len(held)
    stack = jnp.stack([held[i] for i in range(n)])
    order = jnp.arange(n) ^ d
    placed = jnp.take(stack, order, axis=0)
    placed = jnp.moveaxis(placed, 0, 1).reshape((stack.shape[1], -1, stack.shape[-1]))
    return [own] + [placed[r] for r in range(placed.shape[0])]


def scatter(blocks, flip):
    n_dp = lax.axis_size("dp")
    for bit in plane_bits(n_dp, flip):
        keep = sorted(i for i in blocks if not i >> bit & 1)
        got = cross(jnp.stack([blocks[i ^ (1 << bit)] for i in keep]), bit)
        blocks = {
            i: (blocks[i].astype(F32) + got[k].astype(F32)).astype(blocks[i].dtype)
            for k, i in enumerate(keep)
        }
    return blocks[0]


def layer_norm(v, gain, bias):
    center = v - jnp.mean(v, -1, keepdims=True)
    inverse = lax.rsqrt(jnp.mean(center * center, -1, keepdims=True) + EPS)
    unit = center * inverse
    return unit * gain + bias, unit, inverse


def norm_back(up, unit, inverse, gain):
    u = up * gain
    return inverse * (
        u - jnp.mean(u, -1, keepdims=True) - unit * jnp.mean(u * unit, -1, keepdims=True)
    )


def gelu_pair(v):
    cumulative = 0.5 * (1.0 + lax.erf(v * 0.7071067811865476))
    density = jnp.exp(-0.5 * v * v) * 0.3989422804014327
    return v * cumulative, cumulative + v * density


def attend(q, k, v, allowed):
    heads = q.shape[1] // HD
    qh = q.reshape(-1, heads, HD)
    kh = k.reshape(-1, heads, HD)
    vh = v.reshape(-1, heads, HD)
    s = jnp.einsum("qhd,khd->hqk", qh, kh, preferred_element_type=F32) * HD**-0.5
    s = jnp.where(allowed[None, None, :], s, -1e30)
    e = jnp.exp(s - jnp.max(s, -1, keepdims=True))
    p = (e / jnp.sum(e, -1, keepdims=True)).astype(BF)
    mixed = jnp.einsum("hqk,khd->qhd", p, vh, preferred_element_type=F32)
    return mixed.astype(BF).reshape(q.shape), p


def attend_back(q, k, v, p, mixed, dm):
    heads = q.shape[1] // HD
    qh = q.reshape(-1, heads, HD)
    kh = k.reshape(-1, heads, HD)
    vh = v.reshape(-1, heads, HD)
    dh = dm.reshape(-1, heads, HD)
    pf = p.astype(F32)
    dp = jnp.einsum("qhd,khd->hqk", dh, vh, preferred_element_type=F32)
    total = jnp.sum(dp * pf, -1, keepdims=True)
    ds = (pf * (dp - total)).astype(BF)
    dv = jnp.einsum("hqk,qhd->khd", p, dh, preferred_element_type=F32)
    dq = jnp.einsum("hqk,khd->qhd", ds, kh, preferred_element_type=F32) * HD**-0.5
    dk = jnp.einsum("hqk,qhd->khd", ds, qh, preferred_element_type=F32) * HD**-0.5
    return (
        dq.astype(BF).reshape(q.shape),
        dk.astype(BF).reshape(k.shape),
        dv.astype(BF).reshape(k.shape),
    )


def plain_body(
    cells,
    lengths,
    query_matrix,
    key_matrix,
    value_matrix,
    query_bias,
    value_bias,
    output_matrix,
    b_out,
    gain_one,
    shift_one,
    gain_two,
    shift_two,
    expand_weight,
    expand_bias,
    contract_weight,
    b_down,
    grad_out,
):
    slots, rows, width = cells.shape
    n_dp, n_mp = lax.axis_size("dp"), lax.axis_size("mp")
    d, z = lax.axis_index("dp"), lax.axis_index("mp")
    per = n_mp // slots
    core = d % per
    tokens = slots * rows
    part = width // n_dp
    hw = query_matrix.shape[1]
    turns = moves(n_dp, n_mp, slots)

    def bring(x):
        got = [
            lax.ppermute(
                lax.dynamic_index_in_dim(x, (t + z) % slots, 0, False), ("dp", "mp"), turns[t]
            )
            for t in range(slots)
        ]
        even = z % slots == 0
        return jnp.concatenate(
            [jnp.where(even, got[0], got[1]), jnp.where(even, got[1], got[0])], 0
        )

    def give_back(x):
        x = x.reshape(slots, rows, width)
        got = [
            lax.ppermute(
                lax.dynamic_index_in_dim(x, (t + z) % slots, 0, False),
                ("dp", "mp"),
                [(b, a) for a, b in turns[t]],
            )
            for t in range(slots)
        ]
        even = z % slots == 0
        return jnp.stack(
            [jnp.where(even, got[0], got[1]), jnp.where(even, got[1], got[0])], 0
        )

    mine = bring(cells)
    attn_own = jnp.concatenate(
        [query_matrix, key_matrix, value_matrix, output_matrix.T], 1
    )
    first = d * part

    def piece_of(w):
        return lax.dynamic_slice_in_dim(w, first, part, 0)

    half = attn_own.shape[1] // 2
    a_piece = piece_of(attn_own)
    a_left = gather(a_piece[:, :half], False)
    a_right = gather(a_piece[:, half:], True)
    u_held = gather(piece_of(expand_weight), False)
    d_held = gather(piece_of(contract_weight), True)
    grad_rows = bring(grad_out)
    small = jnp.concatenate([query_bias, value_bias, expand_bias])
    small = [small] + [shift(small, n_mp - r) for r in range(1, n_mp)]
    both = cross(lengths, 0)
    length_all = jnp.where(core == 0, jnp.concatenate([lengths, both]), jnp.concatenate([both, lengths]))
    length = lax.dynamic_index_in_dim(length_all, z, 0, False)

    attn_w = [
        jnp.concatenate([a, b], 1)
        for a, b in zip(
            assemble(a_left, attn_own[:, :half], d), assemble(a_right, attn_own[:, half:], d)
        )
    ]
    up_w = assemble(u_held, expand_weight, d)
    down_w = assemble(d_held, contract_weight, d)

    position = core * tokens + jnp.arange(tokens)
    keep = (position < length).astype(F32)[:, None]
    sib_position = (per - 1 - core) * tokens + jnp.arange(tokens)
    allowed = jnp.concatenate([position, sib_position]) < length

    x = mine.astype(F32)
    rows_one, unit_one, inv_one = layer_norm(x, gain_one, shift_one)
    rows_one = rows_one.astype(BF)
    kept = []
    attention = jnp.zeros((tokens, width), F32)
    for r in range(n_mp):
        w = attn_w[r]
        q = (dot(rows_one, w[:, :hw], 1, 0) + small[r][:hw]).astype(BF)
        k = dot(rows_one, w[:, hw : 2 * hw], 1, 0).astype(BF)
        v = (dot(rows_one, w[:, 2 * hw : 3 * hw], 1, 0) + small[r][hw : 2 * hw]).astype(BF)
        k = jnp.concatenate([k, cross(k, 0)], 0)
        v = jnp.concatenate([v, cross(v, 0)], 0)
        mixed, p = attend(q, k, v, allowed)
        kept.append((q, k, v, mixed, p))
        attention = attention + dot(mixed, w[:, 3 * hw :], 1, 1)
    middle = x + attention + b_out
    rows_two, unit_two, inv_two = layer_norm(middle, gain_two, shift_two)
    rows_two = rows_two.astype(BF)
    g = keep * grad_rows.astype(F32)
    gz = g.astype(BF)

    order = jnp.arange(0, n_dp, 2) ^ d

    def chosen(v):
        return jnp.take(v.reshape(v.shape[0], n_dp, part), order, axis=1).reshape(v.shape[0], -1)

    def other(v):
        return jnp.take(v.reshape(v.shape[0], n_dp, part), order ^ 1, axis=1).reshape(v.shape[0], -1)

    def both_cores(v):
        return jnp.concatenate([chosen(v), cross(other(v), 0)], 0)

    def weight_grad(left, right, flip):
        right = jnp.concatenate([right, cross(right, 0)], 0)
        return weight_grad_all(left, right, flip)

    def weight_grad_all(left, right, flip):
        got = dot(left, right, 0, 0).astype(BF).reshape(-1, part, right.shape[1])
        return scatter({2 * i: got[i] for i in range(got.shape[0])}, flip)

    def finish(pieces):
        total = pieces[0].astype(F32)
        for r in range(1, n_mp):
            total = total + shift(pieces[r], r).astype(F32)
        return total

    two_both = both_cores(rows_two)
    gz_both = both_cores(gz)
    result = middle + b_down
    e2 = jnp.zeros((tokens, width), F32)
    up_parts, down_parts, b_up = [], [], []
    for r in range(n_mp):
        upper = dot(rows_two, up_w[r], 1, 0) + small[r][2 * hw :]
        hidden, slope = gelu_pair(upper)
        hidden = hidden.astype(BF)
        result = result + dot(hidden, down_w[r], 1, 0)
        d_upper = (dot(gz, down_w[r], 1, 1) * slope).astype(BF)
        e2 = e2 + dot(d_upper, up_w[r], 1, 1)
        up_parts.append(weight_grad(two_both, d_upper, False))
        down_parts.append(weight_grad(gz_both, hidden, True))
        b_up.append(jnp.sum(d_upper.astype(F32), 0))
    out_cells = give_back((keep * result).astype(BF))
    grad_up = finish(up_parts)
    grad_down = finish(down_parts).T

    d_middle = g + norm_back(e2, unit_two, inv_two, gain_two)
    gm = d_middle.astype(BF)
    gm_both = both_cores(gm)
    one_both = both_cores(rows_one)
    e1 = jnp.zeros((tokens, width), F32)
    a_parts, b_q, b_v = [], [], []
    for r in range(n_mp):
        q, k, v, mixed, p = kept[r]
        w = attn_w[r]
        d_mixed = dot(gm, w[:, 3 * hw :], 1, 0).astype(BF)
        dq, dk, dv = attend_back(q, k, v, p, mixed, d_mixed)
        dk_all = (dk.astype(F32) + jnp.roll(cross(dk, 0), tokens, 0).astype(F32)).astype(BF)
        dv_all = (dv.astype(F32) + jnp.roll(cross(dv, 0), tokens, 0).astype(F32)).astype(BF)
        dq_all = jnp.concatenate([dq, cross(dq, 0)], 0)
        e1 = (
            e1
            + dot(dq, w[:, :hw], 1, 1)
            + dot(dk_all[:tokens], w[:, hw : 2 * hw], 1, 1)
            + dot(dv_all[:tokens], w[:, 2 * hw : 3 * hw], 1, 1)
        )
        b_q.append(jnp.sum(dq.astype(F32), 0))
        b_v.append(jnp.sum(dv_all[:tokens].astype(F32), 0))
        qkv_part = weight_grad_all(one_both, jnp.concatenate([dq_all, dk_all, dv_all], 1), r % 2 == 1)
        o_part = weight_grad(gm_both, mixed, r % 2 == 0)
        a_parts.append(jnp.concatenate([qkv_part, o_part], 1))
    d_cells = d_middle + norm_back(e1, unit_one, inv_one, gain_one)
    grad_cells = give_back(d_cells.astype(BF)).astype(F32)
    grad_attn = finish(a_parts)

    split_mp = [jnp.stack(b_q).reshape(n_mp, n_dp, -1), jnp.stack(b_v).reshape(n_mp, n_dp, -1), jnp.stack(b_up).reshape(n_mp, n_dp, -1)]
    sums = [
        jnp.sum(d_middle, 0),
        jnp.sum(e1 * unit_one, 0),
        jnp.sum(e1, 0),
        jnp.sum(e2 * unit_two, 0),
        jnp.sum(e2, 0),
        jnp.sum(g, 0),
    ]
    split_dp = [jnp.roll(jnp.swapaxes(s.reshape(n_dp, n_mp, -1), 0, 1), -z, 0) for s in sums]
    packed = jnp.concatenate(split_mp + split_dp, 2)
    packed = jnp.take(packed, jnp.arange(n_dp) ^ d, axis=1)
    packed = packed[:, 0::2] + cross(packed[:, 1::2], 0)
    packed = scatter({2 * i: packed[:, i] for i in range(packed.shape[1])}, False)
    vec = packed[0]
    for r in range(1, n_mp):
        vec = vec + shift(packed[r], r)
    nq = split_mp[0].shape[2]
    nu = split_mp[2].shape[2]
    ns = split_dp[0].shape[2]
    vq, vv, vu = vec[:nq], vec[nq : 2 * nq], vec[2 * nq : 2 * nq + nu]
    rest = [vec[2 * nq + nu + i * ns : 2 * nq + nu + (i + 1) * ns] for i in range(6)]
    return (
        out_cells,
        grad_cells,
        grad_attn[:, :hw],
        grad_attn[:, hw : 2 * hw],
        grad_attn[:, 2 * hw : 3 * hw],
        vq,
        vv,
        grad_attn[:, 3 * hw :].T,
        rest[0],
        rest[1],
        rest[2],
        rest[3],
        rest[4],
        grad_up,
        vu,
        grad_down,
        rest[5],
    )


def dg(a, b, ca, cb):
    return lax.dot_general(a, b, (((ca,), (cb,)), ((), ())), preferred_element_type=F32)


def lane_block(start, size=128):
    return pl.ds(pl.multiple_of(start, size), size)


class Place:
    def __init__(self):
        self.d, self.z = lax.axis_index("dp"), lax.axis_index("mp")
        self.bit = [lax.rem(self.d // (1 << b), 2) for b in range(3)]
        self.core = self.bit[0]
        self.base = self.d - self.core
        self.inner = jnp.logical_and(self.z >= 1, self.z <= 2)
        odd = lax.rem(self.z, 2)
        self.z_next, self.z_over = self.z + 1 - 2 * odd, self.z + 2 - 4 * (self.z // 2)
        self.slot_next = 1 + 2 * odd
        self.outer = jnp.logical_not(self.inner)

    def across(self, i):
        v = self.d
        for b in range(3):
            if i >> b & 1:
                v = v + (1 << b) * (1 - 2 * self.bit[b])
        return v

    def rows(self, i):
        return lane_block(self.across(i) * PART, PART)

    def greet(self):
        barrier = pltpu.get_barrier_semaphore()
        for step in range(1, 4):
            for c in range(2):
                pl.semaphore_signal(
                    barrier,
                    inc=1,
                    device_id=(self.base + c, lax.rem(self.z + step, 4)),
                    device_id_type=MESH,
                )
        for i in (1, 2, 4):
            pl.semaphore_signal(barrier, inc=1, device_id=(self.across(i), self.z), device_id_type=MESH)
        pl.semaphore_wait(barrier, 9)


def remote(src, dst, send, recv, device):
    return pltpu.make_async_remote_copy(
        src_ref=src, dst_ref=dst, send_sem=send, recv_sem=recv, device_id=device, device_id_type=MESH
    )


STEPS = {
    "ln1": (("a10", "a11", "a20", "a12", "a21", "u10", "u11", "a22", "a30", "d10", "d11", "a31", "u20", "u21", "a32", "d20", "d21"), ("a10", "a11", "a20", "a12", "a21", "u10", "a22", "a30", "d10", "a31", "u20", "d20", "a32", "u30")),
    "proj0": (("o10",), ("o10", "d30")),
    "proj1": ((), ("o11",)),
    "proj2": (("o11", "u30"), ("o20", "o12")),
    "proj3": (("o12",), ("o21",)),
    "att00": (("u31",), ("o22",)),
    "att01": (("u12",), ("o30", "o31", "u11")),
    "att10": (("d31",), ("o32",)),
    "att11": (("o21", "d30", "d12"), ("d11", "u12", "u21")),
    "att20": (("o20", "o22"), ()),
    "att21": ((), ("d12", "d21")),
    "att30": (("o30", "d22", "o31", "u22"), ()),
    "att31": (("o32",), ("u22",)),
    "oproj": ((), ("d22",)),
    "f0": (("d32", "u32"), ()),
    "b0": ((), ("d31", "u31")),
    "b1": ((), ("d32", "u32")),
}


class Unit:
    def __init__(self, place, own, at, parts, zsend, zrecv, send, recv, flip, slots):
        self.p, self.own, self.at, self.parts = place, own, at, parts
        self.zsend, self.zrecv, self.send, self.recv = zsend, zrecv, send, recv
        self.flip, self.slots = flip, slots

    def bits(self, n):
        return (4, 2) if (n % 2 == 1) == self.flip else (2, 4)

    def copy(self, k, slot_from, slot_to, device):
        return [
            remote(
                self.own(q) if slot_from is None else self.at(slot_from, 0, q),
                self.at(slot_to, 0, q),
                self.zsend.at[k, q],
                self.zrecv.at[slot_to - 1, q],
                device,
            )
            for q in range(self.parts)
        ]

    def direct(self, k):
        return self.copy(k - 1, None, k, (self.p.d, lax.rem(self.p.z + 4 - k, 4)))

    def along(self, k, slot_from, slot_to, right):
        return self.copy(k, slot_from, slot_to, (self.p.d, self.p.z + 1 if right else self.p.z - 1))

    def steps(self):
        z = self.p.z
        inner = self.p.inner
        return [
            (z <= 2, (0, None, 3, True)),
            (z >= 1, (1, None, 1, False)),
            (inner, (2, 3, 2, True)),
            (inner, (3, 1, 2, False)),
            (z == 1, (4, 2, 3, False)),
            (z == 2, (5, 2, 1, True)),
        ]

    def go(self, k):
        cond, what = self.steps()[k]

        @pl.when(cond)
        def _():
            for c in self.along(*what):
                c.start()

    def start(self):
        self.go(0)
        self.go(1)

    def start_direct(self):
        for k in (1, 3, 2):
            for c in self.direct(k):
                c.start()

    def landed(self, slot):
        for q in range(self.parts):
            here = self.at(slot, 0, q)
            remote(here, here, self.zsend.at[0, q], self.zrecv.at[slot - 1, q], (self.p.across(1), self.p.z)).wait_recv()

    def xy(self, n, k, i, bit):
        slot = self.slots[n]
        here = self.at(slot, i, None)
        return remote(
            here,
            here,
            self.send.at[slot - 1, k],
            self.recv.at[slot - 1, i ^ bit],
            (self.p.across(bit), self.p.z),
        )

    def arrived(self, n, i):
        slot = self.slots[n]
        here = self.at(slot, i, None)
        remote(here, here, self.send.at[slot - 1, 0], self.recv.at[slot - 1, i], (self.p.across(1), self.p.z)).wait_recv()

    def one(self, n):
        self.xy(n, 0, 0, self.bits(n)[0]).start()

    def take(self, n, inner=False, chained=False):
        self.landed(self.slots[n])
        if chained and inner and n < 2:
            for c in self.along(*self.steps()[3 - n][1]):
                c.start()
        if chained and inner and n == 2:
            self.go(4)
            self.go(5)
        self.one(n)

    def two(self, n):
        first, second = self.bits(n)
        self.arrived(n, first)
        self.xy(n, 1, 0, second).start()
        self.xy(n, 2, first, second).start()

    def three(self, n):
        first, second = self.bits(n)
        self.arrived(n, second)
        self.arrived(n, 6)
        for k, i in enumerate((0, 2, 4, 6)):
            self.xy(n, 3 + k, i, 1).start()

    def whole(self, n):
        for i in (1, 3, 5, 7):
            self.arrived(n, i)

    def finish(self, direct):
        if direct:
            for k in (1, 2, 3):
                for c in self.direct(k):
                    c.wait_send()
        else:
            for cond, what in self.steps():

                @pl.when(cond)
                def _(what=what):
                    for c in self.along(*what):
                        c.wait_send()

        for n in range(3):
            first, second = self.bits(n)
            self.xy(n, 0, 0, first).wait_send()
            self.xy(n, 1, 0, second).wait_send()
            self.xy(n, 2, first, second).wait_send()
            for k, i in enumerate((0, 2, 4, 6)):
                self.xy(n, 3 + k, i, 1).wait_send()


def bring_copies(p, src, dst, sends, recvs, here, which=(0, 1)):
    for s in which:
        target = (p.base + p.z // 2, 2 * p.core + s)
        half = lax.rem(p.z, 2)
        rows = lane_block(half * 256, 256)
        same = jnp.logical_and(p.core == p.z // 2, p.z == 2 * p.core + s)

        @pl.when(same)
        def _():
            pltpu.make_async_copy(src.at[s], dst.at[rows], here).start()

        @pl.when(jnp.logical_not(same))
        def _():
            remote(src.at[s], dst.at[rows], sends.at[s], recvs.at[half], target).start()


def bring_wait(p, dst, recvs, here):
    for half in range(2):
        block = dst.at[pl.ds(half * 256, 256)]
        same = jnp.logical_and(p.core == p.z // 2, lax.rem(p.z, 2) == half)

        @pl.when(same)
        def _():
            pltpu.make_async_copy(block, block, here).wait()

        @pl.when(jnp.logical_not(same))
        def _():
            remote(block, block, recvs.at[half], recvs.at[half], (p.across(1), p.z)).wait_recv()


def bring_sent(p, src, sends):
    for s in range(2):
        same = jnp.logical_and(p.core == p.z // 2, p.z == 2 * p.core + s)

        @pl.when(jnp.logical_not(same))
        def _():
            remote(src.at[s], src.at[s], sends.at[s], sends.at[s], (p.across(1), p.z)).wait_send()


def norm_stats(x):
    center = x - jnp.mean(x, -1, keepdims=True)
    inverse = lax.rsqrt(jnp.mean(center * center, -1, keepdims=True) + EPS)
    return center * inverse, inverse


def each_rows(size, total, f):
    def step(i, carry):
        f(pl.ds(pl.multiple_of(i * size, size), size))
        return carry

    lax.fori_loop(0, total // size, step, 0)


def chosen_both(p, t_ref, both_ref, sends, recvs):
    copies = []
    for k, i in enumerate((0, 2, 4, 6)):
        block = pl.ds(k * PART, PART)
        both_ref[block, 0:T] = t_ref[p.rows(i), :]
        copies.append(
            remote(
                t_ref.at[p.rows(i ^ 1)],
                both_ref.at[block, T : 2 * T],
                sends.at[k],
                recvs.at[k],
                (p.across(1), p.z),
            )
        )
    for c in copies:
        c.start()
    return copies


def forward_kernel(
    cells, grad, len_own, wq, wk, wv, wo, up, down, small_own, b_out, gain1, shift1, gain2, shift2, b_down,
    x_out, rows1_out, q_out, k_out, v_out, mix_out, e_out, r_out, wa_out, wo_out, wu, wd, out_land, dm_out, gu_out, gd_out, keep_out, la_out, lc_out, vec_out, bup_out,
    xv, gv, rows1, wav, wov, qv, kv, vv, mix, eb, rv, bias, vt, ot, middle, rows2, tt, xb, gb, acc, e2,
    uv, dv, ho, du, hs, ds, slope_v, gs, land_b, len_sib, small,
    a_zs, a_zr, a_s, a_r, o_zs, o_zr, o_s, o_r, u_zs, u_zr, u_s, u_r, d_zs, d_zr, d_s, d_r,
    act_s, act_r, sm_s, sm_r, kv_s, kv_r, both_s, both_r, hd_s, hd_r, ch_s, ch_r, credit, loc, load, store,
):
    p = Place()
    sibling = (p.across(1), p.z)

    ws = (wq, wk, wv)
    own_rows = p.rows(0)

    def a_at(slot, i, part):
        if part is None:
            return wav.at[slot, p.rows(i)]
        return wav.at[slot, p.rows(i), pl.ds(part * 256, 256)]

    fixed = (1, 3, 2)
    inner = p.inner
    by_arrival = (
        jnp.where(p.z <= 2, 1, 3),
        jnp.where(inner, 3, 2),
        jnp.where(inner, 2, jnp.where(p.z == 0, 3, 1)),
    )
    unit_a = Unit(p, lambda q: ws[q].at[own_rows], a_at, 3, a_zs, a_zr, a_s, a_r, True, fixed)
    unit_o = Unit(
        p,
        lambda q: wo.at[:, own_rows],
        lambda slot, i, q: wov.at[pl.ds(slot * 256, 256), p.rows(i)],
        1, o_zs, o_zr, o_s, o_r, False, fixed,
    )
    unit_u = Unit(
        p, lambda q: up.at[own_rows], lambda slot, i, q: wu.at[slot - 1, p.rows(i)], 1, u_zs, u_zr, u_s, u_r, False, by_arrival
    )
    unit_d = Unit(
        p, lambda q: down.at[own_rows], lambda slot, i, q: wd.at[slot - 1, p.rows(i)], 1, d_zs, d_zr, d_s, d_r, True, by_arrival
    )

    own_loads = [pltpu.make_async_copy(w, wav.at[0, :, pl.ds(k * 256, 256)], loc.at[k]) for k, w in enumerate(ws)]
    own_loads.append(pltpu.make_async_copy(wo, wov.at[pl.ds(0, 256)], loc.at[3]))
    for c in own_loads:
        c.start()
    first_loads = [pltpu.make_async_copy(up, uv.at[0], load.at[0, 0]), pltpu.make_async_copy(down, dv.at[0], load.at[1, 0])]
    for c in first_loads:
        c.start()

    p.greet()
    unit_a.start_direct()
    unit_u.start()
    unit_d.start()
    bring_copies(p, cells, xv, act_s.at[0], act_r.at[0], loc.at[4])
    unit_o.start_direct()
    small_copies = []
    for r in (1, 2, 3):
        small_copies.append(remote(small_own, small.at[r], sm_s.at[r], sm_r.at[r], (p.d, lax.rem(p.z + 4 - r, 4))))
    small_copies.append(remote(len_own, len_sib, sm_s.at[0], sm_r.at[0], sibling))
    for c in small_copies:
        c.start()
    small[0] = small_own[...]

    units = {"a": (unit_a, False), "o": (unit_o, False), "u": (unit_u, True), "d": (unit_d, True)}

    def advance(point):
        for inner, names in zip((True, False), STEPS.get(point, ((), ()))):
            if names:

                @pl.when(p.inner if inner else p.outer)
                def _(inner=inner, names=names):
                    for name in names:
                        (unit, chained), n = units[name[0]], int(name[2])
                        if name[1] == "1":
                            unit.take(n, inner, chained)
                        elif name[1] == "2":
                            unit.two(n)
                        else:
                            unit.three(n)

    small_copies[3].wait_recv()
    slot_row = lax.rem(p.z, 2)
    near = jnp.where(p.z // 2 == p.core, 1.0, 0.0)
    length = near * len_own[pl.ds(slot_row, 1), :] + (1.0 - near) * len_sib[pl.ds(slot_row, 1), :]
    length = length[:, :1]
    lane = lax.broadcasted_iota(jnp.int32, (1, 128), 1)
    key = lax.broadcasted_iota(jnp.int32, (2 * T, 128), 0)
    key = jnp.where(key < T, key + p.core * T, key - T + (1 - p.core) * T)
    barred = jnp.where(key.astype(F32) < length, 0.0, -1e30)
    bias[0] = jnp.where(lane == 64, barred, 0.0).astype(BF)
    bias[1] = jnp.where(lane == 0, barred, 0.0).astype(BF)

    def kept(rows_start, size):
        row = lax.broadcasted_iota(jnp.int32, (size, 1), 0) + rows_start + p.core * T
        return row.astype(F32) < length

    advance("ln1")

    bring_wait(p, xv, act_r.at[0], loc.at[4])

    def first_norm(rows):
        unit, _ = norm_stats(xv[rows, :].astype(F32))
        rows1[rows, :] = (unit * gain1[...] + shift1[...]).astype(BF)

    each_rows(128, T, first_norm)
    outs = [pltpu.make_async_copy(xv, x_out, store.at[0]), pltpu.make_async_copy(rows1, rows1_out, store.at[1])]
    for c in outs:
        c.start()
    for c in own_loads:
        c.wait()
    for r in (1, 2, 3):
        small_copies[r - 1].wait_recv()

    kv_copies = []

    def project(r):
        b = small.at[r]
        x = rows1[...]
        qv[r] = (dg(x, wav[r, :, 0:256], 1, 0) + b[:, 0:256]).astype(BF)
        kv[r, 0:T, :] = dg(x, wav[r, :, 256:512], 1, 0).astype(BF)
        vv[r, 0:T, :] = (dg(x, wav[r, :, 512:768], 1, 0) + b[:, 256:512]).astype(BF)
        cs = [
            remote(ref.at[r, pl.ds(0, T)], ref.at[r, pl.ds(T, T)], kv_s.at[r, n], kv_r.at[r, n], sibling)
            for n, ref in enumerate((kv, vv))
        ]
        for c in cs:
            c.start()
        kv_copies.append(cs)

    def e_copy(head, slot):
        return pltpu.make_async_copy(eb.at[slot], e_out.at[head], store.at[2 + slot])

    def attend_pair(r, j):
        cols = pl.ds(j * 128, 128)
        kp = kv[r, :, cols]
        qp = qv[r, :, cols] * BF(HD**-0.5)
        for h in range(2):
            mine = (lane < 64) if h == 0 else (lane >= 64)
            one = lane == (64 if h == 0 else 0)
            ka = jnp.where(mine, kp, bias[h])
            qa = jnp.where(mine, qp, jnp.where(one, BF(1), BF(0)))
            s = dg(ka, qa, 1, 1)
            e = jnp.exp(s - jnp.max(s, 0, keepdims=True))
            inv = 1.0 / jnp.sum(e, 0, keepdims=True)
            head = r * 4 + 2 * j + h
            if head >= 2:
                e_copy(head - 2, h).wait()
            eb[h] = e.astype(BF)
            e_copy(head, h).start()
            feats = pl.ds(j * 128 + h * 64, 64)
            ot[feats, :] = (dg(vt[feats, :], eb[h], 1, 0) * inv).astype(BF)
            rv[head] = inv

    def attend(r):
        advance(f"att{r}0")
        for c in kv_copies[r]:
            c.wait_recv()
        vt[...] = jnp.transpose(vv[r], (1, 0))
        attend_pair(r, 0)
        advance(f"att{r}1")
        attend_pair(r, 1)
        mix[:, r * 256 : (r + 1) * 256] = jnp.transpose(ot[...], (1, 0))

    bring_copies(p, grad, gv, act_s.at[1], act_r.at[1], loc.at[5])
    advance("proj0")
    project(0)
    for n in range(3):
        unit_a.whole(n)
    for r in (1, 2, 3):
        advance(f"proj{r}")
        project(r)
    for r in range(4):
        attend(r)
    advance("oproj")
    for n in range(3):
        unit_o.whole(n)
    for h in range(2):
        e_copy(14 + h, h).wait()

    outs += [
        pltpu.make_async_copy(wav, wa_out, store.at[4]),
        pltpu.make_async_copy(wov, wo_out, store.at[5]),
        pltpu.make_async_copy(qv, q_out, store.at[6]),
        pltpu.make_async_copy(kv, k_out, store.at[7]),
        pltpu.make_async_copy(vv, v_out, store.at[8]),
        pltpu.make_async_copy(mix, mix_out, store.at[9]),
        pltpu.make_async_copy(rv, r_out, store.at[10]),
    ]
    for c in outs[2:]:
        c.start()

    for n in range(2):
        cols = pl.ds(n * 512, 512)
        middle[:, cols] = dg(mix[...], wov[:, cols], 1, 0)

    advance("ln2")

    def second_norm(rows):
        m = middle[rows, :] + xv[rows, :].astype(F32) + b_out[...]
        middle[rows, :] = m
        unit, _ = norm_stats(m)
        rows2[rows, :] = (unit * gain2[...] + shift2[...]).astype(BF)
        acc[rows, :] = m + b_down[...]

    each_rows(128, T, second_norm)
    tt[...] = jnp.transpose(rows2[...], (1, 0))
    both = chosen_both(p, tt, xb, both_s.at[0], both_r.at[0])

    def mask_grad(i, carry):
        rows = pl.ds(pl.multiple_of(i * 128, 128), 128)
        gv[rows, :] = jnp.where(kept(i * 128, 128), gv[rows, :].astype(F32), 0.0).astype(BF)
        return carry

    order = (0,) + by_arrival

    def load_copies(n):
        r = order[n]
        return [
            pltpu.make_async_copy(wu.at[r - 1], uv.at[n % 2], load.at[0, n % 2]),
            pltpu.make_async_copy(wd.at[r - 1], dv.at[n % 2], load.at[1, n % 2]),
        ]

    def hidden(n):
        r, slot = order[n], n % 2
        for k in range(2):
            c = pl.ds(k * 512, 512)
            upper = dg(rows2[...], uv[slot, :, c], 1, 0) + small[r, :, pl.ds(512 + k * 512, 512)]
            act, slope = gelu_pair(upper)
            ho[slot, :, c] = act.astype(BF)
            slope_v[:, c] = slope
        if n >= 2:
            pl.semaphore_wait(credit, 1)
        copy = remote(ho.at[slot], hs.at[slot], hd_s.at[0, slot], hd_r.at[0, slot], sibling)
        copy.start()
        for k in range(2):
            c = pl.ds(k * 512, 512)
            acc[:, c] = acc[:, c] + dg(ho[slot], dv[slot, :, c], 1, 0)
        return copy

    def hidden_back(n):
        r, slot = order[n], n % 2
        for k in range(2):
            c = pl.ds(k * 512, 512)
            d_up = (dg(gv[...], dv[slot, c, :], 1, 1) * slope_v[:, c]).astype(BF)
            du[slot, :, c] = d_up
            bup_out[r, :, c] = jnp.sum(d_up.astype(F32), 0, keepdims=True)
        copy = remote(du.at[slot], ds.at[slot], hd_s.at[1, slot], hd_r.at[1, slot], sibling)
        copy.start()
        for k in range(2):
            c = pl.ds(k * 512, 512)
            new = dg(du[slot], uv[slot, c, :], 1, 1)
            e2[:, c] = new if n == 0 else e2[:, c] + new
        return copy

    g_stores = []

    def chain(n, u):
        j = 2 * n + u
        first, second = (4, 2) if u else (2, 4)
        block = lambda i: gs.at[n, u, pl.ds(i // 2 * PART, PART)]
        near, far = (p.across(first), p.z), (p.across(second), p.z)
        return (
            remote(block(first), la_out.at[j], ch_s.at[j, 0], ch_r.at[j, 0], near),
            remote(block(first + second), land_b.at[j], ch_s.at[j, 1], ch_r.at[j, 1], near),
            remote(block(second), lc_out.at[j], ch_s.at[j, 2], ch_r.at[j, 2], far),
        )

    chains = {(n, u): chain(n, u) for n in range(2) for u in range(2)}

    def weight_grads(n, cs):
        slot, at = n % 2, min(n, 2)
        for c in cs:
            c.wait_recv()
        if n == 3:
            for c in g_stores[-2:]:
                c.wait()
        gs[at, 0] = (dg(xb[:, 0:T], du[slot], 1, 0) + dg(xb[:, T : 2 * T], ds[slot], 1, 0)).astype(BF)
        gs[at, 1] = (dg(gb[:, 0:T], ho[slot], 1, 0) + dg(gb[:, T : 2 * T], hs[slot], 1, 0)).astype(BF)
        if n < 2:
            pl.semaphore_signal(credit, inc=1, device_id=sibling, device_id_type=MESH)
        for u, out in enumerate((gu_out, gd_out)):
            if n < 2:
                for c in chains[n, u][:2]:
                    c.start()
                c = pltpu.make_async_copy(gs.at[n, u, pl.ds(0, PART)], keep_out.at[2 * n + u], store.at[11 + 2 * n + u])
            else:
                c = pltpu.make_async_copy(gs.at[2, u], out.at[n - 2], store.at[11 + 2 * n + u])
            c.start()
            g_stores.append(c)
        for c in cs:
            c.wait_send()

    def second_exchange(n):
        for u in range(2):
            one, other, two = chains[n, u]
            other.wait_recv()
            rows = pl.ds((2 if u else 4) // 2 * PART, PART)
            gs[n, u, rows, :] = (gs[n, u, rows, :].astype(F32) + land_b[2 * n + u].astype(F32)).astype(BF)
            two.start()

    for c in first_loads:
        c.wait()
    advance("f0")
    held = [[hidden(0)]]
    for c in both:
        c.wait_send()
    advance("b0")
    bring_wait(p, gv, act_r.at[1], loc.at[5])
    lax.fori_loop(0, T // 128, mask_grad, 0)
    tt[...] = jnp.transpose(gv[...], (1, 0))
    both2 = chosen_both(p, tt, gb, both_s.at[1], both_r.at[1])
    held[0].append(hidden_back(0))
    for n in range(1, 4):
        advance(f"w{n - 1}")
        if n < 3:
            unit_u.whole(n - 1)
            unit_d.whole(n - 1)
            loads = load_copies(n)
            for c in loads:
                c.start()
            if n == 1:
                for c in both + both2:
                    c.wait_recv()
            weight_grads(n - 1, held[n - 1])
        else:
            second_exchange(0)
            unit_u.whole(2)
            unit_d.whole(2)
            loads = load_copies(3)
            for c in loads:
                c.start()
        advance(f"f{n}")
        for c in loads:
            c.wait()
        held.append([hidden(n)])
        advance(f"b{n}")
        if n == 3:

            def result(i, carry):
                rows = pl.ds(pl.multiple_of(i * 128, 128), 128)
                rows2[rows, :] = jnp.where(kept(i * 128, 128), acc[rows, :], 0.0).astype(BF)
                return carry

            lax.fori_loop(0, T // 128, result, 0)
            return_copies(p, rows2, out_land, act_s.at[2], act_r.at[2], loc.at[6])
            second_exchange(1)
        held[n].append(hidden_back(n))
    weight_grads(2, held[2])
    weight_grads(3, held[3])

    vec_out[...] = jnp.zeros(vec_out.shape, F32)

    def last(i, carry):
        rows = pl.ds(pl.multiple_of(i * 128, 128), 128)
        unit, inverse = norm_stats(middle[rows, :])
        e = e2[rows, :]
        g = gv[rows, :].astype(F32)
        u = e * gain2[...]
        d_mid = g + inverse * (u - jnp.mean(u, -1, keepdims=True) - unit * jnp.mean(u * unit, -1, keepdims=True))
        middle[rows, :] = d_mid
        for k, v in enumerate((d_mid, e * unit, e, g)):
            vec_out[4 + k : 5 + k, :] += jnp.sum(v, 0, keepdims=True)
        return carry

    lax.fori_loop(0, T // 128, last, 0)
    ends = [pltpu.make_async_copy(middle, dm_out, store.at[19])]
    for c in ends:
        c.start()
    for c in ends + outs + g_stores[:4] + g_stores[6:]:
        c.wait()
    for cs in chains.values():
        cs[0].wait_recv()
        cs[2].wait_recv()
        for c in cs:
            c.wait_send()
    return_wait(p, out_land, act_r.at[2], loc.at[6])
    return_sent(p, rows2, act_s.at[2])
    for c in both2 + small_copies:
        c.wait_send()
    for cs in kv_copies:
        for c in cs:
            c.wait_send()
    for unit in (unit_a, unit_o, unit_u, unit_d):
        unit.finish(unit is unit_a or unit is unit_o)
    bring_sent(p, cells, act_s.at[0])
    bring_sent(p, grad, act_s.at[1])


def return_copies(p, src, dst, sends, recvs, here):
    slot = lax.rem(p.z, 2)
    for h in range(2):
        rows = src.at[pl.ds(h * 256, 256)]
        same = jnp.logical_and(p.core == p.z // 2, p.z == 2 * p.core + h)

        @pl.when(same)
        def _():
            pltpu.make_async_copy(rows, dst.at[slot], here).start()

        @pl.when(jnp.logical_not(same))
        def _():
            remote(rows, dst.at[slot], sends.at[h], recvs.at[slot], (p.base + p.z // 2, 2 * p.core + h)).start()


def return_wait(p, dst, recvs, here):
    for s in range(2):
        same = jnp.logical_and(p.core == p.z // 2, p.z == 2 * p.core + s)

        @pl.when(same)
        def _():
            pltpu.make_async_copy(dst.at[s], dst.at[s], here).wait()

        @pl.when(jnp.logical_not(same))
        def _():
            remote(dst.at[s], dst.at[s], recvs.at[s], recvs.at[s], (p.across(1), p.z)).wait_recv()


def return_sent(p, src, sends):
    for h in range(2):
        rows = src.at[pl.ds(h * 256, 256)]
        same = jnp.logical_and(p.core == p.z // 2, p.z == 2 * p.core + h)

        @pl.when(jnp.logical_not(same))
        def _():
            remote(rows, rows, sends.at[h], sends.at[h], (p.across(1), p.z)).wait_send()


class Chain:
    def __init__(self, p, r, block, keep0, keep1, land1, land2, land3, send, recv, zsend, zrecv, flip):
        first, second = (4, 2) if flip else (2, 4)
        self.r, self.keep0, self.keep1, self.land1, self.land2 = r, keep0, keep1, land1, land2
        near = (p.across(first), p.z)
        self.one = [remote(block(first + k * second), land1.at[k], send.at[k], recv.at[k], near) for k in range(2)]
        self.two = remote(keep1, land2, send.at[2], recv.at[2], (p.across(second), p.z))
        self.three = None
        if not (isinstance(r, int) and r == 0):
            k = jnp.where(r == 2, 2, jnp.where(r == p.slot_next, 0, 1))
            device = (p.d, jnp.where(r == 2, p.z_over, p.z_next))
            self.three = remote(keep0, land3.at[k], zsend.at[k], zrecv.at[k], device)

    def start(self):
        for c in self.one:
            c.start()

    def middle(self):
        for c in self.one:
            c.wait_recv()
        self.keep1[...] = (self.keep1[...].astype(F32) + self.land1[1].astype(F32)).astype(BF)
        self.two.start()

    def total(self):
        return self.keep0[...].astype(F32) + self.land1[0].astype(F32) + self.land2[...].astype(F32)

    def end(self, summed=False):
        if not summed:
            self.two.wait_recv()
        if self.three is not None:
            self.keep0[...] = self.total().astype(BF)

            @pl.when(self.r != 2)
            def _():
                self.three.start()

    def over(self, land):
        @pl.when(self.r == 2)
        def _():
            self.keep0[...] = (self.keep0[...].astype(F32) + land[...].astype(F32)).astype(BF)
            self.three.start()

    def sent(self, summed=False):
        for c in ([] if summed else self.one + [self.two]) + ([] if self.three is None else [self.three]):
            c.wait_send()


class Vectors:
    def __init__(self, p, acc, land, zland, send, recv, zsend, zrecv):
        self.acc, self.land, self.zland = acc, land, zland
        self.steps = [
            remote(acc, land.at[b], send.at[b], recv.at[b], (p.across(1 << b), p.z)) for b in range(3)
        ]
        self.along = [
            remote(acc, zland.at[r - 1], zsend.at[r - 1], zrecv.at[r - 1], (p.d, lax.rem(p.z + r, 4)))
            for r in (1, 2, 3)
        ]

    def start(self, b):
        self.steps[b].start()

    def take(self, b):
        self.steps[b].wait()
        self.acc[...] = self.acc[...] + self.land[b]

    def z_start(self):
        for c in self.along:
            c.start()

    def z_wait(self):
        for c in self.along:
            c.wait()


def backward_kernel(
    x_in, rows1_in, q_in, k_in, v_in, mix_in, e_in, r_in, wa_in, wo_in, dm_in, gu_in, gd_in, keep_in, la_in, lc_in, vec_in, bup_in, gain1,
    gcl, attn_out, gup_out, gdown_out, early_out, late_out,
    land1, land2, land3, land1a, land2a, land3a, udk, ga, wav, wov, qv, kv, vv, mix, mixs, dm, e1, gmb, r1b, tt, gm, xv, rows1, eb, rv, xs, xr, da,
    kt, mixt, dmt_all, dqt, early, late, eland, lland, ezland, lzland,
    ch_s, ch_r, z_s, z_r, gc_s, gc_r, both_s, both_r, x_s, x_r, mix_s, mix_r, ev_s, ev_r, ez_s, ez_r,
    lv_s, lv_r, lz_s, lz_r, credit, here, load, eload,
):
    p = Place()
    sibling = (p.across(1), p.z)
    order = (1, 3, 2, 0)

    loads = {}
    for n, (name, src, dst) in enumerate(
        (
            ("dm", dm_in, dm), ("wo", wo_in, wov), ("rows1", rows1_in, rows1), ("mix", mix_in, mix), ("r", r_in, rv),
            ("q", q_in, qv), ("k", k_in, kv), ("v", v_in, vv), ("x", x_in, xv),
        )
    ):
        loads[name] = pltpu.make_async_copy(src, dst, load.at[n])
        loads[name].start()

    def wa_load(n):
        return pltpu.make_async_copy(wa_in.at[order[n]], wav.at[n % 2], load.at[9 + n % 2])

    def e_load(head, slot):
        return pltpu.make_async_copy(e_in.at[head], eb.at[slot], eload.at[slot])

    for h in range(2):
        e_load(order[0] * 4 + h, h).start()
    wa_load(0).start()

    p.greet()
    mix_copy = remote(mix_in, mixs, mix_s, mix_r, sibling)
    mix_copy.start()

    chains = {}
    keep_loads = []
    shards = (
        0,
        jnp.where(p.z <= 2, 1, 3),
        jnp.where(p.inner, 3, 2),
        jnp.where(p.inner, 2, jnp.where(p.z == 0, 3, 1)),
    )
    for n in (1, 0, 2, 3):
        r = shards[n]
        for u, src in enumerate((gu_in, gd_in)):
            flip = u == 1
            second = 2 if flip else 4
            j = u * 4 + n
            if n < 2:
                parts = ((keep_in, udk.at[j, 0]), (la_in, land1.at[j, 0]), (lc_in, land2.at[j]))
                for k, (held, to) in enumerate(parts):
                    c = pltpu.make_async_copy(held.at[2 * n + u], to, load.at[19 + 3 * (2 * n + u) + k])
                    c.start()
                    keep_loads.append(c)
                blocks = lambda i, j=j: udk.at[j, 0]
            else:
                blocks = lambda i, src=src, n=n: src.at[n - 2, pl.ds(i // 2 * PART, PART)]
                for k, i in enumerate((0, second)):
                    pltpu.make_async_copy(blocks(i), udk.at[j, k], load.at[11 + j]).start()
                keep_loads.append(pltpu.make_async_copy(udk.at[j], udk.at[j], load.at[11 + j]))
            chains[u, n] = Chain(
                p, r, blocks, udk.at[j, 0], udk.at[j, 1], land1.at[j], land2.at[j], land3.at[u],
                ch_s.at[j], ch_r.at[j], z_s.at[u], z_r.at[u], flip,
            )
    for n, r in enumerate(order):
        for half in range(2):
            second = 2 if half else 4
            blocks = lambda i, r=r, half=half: ga.at[r, half, pl.ds(i // 2 * PART, PART)]
            chains[2 + half, n] = Chain(
                p, r, blocks, blocks(0), blocks(second), land1a.at[r, half], land2a.at[r, half], land3a.at[half],
                ch_s.at[8 + 2 * r + half], ch_r.at[8 + 2 * r + half], z_s.at[2 + half], z_r.at[2 + half],
                half == 1,
            )

    def start(kind, n):
        for u in (0, 1) if kind == "f" else (2, 3):
            chains[u, n].start()

    def middle(kind, n):
        for u in (0, 1) if kind == "f" else (2, 3):
            chains[u, n].middle()

    def end(kind, n):
        for u in (0, 1) if kind == "f" else (2, 3):
            chains[u, n].end()

    def z_got(u, k, land):
        remote(land.at[k], land.at[k], z_s.at[u, k], z_r.at[u, k], sibling).wait_recv()

    def over(kind, ns):
        for u in (0, 1) if kind == "f" else (2, 3):
            land = land3.at[u] if kind == "f" else land3a.at[u - 2]
            z_got(u, 1, land)
            for n in ns:
                chains[u, n].over(land.at[1])

    start("f", 2)
    start("f", 3)

    early[...] = vec_in[0:8, :]
    for r in range(4):
        early[r : r + 1, :] = bup_in[r]
    ev = Vectors(p, early, eland, ezland, ev_s, ev_r, ez_s, ez_r)
    ev.start(0)
    late[...] = jnp.zeros((8, 1024), F32)

    loads["rows1"].wait()
    tt[...] = jnp.transpose(rows1[...], (1, 0))
    both = chosen_both(p, tt, r1b, both_s.at[0], both_r.at[0])
    loads["dm"].wait()

    def cast(rows):
        gm[rows, :] = dm[rows, :].astype(BF)

    each_rows(128, T, cast)
    for name in ("wo", "mix", "r", "q", "k", "v"):
        loads[name].wait()
    lane = lax.broadcasted_iota(jnp.int32, (1, 128), 1)

    def attend_back(n):
        r, slot = order[n], n % 2
        cols_r = pl.ds(r * 256, 256)
        kt[...] = jnp.transpose(kv[r], (1, 0))
        mixt[...] = jnp.transpose(mix[:, cols_r], (1, 0))
        dmt_all[...] = dg(wov[cols_r, :], gm[...], 1, 1).astype(BF)
        if n >= 2:
            for c in [x_copies[n - 2]]:
                c.wait_send()

        def pair(j, carry):
            cols = lane_block(j * 128)
            kp = kv[r, :, cols]
            vp = vv[r, :, cols]
            qp = qv[r, :, cols] * BF(HD**-0.5)
            dk = jnp.zeros((2 * T, 128), F32)
            d_v = jnp.zeros((2 * T, 128), F32)
            for h in range(2):
                head = r * 4 + 2 * j + h
                feats = pl.ds(pl.multiple_of(j * 128 + h * 64, 64), 64)
                mine = (lane < 64) if h == 0 else (lane >= 64)
                dmt = (dmt_all[feats, :].astype(F32) * rv[head]).astype(BF)
                delta = jnp.sum(dmt.astype(F32) * mixt[feats, :].astype(F32), 0, keepdims=True)
                zero = jnp.zeros((64, T), BF)
                dmt2 = jnp.concatenate([dmt, zero] if h == 0 else [zero, dmt], 0)
                dma = jnp.transpose(dmt2, (1, 0))
                dp = dg(vp, dmt2, 1, 0)
                e_load(head, h).wait()
                ds = (eb[h].astype(F32) * (dp - delta)).astype(BF)
                qa = jnp.where(mine, qp, BF(0))
                d_v = d_v + dg(eb[h], dma, 1, 0)
                if n < 3:
                    nxt = jnp.where(j == 0, head + 2, order[n + 1] * 4 + h)
                    e_load(nxt, h).start()
                else:
                    @pl.when(j == 0)
                    def _():
                        e_load(head + 2, h).start()
                dk = dk + dg(ds, qa, 1, 0)
                dqt[feats, :] = (dg(kt[feats, :], ds, 1, 0) * HD**-0.5).astype(BF)
            xs[slot, T : 3 * T, cols] = dk.astype(BF)
            xs[slot, 3 * T : 5 * T, cols] = d_v.astype(BF)
            return carry

        lax.fori_loop(0, 2, pair, 0)
        xs[slot, 0:T, :] = jnp.transpose(dqt[...], (1, 0))
        if n >= 2:
            pl.semaphore_wait(credit, 1)
        c = remote(xs.at[slot], xr.at[slot], x_s.at[slot], x_r.at[slot], sibling)
        c.start()
        return c

    x_copies = []

    def gather_up(n):
        r, slot = order[n], n % 2
        x_copies[n].wait_recv()
        da[0:T, 0:256] = xs[slot, 0:T, :]
        da[T : 2 * T, 0:256] = xr[slot, 0:T, :]
        for k in range(2):
            base = T + 2 * T * k
            cols = pl.ds(256 * (k + 1), 256)
            da[0:T, cols] = (
                xs[slot, base : base + T, :].astype(F32) + xr[slot, base + T : base + 2 * T, :].astype(F32)
            ).astype(BF)
            da[T : 2 * T, cols] = (
                xs[slot, base + T : base + 2 * T, :].astype(F32) + xr[slot, base : base + T, :].astype(F32)
            ).astype(BF)
        if n < 2:
            pl.semaphore_signal(credit, inc=1, device_id=sibling, device_id_type=MESH)
        ga[r, 0] = dg(r1b[...], da[:, 0:512], 1, 0).astype(BF)
        ga[r, 1, :, 0:256] = dg(r1b[...], da[:, 512:768], 1, 0).astype(BF)
        cols_r = pl.ds(r * 256, 256)
        ga[r, 1, :, 256:512] = (dg(gmb[:, 0:T], mix[:, cols_r], 1, 0) + dg(gmb[:, T : 2 * T], mixs[:, cols_r], 1, 0)).astype(BF)
        wa_load(n).wait()
        if n + 1 < 4:
            wa_load(n + 1).start()
        new = dg(da[0:T, :], wav[slot], 1, 1)
        e1[...] = new if n == 0 else e1[...] + new
        late[2:3, r * 256 : (r + 1) * 256] = jnp.sum(da[0:T, 0:256].astype(F32), 0, keepdims=True)
        late[3:4, r * 256 : (r + 1) * 256] = jnp.sum(da[0:T, 512:768].astype(F32), 0, keepdims=True)

    for c in keep_loads:
        c.wait()
    for u in range(2):
        chains[u, 1].end(True)
    x_copies.append(attend_back(0))
    for c in both:
        c.wait_send()
    tt[...] = jnp.transpose(gm[...], (1, 0))
    both2 = chosen_both(p, tt, gmb, both_s.at[1], both_r.at[1])
    middle("f", 2)
    ev.take(0)
    ev.start(1)
    x_copies.append(attend_back(1))
    middle("f", 3)
    for c in both + both2:
        c.wait_recv()
    mix_copy.wait_recv()
    gather_up(0)
    start("a", 0)
    end("f", 2)
    x_copies.append(attend_back(2))
    ev.take(1)
    ev.start(2)
    gather_up(1)
    start("a", 1)
    end("f", 3)
    middle("a", 0)
    x_copies.append(attend_back(3))
    middle("a", 1)
    over("f", (2, 3))
    gather_up(2)
    start("a", 2)
    end("a", 0)
    gather_up(3)
    start("a", 3)
    end("a", 1)
    ev.take(2)
    ev.z_start()

    loads["x"].wait()

    def first_back(i, carry):
        rows = pl.ds(pl.multiple_of(i * 128, 128), 128)
        unit, inverse = norm_stats(xv[rows, :].astype(F32))
        e = e1[rows, :]
        u = e * gain1[...]
        d = dm[rows, :] + inverse * (u - jnp.mean(u, -1, keepdims=True) - unit * jnp.mean(u * unit, -1, keepdims=True))
        gm[rows, :] = d.astype(BF)
        for k, v in enumerate((e * unit, e)):
            late[k : k + 1, :] += jnp.sum(v, 0, keepdims=True)
        return carry

    lax.fori_loop(0, T // 128, first_back, 0)
    return_copies(p, gm, gcl, gc_s, gc_r, here.at[1])
    lv = Vectors(p, late, lland, lzland, lv_s, lv_r, lz_s, lz_r)
    lv.start(0)
    middle("a", 2)
    lv.take(0)
    lv.start(1)
    end("a", 2)
    over("a", (2,))
    middle("a", 3)
    lv.take(1)
    lv.start(2)

    def final(u, n, land):
        z_got(u, 0, land)
        z_got(u, 2, land)
        return chains[u, n].total() + land[0].astype(F32) + land[2].astype(F32)

    gup_out[...] = final(0, 0, land3.at[0])
    gdown_out[...] = final(1, 0, land3.at[1])
    lv.take(2)
    lv.z_start()
    ev.z_wait()
    shard = early[0:1, :]
    for r in (1, 2, 3):
        shard = shard + ezland[r - 1, r : r + 1, :]
    early_out[...] = early[...] + ezland[0] + ezland[1] + ezland[2]
    early_out[0:1, :] = shard
    end("a", 3)

    lv.z_wait()
    late_out[...] = late[...] + lzland[0] + lzland[1] + lzland[2]
    for k in (2, 3):
        shard = late[k : k + 1, 0:256]
        for r in (1, 2, 3):
            shard = shard + lzland[r - 1, k : k + 1, r * 256 : (r + 1) * 256]
        late_out[k : k + 1, 0:256] = shard
    total = final(2, 3, land3a.at[0])
    attn_out[:, 0:512] = total
    attn_out[:, 512:1024] = final(3, 3, land3a.at[1])
    return_wait(p, gcl, gc_r, here.at[1])

    for c in both2 + [mix_copy, x_copies[2], x_copies[3]]:
        c.wait_send()
    for (u, n), c in chains.items():
        c.sent(u < 2 and n < 2)
    return_sent(p, gm, gc_s)


def backward(*args):
    s = jax.ShapeDtypeStruct
    hbm, fast = pl.BlockSpec(memory_space=pltpu.HBM), pl.BlockSpec(memory_space=pltpu.VMEM)
    b, f, dma = (lambda *x: pltpu.VMEM(x, BF)), (lambda *x: pltpu.VMEM(x, F32)), (lambda *x: pltpu.SemaphoreType.DMA(x))
    return pl.pallas_call(
        backward_kernel,
        out_shape=[
            s((2, 256, 1024), BF), s((PART, 1024), F32), s((PART, 1024), F32), s((PART, 1024), F32),
            s((8, 1024), F32), s((8, 1024), F32),
        ],
        in_specs=[hbm] * 16 + [fast] * 3,
        out_specs=[hbm] + [fast] * 5,
        scratch_shapes=[
            b(8, 2, PART, 1024), b(8, PART, 1024), b(2, 3, PART, 1024), b(4, 2, 2, PART, 512), b(4, 2, PART, 512), b(2, 3, PART, 512),
            b(8, 2, PART, 1024), b(4, 2, 4 * PART, 512), b(2, 1024, 768),
            b(1024, 1024), b(4, T, 256), b(4, 2 * T, 256), b(4, 2 * T, 256), b(T, 1024), b(T, 1024), f(T, 1024), f(T, 1024),
            b(T, 2 * T), b(T, 2 * T), b(1024, T), b(T, 1024), b(T, 1024), b(T, 1024), b(2, 2 * T, T), f(16, 1, T),
            b(2, 5 * T, 256), b(2, 5 * T, 256), b(2 * T, 768),
            b(256, 2 * T), b(256, T), b(256, T), b(256, T), f(8, 1024), f(8, 1024), f(3, 8, 1024), f(3, 8, 1024), f(3, 8, 1024), f(3, 8, 1024),
            dma(16, 3), dma(16, 3), dma(4, 3), dma(4, 3), dma(2), dma(2), dma(2, 4), dma(2, 4), dma(2), dma(2),
            pltpu.SemaphoreType.DMA, pltpu.SemaphoreType.DMA, dma(3), dma(3), dma(3), dma(3), dma(3), dma(3), dma(3), dma(3),
            pltpu.SemaphoreType.REGULAR, dma(2), dma(31), dma(2),
        ],
        compiler_params=pltpu.CompilerParams(collective_id=1, has_side_effects=True, vmem_limit_bytes=63 * 2**20),
    )(*args)


def spread_kernel(
    out_in, cells_hbm, attn_hbm, up_hbm, down_hbm, early_hbm, late_hbm,
    out_cells, grad_cells, gq, gk, gv, bq, bv, go, bo, g1, s1, g2, s2, gup, bu, gdown, bd,
    cells_in, wide, attn, down, early, late, up, res, sems,
):
    p = Place()
    copies = [
        pltpu.make_async_copy(a, b, sems.at[k])
        for k, (a, b) in enumerate(
            (
                (cells_hbm, cells_in), (early_hbm, early), (late_hbm, late), (attn_hbm, attn), (down_hbm, down),
                (up_hbm, up), (out_in, res),
            )
        )
    ]
    for c in copies:
        c.start()
    copies[6].wait()
    backs = [pltpu.make_async_copy(res, out_cells, sems.at[8])]
    copies[0].wait()
    wide[...] = cells_in[...].astype(F32)
    backs.append(pltpu.make_async_copy(wide, grad_cells, sems.at[7]))
    for c in copies[1:6]:
        c.wait()
    backs.append(pltpu.make_async_copy(up, gup, sems.at[9]))
    for c in backs:
        c.start()
    gq[...] = attn[:, 0:256]
    gk[...] = attn[:, 256:512]
    gv[...] = attn[:, 512:768]
    go[...] = jnp.transpose(attn[:, 768:1024], (1, 0))
    gdown[...] = jnp.transpose(down[...], (1, 0))

    def cut(ref, k, block, part):
        row = ref[k : k + 1, lane_block(block * 128)]
        return pltpu.roll(row, lax.rem(128 - part * 32, 128), 1)[:, 0:32]

    for out, ref, k in ((bo, early, 4), (g1, late, 0), (s1, late, 1), (g2, early, 5), (s2, early, 6), (bd, early, 7)):
        out[...] = cut(ref, k, p.d, p.z)
    for out, k in ((bq, 2), (bv, 3)):
        out[...] = cut(late, k, p.d // 4, lax.rem(p.d, 4))
    bu[...] = early[0:1, lane_block(p.d * 128)]
    for c in backs:
        c.wait()


def spread(*args):
    s = jax.ShapeDtypeStruct
    hbm, fast = pl.BlockSpec(memory_space=pltpu.HBM), pl.BlockSpec(memory_space=pltpu.VMEM)
    v, w = s((1, 32), F32), s((PART, 256), F32)
    return pl.pallas_call(
        spread_kernel,
        out_shape=[
            s((2, 256, 1024), BF), s((2, 256, 1024), F32), w, w, w, v, v, s((256, PART), F32), v, v, v, v, v,
            s((PART, 1024), F32), s((1, PART), F32), s((1024, PART), F32), v,
        ],
        in_specs=[hbm] * 7,
        out_specs=[hbm, hbm] + [fast] * 11 + [hbm] + [fast] * 3,
        scratch_shapes=[
            pltpu.VMEM((2, 256, 1024), BF), pltpu.VMEM((2, 256, 1024), F32), pltpu.VMEM((PART, 1024), F32),
            pltpu.VMEM((PART, 1024), F32), pltpu.VMEM((8, 1024), F32), pltpu.VMEM((8, 1024), F32), pltpu.VMEM((PART, 1024), F32),
            pltpu.VMEM((2, 256, 1024), BF), pltpu.SemaphoreType.DMA((10,)),
        ],
        compiler_params=pltpu.CompilerParams(vmem_limit_bytes=62 * 2**20),
    )(*args)


def forward(*args):
    s = jax.ShapeDtypeStruct
    outs = [
        (T, 1024), (T, 1024), (4, T, 256), (4, 2 * T, 256), (4, 2 * T, 256), (T, 1024), (16, 2 * T, T), (16, 1, T),
        (4, 1024, 768), (1024, 1024), (3, 1024, 1024), (3, 1024, 1024), (2, 256, 1024), (T, 1024), (2, T, 1024), (2, T, 1024),
        (4, PART, 1024), (4, PART, 1024), (4, PART, 1024), (16, 1024), (4, 1, 1024),
    ]
    wide = (7, 13, 19, 20)
    hbm, fast = pl.BlockSpec(memory_space=pltpu.HBM), pl.BlockSpec(memory_space=pltpu.VMEM)
    b, f, dma = (lambda *x: pltpu.VMEM(x, BF)), (lambda *x: pltpu.VMEM(x, F32)), (lambda *x: pltpu.SemaphoreType.DMA(x))
    sems = []
    for parts in (3, 1, 1, 1):
        sems += [dma(6, parts), dma(3, parts), dma(3, 7), dma(3, 8)]
    return pl.pallas_call(
        forward_kernel,
        out_shape=[s(o, F32 if n in wide else BF) for n, o in enumerate(outs)],
        in_specs=[hbm, hbm, fast] + [hbm] * 6 + [fast] * 7,
        out_specs=[hbm] * 19 + [fast] * 2,
        scratch_shapes=[
            b(T, 1024), b(T, 1024), b(T, 1024), b(4, 1024, 768), b(1024, 1024), b(4, T, 256), b(4, 2 * T, 256), b(4, 2 * T, 256),
            b(T, 1024), b(2, 2 * T, T), f(16, 1, T), b(2, 2 * T, 128), b(256, 2 * T), b(256, T), f(T, 1024), b(T, 1024),
            b(1024, T), b(T, 2 * T), b(T, 2 * T), f(T, 1024), f(T, 1024),
            b(2, 1024, 1024), b(2, 1024, 1024), b(2, T, 1024), b(2, T, 1024), b(2, T, 1024), b(2, T, 1024), f(T, 1024), b(3, 2, T, 1024), b(4, PART, 1024),
            f(8, 128), f(4, 1, 1536),
        ]
        + sems
        + [dma(3, 2), dma(3, 2), dma(4), dma(4), dma(4, 2), dma(4, 2), dma(2, 4), dma(2, 4), dma(2, 2), dma(2, 2), dma(4, 3), dma(4, 3),
           pltpu.SemaphoreType.REGULAR, dma(7), dma(2, 2), dma(20)],
        compiler_params=pltpu.CompilerParams(collective_id=0, has_side_effects=True, vmem_limit_bytes=62 * 2**20),
    )(*args)


def body(*args):
    if lax.axis_size("dp") == 8 and lax.axis_size("mp") == 4:
        return fused_body(*args)
    return plain_body(*args)


def fused_body(
    cells,
    lengths,
    query_matrix,
    key_matrix,
    value_matrix,
    query_bias,
    value_bias,
    output_matrix,
    b_out,
    gain_one,
    shift_one,
    gain_two,
    shift_two,
    expand_weight,
    expand_bias,
    contract_weight,
    b_down,
    grad_out,
):
    slots = cells.shape[0]
    row = lambda v: v.reshape(1, -1)
    small = row(jnp.concatenate([query_bias, value_bias, expand_bias]))
    len_own = jnp.pad(jnp.broadcast_to(lengths.astype(F32)[:, None], (slots, 128)), ((0, 8 - slots), (0, 0)))
    (x, rows_one, q_all, k_all, v_all, mixed_all, e_all, r_all, wa, wo, _, _, out_land, d_middle, gu, gd, keep, la, lc, vec, bup) = forward(
        cells, grad_out, len_own, query_matrix, key_matrix, value_matrix, output_matrix, expand_weight, contract_weight,
        small, row(b_out), row(gain_one), row(shift_one), row(gain_two), row(shift_two), row(b_down),
    )
    left = backward(
        x, rows_one, q_all, k_all, v_all, mixed_all, e_all, r_all, wa, wo, d_middle, gu, gd, keep, la, lc, vec, bup, row(gain_one)
    )
    return tuple(v.reshape(-1) if v.shape[0] == 1 else v for v in spread(out_land, *left))


def solution(mesh):
    return jax.shard_map(
        body,
        mesh=mesh,
        in_specs=(
            P("dp", "mp", None),
            P("dp"),
            P(None, "mp"),
            P(None, "mp"),
            P(None, "mp"),
            P("mp"),
            P("mp"),
            P("mp", None),
            P(),
            P(),
            P(),
            P(),
            P(),
            P(None, "mp"),
            P("mp"),
            P("mp", None),
            P(),
            P("dp", "mp", None),
        ),
        out_specs=(
            P("dp", "mp", None),
            P("dp", "mp", None),
            P("dp", "mp"),
            P("dp", "mp"),
            P("dp", "mp"),
            P(("mp", "dp")),
            P(("mp", "dp")),
            P("mp", "dp"),
            P(("dp", "mp")),
            P(("dp", "mp")),
            P(("dp", "mp")),
            P(("dp", "mp")),
            P(("dp", "mp")),
            P("dp", "mp"),
            P(("mp", "dp")),
            P("mp", "dp"),
            P(("dp", "mp")),
        ),
        check_vma=False,
    )
```

```python
import jax
import jax.numpy as jnp
from jax import lax
from jax.experimental import pallas as pl
from jax.experimental.pallas import tpu as pltpu
from jax.sharding import PartitionSpec as P

HD = 64
EPS = 1e-05
BF = jnp.bfloat16
F32 = jnp.float32
MESH = pl.DeviceIdType.MESH
T = 512
PART = 128


def dot(a, b, ca, cb):
    return lax.dot_general(a, b, (((ca,), (cb,)), ((), ())), preferred_element_type=F32)


def cross(x, bit):
    n = lax.axis_size("dp")
    return lax.ppermute(x, "dp", [(i, i ^ (1 << bit)) for i in range(n)])


def shift(x, by):
    n = lax.axis_size("mp")
    return lax.ppermute(x, "mp", [(i, (i + by) % n) for i in range(n)])


def moves(n_dp, n_mp, slots):
    per = n_mp // slots
    turns = []
    for t in range(slots):
        pairs = []
        for d in range(n_dp):
            for m in range(n_mp):
                s = (t + m) % slots
                base, c = d - d % per, d % per
                target = (base + m // slots, c * slots + s)
                pairs.append((d * n_mp + m, target[0] * n_mp + target[1]))
        turns.append(pairs)
    return turns


def plane_bits(n_dp, flip):
    bits = list(range(1, n_dp.bit_length() - 1))
    return bits[::-1] if flip else bits


def gather(piece, flip):
    n_dp, n_mp = lax.axis_size("dp"), lax.axis_size("mp")
    stack = jnp.stack([shift(piece, n_mp - r) for r in range(1, n_mp)])
    held = {0: stack}
    for bit in plane_bits(n_dp, flip) + [0]:
        held.update({i ^ (1 << bit): cross(v, bit) for i, v in list(held.items())})
    return held


def assemble(held, own, d):
    n = len(held)
    stack = jnp.stack([held[i] for i in range(n)])
    order = jnp.arange(n) ^ d
    placed = jnp.take(stack, order, axis=0)
    placed = jnp.moveaxis(placed, 0, 1).reshape((stack.shape[1], -1, stack.shape[-1]))
    return [own] + [placed[r] for r in range(placed.shape[0])]


def scatter(blocks, flip):
    n_dp = lax.axis_size("dp")
    for bit in plane_bits(n_dp, flip):
        keep = sorted(i for i in blocks if not i >> bit & 1)
        got = cross(jnp.stack([blocks[i ^ (1 << bit)] for i in keep]), bit)
        blocks = {
            i: (blocks[i].astype(F32) + got[k].astype(F32)).astype(blocks[i].dtype)
            for k, i in enumerate(keep)
        }
    return blocks[0]


def layer_norm(v, gain, bias):
    center = v - jnp.mean(v, -1, keepdims=True)
    inverse = lax.rsqrt(jnp.mean(center * center, -1, keepdims=True) + EPS)
    unit = center * inverse
    return unit * gain + bias, unit, inverse


def norm_back(up, unit, inverse, gain):
    u = up * gain
    return inverse * (
        u - jnp.mean(u, -1, keepdims=True) - unit * jnp.mean(u * unit, -1, keepdims=True)
    )


def gelu_pair(v):
    cumulative = 0.5 * (1.0 + lax.erf(v * 0.7071067811865476))
    density = jnp.exp(-0.5 * v * v) * 0.3989422804014327
    return v * cumulative, cumulative + v * density


def attend(q, k, v, allowed):
    heads = q.shape[1] // HD
    qh = q.reshape(-1, heads, HD)
    kh = k.reshape(-1, heads, HD)
    vh = v.reshape(-1, heads, HD)
    s = jnp.einsum("qhd,khd->hqk", qh, kh, preferred_element_type=F32) * HD**-0.5
    s = jnp.where(allowed[None, None, :], s, -1e30)
    e = jnp.exp(s - jnp.max(s, -1, keepdims=True))
    p = (e / jnp.sum(e, -1, keepdims=True)).astype(BF)
    mixed = jnp.einsum("hqk,khd->qhd", p, vh, preferred_element_type=F32)
    return mixed.astype(BF).reshape(q.shape), p


def attend_back(q, k, v, p, mixed, dm):
    heads = q.shape[1] // HD
    qh = q.reshape(-1, heads, HD)
    kh = k.reshape(-1, heads, HD)
    vh = v.reshape(-1, heads, HD)
    dh = dm.reshape(-1, heads, HD)
    pf = p.astype(F32)
    dp = jnp.einsum("qhd,khd->hqk", dh, vh, preferred_element_type=F32)
    total = jnp.sum(dp * pf, -1, keepdims=True)
    ds = (pf * (dp - total)).astype(BF)
    dv = jnp.einsum("hqk,qhd->khd", p, dh, preferred_element_type=F32)
    dq = jnp.einsum("hqk,khd->qhd", ds, kh, preferred_element_type=F32) * HD**-0.5
    dk = jnp.einsum("hqk,qhd->khd", ds, qh, preferred_element_type=F32) * HD**-0.5
    return (
        dq.astype(BF).reshape(q.shape),
        dk.astype(BF).reshape(k.shape),
        dv.astype(BF).reshape(k.shape),
    )


def plain_body(
    cells,
    lengths,
    query_matrix,
    key_matrix,
    value_matrix,
    query_bias,
    value_bias,
    output_matrix,
    b_out,
    gain_one,
    shift_one,
    gain_two,
    shift_two,
    expand_weight,
    expand_bias,
    contract_weight,
    b_down,
    grad_out,
):
    slots, rows, width = cells.shape
    n_dp, n_mp = lax.axis_size("dp"), lax.axis_size("mp")
    d, z = lax.axis_index("dp"), lax.axis_index("mp")
    per = n_mp // slots
    core = d % per
    tokens = slots * rows
    part = width // n_dp
    hw = query_matrix.shape[1]
    turns = moves(n_dp, n_mp, slots)

    def bring(x):
        got = [
            lax.ppermute(
                lax.dynamic_index_in_dim(x, (t + z) % slots, 0, False), ("dp", "mp"), turns[t]
            )
            for t in range(slots)
        ]
        even = z % slots == 0
        return jnp.concatenate(
            [jnp.where(even, got[0], got[1]), jnp.where(even, got[1], got[0])], 0
        )

    def give_back(x):
        x = x.reshape(slots, rows, width)
        got = [
            lax.ppermute(
                lax.dynamic_index_in_dim(x, (t + z) % slots, 0, False),
                ("dp", "mp"),
                [(b, a) for a, b in turns[t]],
            )
            for t in range(slots)
        ]
        even = z % slots == 0
        return jnp.stack(
            [jnp.where(even, got[0], got[1]), jnp.where(even, got[1], got[0])], 0
        )

    mine = bring(cells)
    attn_own = jnp.concatenate(
        [query_matrix, key_matrix, value_matrix, output_matrix.T], 1
    )
    first = d * part

    def piece_of(w):
        return lax.dynamic_slice_in_dim(w, first, part, 0)

    half = attn_own.shape[1] // 2
    a_piece = piece_of(attn_own)
    a_left = gather(a_piece[:, :half], False)
    a_right = gather(a_piece[:, half:], True)
    u_held = gather(piece_of(expand_weight), False)
    d_held = gather(piece_of(contract_weight), True)
    grad_rows = bring(grad_out)
    small = jnp.concatenate([query_bias, value_bias, expand_bias])
    small = [small] + [shift(small, n_mp - r) for r in range(1, n_mp)]
    both = cross(lengths, 0)
    length_all = jnp.where(core == 0, jnp.concatenate([lengths, both]), jnp.concatenate([both, lengths]))
    length = lax.dynamic_index_in_dim(length_all, z, 0, False)

    attn_w = [
        jnp.concatenate([a, b], 1)
        for a, b in zip(
            assemble(a_left, attn_own[:, :half], d), assemble(a_right, attn_own[:, half:], d)
        )
    ]
    up_w = assemble(u_held, expand_weight, d)
    down_w = assemble(d_held, contract_weight, d)

    position = core * tokens + jnp.arange(tokens)
    keep = (position < length).astype(F32)[:, None]
    sib_position = (per - 1 - core) * tokens + jnp.arange(tokens)
    allowed = jnp.concatenate([position, sib_position]) < length

    x = mine.astype(F32)
    rows_one, unit_one, inv_one = layer_norm(x, gain_one, shift_one)
    rows_one = rows_one.astype(BF)
    kept = []
    attention = jnp.zeros((tokens, width), F32)
    for r in range(n_mp):
        w = attn_w[r]
        q = (dot(rows_one, w[:, :hw], 1, 0) + small[r][:hw]).astype(BF)
        k = dot(rows_one, w[:, hw : 2 * hw], 1, 0).astype(BF)
        v = (dot(rows_one, w[:, 2 * hw : 3 * hw], 1, 0) + small[r][hw : 2 * hw]).astype(BF)
        k = jnp.concatenate([k, cross(k, 0)], 0)
        v = jnp.concatenate([v, cross(v, 0)], 0)
        mixed, p = attend(q, k, v, allowed)
        kept.append((q, k, v, mixed, p))
        attention = attention + dot(mixed, w[:, 3 * hw :], 1, 1)
    middle = x + attention + b_out
    rows_two, unit_two, inv_two = layer_norm(middle, gain_two, shift_two)
    rows_two = rows_two.astype(BF)
    g = keep * grad_rows.astype(F32)
    gz = g.astype(BF)

    order = jnp.arange(0, n_dp, 2) ^ d

    def chosen(v):
        return jnp.take(v.reshape(v.shape[0], n_dp, part), order, axis=1).reshape(v.shape[0], -1)

    def other(v):
        return jnp.take(v.reshape(v.shape[0], n_dp, part), order ^ 1, axis=1).reshape(v.shape[0], -1)

    def both_cores(v):
        return jnp.concatenate([chosen(v), cross(other(v), 0)], 0)

    def weight_grad(left, right, flip):
        right = jnp.concatenate([right, cross(right, 0)], 0)
        return weight_grad_all(left, right, flip)

    def weight_grad_all(left, right, flip):
        got = dot(left, right, 0, 0).astype(BF).reshape(-1, part, right.shape[1])
        return scatter({2 * i: got[i] for i in range(got.shape[0])}, flip)

    def finish(pieces):
        total = pieces[0].astype(F32)
        for r in range(1, n_mp):
            total = total + shift(pieces[r], r).astype(F32)
        return total

    two_both = both_cores(rows_two)
    gz_both = both_cores(gz)
    result = middle + b_down
    e2 = jnp.zeros((tokens, width), F32)
    up_parts, down_parts, b_up = [], [], []
    for r in range(n_mp):
        upper = dot(rows_two, up_w[r], 1, 0) + small[r][2 * hw :]
        hidden, slope = gelu_pair(upper)
        hidden = hidden.astype(BF)
        result = result + dot(hidden, down_w[r], 1, 0)
        d_upper = (dot(gz, down_w[r], 1, 1) * slope).astype(BF)
        e2 = e2 + dot(d_upper, up_w[r], 1, 1)
        up_parts.append(weight_grad(two_both, d_upper, False))
        down_parts.append(weight_grad(gz_both, hidden, True))
        b_up.append(jnp.sum(d_upper.astype(F32), 0))
    out_cells = give_back((keep * result).astype(BF))
    grad_up = finish(up_parts)
    grad_down = finish(down_parts).T

    d_middle = g + norm_back(e2, unit_two, inv_two, gain_two)
    gm = d_middle.astype(BF)
    gm_both = both_cores(gm)
    one_both = both_cores(rows_one)
    e1 = jnp.zeros((tokens, width), F32)
    a_parts, b_q, b_v = [], [], []
    for r in range(n_mp):
        q, k, v, mixed, p = kept[r]
        w = attn_w[r]
        d_mixed = dot(gm, w[:, 3 * hw :], 1, 0).astype(BF)
        dq, dk, dv = attend_back(q, k, v, p, mixed, d_mixed)
        dk_all = (dk.astype(F32) + jnp.roll(cross(dk, 0), tokens, 0).astype(F32)).astype(BF)
        dv_all = (dv.astype(F32) + jnp.roll(cross(dv, 0), tokens, 0).astype(F32)).astype(BF)
        dq_all = jnp.concatenate([dq, cross(dq, 0)], 0)
        e1 = (
            e1
            + dot(dq, w[:, :hw], 1, 1)
            + dot(dk_all[:tokens], w[:, hw : 2 * hw], 1, 1)
            + dot(dv_all[:tokens], w[:, 2 * hw : 3 * hw], 1, 1)
        )
        b_q.append(jnp.sum(dq.astype(F32), 0))
        b_v.append(jnp.sum(dv_all[:tokens].astype(F32), 0))
        qkv_part = weight_grad_all(one_both, jnp.concatenate([dq_all, dk_all, dv_all], 1), r % 2 == 1)
        o_part = weight_grad(gm_both, mixed, r % 2 == 0)
        a_parts.append(jnp.concatenate([qkv_part, o_part], 1))
    d_cells = d_middle + norm_back(e1, unit_one, inv_one, gain_one)
    grad_cells = give_back(d_cells.astype(BF)).astype(F32)
    grad_attn = finish(a_parts)

    split_mp = [jnp.stack(b_q).reshape(n_mp, n_dp, -1), jnp.stack(b_v).reshape(n_mp, n_dp, -1), jnp.stack(b_up).reshape(n_mp, n_dp, -1)]
    sums = [
        jnp.sum(d_middle, 0),
        jnp.sum(e1 * unit_one, 0),
        jnp.sum(e1, 0),
        jnp.sum(e2 * unit_two, 0),
        jnp.sum(e2, 0),
        jnp.sum(g, 0),
    ]
    split_dp = [jnp.roll(jnp.swapaxes(s.reshape(n_dp, n_mp, -1), 0, 1), -z, 0) for s in sums]
    packed = jnp.concatenate(split_mp + split_dp, 2)
    packed = jnp.take(packed, jnp.arange(n_dp) ^ d, axis=1)
    packed = packed[:, 0::2] + cross(packed[:, 1::2], 0)
    packed = scatter({2 * i: packed[:, i] for i in range(packed.shape[1])}, False)
    vec = packed[0]
    for r in range(1, n_mp):
        vec = vec + shift(packed[r], r)
    nq = split_mp[0].shape[2]
    nu = split_mp[2].shape[2]
    ns = split_dp[0].shape[2]
    vq, vv, vu = vec[:nq], vec[nq : 2 * nq], vec[2 * nq : 2 * nq + nu]
    rest = [vec[2 * nq + nu + i * ns : 2 * nq + nu + (i + 1) * ns] for i in range(6)]
    return (
        out_cells,
        grad_cells,
        grad_attn[:, :hw],
        grad_attn[:, hw : 2 * hw],
        grad_attn[:, 2 * hw : 3 * hw],
        vq,
        vv,
        grad_attn[:, 3 * hw :].T,
        rest[0],
        rest[1],
        rest[2],
        rest[3],
        rest[4],
        grad_up,
        vu,
        grad_down,
        rest[5],
    )


def dg(a, b, ca, cb):
    return lax.dot_general(a, b, (((ca,), (cb,)), ((), ())), preferred_element_type=F32)


def lane_block(start, size=128):
    return pl.ds(pl.multiple_of(start, size), size)


class Place:
    def __init__(self):
        self.d, self.z = lax.axis_index("dp"), lax.axis_index("mp")
        self.bit = [lax.rem(self.d // (1 << b), 2) for b in range(3)]
        self.core = self.bit[0]
        self.base = self.d - self.core
        self.inner = jnp.logical_and(self.z >= 1, self.z <= 2)
        odd = lax.rem(self.z, 2)
        self.z_next, self.z_over = self.z + 1 - 2 * odd, self.z + 2 - 4 * (self.z // 2)
        self.slot_next = 1 + 2 * odd
        self.outer = jnp.logical_not(self.inner)

    def across(self, i):
        v = self.d
        for b in range(3):
            if i >> b & 1:
                v = v + (1 << b) * (1 - 2 * self.bit[b])
        return v

    def rows(self, i):
        return lane_block(self.across(i) * PART, PART)

    def greet(self):
        barrier = pltpu.get_barrier_semaphore()
        for step in range(1, 4):
            for c in range(2):
                pl.semaphore_signal(
                    barrier,
                    inc=1,
                    device_id=(self.base + c, lax.rem(self.z + step, 4)),
                    device_id_type=MESH,
                )
        for i in (1, 2, 4):
            pl.semaphore_signal(barrier, inc=1, device_id=(self.across(i), self.z), device_id_type=MESH)
        pl.semaphore_wait(barrier, 9)


def remote(src, dst, send, recv, device):
    return pltpu.make_async_remote_copy(
        src_ref=src, dst_ref=dst, send_sem=send, recv_sem=recv, device_id=device, device_id_type=MESH
    )


STEPS = {
    "ln1": (("a10", "a11", "a20", "a12", "a21", "u10", "u11", "a22", "a30", "d10", "d11", "a31", "u20", "u21", "a32", "d20", "d21"), ("a10", "a11", "a20", "a12", "a21", "u10", "a22", "a30", "d10", "a31", "u20", "d20", "a32", "u30")),
    "proj0": (("o10",), ("o10", "d30")),
    "proj1": ((), ("o11",)),
    "proj2": (("o11", "u30"), ("o20", "o12")),
    "proj3": (("o12",), ("o21",)),
    "att00": (("u31",), ("o22",)),
    "att01": (("u12",), ("o30", "o31", "u11")),
    "att10": (("d31",), ("o32",)),
    "att11": (("o21", "d30", "d12"), ("d11",)),
    "att20": (("o20", "o22"), ("u21", "u12")),
    "att30": (("o30", "d22", "o31", "u22"), ("d21", "d12")),
    "att31": (("o32",), ()),
    "ln2": ((), ("u31",)),
    "f0": (("d32", "u32"), ("d31",)),
    "b0": ((), ("u22", "d22")),
    "w1": ((), ("d32", "u32")),
}


class Unit:
    def __init__(self, place, own, at, parts, zsend, zrecv, send, recv, flip, slots):
        self.p, self.own, self.at, self.parts = place, own, at, parts
        self.zsend, self.zrecv, self.send, self.recv = zsend, zrecv, send, recv
        self.flip, self.slots = flip, slots

    def bits(self, n):
        return (4, 2) if (n % 2 == 1) == self.flip else (2, 4)

    def copy(self, k, slot_from, slot_to, device):
        return [
            remote(
                self.own(q) if slot_from is None else self.at(slot_from, 0, q),
                self.at(slot_to, 0, q),
                self.zsend.at[k, q],
                self.zrecv.at[slot_to - 1, q],
                device,
            )
            for q in range(self.parts)
        ]

    def direct(self, k):
        return self.copy(k - 1, None, k, (self.p.d, lax.rem(self.p.z + 4 - k, 4)))

    def along(self, k, slot_from, slot_to, right):
        return self.copy(k, slot_from, slot_to, (self.p.d, self.p.z + 1 if right else self.p.z - 1))

    def steps(self):
        z = self.p.z
        inner = self.p.inner
        return [
            (z <= 2, (0, None, 3, True)),
            (z >= 1, (1, None, 1, False)),
            (inner, (2, 3, 2, True)),
            (inner, (3, 1, 2, False)),
            (z == 1, (4, 2, 3, False)),
            (z == 2, (5, 2, 1, True)),
        ]

    def go(self, k):
        cond, what = self.steps()[k]

        @pl.when(cond)
        def _():
            for c in self.along(*what):
                c.start()

    def start(self):
        self.go(0)
        self.go(1)

    def start_direct(self):
        for k in (1, 3, 2):
            for c in self.direct(k):
                c.start()

    def landed(self, slot):
        for q in range(self.parts):
            here = self.at(slot, 0, q)
            remote(here, here, self.zsend.at[0, q], self.zrecv.at[slot - 1, q], (self.p.across(1), self.p.z)).wait_recv()

    def xy(self, n, k, i, bit):
        slot = self.slots[n]
        here = self.at(slot, i, None)
        return remote(
            here,
            here,
            self.send.at[slot - 1, k],
            self.recv.at[slot - 1, i ^ bit],
            (self.p.across(bit), self.p.z),
        )

    def arrived(self, n, i):
        slot = self.slots[n]
        here = self.at(slot, i, None)
        remote(here, here, self.send.at[slot - 1, 0], self.recv.at[slot - 1, i], (self.p.across(1), self.p.z)).wait_recv()

    def one(self, n):
        self.xy(n, 0, 0, self.bits(n)[0]).start()

    def take(self, n, inner=False, chained=False):
        self.landed(self.slots[n])
        if chained and inner and n < 2:
            for c in self.along(*self.steps()[3 - n][1]):
                c.start()
        if chained and inner and n == 2:
            self.go(4)
            self.go(5)
        self.one(n)

    def two(self, n):
        first, second = self.bits(n)
        self.arrived(n, first)
        self.xy(n, 1, 0, second).start()
        self.xy(n, 2, first, second).start()

    def three(self, n):
        first, second = self.bits(n)
        self.arrived(n, second)
        self.arrived(n, 6)
        for k, i in enumerate((0, 2, 4, 6)):
            self.xy(n, 3 + k, i, 1).start()

    def whole(self, n):
        for i in (1, 3, 5, 7):
            self.arrived(n, i)

    def finish(self, direct):
        if direct:
            for k in (1, 2, 3):
                for c in self.direct(k):
                    c.wait_send()
        else:
            for cond, what in self.steps():

                @pl.when(cond)
                def _(what=what):
                    for c in self.along(*what):
                        c.wait_send()

        for n in range(3):
            first, second = self.bits(n)
            self.xy(n, 0, 0, first).wait_send()
            self.xy(n, 1, 0, second).wait_send()
            self.xy(n, 2, first, second).wait_send()
            for k, i in enumerate((0, 2, 4, 6)):
                self.xy(n, 3 + k, i, 1).wait_send()


def bring_copies(p, src, dst, sends, recvs, here, which=(0, 1)):
    for s in which:
        target = (p.base + p.z // 2, 2 * p.core + s)
        half = lax.rem(p.z, 2)
        rows = lane_block(half * 256, 256)
        same = jnp.logical_and(p.core == p.z // 2, p.z == 2 * p.core + s)

        @pl.when(same)
        def _():
            pltpu.make_async_copy(src.at[s], dst.at[rows], here).start()

        @pl.when(jnp.logical_not(same))
        def _():
            remote(src.at[s], dst.at[rows], sends.at[s], recvs.at[half], target).start()


def bring_wait(p, dst, recvs, here):
    for half in range(2):
        block = dst.at[pl.ds(half * 256, 256)]
        same = jnp.logical_and(p.core == p.z // 2, lax.rem(p.z, 2) == half)

        @pl.when(same)
        def _():
            pltpu.make_async_copy(block, block, here).wait()

        @pl.when(jnp.logical_not(same))
        def _():
            remote(block, block, recvs.at[half], recvs.at[half], (p.across(1), p.z)).wait_recv()


def bring_sent(p, src, sends):
    for s in range(2):
        same = jnp.logical_and(p.core == p.z // 2, p.z == 2 * p.core + s)

        @pl.when(jnp.logical_not(same))
        def _():
            remote(src.at[s], src.at[s], sends.at[s], sends.at[s], (p.across(1), p.z)).wait_send()


def norm_stats(x):
    center = x - jnp.mean(x, -1, keepdims=True)
    inverse = lax.rsqrt(jnp.mean(center * center, -1, keepdims=True) + EPS)
    return center * inverse, inverse


def each_rows(size, total, f):
    def step(i, carry):
        f(pl.ds(pl.multiple_of(i * size, size), size))
        return carry

    lax.fori_loop(0, total // size, step, 0)


def chosen_both(p, t_ref, both_ref, sends, recvs):
    copies = []
    for k, i in enumerate((0, 2, 4, 6)):
        block = pl.ds(k * PART, PART)
        both_ref[block, 0:T] = t_ref[p.rows(i), :]
        copies.append(
            remote(
                t_ref.at[p.rows(i ^ 1)],
                both_ref.at[block, T : 2 * T],
                sends.at[k],
                recvs.at[k],
                (p.across(1), p.z),
            )
        )
    for c in copies:
        c.start()
    return copies


def forward_kernel(
    cells, grad, len_own, wq, wk, wv, wo, up, down, small_own, b_out, gain1, shift1, gain2, shift2, b_down,
    x_out, rows1_out, q_out, k_out, v_out, mix_out, e_out, r_out, wa_out, wo_out, wu, wd, out_land, dm_out, gu_out, gd_out, keep_out, la_out, lc_out, vec_out, bup_out,
    xv, gv, rows1, wav, wov, qv, kv, vv, mix, eb, rv, bias, vt, ot, middle, rows2, tt, xb, gb, acc, e2,
    uv, dv, ho, du, hs, ds, slope_v, gs, land_b, len_sib, small,
    a_zs, a_zr, a_s, a_r, o_zs, o_zr, o_s, o_r, u_zs, u_zr, u_s, u_r, d_zs, d_zr, d_s, d_r,
    act_s, act_r, sm_s, sm_r, kv_s, kv_r, both_s, both_r, hd_s, hd_r, ch_s, ch_r, credit, loc, load, store,
):
    p = Place()
    sibling = (p.across(1), p.z)

    ws = (wq, wk, wv)
    own_rows = p.rows(0)

    def a_at(slot, i, part):
        if part is None:
            return wav.at[slot, p.rows(i)]
        return wav.at[slot, p.rows(i), pl.ds(part * 256, 256)]

    fixed = (1, 3, 2)
    inner = p.inner
    by_arrival = (
        jnp.where(p.z <= 2, 1, 3),
        jnp.where(inner, 3, 2),
        jnp.where(inner, 2, jnp.where(p.z == 0, 3, 1)),
    )
    unit_a = Unit(p, lambda q: ws[q].at[own_rows], a_at, 3, a_zs, a_zr, a_s, a_r, True, fixed)
    unit_o = Unit(
        p,
        lambda q: wo.at[:, own_rows],
        lambda slot, i, q: wov.at[pl.ds(slot * 256, 256), p.rows(i)],
        1, o_zs, o_zr, o_s, o_r, False, fixed,
    )
    unit_u = Unit(
        p, lambda q: up.at[own_rows], lambda slot, i, q: wu.at[slot - 1, p.rows(i)], 1, u_zs, u_zr, u_s, u_r, False, by_arrival
    )
    unit_d = Unit(
        p, lambda q: down.at[own_rows], lambda slot, i, q: wd.at[slot - 1, p.rows(i)], 1, d_zs, d_zr, d_s, d_r, True, by_arrival
    )

    own_loads = [pltpu.make_async_copy(w, wav.at[0, :, pl.ds(k * 256, 256)], loc.at[k]) for k, w in enumerate(ws)]
    own_loads.append(pltpu.make_async_copy(wo, wov.at[pl.ds(0, 256)], loc.at[3]))
    for c in own_loads:
        c.start()
    first_loads = [pltpu.make_async_copy(up, uv.at[0], load.at[0, 0]), pltpu.make_async_copy(down, dv.at[0], load.at[1, 0])]
    for c in first_loads:
        c.start()

    p.greet()
    unit_a.start_direct()
    unit_u.start()
    unit_d.start()
    bring_copies(p, cells, xv, act_s.at[0], act_r.at[0], loc.at[4])
    unit_o.start_direct()
    small_copies = []
    for r in (1, 2, 3):
        small_copies.append(remote(small_own, small.at[r], sm_s.at[r], sm_r.at[r], (p.d, lax.rem(p.z + 4 - r, 4))))
    small_copies.append(remote(len_own, len_sib, sm_s.at[0], sm_r.at[0], sibling))
    for c in small_copies:
        c.start()
    small[0] = small_own[...]

    units = {"a": (unit_a, False), "o": (unit_o, False), "u": (unit_u, True), "d": (unit_d, True)}

    def advance(point):
        for inner, names in zip((True, False), STEPS.get(point, ((), ()))):
            if names:

                @pl.when(p.inner if inner else p.outer)
                def _(inner=inner, names=names):
                    for name in names:
                        (unit, chained), n = units[name[0]], int(name[2])
                        if name[1] == "1":
                            unit.take(n, inner, chained)
                        elif name[1] == "2":
                            unit.two(n)
                        else:
                            unit.three(n)

    small_copies[3].wait_recv()
    slot_row = lax.rem(p.z, 2)
    near = jnp.where(p.z // 2 == p.core, 1.0, 0.0)
    length = near * len_own[pl.ds(slot_row, 1), :] + (1.0 - near) * len_sib[pl.ds(slot_row, 1), :]
    length = length[:, :1]
    lane = lax.broadcasted_iota(jnp.int32, (1, 128), 1)
    key = lax.broadcasted_iota(jnp.int32, (2 * T, 128), 0)
    key = jnp.where(key < T, key + p.core * T, key - T + (1 - p.core) * T)
    barred = jnp.where(key.astype(F32) < length, 0.0, -1e30)
    bias[0] = jnp.where(lane == 64, barred, 0.0).astype(BF)
    bias[1] = jnp.where(lane == 0, barred, 0.0).astype(BF)

    def kept(rows_start, size):
        row = lax.broadcasted_iota(jnp.int32, (size, 1), 0) + rows_start + p.core * T
        return row.astype(F32) < length

    advance("ln1")

    bring_wait(p, xv, act_r.at[0], loc.at[4])

    def first_norm(rows):
        unit, _ = norm_stats(xv[rows, :].astype(F32))
        rows1[rows, :] = (unit * gain1[...] + shift1[...]).astype(BF)

    each_rows(128, T, first_norm)
    outs = [pltpu.make_async_copy(xv, x_out, store.at[0]), pltpu.make_async_copy(rows1, rows1_out, store.at[1])]
    for c in outs:
        c.start()
    for c in own_loads:
        c.wait()
    for r in (1, 2, 3):
        small_copies[r - 1].wait_recv()

    kv_copies = []

    def project(r):
        b = small.at[r]
        x = rows1[...]
        qv[r] = (dg(x, wav[r, :, 0:256], 1, 0) + b[:, 0:256]).astype(BF)
        kv[r, 0:T, :] = dg(x, wav[r, :, 256:512], 1, 0).astype(BF)
        vv[r, 0:T, :] = (dg(x, wav[r, :, 512:768], 1, 0) + b[:, 256:512]).astype(BF)
        cs = [
            remote(ref.at[r, pl.ds(0, T)], ref.at[r, pl.ds(T, T)], kv_s.at[r, n], kv_r.at[r, n], sibling)
            for n, ref in enumerate((kv, vv))
        ]
        for c in cs:
            c.start()
        kv_copies.append(cs)

    def e_copy(head, slot):
        return pltpu.make_async_copy(eb.at[slot], e_out.at[head], store.at[2 + slot])

    def attend_pair(r, j):
        cols = pl.ds(j * 128, 128)
        kp = kv[r, :, cols]
        qp = qv[r, :, cols] * BF(HD**-0.5)
        for h in range(2):
            mine = (lane < 64) if h == 0 else (lane >= 64)
            one = lane == (64 if h == 0 else 0)
            ka = jnp.where(mine, kp, bias[h])
            qa = jnp.where(mine, qp, jnp.where(one, BF(1), BF(0)))
            s = dg(ka, qa, 1, 1)
            e = jnp.exp(s - jnp.max(s, 0, keepdims=True))
            inv = 1.0 / jnp.sum(e, 0, keepdims=True)
            head = r * 4 + 2 * j + h
            if head >= 2:
                e_copy(head - 2, h).wait()
            eb[h] = e.astype(BF)
            e_copy(head, h).start()
            feats = pl.ds(j * 128 + h * 64, 64)
            ot[feats, :] = (dg(vt[feats, :], eb[h], 1, 0) * inv).astype(BF)
            rv[head] = inv

    def attend(r):
        advance(f"att{r}0")
        if r == 2:
            bring_copies(p, grad, gv, act_s.at[1], act_r.at[1], loc.at[5])
        for c in kv_copies[r]:
            c.wait_recv()
        vt[...] = jnp.transpose(vv[r], (1, 0))
        attend_pair(r, 0)
        advance(f"att{r}1")
        attend_pair(r, 1)
        mix[:, r * 256 : (r + 1) * 256] = jnp.transpose(ot[...], (1, 0))

    advance("proj0")
    project(0)
    for n in range(3):
        unit_a.whole(n)
    for r in (1, 2, 3):
        advance(f"proj{r}")
        project(r)
    for r in range(4):
        attend(r)
    advance("oproj")
    for n in range(3):
        unit_o.whole(n)
    for h in range(2):
        e_copy(14 + h, h).wait()

    outs += [
        pltpu.make_async_copy(wav, wa_out, store.at[4]),
        pltpu.make_async_copy(wov, wo_out, store.at[5]),
        pltpu.make_async_copy(qv, q_out, store.at[6]),
        pltpu.make_async_copy(kv, k_out, store.at[7]),
        pltpu.make_async_copy(vv, v_out, store.at[8]),
        pltpu.make_async_copy(mix, mix_out, store.at[9]),
        pltpu.make_async_copy(rv, r_out, store.at[10]),
    ]
    for c in outs[2:]:
        c.start()

    for n in range(2):
        cols = pl.ds(n * 512, 512)
        middle[:, cols] = dg(mix[...], wov[:, cols], 1, 0)

    advance("ln2")

    def second_norm(rows):
        m = middle[rows, :] + xv[rows, :].astype(F32) + b_out[...]
        middle[rows, :] = m
        unit, _ = norm_stats(m)
        rows2[rows, :] = (unit * gain2[...] + shift2[...]).astype(BF)
        acc[rows, :] = m + b_down[...]

    each_rows(128, T, second_norm)
    tt[...] = jnp.transpose(rows2[...], (1, 0))
    both = chosen_both(p, tt, xb, both_s.at[0], both_r.at[0])

    def mask_grad(i, carry):
        rows = pl.ds(pl.multiple_of(i * 128, 128), 128)
        gv[rows, :] = jnp.where(kept(i * 128, 128), gv[rows, :].astype(F32), 0.0).astype(BF)
        return carry

    order = (0,) + by_arrival

    def load_copies(n):
        r = order[n]
        return [
            pltpu.make_async_copy(wu.at[r - 1], uv.at[n % 2], load.at[0, n % 2]),
            pltpu.make_async_copy(wd.at[r - 1], dv.at[n % 2], load.at[1, n % 2]),
        ]

    def hidden(n):
        r, slot = order[n], n % 2
        for k in range(2):
            c = pl.ds(k * 512, 512)
            upper = dg(rows2[...], uv[slot, :, c], 1, 0) + small[r, :, pl.ds(512 + k * 512, 512)]
            act, slope = gelu_pair(upper)
            ho[slot, :, c] = act.astype(BF)
            slope_v[:, c] = slope
        if n >= 2:
            pl.semaphore_wait(credit, 1)
        copy = remote(ho.at[slot], hs.at[slot], hd_s.at[0, slot], hd_r.at[0, slot], sibling)
        copy.start()
        for k in range(2):
            c = pl.ds(k * 512, 512)
            acc[:, c] = acc[:, c] + dg(ho[slot], dv[slot, :, c], 1, 0)
        return copy

    def hidden_back(n):
        r, slot = order[n], n % 2
        for k in range(2):
            c = pl.ds(k * 512, 512)
            d_up = (dg(gv[...], dv[slot, c, :], 1, 1) * slope_v[:, c]).astype(BF)
            du[slot, :, c] = d_up
            bup_out[r, :, c] = jnp.sum(d_up.astype(F32), 0, keepdims=True)
        copy = remote(du.at[slot], ds.at[slot], hd_s.at[1, slot], hd_r.at[1, slot], sibling)
        copy.start()
        for k in range(2):
            c = pl.ds(k * 512, 512)
            new = dg(du[slot], uv[slot, c, :], 1, 1)
            e2[:, c] = new if n == 0 else e2[:, c] + new
        return copy

    g_stores = []

    def chain(n, u):
        j = 2 * n + u
        first, second = (4, 2) if u else (2, 4)
        block = lambda i: gs.at[n, u, pl.ds(i // 2 * PART, PART)]
        near, far = (p.across(first), p.z), (p.across(second), p.z)
        return (
            remote(block(first), la_out.at[j], ch_s.at[j, 0], ch_r.at[j, 0], near),
            remote(block(first + second), land_b.at[j], ch_s.at[j, 1], ch_r.at[j, 1], near),
            remote(block(second), lc_out.at[j], ch_s.at[j, 2], ch_r.at[j, 2], far),
        )

    chains = {(n, u): chain(n, u) for n in range(2) for u in range(2)}

    def weight_grads(n, cs):
        slot, at = n % 2, min(n, 2)
        for c in cs:
            c.wait_recv()
        if n == 3:
            for c in g_stores[-2:]:
                c.wait()
        gs[at, 0] = (dg(xb[:, 0:T], du[slot], 1, 0) + dg(xb[:, T : 2 * T], ds[slot], 1, 0)).astype(BF)
        gs[at, 1] = (dg(gb[:, 0:T], ho[slot], 1, 0) + dg(gb[:, T : 2 * T], hs[slot], 1, 0)).astype(BF)
        if n < 2:
            pl.semaphore_signal(credit, inc=1, device_id=sibling, device_id_type=MESH)
        for u, out in enumerate((gu_out, gd_out)):
            if n < 2:
                for c in chains[n, u][:2]:
                    c.start()
                c = pltpu.make_async_copy(gs.at[n, u, pl.ds(0, PART)], keep_out.at[2 * n + u], store.at[11 + 2 * n + u])
            else:
                c = pltpu.make_async_copy(gs.at[2, u], out.at[n - 2], store.at[11 + 2 * n + u])
            c.start()
            g_stores.append(c)
        for c in cs:
            c.wait_send()

    def second_exchange(n):
        for u in range(2):
            one, other, two = chains[n, u]
            other.wait_recv()
            rows = pl.ds((2 if u else 4) // 2 * PART, PART)
            gs[n, u, rows, :] = (gs[n, u, rows, :].astype(F32) + land_b[2 * n + u].astype(F32)).astype(BF)
            two.start()

    for c in first_loads:
        c.wait()
    advance("f0")
    held = [[hidden(0)]]
    for c in both:
        c.wait_send()
    advance("b0")
    bring_wait(p, gv, act_r.at[1], loc.at[5])
    lax.fori_loop(0, T // 128, mask_grad, 0)
    tt[...] = jnp.transpose(gv[...], (1, 0))
    both2 = chosen_both(p, tt, gb, both_s.at[1], both_r.at[1])
    held[0].append(hidden_back(0))
    for n in range(1, 4):
        advance(f"w{n - 1}")
        if n < 3:
            unit_u.whole(n - 1)
            unit_d.whole(n - 1)
            loads = load_copies(n)
            for c in loads:
                c.start()
            if n == 1:
                for c in both + both2:
                    c.wait_recv()
            weight_grads(n - 1, held[n - 1])
        else:
            second_exchange(0)
            unit_u.whole(2)
            unit_d.whole(2)
            loads = load_copies(3)
            for c in loads:
                c.start()
        advance(f"f{n}")
        for c in loads:
            c.wait()
        held.append([hidden(n)])
        advance(f"b{n}")
        if n == 3:

            def result(i, carry):
                rows = pl.ds(pl.multiple_of(i * 128, 128), 128)
                rows2[rows, :] = jnp.where(kept(i * 128, 128), acc[rows, :], 0.0).astype(BF)
                return carry

            lax.fori_loop(0, T // 128, result, 0)
            return_copies(p, rows2, out_land, act_s.at[2], act_r.at[2], loc.at[6])
            second_exchange(1)
        held[n].append(hidden_back(n))
    weight_grads(2, held[2])
    weight_grads(3, held[3])

    vec_out[...] = jnp.zeros(vec_out.shape, F32)

    def last(i, carry):
        rows = pl.ds(pl.multiple_of(i * 128, 128), 128)
        unit, inverse = norm_stats(middle[rows, :])
        e = e2[rows, :]
        g = gv[rows, :].astype(F32)
        u = e * gain2[...]
        d_mid = g + inverse * (u - jnp.mean(u, -1, keepdims=True) - unit * jnp.mean(u * unit, -1, keepdims=True))
        middle[rows, :] = d_mid
        for k, v in enumerate((d_mid, e * unit, e, g)):
            vec_out[4 + k : 5 + k, :] += jnp.sum(v, 0, keepdims=True)
        return carry

    lax.fori_loop(0, T // 128, last, 0)
    ends = [pltpu.make_async_copy(middle, dm_out, store.at[19])]
    for c in ends:
        c.start()
    for c in ends + outs + g_stores[:4] + g_stores[6:]:
        c.wait()
    for cs in chains.values():
        cs[0].wait_recv()
        cs[2].wait_recv()
        for c in cs:
            c.wait_send()
    return_wait(p, out_land, act_r.at[2], loc.at[6])
    return_sent(p, rows2, act_s.at[2])
    for c in both2 + small_copies:
        c.wait_send()
    for cs in kv_copies:
        for c in cs:
            c.wait_send()
    for unit in (unit_a, unit_o, unit_u, unit_d):
        unit.finish(unit is unit_a or unit is unit_o)
    bring_sent(p, cells, act_s.at[0])
    bring_sent(p, grad, act_s.at[1])


def return_copies(p, src, dst, sends, recvs, here):
    slot = lax.rem(p.z, 2)
    for h in range(2):
        rows = src.at[pl.ds(h * 256, 256)]
        same = jnp.logical_and(p.core == p.z // 2, p.z == 2 * p.core + h)

        @pl.when(same)
        def _():
            pltpu.make_async_copy(rows, dst.at[slot], here).start()

        @pl.when(jnp.logical_not(same))
        def _():
            remote(rows, dst.at[slot], sends.at[h], recvs.at[slot], (p.base + p.z // 2, 2 * p.core + h)).start()


def return_wait(p, dst, recvs, here):
    for s in range(2):
        same = jnp.logical_and(p.core == p.z // 2, p.z == 2 * p.core + s)

        @pl.when(same)
        def _():
            pltpu.make_async_copy(dst.at[s], dst.at[s], here).wait()

        @pl.when(jnp.logical_not(same))
        def _():
            remote(dst.at[s], dst.at[s], recvs.at[s], recvs.at[s], (p.across(1), p.z)).wait_recv()


def return_sent(p, src, sends):
    for h in range(2):
        rows = src.at[pl.ds(h * 256, 256)]
        same = jnp.logical_and(p.core == p.z // 2, p.z == 2 * p.core + h)

        @pl.when(jnp.logical_not(same))
        def _():
            remote(rows, rows, sends.at[h], sends.at[h], (p.across(1), p.z)).wait_send()


class Chain:
    def __init__(self, p, r, block, keep0, keep1, land1, land2, land3, send, recv, zsend, zrecv, flip):
        first, second = (4, 2) if flip else (2, 4)
        self.r, self.keep0, self.keep1, self.land1, self.land2 = r, keep0, keep1, land1, land2
        near = (p.across(first), p.z)
        self.one = [remote(block(first + k * second), land1.at[k], send.at[k], recv.at[k], near) for k in range(2)]
        self.two = remote(keep1, land2, send.at[2], recv.at[2], (p.across(second), p.z))
        self.three = None
        if not (isinstance(r, int) and r == 0):
            k = jnp.where(r == 2, 2, jnp.where(r == p.slot_next, 0, 1))
            device = (p.d, jnp.where(r == 2, p.z_over, p.z_next))
            self.three = remote(keep0, land3.at[k], zsend.at[k], zrecv.at[k], device)

    def start(self):
        for c in self.one:
            c.start()

    def middle(self):
        for c in self.one:
            c.wait_recv()
        self.keep1[...] = (self.keep1[...].astype(F32) + self.land1[1].astype(F32)).astype(BF)
        self.two.start()

    def total(self):
        return self.keep0[...].astype(F32) + self.land1[0].astype(F32) + self.land2[...].astype(F32)

    def end(self, summed=False):
        if not summed:
            self.two.wait_recv()
        if self.three is not None:
            self.keep0[...] = self.total().astype(BF)

            @pl.when(self.r != 2)
            def _():
                self.three.start()

    def over(self, land):
        @pl.when(self.r == 2)
        def _():
            self.keep0[...] = (self.keep0[...].astype(F32) + land[...].astype(F32)).astype(BF)
            self.three.start()

    def sent(self, summed=False):
        for c in ([] if summed else self.one + [self.two]) + ([] if self.three is None else [self.three]):
            c.wait_send()


class Vectors:
    def __init__(self, p, acc, land, zland, send, recv, zsend, zrecv):
        self.acc, self.land, self.zland = acc, land, zland
        self.steps = [
            remote(acc, land.at[b], send.at[b], recv.at[b], (p.across(1 << b), p.z)) for b in range(3)
        ]
        self.along = [
            remote(acc, zland.at[r - 1], zsend.at[r - 1], zrecv.at[r - 1], (p.d, lax.rem(p.z + r, 4)))
            for r in (1, 2, 3)
        ]

    def start(self, b):
        self.steps[b].start()

    def take(self, b):
        self.steps[b].wait()
        self.acc[...] = self.acc[...] + self.land[b]

    def z_start(self):
        for c in self.along:
            c.start()

    def z_wait(self):
        for c in self.along:
            c.wait()


def backward_kernel(
    x_in, rows1_in, q_in, k_in, v_in, mix_in, e_in, r_in, wa_in, wo_in, dm_in, gu_in, gd_in, keep_in, la_in, lc_in, vec_in, bup_in, gain1,
    gcl, attn_out, gup_out, gdown_out, early_out, late_out,
    land1, land2, land3, land1a, land2a, land3a, udk, ga, wav, wov, qv, kv, vv, mix, mixs, dm, e1, gmb, r1b, tt, gm, xv, rows1, eb, rv, xs, xr, da,
    kt, mixt, dmt_all, dqt, early, late, eland, lland, ezland, lzland,
    ch_s, ch_r, z_s, z_r, gc_s, gc_r, both_s, both_r, x_s, x_r, mix_s, mix_r, ev_s, ev_r, ez_s, ez_r,
    lv_s, lv_r, lz_s, lz_r, credit, here, load, eload,
):
    p = Place()
    sibling = (p.across(1), p.z)
    order = (1, 3, 2, 0)

    loads = {}
    for n, (name, src, dst) in enumerate(
        (
            ("dm", dm_in, dm), ("wo", wo_in, wov), ("rows1", rows1_in, rows1), ("mix", mix_in, mix), ("r", r_in, rv),
            ("q", q_in, qv), ("k", k_in, kv), ("v", v_in, vv), ("x", x_in, xv),
        )
    ):
        loads[name] = pltpu.make_async_copy(src, dst, load.at[n])
        loads[name].start()

    def wa_load(n):
        return pltpu.make_async_copy(wa_in.at[order[n]], wav.at[n % 2], load.at[9 + n % 2])

    def e_load(head, slot):
        return pltpu.make_async_copy(e_in.at[head], eb.at[slot], eload.at[slot])

    for h in range(2):
        e_load(order[0] * 4 + h, h).start()
    wa_load(0).start()

    p.greet()
    mix_copy = remote(mix_in, mixs, mix_s, mix_r, sibling)
    mix_copy.start()

    chains = {}
    keep_loads = []
    shards = (
        0,
        jnp.where(p.z <= 2, 1, 3),
        jnp.where(p.inner, 3, 2),
        jnp.where(p.inner, 2, jnp.where(p.z == 0, 3, 1)),
    )
    for n in (1, 0, 2, 3):
        r = shards[n]
        for u, src in enumerate((gu_in, gd_in)):
            flip = u == 1
            second = 2 if flip else 4
            j = u * 4 + n
            if n < 2:
                parts = ((keep_in, udk.at[j, 0]), (la_in, land1.at[j, 0]), (lc_in, land2.at[j]))
                for k, (held, to) in enumerate(parts):
                    c = pltpu.make_async_copy(held.at[2 * n + u], to, load.at[19 + 3 * (2 * n + u) + k])
                    c.start()
                    keep_loads.append(c)
                blocks = lambda i, j=j: udk.at[j, 0]
            else:
                blocks = lambda i, src=src, n=n: src.at[n - 2, pl.ds(i // 2 * PART, PART)]
                for k, i in enumerate((0, second)):
                    pltpu.make_async_copy(blocks(i), udk.at[j, k], load.at[11 + j]).start()
                keep_loads.append(pltpu.make_async_copy(udk.at[j], udk.at[j], load.at[11 + j]))
            chains[u, n] = Chain(
                p, r, blocks, udk.at[j, 0], udk.at[j, 1], land1.at[j], land2.at[j], land3.at[u],
                ch_s.at[j], ch_r.at[j], z_s.at[u], z_r.at[u], flip,
            )
    for n, r in enumerate(order):
        for half in range(2):
            second = 2 if half else 4
            blocks = lambda i, r=r, half=half: ga.at[r, half, pl.ds(i // 2 * PART, PART)]
            chains[2 + half, n] = Chain(
                p, r, blocks, blocks(0), blocks(second), land1a.at[r, half], land2a.at[r, half], land3a.at[half],
                ch_s.at[8 + 2 * r + half], ch_r.at[8 + 2 * r + half], z_s.at[2 + half], z_r.at[2 + half],
                half == 1,
            )

    def start(kind, n):
        for u in (0, 1) if kind == "f" else (2, 3):
            chains[u, n].start()

    def middle(kind, n):
        for u in (0, 1) if kind == "f" else (2, 3):
            chains[u, n].middle()

    def end(kind, n):
        for u in (0, 1) if kind == "f" else (2, 3):
            chains[u, n].end()

    def z_got(u, k, land):
        remote(land.at[k], land.at[k], z_s.at[u, k], z_r.at[u, k], sibling).wait_recv()

    def over(kind, ns):
        for u in (0, 1) if kind == "f" else (2, 3):
            land = land3.at[u] if kind == "f" else land3a.at[u - 2]
            z_got(u, 1, land)
            for n in ns:
                chains[u, n].over(land.at[1])

    start("f", 2)
    start("f", 3)

    early[...] = vec_in[0:8, :]
    for r in range(4):
        early[r : r + 1, :] = bup_in[r]
    ev = Vectors(p, early, eland, ezland, ev_s, ev_r, ez_s, ez_r)
    ev.start(0)
    late[...] = jnp.zeros((8, 1024), F32)

    loads["rows1"].wait()
    tt[...] = jnp.transpose(rows1[...], (1, 0))
    both = chosen_both(p, tt, r1b, both_s.at[0], both_r.at[0])
    loads["dm"].wait()

    def cast(rows):
        gm[rows, :] = dm[rows, :].astype(BF)

    each_rows(128, T, cast)
    for name in ("wo", "mix", "r", "q", "k", "v"):
        loads[name].wait()
    lane = lax.broadcasted_iota(jnp.int32, (1, 128), 1)

    def attend_back(n):
        r, slot = order[n], n % 2
        cols_r = pl.ds(r * 256, 256)
        kt[...] = jnp.transpose(kv[r], (1, 0))
        mixt[...] = jnp.transpose(mix[:, cols_r], (1, 0))
        dmt_all[...] = dg(wov[cols_r, :], gm[...], 1, 1).astype(BF)
        if n >= 2:
            for c in [x_copies[n - 2]]:
                c.wait_send()

        def pair(j, carry):
            cols = lane_block(j * 128)
            kp = kv[r, :, cols]
            vp = vv[r, :, cols]
            qp = qv[r, :, cols] * BF(HD**-0.5)
            dk = jnp.zeros((2 * T, 128), F32)
            d_v = jnp.zeros((2 * T, 128), F32)
            for h in range(2):
                head = r * 4 + 2 * j + h
                feats = pl.ds(pl.multiple_of(j * 128 + h * 64, 64), 64)
                mine = (lane < 64) if h == 0 else (lane >= 64)
                dmt = (dmt_all[feats, :].astype(F32) * rv[head]).astype(BF)
                delta = jnp.sum(dmt.astype(F32) * mixt[feats, :].astype(F32), 0, keepdims=True)
                zero = jnp.zeros((64, T), BF)
                dmt2 = jnp.concatenate([dmt, zero] if h == 0 else [zero, dmt], 0)
                dma = jnp.transpose(dmt2, (1, 0))
                dp = dg(vp, dmt2, 1, 0)
                e_load(head, h).wait()
                ds = (eb[h].astype(F32) * (dp - delta)).astype(BF)
                qa = jnp.where(mine, qp, BF(0))
                d_v = d_v + dg(eb[h], dma, 1, 0)
                if n < 3:
                    nxt = jnp.where(j == 0, head + 2, order[n + 1] * 4 + h)
                    e_load(nxt, h).start()
                else:
                    @pl.when(j == 0)
                    def _():
                        e_load(head + 2, h).start()
                dk = dk + dg(ds, qa, 1, 0)
                dqt[feats, :] = (dg(kt[feats, :], ds, 1, 0) * HD**-0.5).astype(BF)
            xs[slot, T : 3 * T, cols] = dk.astype(BF)
            xs[slot, 3 * T : 5 * T, cols] = d_v.astype(BF)
            return carry

        lax.fori_loop(0, 2, pair, 0)
        xs[slot, 0:T, :] = jnp.transpose(dqt[...], (1, 0))
        if n >= 2:
            pl.semaphore_wait(credit, 1)
        c = remote(xs.at[slot], xr.at[slot], x_s.at[slot], x_r.at[slot], sibling)
        c.start()
        return c

    x_copies = []

    def gather_up(n):
        r, slot = order[n], n % 2
        x_copies[n].wait_recv()
        da[0:T, 0:256] = xs[slot, 0:T, :]
        da[T : 2 * T, 0:256] = xr[slot, 0:T, :]
        for k in range(2):
            base = T + 2 * T * k
            cols = pl.ds(256 * (k + 1), 256)
            da[0:T, cols] = (
                xs[slot, base : base + T, :].astype(F32) + xr[slot, base + T : base + 2 * T, :].astype(F32)
            ).astype(BF)
            da[T : 2 * T, cols] = (
                xs[slot, base + T : base + 2 * T, :].astype(F32) + xr[slot, base : base + T, :].astype(F32)
            ).astype(BF)
        if n < 2:
            pl.semaphore_signal(credit, inc=1, device_id=sibling, device_id_type=MESH)
        ga[r, 0] = dg(r1b[...], da[:, 0:512], 1, 0).astype(BF)
        ga[r, 1, :, 0:256] = dg(r1b[...], da[:, 512:768], 1, 0).astype(BF)
        cols_r = pl.ds(r * 256, 256)
        ga[r, 1, :, 256:512] = (dg(gmb[:, 0:T], mix[:, cols_r], 1, 0) + dg(gmb[:, T : 2 * T], mixs[:, cols_r], 1, 0)).astype(BF)
        wa_load(n).wait()
        if n + 1 < 4:
            wa_load(n + 1).start()
        new = dg(da[0:T, :], wav[slot], 1, 1)
        e1[...] = new if n == 0 else e1[...] + new
        late[2:3, r * 256 : (r + 1) * 256] = jnp.sum(da[0:T, 0:256].astype(F32), 0, keepdims=True)
        late[3:4, r * 256 : (r + 1) * 256] = jnp.sum(da[0:T, 512:768].astype(F32), 0, keepdims=True)

    for c in keep_loads:
        c.wait()
    for u in range(2):
        chains[u, 1].end(True)
    x_copies.append(attend_back(0))
    for c in both:
        c.wait_send()
    tt[...] = jnp.transpose(gm[...], (1, 0))
    both2 = chosen_both(p, tt, gmb, both_s.at[1], both_r.at[1])
    middle("f", 2)
    ev.take(0)
    ev.start(1)
    x_copies.append(attend_back(1))
    for c in both + both2:
        c.wait_recv()
    mix_copy.wait_recv()
    gather_up(0)
    middle("f", 3)
    start("a", 0)
    x_copies.append(attend_back(2))
    end("f", 2)
    ev.take(1)
    ev.start(2)
    gather_up(1)
    start("a", 1)
    end("f", 3)
    x_copies.append(attend_back(3))
    middle("a", 0)
    gather_up(2)
    start("a", 2)
    over("f", (2, 3))
    middle("a", 1)
    gather_up(3)
    start("a", 3)
    end("a", 0)
    ev.take(2)
    ev.z_start()

    loads["x"].wait()

    def first_back(i, carry):
        rows = pl.ds(pl.multiple_of(i * 128, 128), 128)
        unit, inverse = norm_stats(xv[rows, :].astype(F32))
        e = e1[rows, :]
        u = e * gain1[...]
        d = dm[rows, :] + inverse * (u - jnp.mean(u, -1, keepdims=True) - unit * jnp.mean(u * unit, -1, keepdims=True))
        gm[rows, :] = d.astype(BF)
        for k, v in enumerate((e * unit, e)):
            late[k : k + 1, :] += jnp.sum(v, 0, keepdims=True)
        return carry

    lax.fori_loop(0, T // 128, first_back, 0)
    return_copies(p, gm, gcl, gc_s, gc_r, here.at[1])
    lv = Vectors(p, late, lland, lzland, lv_s, lv_r, lz_s, lz_r)
    lv.start(0)
    end("a", 1)
    middle("a", 2)
    lv.take(0)
    lv.start(1)
    end("a", 2)
    over("a", (2,))
    middle("a", 3)
    lv.take(1)
    lv.start(2)

    def final(u, n, land):
        z_got(u, 0, land)
        z_got(u, 2, land)
        return chains[u, n].total() + land[0].astype(F32) + land[2].astype(F32)

    gup_out[...] = final(0, 0, land3.at[0])
    gdown_out[...] = final(1, 0, land3.at[1])
    lv.take(2)
    lv.z_start()
    ev.z_wait()
    shard = early[0:1, :]
    for r in (1, 2, 3):
        shard = shard + ezland[r - 1, r : r + 1, :]
    early_out[...] = early[...] + ezland[0] + ezland[1] + ezland[2]
    early_out[0:1, :] = shard
    end("a", 3)

    lv.z_wait()
    late_out[...] = late[...] + lzland[0] + lzland[1] + lzland[2]
    for k in (2, 3):
        shard = late[k : k + 1, 0:256]
        for r in (1, 2, 3):
            shard = shard + lzland[r - 1, k : k + 1, r * 256 : (r + 1) * 256]
        late_out[k : k + 1, 0:256] = shard
    total = final(2, 3, land3a.at[0])
    attn_out[:, 0:512] = total
    attn_out[:, 512:1024] = final(3, 3, land3a.at[1])
    return_wait(p, gcl, gc_r, here.at[1])

    for c in both2 + [mix_copy, x_copies[2], x_copies[3]]:
        c.wait_send()
    for (u, n), c in chains.items():
        c.sent(u < 2 and n < 2)
    return_sent(p, gm, gc_s)


def backward(*args):
    s = jax.ShapeDtypeStruct
    hbm, fast = pl.BlockSpec(memory_space=pltpu.HBM), pl.BlockSpec(memory_space=pltpu.VMEM)
    b, f, dma = (lambda *x: pltpu.VMEM(x, BF)), (lambda *x: pltpu.VMEM(x, F32)), (lambda *x: pltpu.SemaphoreType.DMA(x))
    return pl.pallas_call(
        backward_kernel,
        out_shape=[
            s((2, 256, 1024), BF), s((PART, 1024), F32), s((PART, 1024), F32), s((PART, 1024), F32),
            s((8, 1024), F32), s((8, 1024), F32),
        ],
        in_specs=[hbm] * 16 + [fast] * 3,
        out_specs=[hbm] + [fast] * 5,
        scratch_shapes=[
            b(8, 2, PART, 1024), b(8, PART, 1024), b(2, 3, PART, 1024), b(4, 2, 2, PART, 512), b(4, 2, PART, 512), b(2, 3, PART, 512),
            b(8, 2, PART, 1024), b(4, 2, 4 * PART, 512), b(2, 1024, 768),
            b(1024, 1024), b(4, T, 256), b(4, 2 * T, 256), b(4, 2 * T, 256), b(T, 1024), b(T, 1024), f(T, 1024), f(T, 1024),
            b(T, 2 * T), b(T, 2 * T), b(1024, T), b(T, 1024), b(T, 1024), b(T, 1024), b(2, 2 * T, T), f(16, 1, T),
            b(2, 5 * T, 256), b(2, 5 * T, 256), b(2 * T, 768),
            b(256, 2 * T), b(256, T), b(256, T), b(256, T), f(8, 1024), f(8, 1024), f(3, 8, 1024), f(3, 8, 1024), f(3, 8, 1024), f(3, 8, 1024),
            dma(16, 3), dma(16, 3), dma(4, 3), dma(4, 3), dma(2), dma(2), dma(2, 4), dma(2, 4), dma(2), dma(2),
            pltpu.SemaphoreType.DMA, pltpu.SemaphoreType.DMA, dma(3), dma(3), dma(3), dma(3), dma(3), dma(3), dma(3), dma(3),
            pltpu.SemaphoreType.REGULAR, dma(2), dma(31), dma(2),
        ],
        compiler_params=pltpu.CompilerParams(collective_id=1, has_side_effects=True, vmem_limit_bytes=63 * 2**20),
    )(*args)


def spread_kernel(
    out_in, cells_hbm, attn_hbm, up_hbm, down_hbm, early_hbm, late_hbm,
    out_cells, grad_cells, gq, gk, gv, bq, bv, go, bo, g1, s1, g2, s2, gup, bu, gdown, bd,
    cells_in, wide, attn, down, early, late, up, res, sems,
):
    p = Place()
    copies = [
        pltpu.make_async_copy(a, b, sems.at[k])
        for k, (a, b) in enumerate(
            (
                (cells_hbm, cells_in), (early_hbm, early), (late_hbm, late), (attn_hbm, attn), (down_hbm, down),
                (up_hbm, up), (out_in, res),
            )
        )
    ]
    for c in copies:
        c.start()
    copies[6].wait()
    backs = [pltpu.make_async_copy(res, out_cells, sems.at[8])]
    copies[0].wait()
    wide[...] = cells_in[...].astype(F32)
    backs.append(pltpu.make_async_copy(wide, grad_cells, sems.at[7]))
    for c in copies[1:6]:
        c.wait()
    backs.append(pltpu.make_async_copy(up, gup, sems.at[9]))
    for c in backs:
        c.start()
    gq[...] = attn[:, 0:256]
    gk[...] = attn[:, 256:512]
    gv[...] = attn[:, 512:768]
    go[...] = jnp.transpose(attn[:, 768:1024], (1, 0))
    gdown[...] = jnp.transpose(down[...], (1, 0))

    def cut(ref, k, block, part):
        row = ref[k : k + 1, lane_block(block * 128)]
        return pltpu.roll(row, lax.rem(128 - part * 32, 128), 1)[:, 0:32]

    for out, ref, k in ((bo, early, 4), (g1, late, 0), (s1, late, 1), (g2, early, 5), (s2, early, 6), (bd, early, 7)):
        out[...] = cut(ref, k, p.d, p.z)
    for out, k in ((bq, 2), (bv, 3)):
        out[...] = cut(late, k, p.d // 4, lax.rem(p.d, 4))
    bu[...] = early[0:1, lane_block(p.d * 128)]
    for c in backs:
        c.wait()


def spread(*args):
    s = jax.ShapeDtypeStruct
    hbm, fast = pl.BlockSpec(memory_space=pltpu.HBM), pl.BlockSpec(memory_space=pltpu.VMEM)
    v, w = s((1, 32), F32), s((PART, 256), F32)
    return pl.pallas_call(
        spread_kernel,
        out_shape=[
            s((2, 256, 1024), BF), s((2, 256, 1024), F32), w, w, w, v, v, s((256, PART), F32), v, v, v, v, v,
            s((PART, 1024), F32), s((1, PART), F32), s((1024, PART), F32), v,
        ],
        in_specs=[hbm] * 7,
        out_specs=[hbm, hbm] + [fast] * 11 + [hbm] + [fast] * 3,
        scratch_shapes=[
            pltpu.VMEM((2, 256, 1024), BF), pltpu.VMEM((2, 256, 1024), F32), pltpu.VMEM((PART, 1024), F32),
            pltpu.VMEM((PART, 1024), F32), pltpu.VMEM((8, 1024), F32), pltpu.VMEM((8, 1024), F32), pltpu.VMEM((PART, 1024), F32),
            pltpu.VMEM((2, 256, 1024), BF), pltpu.SemaphoreType.DMA((10,)),
        ],
        compiler_params=pltpu.CompilerParams(vmem_limit_bytes=62 * 2**20),
    )(*args)


def forward(*args):
    s = jax.ShapeDtypeStruct
    outs = [
        (T, 1024), (T, 1024), (4, T, 256), (4, 2 * T, 256), (4, 2 * T, 256), (T, 1024), (16, 2 * T, T), (16, 1, T),
        (4, 1024, 768), (1024, 1024), (3, 1024, 1024), (3, 1024, 1024), (2, 256, 1024), (T, 1024), (2, T, 1024), (2, T, 1024),
        (4, PART, 1024), (4, PART, 1024), (4, PART, 1024), (16, 1024), (4, 1, 1024),
    ]
    wide = (7, 13, 19, 20)
    hbm, fast = pl.BlockSpec(memory_space=pltpu.HBM), pl.BlockSpec(memory_space=pltpu.VMEM)
    b, f, dma = (lambda *x: pltpu.VMEM(x, BF)), (lambda *x: pltpu.VMEM(x, F32)), (lambda *x: pltpu.SemaphoreType.DMA(x))
    sems = []
    for parts in (3, 1, 1, 1):
        sems += [dma(6, parts), dma(3, parts), dma(3, 7), dma(3, 8)]
    return pl.pallas_call(
        forward_kernel,
        out_shape=[s(o, F32 if n in wide else BF) for n, o in enumerate(outs)],
        in_specs=[hbm, hbm, fast] + [hbm] * 6 + [fast] * 7,
        out_specs=[hbm] * 19 + [fast] * 2,
        scratch_shapes=[
            b(T, 1024), b(T, 1024), b(T, 1024), b(4, 1024, 768), b(1024, 1024), b(4, T, 256), b(4, 2 * T, 256), b(4, 2 * T, 256),
            b(T, 1024), b(2, 2 * T, T), f(16, 1, T), b(2, 2 * T, 128), b(256, 2 * T), b(256, T), f(T, 1024), b(T, 1024),
            b(1024, T), b(T, 2 * T), b(T, 2 * T), f(T, 1024), f(T, 1024),
            b(2, 1024, 1024), b(2, 1024, 1024), b(2, T, 1024), b(2, T, 1024), b(2, T, 1024), b(2, T, 1024), f(T, 1024), b(3, 2, T, 1024), b(4, PART, 1024),
            f(8, 128), f(4, 1, 1536),
        ]
        + sems
        + [dma(3, 2), dma(3, 2), dma(4), dma(4), dma(4, 2), dma(4, 2), dma(2, 4), dma(2, 4), dma(2, 2), dma(2, 2), dma(4, 3), dma(4, 3),
           pltpu.SemaphoreType.REGULAR, dma(7), dma(2, 2), dma(20)],
        compiler_params=pltpu.CompilerParams(collective_id=0, has_side_effects=True, vmem_limit_bytes=62 * 2**20),
    )(*args)


def body(*args):
    if lax.axis_size("dp") == 8 and lax.axis_size("mp") == 4:
        return fused_body(*args)
    return plain_body(*args)


def fused_body(
    cells,
    lengths,
    query_matrix,
    key_matrix,
    value_matrix,
    query_bias,
    value_bias,
    output_matrix,
    b_out,
    gain_one,
    shift_one,
    gain_two,
    shift_two,
    expand_weight,
    expand_bias,
    contract_weight,
    b_down,
    grad_out,
):
    slots = cells.shape[0]
    row = lambda v: v.reshape(1, -1)
    small = row(jnp.concatenate([query_bias, value_bias, expand_bias]))
    len_own = jnp.pad(jnp.broadcast_to(lengths.astype(F32)[:, None], (slots, 128)), ((0, 8 - slots), (0, 0)))
    (x, rows_one, q_all, k_all, v_all, mixed_all, e_all, r_all, wa, wo, _, _, out_land, d_middle, gu, gd, keep, la, lc, vec, bup) = forward(
        cells, grad_out, len_own, query_matrix, key_matrix, value_matrix, output_matrix, expand_weight, contract_weight,
        small, row(b_out), row(gain_one), row(shift_one), row(gain_two), row(shift_two), row(b_down),
    )
    left = backward(
        x, rows_one, q_all, k_all, v_all, mixed_all, e_all, r_all, wa, wo, d_middle, gu, gd, keep, la, lc, vec, bup, row(gain_one)
    )
    return tuple(v.reshape(-1) if v.shape[0] == 1 else v for v in spread(out_land, *left))


def solution(mesh):
    return jax.shard_map(
        body,
        mesh=mesh,
        in_specs=(
            P("dp", "mp", None),
            P("dp"),
            P(None, "mp"),
            P(None, "mp"),
            P(None, "mp"),
            P("mp"),
            P("mp"),
            P("mp", None),
            P(),
            P(),
            P(),
            P(),
            P(),
            P(None, "mp"),
            P("mp"),
            P("mp", None),
            P(),
            P("dp", "mp", None),
        ),
        out_specs=(
            P("dp", "mp", None),
            P("dp", "mp", None),
            P("dp", "mp"),
            P("dp", "mp"),
            P("dp", "mp"),
            P(("mp", "dp")),
            P(("mp", "dp")),
            P("mp", "dp"),
            P(("dp", "mp")),
            P(("dp", "mp")),
            P(("dp", "mp")),
            P(("dp", "mp")),
            P(("dp", "mp")),
            P("dp", "mp"),
            P(("mp", "dp")),
            P("mp", "dp"),
            P(("dp", "mp")),
        ),
        check_vma=False,
    )
```

```python
import jax
import jax.numpy as jnp
from jax import lax
from jax.experimental import pallas as pl
from jax.experimental.pallas import tpu as pltpu
from jax.sharding import PartitionSpec as P

HD = 64
EPS = 1e-05
BF = jnp.bfloat16
F32 = jnp.float32
MESH = pl.DeviceIdType.MESH
T = 512
PART = 128


def dot(a, b, ca, cb):
    return lax.dot_general(a, b, (((ca,), (cb,)), ((), ())), preferred_element_type=F32)


def cross(x, bit):
    n = lax.axis_size("dp")
    return lax.ppermute(x, "dp", [(i, i ^ (1 << bit)) for i in range(n)])


def shift(x, by):
    n = lax.axis_size("mp")
    return lax.ppermute(x, "mp", [(i, (i + by) % n) for i in range(n)])


def moves(n_dp, n_mp, slots):
    per = n_mp // slots
    turns = []
    for t in range(slots):
        pairs = []
        for d in range(n_dp):
            for m in range(n_mp):
                s = (t + m) % slots
                base, c = d - d % per, d % per
                target = (base + m // slots, c * slots + s)
                pairs.append((d * n_mp + m, target[0] * n_mp + target[1]))
        turns.append(pairs)
    return turns


def plane_bits(n_dp, flip):
    bits = list(range(1, n_dp.bit_length() - 1))
    return bits[::-1] if flip else bits


def gather(piece, flip):
    n_dp, n_mp = lax.axis_size("dp"), lax.axis_size("mp")
    stack = jnp.stack([shift(piece, n_mp - r) for r in range(1, n_mp)])
    held = {0: stack}
    for bit in plane_bits(n_dp, flip) + [0]:
        held.update({i ^ (1 << bit): cross(v, bit) for i, v in list(held.items())})
    return held


def assemble(held, own, d):
    n = len(held)
    stack = jnp.stack([held[i] for i in range(n)])
    order = jnp.arange(n) ^ d
    placed = jnp.take(stack, order, axis=0)
    placed = jnp.moveaxis(placed, 0, 1).reshape((stack.shape[1], -1, stack.shape[-1]))
    return [own] + [placed[r] for r in range(placed.shape[0])]


def scatter(blocks, flip):
    n_dp = lax.axis_size("dp")
    for bit in plane_bits(n_dp, flip):
        keep = sorted(i for i in blocks if not i >> bit & 1)
        got = cross(jnp.stack([blocks[i ^ (1 << bit)] for i in keep]), bit)
        blocks = {
            i: (blocks[i].astype(F32) + got[k].astype(F32)).astype(blocks[i].dtype)
            for k, i in enumerate(keep)
        }
    return blocks[0]


def layer_norm(v, gain, bias):
    center = v - jnp.mean(v, -1, keepdims=True)
    inverse = lax.rsqrt(jnp.mean(center * center, -1, keepdims=True) + EPS)
    unit = center * inverse
    return unit * gain + bias, unit, inverse


def norm_back(up, unit, inverse, gain):
    u = up * gain
    return inverse * (
        u - jnp.mean(u, -1, keepdims=True) - unit * jnp.mean(u * unit, -1, keepdims=True)
    )


def gelu_pair(v):
    cumulative = 0.5 * (1.0 + lax.erf(v * 0.7071067811865476))
    density = jnp.exp(-0.5 * v * v) * 0.3989422804014327
    return v * cumulative, cumulative + v * density


def attend(q, k, v, allowed):
    heads = q.shape[1] // HD
    qh = q.reshape(-1, heads, HD)
    kh = k.reshape(-1, heads, HD)
    vh = v.reshape(-1, heads, HD)
    s = jnp.einsum("qhd,khd->hqk", qh, kh, preferred_element_type=F32) * HD**-0.5
    s = jnp.where(allowed[None, None, :], s, -1e30)
    e = jnp.exp(s - jnp.max(s, -1, keepdims=True))
    p = (e / jnp.sum(e, -1, keepdims=True)).astype(BF)
    mixed = jnp.einsum("hqk,khd->qhd", p, vh, preferred_element_type=F32)
    return mixed.astype(BF).reshape(q.shape), p


def attend_back(q, k, v, p, mixed, dm):
    heads = q.shape[1] // HD
    qh = q.reshape(-1, heads, HD)
    kh = k.reshape(-1, heads, HD)
    vh = v.reshape(-1, heads, HD)
    dh = dm.reshape(-1, heads, HD)
    pf = p.astype(F32)
    dp = jnp.einsum("qhd,khd->hqk", dh, vh, preferred_element_type=F32)
    total = jnp.sum(dp * pf, -1, keepdims=True)
    ds = (pf * (dp - total)).astype(BF)
    dv = jnp.einsum("hqk,qhd->khd", p, dh, preferred_element_type=F32)
    dq = jnp.einsum("hqk,khd->qhd", ds, kh, preferred_element_type=F32) * HD**-0.5
    dk = jnp.einsum("hqk,qhd->khd", ds, qh, preferred_element_type=F32) * HD**-0.5
    return (
        dq.astype(BF).reshape(q.shape),
        dk.astype(BF).reshape(k.shape),
        dv.astype(BF).reshape(k.shape),
    )


def plain_body(
    cells,
    lengths,
    query_matrix,
    key_matrix,
    value_matrix,
    query_bias,
    value_bias,
    output_matrix,
    b_out,
    gain_one,
    shift_one,
    gain_two,
    shift_two,
    expand_weight,
    expand_bias,
    contract_weight,
    b_down,
    grad_out,
):
    slots, rows, width = cells.shape
    n_dp, n_mp = lax.axis_size("dp"), lax.axis_size("mp")
    d, z = lax.axis_index("dp"), lax.axis_index("mp")
    per = n_mp // slots
    core = d % per
    tokens = slots * rows
    part = width // n_dp
    hw = query_matrix.shape[1]
    turns = moves(n_dp, n_mp, slots)

    def bring(x):
        got = [
            lax.ppermute(
                lax.dynamic_index_in_dim(x, (t + z) % slots, 0, False), ("dp", "mp"), turns[t]
            )
            for t in range(slots)
        ]
        even = z % slots == 0
        return jnp.concatenate(
            [jnp.where(even, got[0], got[1]), jnp.where(even, got[1], got[0])], 0
        )

    def give_back(x):
        x = x.reshape(slots, rows, width)
        got = [
            lax.ppermute(
                lax.dynamic_index_in_dim(x, (t + z) % slots, 0, False),
                ("dp", "mp"),
                [(b, a) for a, b in turns[t]],
            )
            for t in range(slots)
        ]
        even = z % slots == 0
        return jnp.stack(
            [jnp.where(even, got[0], got[1]), jnp.where(even, got[1], got[0])], 0
        )

    mine = bring(cells)
    attn_own = jnp.concatenate(
        [query_matrix, key_matrix, value_matrix, output_matrix.T], 1
    )
    first = d * part

    def piece_of(w):
        return lax.dynamic_slice_in_dim(w, first, part, 0)

    half = attn_own.shape[1] // 2
    a_piece = piece_of(attn_own)
    a_left = gather(a_piece[:, :half], False)
    a_right = gather(a_piece[:, half:], True)
    u_held = gather(piece_of(expand_weight), False)
    d_held = gather(piece_of(contract_weight), True)
    grad_rows = bring(grad_out)
    small = jnp.concatenate([query_bias, value_bias, expand_bias])
    small = [small] + [shift(small, n_mp - r) for r in range(1, n_mp)]
    both = cross(lengths, 0)
    length_all = jnp.where(core == 0, jnp.concatenate([lengths, both]), jnp.concatenate([both, lengths]))
    length = lax.dynamic_index_in_dim(length_all, z, 0, False)

    attn_w = [
        jnp.concatenate([a, b], 1)
        for a, b in zip(
            assemble(a_left, attn_own[:, :half], d), assemble(a_right, attn_own[:, half:], d)
        )
    ]
    up_w = assemble(u_held, expand_weight, d)
    down_w = assemble(d_held, contract_weight, d)

    position = core * tokens + jnp.arange(tokens)
    keep = (position < length).astype(F32)[:, None]
    sib_position = (per - 1 - core) * tokens + jnp.arange(tokens)
    allowed = jnp.concatenate([position, sib_position]) < length

    x = mine.astype(F32)
    rows_one, unit_one, inv_one = layer_norm(x, gain_one, shift_one)
    rows_one = rows_one.astype(BF)
    kept = []
    attention = jnp.zeros((tokens, width), F32)
    for r in range(n_mp):
        w = attn_w[r]
        q = (dot(rows_one, w[:, :hw], 1, 0) + small[r][:hw]).astype(BF)
        k = dot(rows_one, w[:, hw : 2 * hw], 1, 0).astype(BF)
        v = (dot(rows_one, w[:, 2 * hw : 3 * hw], 1, 0) + small[r][hw : 2 * hw]).astype(BF)
        k = jnp.concatenate([k, cross(k, 0)], 0)
        v = jnp.concatenate([v, cross(v, 0)], 0)
        mixed, p = attend(q, k, v, allowed)
        kept.append((q, k, v, mixed, p))
        attention = attention + dot(mixed, w[:, 3 * hw :], 1, 1)
    middle = x + attention + b_out
    rows_two, unit_two, inv_two = layer_norm(middle, gain_two, shift_two)
    rows_two = rows_two.astype(BF)
    g = keep * grad_rows.astype(F32)
    gz = g.astype(BF)

    order = jnp.arange(0, n_dp, 2) ^ d

    def chosen(v):
        return jnp.take(v.reshape(v.shape[0], n_dp, part), order, axis=1).reshape(v.shape[0], -1)

    def other(v):
        return jnp.take(v.reshape(v.shape[0], n_dp, part), order ^ 1, axis=1).reshape(v.shape[0], -1)

    def both_cores(v):
        return jnp.concatenate([chosen(v), cross(other(v), 0)], 0)

    def weight_grad(left, right, flip):
        right = jnp.concatenate([right, cross(right, 0)], 0)
        return weight_grad_all(left, right, flip)

    def weight_grad_all(left, right, flip):
        got = dot(left, right, 0, 0).astype(BF).reshape(-1, part, right.shape[1])
        return scatter({2 * i: got[i] for i in range(got.shape[0])}, flip)

    def finish(pieces):
        total = pieces[0].astype(F32)
        for r in range(1, n_mp):
            total = total + shift(pieces[r], r).astype(F32)
        return total

    two_both = both_cores(rows_two)
    gz_both = both_cores(gz)
    result = middle + b_down
    e2 = jnp.zeros((tokens, width), F32)
    up_parts, down_parts, b_up = [], [], []
    for r in range(n_mp):
        upper = dot(rows_two, up_w[r], 1, 0) + small[r][2 * hw :]
        hidden, slope = gelu_pair(upper)
        hidden = hidden.astype(BF)
        result = result + dot(hidden, down_w[r], 1, 0)
        d_upper = (dot(gz, down_w[r], 1, 1) * slope).astype(BF)
        e2 = e2 + dot(d_upper, up_w[r], 1, 1)
        up_parts.append(weight_grad(two_both, d_upper, False))
        down_parts.append(weight_grad(gz_both, hidden, True))
        b_up.append(jnp.sum(d_upper.astype(F32), 0))
    out_cells = give_back((keep * result).astype(BF))
    grad_up = finish(up_parts)
    grad_down = finish(down_parts).T

    d_middle = g + norm_back(e2, unit_two, inv_two, gain_two)
    gm = d_middle.astype(BF)
    gm_both = both_cores(gm)
    one_both = both_cores(rows_one)
    e1 = jnp.zeros((tokens, width), F32)
    a_parts, b_q, b_v = [], [], []
    for r in range(n_mp):
        q, k, v, mixed, p = kept[r]
        w = attn_w[r]
        d_mixed = dot(gm, w[:, 3 * hw :], 1, 0).astype(BF)
        dq, dk, dv = attend_back(q, k, v, p, mixed, d_mixed)
        dk_all = (dk.astype(F32) + jnp.roll(cross(dk, 0), tokens, 0).astype(F32)).astype(BF)
        dv_all = (dv.astype(F32) + jnp.roll(cross(dv, 0), tokens, 0).astype(F32)).astype(BF)
        dq_all = jnp.concatenate([dq, cross(dq, 0)], 0)
        e1 = (
            e1
            + dot(dq, w[:, :hw], 1, 1)
            + dot(dk_all[:tokens], w[:, hw : 2 * hw], 1, 1)
            + dot(dv_all[:tokens], w[:, 2 * hw : 3 * hw], 1, 1)
        )
        b_q.append(jnp.sum(dq.astype(F32), 0))
        b_v.append(jnp.sum(dv_all[:tokens].astype(F32), 0))
        qkv_part = weight_grad_all(one_both, jnp.concatenate([dq_all, dk_all, dv_all], 1), r % 2 == 1)
        o_part = weight_grad(gm_both, mixed, r % 2 == 0)
        a_parts.append(jnp.concatenate([qkv_part, o_part], 1))
    d_cells = d_middle + norm_back(e1, unit_one, inv_one, gain_one)
    grad_cells = give_back(d_cells.astype(BF)).astype(F32)
    grad_attn = finish(a_parts)

    split_mp = [jnp.stack(b_q).reshape(n_mp, n_dp, -1), jnp.stack(b_v).reshape(n_mp, n_dp, -1), jnp.stack(b_up).reshape(n_mp, n_dp, -1)]
    sums = [
        jnp.sum(d_middle, 0),
        jnp.sum(e1 * unit_one, 0),
        jnp.sum(e1, 0),
        jnp.sum(e2 * unit_two, 0),
        jnp.sum(e2, 0),
        jnp.sum(g, 0),
    ]
    split_dp = [jnp.roll(jnp.swapaxes(s.reshape(n_dp, n_mp, -1), 0, 1), -z, 0) for s in sums]
    packed = jnp.concatenate(split_mp + split_dp, 2)
    packed = jnp.take(packed, jnp.arange(n_dp) ^ d, axis=1)
    packed = packed[:, 0::2] + cross(packed[:, 1::2], 0)
    packed = scatter({2 * i: packed[:, i] for i in range(packed.shape[1])}, False)
    vec = packed[0]
    for r in range(1, n_mp):
        vec = vec + shift(packed[r], r)
    nq = split_mp[0].shape[2]
    nu = split_mp[2].shape[2]
    ns = split_dp[0].shape[2]
    vq, vv, vu = vec[:nq], vec[nq : 2 * nq], vec[2 * nq : 2 * nq + nu]
    rest = [vec[2 * nq + nu + i * ns : 2 * nq + nu + (i + 1) * ns] for i in range(6)]
    return (
        out_cells,
        grad_cells,
        grad_attn[:, :hw],
        grad_attn[:, hw : 2 * hw],
        grad_attn[:, 2 * hw : 3 * hw],
        vq,
        vv,
        grad_attn[:, 3 * hw :].T,
        rest[0],
        rest[1],
        rest[2],
        rest[3],
        rest[4],
        grad_up,
        vu,
        grad_down,
        rest[5],
    )


def dg(a, b, ca, cb):
    return lax.dot_general(a, b, (((ca,), (cb,)), ((), ())), preferred_element_type=F32)


def lane_block(start, size=128):
    return pl.ds(pl.multiple_of(start, size), size)


class Place:
    def __init__(self):
        self.d, self.z = lax.axis_index("dp"), lax.axis_index("mp")
        self.bit = [lax.rem(self.d // (1 << b), 2) for b in range(3)]
        self.core = self.bit[0]
        self.base = self.d - self.core
        self.inner = jnp.logical_and(self.z >= 1, self.z <= 2)
        odd = lax.rem(self.z, 2)
        self.z_next, self.z_over = self.z + 1 - 2 * odd, self.z + 2 - 4 * (self.z // 2)
        self.slot_next = 1 + 2 * odd
        self.outer = jnp.logical_not(self.inner)

    def across(self, i):
        v = self.d
        for b in range(3):
            if i >> b & 1:
                v = v + (1 << b) * (1 - 2 * self.bit[b])
        return v

    def rows(self, i):
        return lane_block(self.across(i) * PART, PART)

    def greet(self):
        barrier = pltpu.get_barrier_semaphore()
        for step in range(1, 4):
            for c in range(2):
                pl.semaphore_signal(
                    barrier,
                    inc=1,
                    device_id=(self.base + c, lax.rem(self.z + step, 4)),
                    device_id_type=MESH,
                )
        for i in (1, 2, 4):
            pl.semaphore_signal(barrier, inc=1, device_id=(self.across(i), self.z), device_id_type=MESH)
        pl.semaphore_wait(barrier, 9)


def remote(src, dst, send, recv, device):
    return pltpu.make_async_remote_copy(
        src_ref=src, dst_ref=dst, send_sem=send, recv_sem=recv, device_id=device, device_id_type=MESH
    )


STEPS = {
    "ln1": (("a10", "a11", "a20", "a12", "a21", "u10", "u11", "a22", "a30", "d10", "d11", "a31", "u20", "u21", "a32", "d20", "d21"), ("a10", "a11", "a20", "a12", "a21", "u10", "a22", "a30", "d10", "a31", "u20", "d20", "a32", "u30")),
    "proj0": (("o10",), ("o10", "d30")),
    "proj1": ((), ("o11",)),
    "proj2": (("o11", "u30"), ("o20", "o12")),
    "proj3": (("o12",), ("o21",)),
    "att00": (("u31",), ("o22",)),
    "att01": (("u12",), ("o30", "o31", "u11")),
    "att10": (("d31",), ("o32",)),
    "att11": (("o21", "d30", "d12"), ("d11",)),
    "att20": (("o20", "o22"), ("u21", "u12")),
    "att30": (("o30", "d22", "o31", "u22"), ("d21", "d12")),
    "att31": (("o32",), ()),
    "ln2": ((), ("u31",)),
    "f0": (("d32", "u32"), ("d31",)),
    "b0": ((), ("u22", "d22")),
    "w1": ((), ("d32", "u32")),
}


class Unit:
    def __init__(self, place, own, at, parts, zsend, zrecv, send, recv, flip, slots):
        self.p, self.own, self.at, self.parts = place, own, at, parts
        self.zsend, self.zrecv, self.send, self.recv = zsend, zrecv, send, recv
        self.flip, self.slots = flip, slots

    def bits(self, n):
        return (4, 2) if (n % 2 == 1) == self.flip else (2, 4)

    def copy(self, k, slot_from, slot_to, device):
        return [
            remote(
                self.own(q) if slot_from is None else self.at(slot_from, 0, q),
                self.at(slot_to, 0, q),
                self.zsend.at[k, q],
                self.zrecv.at[slot_to - 1, q],
                device,
            )
            for q in range(self.parts)
        ]

    def direct(self, k):
        return self.copy(k - 1, None, k, (self.p.d, lax.rem(self.p.z + 4 - k, 4)))

    def along(self, k, slot_from, slot_to, right):
        return self.copy(k, slot_from, slot_to, (self.p.d, self.p.z + 1 if right else self.p.z - 1))

    def steps(self):
        z = self.p.z
        inner = self.p.inner
        return [
            (z <= 2, (0, None, 3, True)),
            (z >= 1, (1, None, 1, False)),
            (inner, (2, 3, 2, True)),
            (inner, (3, 1, 2, False)),
            (z == 1, (4, 2, 3, False)),
            (z == 2, (5, 2, 1, True)),
        ]

    def go(self, k):
        cond, what = self.steps()[k]

        @pl.when(cond)
        def _():
            for c in self.along(*what):
                c.start()

    def start(self):
        self.go(0)
        self.go(1)

    def start_direct(self):
        for k in (1, 3, 2):
            for c in self.direct(k):
                c.start()

    def landed(self, slot):
        for q in range(self.parts):
            here = self.at(slot, 0, q)
            remote(here, here, self.zsend.at[0, q], self.zrecv.at[slot - 1, q], (self.p.across(1), self.p.z)).wait_recv()

    def xy(self, n, k, i, bit):
        slot = self.slots[n]
        here = self.at(slot, i, None)
        return remote(
            here,
            here,
            self.send.at[slot - 1, k],
            self.recv.at[slot - 1, i ^ bit],
            (self.p.across(bit), self.p.z),
        )

    def arrived(self, n, i):
        slot = self.slots[n]
        here = self.at(slot, i, None)
        remote(here, here, self.send.at[slot - 1, 0], self.recv.at[slot - 1, i], (self.p.across(1), self.p.z)).wait_recv()

    def one(self, n):
        self.xy(n, 0, 0, self.bits(n)[0]).start()

    def take(self, n, inner=False, chained=False):
        self.landed(self.slots[n])
        if chained and inner and n < 2:
            for c in self.along(*self.steps()[3 - n][1]):
                c.start()
        if chained and inner and n == 2:
            self.go(4)
            self.go(5)
        self.one(n)

    def two(self, n):
        first, second = self.bits(n)
        self.arrived(n, first)
        self.xy(n, 1, 0, second).start()
        self.xy(n, 2, first, second).start()

    def three(self, n):
        first, second = self.bits(n)
        self.arrived(n, second)
        self.arrived(n, 6)
        for k, i in enumerate((0, 2, 4, 6)):
            self.xy(n, 3 + k, i, 1).start()

    def whole(self, n):
        for i in (1, 3, 5, 7):
            self.arrived(n, i)

    def finish(self, direct):
        if direct:
            for k in (1, 2, 3):
                for c in self.direct(k):
                    c.wait_send()
        else:
            for cond, what in self.steps():

                @pl.when(cond)
                def _(what=what):
                    for c in self.along(*what):
                        c.wait_send()

        for n in range(3):
            first, second = self.bits(n)
            self.xy(n, 0, 0, first).wait_send()
            self.xy(n, 1, 0, second).wait_send()
            self.xy(n, 2, first, second).wait_send()
            for k, i in enumerate((0, 2, 4, 6)):
                self.xy(n, 3 + k, i, 1).wait_send()


def bring_copies(p, src, dst, sends, recvs, here, which=(0, 1)):
    for s in which:
        target = (p.base + p.z // 2, 2 * p.core + s)
        half = lax.rem(p.z, 2)
        rows = lane_block(half * 256, 256)
        same = jnp.logical_and(p.core == p.z // 2, p.z == 2 * p.core + s)

        @pl.when(same)
        def _():
            pltpu.make_async_copy(src.at[s], dst.at[rows], here).start()

        @pl.when(jnp.logical_not(same))
        def _():
            remote(src.at[s], dst.at[rows], sends.at[s], recvs.at[half], target).start()


def bring_wait(p, dst, recvs, here):
    for half in range(2):
        block = dst.at[pl.ds(half * 256, 256)]
        same = jnp.logical_and(p.core == p.z // 2, lax.rem(p.z, 2) == half)

        @pl.when(same)
        def _():
            pltpu.make_async_copy(block, block, here).wait()

        @pl.when(jnp.logical_not(same))
        def _():
            remote(block, block, recvs.at[half], recvs.at[half], (p.across(1), p.z)).wait_recv()


def bring_sent(p, src, sends):
    for s in range(2):
        same = jnp.logical_and(p.core == p.z // 2, p.z == 2 * p.core + s)

        @pl.when(jnp.logical_not(same))
        def _():
            remote(src.at[s], src.at[s], sends.at[s], sends.at[s], (p.across(1), p.z)).wait_send()


def norm_stats(x):
    center = x - jnp.mean(x, -1, keepdims=True)
    inverse = lax.rsqrt(jnp.mean(center * center, -1, keepdims=True) + EPS)
    return center * inverse, inverse


def each_rows(size, total, f):
    def step(i, carry):
        f(pl.ds(pl.multiple_of(i * size, size), size))
        return carry

    lax.fori_loop(0, total // size, step, 0)


def chosen_both(p, t_ref, both_ref, sends, recvs):
    copies = []
    for k, i in enumerate((0, 2, 4, 6)):
        block = pl.ds(k * PART, PART)
        both_ref[block, 0:T] = t_ref[p.rows(i), :]
        copies.append(
            remote(
                t_ref.at[p.rows(i ^ 1)],
                both_ref.at[block, T : 2 * T],
                sends.at[k],
                recvs.at[k],
                (p.across(1), p.z),
            )
        )
    for c in copies:
        c.start()
    return copies


def forward_kernel(
    cells, grad, lengths, wq, wk, wv, wo, up, down, small_own, b_out, gain1, shift1, gain2, shift2, b_down,
    x_out, rows1_out, q_out, k_out, v_out, mix_out, e_out, r_out, wa_out, wo_out, wu, wd, out_land, dm_out, gu_out, gd_out, keep_out, la_out, lc_out, vec_out, bup_out,
    xv, gv, rows1, wav, wov, qv, kv, vv, mix, eb, rv, bias, vt, ot, middle, rows2, tt, xb, gb, acc, e2,
    uv, dv, ho, du, hs, ds, slope_v, gs, land_b, len_own, len_sib, small,
    a_zs, a_zr, a_s, a_r, o_zs, o_zr, o_s, o_r, u_zs, u_zr, u_s, u_r, d_zs, d_zr, d_s, d_r,
    act_s, act_r, sm_s, sm_r, kv_s, kv_r, both_s, both_r, hd_s, hd_r, ch_s, ch_r, credit, loc, load, store,
):
    p = Place()
    sibling = (p.across(1), p.z)

    ws = (wq, wk, wv)
    own_rows = p.rows(0)

    def a_at(slot, i, part):
        if part is None:
            return wav.at[slot, p.rows(i)]
        return wav.at[slot, p.rows(i), pl.ds(part * 256, 256)]

    fixed = (1, 3, 2)
    inner = p.inner
    by_arrival = (
        jnp.where(p.z <= 2, 1, 3),
        jnp.where(inner, 3, 2),
        jnp.where(inner, 2, jnp.where(p.z == 0, 3, 1)),
    )
    unit_a = Unit(p, lambda q: ws[q].at[own_rows], a_at, 3, a_zs, a_zr, a_s, a_r, True, fixed)
    unit_o = Unit(
        p,
        lambda q: wo.at[:, own_rows],
        lambda slot, i, q: wov.at[pl.ds(slot * 256, 256), p.rows(i)],
        1, o_zs, o_zr, o_s, o_r, False, fixed,
    )
    unit_u = Unit(
        p, lambda q: up.at[own_rows], lambda slot, i, q: wu.at[slot - 1, p.rows(i)], 1, u_zs, u_zr, u_s, u_r, False, by_arrival
    )
    unit_d = Unit(
        p, lambda q: down.at[own_rows], lambda slot, i, q: wd.at[slot - 1, p.rows(i)], 1, d_zs, d_zr, d_s, d_r, True, by_arrival
    )

    own_loads = [pltpu.make_async_copy(w, wav.at[0, :, pl.ds(k * 256, 256)], loc.at[k]) for k, w in enumerate(ws)]
    own_loads.append(pltpu.make_async_copy(wo, wov.at[pl.ds(0, 256)], loc.at[3]))
    for c in own_loads:
        c.start()
    first_loads = [pltpu.make_async_copy(up, uv.at[0], load.at[0, 0]), pltpu.make_async_copy(down, dv.at[0], load.at[1, 0])]
    for c in first_loads:
        c.start()

    len_own[...] = jnp.zeros((8, 128), F32)
    for k in range(2):
        len_own[k : k + 1, :] = jnp.full((1, 128), lengths[k], jnp.int32).astype(F32)
    p.greet()
    unit_a.start_direct()
    unit_u.start()
    unit_d.start()
    bring_copies(p, cells, xv, act_s.at[0], act_r.at[0], loc.at[4])
    unit_o.start_direct()
    small_copies = []
    for r in (1, 2, 3):
        small_copies.append(remote(small_own, small.at[r], sm_s.at[r], sm_r.at[r], (p.d, lax.rem(p.z + 4 - r, 4))))
    small_copies.append(remote(len_own, len_sib, sm_s.at[0], sm_r.at[0], sibling))
    for c in small_copies:
        c.start()
    small[0] = small_own[...]

    units = {"a": (unit_a, False), "o": (unit_o, False), "u": (unit_u, True), "d": (unit_d, True)}

    def advance(point):
        for inner, names in zip((True, False), STEPS.get(point, ((), ()))):
            if names:

                @pl.when(p.inner if inner else p.outer)
                def _(inner=inner, names=names):
                    for name in names:
                        (unit, chained), n = units[name[0]], int(name[2])
                        if name[1] == "1":
                            unit.take(n, inner, chained)
                        elif name[1] == "2":
                            unit.two(n)
                        else:
                            unit.three(n)

    small_copies[3].wait_recv()
    slot_row = lax.rem(p.z, 2)
    near = jnp.where(p.z // 2 == p.core, 1.0, 0.0)
    length = near * len_own[pl.ds(slot_row, 1), :] + (1.0 - near) * len_sib[pl.ds(slot_row, 1), :]
    length = length[:, :1]
    lane = lax.broadcasted_iota(jnp.int32, (1, 128), 1)
    key = lax.broadcasted_iota(jnp.int32, (2 * T, 128), 0)
    key = jnp.where(key < T, key + p.core * T, key - T + (1 - p.core) * T)
    barred = jnp.where(key.astype(F32) < length, 0.0, -1e30)
    bias[0] = jnp.where(lane == 64, barred, 0.0).astype(BF)
    bias[1] = jnp.where(lane == 0, barred, 0.0).astype(BF)

    def kept(rows_start, size):
        row = lax.broadcasted_iota(jnp.int32, (size, 1), 0) + rows_start + p.core * T
        return row.astype(F32) < length

    advance("ln1")

    bring_wait(p, xv, act_r.at[0], loc.at[4])

    def first_norm(rows):
        unit, _ = norm_stats(xv[rows, :].astype(F32))
        rows1[rows, :] = (unit * gain1[...] + shift1[...]).astype(BF)

    each_rows(128, T, first_norm)
    outs = [pltpu.make_async_copy(xv, x_out, store.at[0]), pltpu.make_async_copy(rows1, rows1_out, store.at[1])]
    for c in outs:
        c.start()
    for c in own_loads:
        c.wait()
    for r in (1, 2, 3):
        small_copies[r - 1].wait_recv()

    kv_copies = []

    def project(r):
        b = small.at[r]
        x = rows1[...]
        qv[r] = (dg(x, wav[r, :, 0:256], 1, 0) + b[:, 0:256]).astype(BF)
        kv[r, 0:T, :] = dg(x, wav[r, :, 256:512], 1, 0).astype(BF)
        vv[r, 0:T, :] = (dg(x, wav[r, :, 512:768], 1, 0) + b[:, 256:512]).astype(BF)
        cs = [
            remote(ref.at[r, pl.ds(0, T)], ref.at[r, pl.ds(T, T)], kv_s.at[r, n], kv_r.at[r, n], sibling)
            for n, ref in enumerate((kv, vv))
        ]
        for c in cs:
            c.start()
        kv_copies.append(cs)

    def e_copy(head, slot):
        return pltpu.make_async_copy(eb.at[slot], e_out.at[head], store.at[2 + slot])

    def attend_pair(r, j):
        cols = pl.ds(j * 128, 128)
        kp = kv[r, :, cols]
        qp = qv[r, :, cols] * BF(HD**-0.5)
        for h in range(2):
            mine = (lane < 64) if h == 0 else (lane >= 64)
            one = lane == (64 if h == 0 else 0)
            ka = jnp.where(mine, kp, bias[h])
            qa = jnp.where(mine, qp, jnp.where(one, BF(1), BF(0)))
            s = dg(ka, qa, 1, 1)
            e = jnp.exp(s - jnp.max(s, 0, keepdims=True))
            inv = 1.0 / jnp.sum(e, 0, keepdims=True)
            head = r * 4 + 2 * j + h
            if head >= 2:
                e_copy(head - 2, h).wait()
            eb[h] = e.astype(BF)
            e_copy(head, h).start()
            feats = pl.ds(j * 128 + h * 64, 64)
            ot[feats, :] = (dg(vt[feats, :], eb[h], 1, 0) * inv).astype(BF)
            rv[head] = inv

    def attend(r):
        advance(f"att{r}0")
        if r == 2:
            bring_copies(p, grad, gv, act_s.at[1], act_r.at[1], loc.at[5])
        for c in kv_copies[r]:
            c.wait_recv()
        vt[...] = jnp.transpose(vv[r], (1, 0))
        attend_pair(r, 0)
        advance(f"att{r}1")
        attend_pair(r, 1)
        mix[:, r * 256 : (r + 1) * 256] = jnp.transpose(ot[...], (1, 0))

    advance("proj0")
    project(0)
    for n in range(3):
        unit_a.whole(n)
    for r in (1, 2, 3):
        advance(f"proj{r}")
        project(r)
    for r in range(4):
        attend(r)
    advance("oproj")
    for n in range(3):
        unit_o.whole(n)
    for h in range(2):
        e_copy(14 + h, h).wait()

    outs += [
        pltpu.make_async_copy(wav, wa_out, store.at[4]),
        pltpu.make_async_copy(wov, wo_out, store.at[5]),
        pltpu.make_async_copy(qv, q_out, store.at[6]),
        pltpu.make_async_copy(kv, k_out, store.at[7]),
        pltpu.make_async_copy(vv, v_out, store.at[8]),
        pltpu.make_async_copy(mix, mix_out, store.at[9]),
        pltpu.make_async_copy(rv, r_out, store.at[10]),
    ]
    for c in outs[2:]:
        c.start()

    for n in range(2):
        cols = pl.ds(n * 512, 512)
        middle[:, cols] = dg(mix[...], wov[:, cols], 1, 0)

    advance("ln2")

    def second_norm(rows):
        m = middle[rows, :] + xv[rows, :].astype(F32) + b_out[...]
        middle[rows, :] = m
        unit, _ = norm_stats(m)
        rows2[rows, :] = (unit * gain2[...] + shift2[...]).astype(BF)
        acc[rows, :] = m + b_down[...]

    each_rows(128, T, second_norm)
    tt[...] = jnp.transpose(rows2[...], (1, 0))
    both = chosen_both(p, tt, xb, both_s.at[0], both_r.at[0])

    def mask_grad(i, carry):
        rows = pl.ds(pl.multiple_of(i * 128, 128), 128)
        gv[rows, :] = jnp.where(kept(i * 128, 128), gv[rows, :].astype(F32), 0.0).astype(BF)
        return carry

    order = (0,) + by_arrival

    def load_copies(n):
        r = order[n]
        return [
            pltpu.make_async_copy(wu.at[r - 1], uv.at[n % 2], load.at[0, n % 2]),
            pltpu.make_async_copy(wd.at[r - 1], dv.at[n % 2], load.at[1, n % 2]),
        ]

    def hidden(n):
        r, slot = order[n], n % 2
        for k in range(2):
            c = pl.ds(k * 512, 512)
            upper = dg(rows2[...], uv[slot, :, c], 1, 0) + small[r, :, pl.ds(512 + k * 512, 512)]
            act, slope = gelu_pair(upper)
            ho[slot, :, c] = act.astype(BF)
            slope_v[:, c] = slope
        if n >= 2:
            pl.semaphore_wait(credit, 1)
        copy = remote(ho.at[slot], hs.at[slot], hd_s.at[0, slot], hd_r.at[0, slot], sibling)
        copy.start()
        for k in range(2):
            c = pl.ds(k * 512, 512)
            acc[:, c] = acc[:, c] + dg(ho[slot], dv[slot, :, c], 1, 0)
        return copy

    def hidden_back(n):
        r, slot = order[n], n % 2
        for k in range(2):
            c = pl.ds(k * 512, 512)
            d_up = (dg(gv[...], dv[slot, c, :], 1, 1) * slope_v[:, c]).astype(BF)
            du[slot, :, c] = d_up
            bup_out[r, :, c] = jnp.sum(d_up.astype(F32), 0, keepdims=True)
        copy = remote(du.at[slot], ds.at[slot], hd_s.at[1, slot], hd_r.at[1, slot], sibling)
        copy.start()
        for k in range(2):
            c = pl.ds(k * 512, 512)
            new = dg(du[slot], uv[slot, c, :], 1, 1)
            e2[:, c] = new if n == 0 else e2[:, c] + new
        return copy

    g_stores = []

    def chain(n, u):
        j = 2 * n + u
        first, second = (4, 2) if u else (2, 4)
        block = lambda i: gs.at[n, u, pl.ds(i // 2 * PART, PART)]
        near, far = (p.across(first), p.z), (p.across(second), p.z)
        return (
            remote(block(first), la_out.at[j], ch_s.at[j, 0], ch_r.at[j, 0], near),
            remote(block(first + second), land_b.at[j], ch_s.at[j, 1], ch_r.at[j, 1], near),
            remote(block(second), lc_out.at[j], ch_s.at[j, 2], ch_r.at[j, 2], far),
        )

    chains = {(n, u): chain(n, u) for n in range(2) for u in range(2)}

    def weight_grads(n, cs):
        slot, at = n % 2, min(n, 2)
        for c in cs:
            c.wait_recv()
        if n == 3:
            for c in g_stores[-2:]:
                c.wait()
        gs[at, 0] = (dg(xb[:, 0:T], du[slot], 1, 0) + dg(xb[:, T : 2 * T], ds[slot], 1, 0)).astype(BF)
        gs[at, 1] = (dg(gb[:, 0:T], ho[slot], 1, 0) + dg(gb[:, T : 2 * T], hs[slot], 1, 0)).astype(BF)
        if n < 2:
            pl.semaphore_signal(credit, inc=1, device_id=sibling, device_id_type=MESH)
        for u, out in enumerate((gu_out, gd_out)):
            if n < 2:
                for c in chains[n, u][:2]:
                    c.start()
                c = pltpu.make_async_copy(gs.at[n, u, pl.ds(0, PART)], keep_out.at[2 * n + u], store.at[11 + 2 * n + u])
            else:
                c = pltpu.make_async_copy(gs.at[2, u], out.at[n - 2], store.at[11 + 2 * n + u])
            c.start()
            g_stores.append(c)
        for c in cs:
            c.wait_send()

    def second_exchange(n):
        for u in range(2):
            one, other, two = chains[n, u]
            other.wait_recv()
            rows = pl.ds((2 if u else 4) // 2 * PART, PART)
            gs[n, u, rows, :] = (gs[n, u, rows, :].astype(F32) + land_b[2 * n + u].astype(F32)).astype(BF)
            two.start()

    for c in first_loads:
        c.wait()
    advance("f0")
    held = [[hidden(0)]]
    for c in both:
        c.wait_send()
    advance("b0")
    bring_wait(p, gv, act_r.at[1], loc.at[5])
    lax.fori_loop(0, T // 128, mask_grad, 0)
    tt[...] = jnp.transpose(gv[...], (1, 0))
    both2 = chosen_both(p, tt, gb, both_s.at[1], both_r.at[1])
    held[0].append(hidden_back(0))
    for n in range(1, 4):
        advance(f"w{n - 1}")
        if n < 3:
            unit_u.whole(n - 1)
            unit_d.whole(n - 1)
            loads = load_copies(n)
            for c in loads:
                c.start()
            if n == 1:
                for c in both + both2:
                    c.wait_recv()
            weight_grads(n - 1, held[n - 1])
        else:
            second_exchange(0)
            unit_u.whole(2)
            unit_d.whole(2)
            loads = load_copies(3)
            for c in loads:
                c.start()
        advance(f"f{n}")
        for c in loads:
            c.wait()
        held.append([hidden(n)])
        advance(f"b{n}")
        if n == 3:

            def result(i, carry):
                rows = pl.ds(pl.multiple_of(i * 128, 128), 128)
                rows2[rows, :] = jnp.where(kept(i * 128, 128), acc[rows, :], 0.0).astype(BF)
                return carry

            lax.fori_loop(0, T // 128, result, 0)
            return_copies(p, rows2, out_land, act_s.at[2], act_r.at[2], loc.at[6])
            second_exchange(1)
        held[n].append(hidden_back(n))
    weight_grads(2, held[2])
    weight_grads(3, held[3])

    vec_out[...] = jnp.zeros(vec_out.shape, F32)

    def last(i, carry):
        rows = pl.ds(pl.multiple_of(i * 128, 128), 128)
        unit, inverse = norm_stats(middle[rows, :])
        e = e2[rows, :]
        g = gv[rows, :].astype(F32)
        u = e * gain2[...]
        d_mid = g + inverse * (u - jnp.mean(u, -1, keepdims=True) - unit * jnp.mean(u * unit, -1, keepdims=True))
        middle[rows, :] = d_mid
        for k, v in enumerate((d_mid, e * unit, e, g)):
            vec_out[4 + k : 5 + k, :] += jnp.sum(v, 0, keepdims=True)
        return carry

    lax.fori_loop(0, T // 128, last, 0)
    ends = [pltpu.make_async_copy(middle, dm_out, store.at[19])]
    for c in ends:
        c.start()
    for c in ends + outs + g_stores[:4] + g_stores[6:]:
        c.wait()
    for cs in chains.values():
        cs[0].wait_recv()
        cs[2].wait_recv()
        for c in cs:
            c.wait_send()
    return_wait(p, out_land, act_r.at[2], loc.at[6])
    return_sent(p, rows2, act_s.at[2])
    for c in both2 + small_copies:
        c.wait_send()
    for cs in kv_copies:
        for c in cs:
            c.wait_send()
    for unit in (unit_a, unit_o, unit_u, unit_d):
        unit.finish(unit is unit_a or unit is unit_o)
    bring_sent(p, cells, act_s.at[0])
    bring_sent(p, grad, act_s.at[1])


def return_copies(p, src, dst, sends, recvs, here):
    slot = lax.rem(p.z, 2)
    for h in range(2):
        rows = src.at[pl.ds(h * 256, 256)]
        same = jnp.logical_and(p.core == p.z // 2, p.z == 2 * p.core + h)

        @pl.when(same)
        def _():
            pltpu.make_async_copy(rows, dst.at[slot], here).start()

        @pl.when(jnp.logical_not(same))
        def _():
            remote(rows, dst.at[slot], sends.at[h], recvs.at[slot], (p.base + p.z // 2, 2 * p.core + h)).start()


def return_wait(p, dst, recvs, here):
    for s in range(2):
        same = jnp.logical_and(p.core == p.z // 2, p.z == 2 * p.core + s)

        @pl.when(same)
        def _():
            pltpu.make_async_copy(dst.at[s], dst.at[s], here).wait()

        @pl.when(jnp.logical_not(same))
        def _():
            remote(dst.at[s], dst.at[s], recvs.at[s], recvs.at[s], (p.across(1), p.z)).wait_recv()


def return_sent(p, src, sends):
    for h in range(2):
        rows = src.at[pl.ds(h * 256, 256)]
        same = jnp.logical_and(p.core == p.z // 2, p.z == 2 * p.core + h)

        @pl.when(jnp.logical_not(same))
        def _():
            remote(rows, rows, sends.at[h], sends.at[h], (p.across(1), p.z)).wait_send()


class Chain:
    def __init__(self, p, r, block, keep0, keep1, land1, land2, land3, send, recv, zsend, zrecv, flip):
        first, second = (4, 2) if flip else (2, 4)
        self.r, self.keep0, self.keep1, self.land1, self.land2 = r, keep0, keep1, land1, land2
        near = (p.across(first), p.z)
        self.one = [remote(block(first + k * second), land1.at[k], send.at[k], recv.at[k], near) for k in range(2)]
        self.two = remote(keep1, land2, send.at[2], recv.at[2], (p.across(second), p.z))
        self.three = None
        if not (isinstance(r, int) and r == 0):
            k = jnp.where(r == 2, 2, jnp.where(r == p.slot_next, 0, 1))
            device = (p.d, jnp.where(r == 2, p.z_over, p.z_next))
            self.three = remote(keep0, land3.at[k], zsend.at[k], zrecv.at[k], device)

    def start(self):
        for c in self.one:
            c.start()

    def middle(self):
        for c in self.one:
            c.wait_recv()
        self.keep1[...] = (self.keep1[...].astype(F32) + self.land1[1].astype(F32)).astype(BF)
        self.two.start()

    def total(self):
        return self.keep0[...].astype(F32) + self.land1[0].astype(F32) + self.land2[...].astype(F32)

    def end(self, summed=False):
        if not summed:
            self.two.wait_recv()
        if self.three is not None:
            self.keep0[...] = self.total().astype(BF)

            @pl.when(self.r != 2)
            def _():
                self.three.start()

    def over(self, land):
        @pl.when(self.r == 2)
        def _():
            self.keep0[...] = (self.keep0[...].astype(F32) + land[...].astype(F32)).astype(BF)
            self.three.start()

    def sent(self, summed=False):
        for c in ([] if summed else self.one + [self.two]) + ([] if self.three is None else [self.three]):
            c.wait_send()


class Vectors:
    def __init__(self, p, acc, land, zland, send, recv, zsend, zrecv):
        self.acc, self.land, self.zland = acc, land, zland
        self.steps = [
            remote(acc, land.at[b], send.at[b], recv.at[b], (p.across(1 << b), p.z)) for b in range(3)
        ]
        self.along = [
            remote(acc, zland.at[r - 1], zsend.at[r - 1], zrecv.at[r - 1], (p.d, lax.rem(p.z + r, 4)))
            for r in (1, 2, 3)
        ]

    def start(self, b):
        self.steps[b].start()

    def take(self, b):
        self.steps[b].wait()
        self.acc[...] = self.acc[...] + self.land[b]

    def z_start(self):
        for c in self.along:
            c.start()

    def z_wait(self):
        for c in self.along:
            c.wait()


def backward_kernel(
    x_in, rows1_in, q_in, k_in, v_in, mix_in, e_in, r_in, wa_in, wo_in, dm_in, gu_in, gd_in, keep_in, la_in, lc_in, vec_in, bup_in, gain1,
    gcl, attn_out, gup_out, gdown_out, early_out, late_out,
    land1, land2, land3, land1a, land2a, land3a, udk, ga, wav, wov, qv, kv, vv, mix, mixs, dm, e1, gmb, r1b, tt, gm, xv, rows1, eb, rv, xs, xr, da,
    kt, mixt, dmt_all, dqt, early, late, eland, lland, ezland, lzland,
    ch_s, ch_r, z_s, z_r, gc_s, gc_r, both_s, both_r, x_s, x_r, mix_s, mix_r, ev_s, ev_r, ez_s, ez_r,
    lv_s, lv_r, lz_s, lz_r, credit, here, load, eload,
):
    p = Place()
    sibling = (p.across(1), p.z)
    order = (1, 3, 2, 0)

    loads = {}
    for n, (name, src, dst) in enumerate(
        (
            ("dm", dm_in, dm), ("wo", wo_in, wov), ("rows1", rows1_in, rows1), ("mix", mix_in, mix), ("r", r_in, rv),
            ("q", q_in, qv), ("k", k_in, kv), ("v", v_in, vv), ("x", x_in, xv),
        )
    ):
        loads[name] = pltpu.make_async_copy(src, dst, load.at[n])
        loads[name].start()

    def wa_load(n):
        return pltpu.make_async_copy(wa_in.at[order[n]], wav.at[n % 2], load.at[9 + n % 2])

    def e_load(head, slot):
        return pltpu.make_async_copy(e_in.at[head], eb.at[slot], eload.at[slot])

    for h in range(2):
        e_load(order[0] * 4 + h, h).start()
    wa_load(0).start()

    p.greet()
    mix_copy = remote(mix_in, mixs, mix_s, mix_r, sibling)
    mix_copy.start()

    chains = {}
    keep_loads = []
    shards = (
        0,
        jnp.where(p.z <= 2, 1, 3),
        jnp.where(p.inner, 3, 2),
        jnp.where(p.inner, 2, jnp.where(p.z == 0, 3, 1)),
    )
    for n in (1, 0, 2, 3):
        r = shards[n]
        for u, src in enumerate((gu_in, gd_in)):
            flip = u == 1
            second = 2 if flip else 4
            j = u * 4 + n
            if n < 2:
                parts = ((keep_in, udk.at[j, 0]), (la_in, land1.at[j, 0]), (lc_in, land2.at[j]))
                for k, (held, to) in enumerate(parts):
                    c = pltpu.make_async_copy(held.at[2 * n + u], to, load.at[19 + 3 * (2 * n + u) + k])
                    c.start()
                    keep_loads.append(c)
                blocks = lambda i, j=j: udk.at[j, 0]
            else:
                blocks = lambda i, src=src, n=n: src.at[n - 2, pl.ds(i // 2 * PART, PART)]
                for k, i in enumerate((0, second)):
                    pltpu.make_async_copy(blocks(i), udk.at[j, k], load.at[11 + j]).start()
                keep_loads.append(pltpu.make_async_copy(udk.at[j], udk.at[j], load.at[11 + j]))
            chains[u, n] = Chain(
                p, r, blocks, udk.at[j, 0], udk.at[j, 1], land1.at[j], land2.at[j], land3.at[u],
                ch_s.at[j], ch_r.at[j], z_s.at[u], z_r.at[u], flip,
            )
    for n, r in enumerate(order):
        for half in range(2):
            second = 2 if half else 4
            blocks = lambda i, r=r, half=half: ga.at[r, half, pl.ds(i // 2 * PART, PART)]
            chains[2 + half, n] = Chain(
                p, r, blocks, blocks(0), blocks(second), land1a.at[r, half], land2a.at[r, half], land3a.at[half],
                ch_s.at[8 + 2 * r + half], ch_r.at[8 + 2 * r + half], z_s.at[2 + half], z_r.at[2 + half],
                half == 1,
            )

    def start(kind, n):
        for u in (0, 1) if kind == "f" else (2, 3):
            chains[u, n].start()

    def middle(kind, n):
        for u in (0, 1) if kind == "f" else (2, 3):
            chains[u, n].middle()

    def end(kind, n):
        for u in (0, 1) if kind == "f" else (2, 3):
            chains[u, n].end()

    def z_got(u, k, land):
        remote(land.at[k], land.at[k], z_s.at[u, k], z_r.at[u, k], sibling).wait_recv()

    def over(kind, ns):
        for u in (0, 1) if kind == "f" else (2, 3):
            land = land3.at[u] if kind == "f" else land3a.at[u - 2]
            z_got(u, 1, land)
            for n in ns:
                chains[u, n].over(land.at[1])

    start("f", 2)
    start("f", 3)

    early[...] = vec_in[0:8, :]
    for r in range(4):
        early[r : r + 1, :] = bup_in[r]
    ev = Vectors(p, early, eland, ezland, ev_s, ev_r, ez_s, ez_r)
    ev.start(0)
    late[...] = jnp.zeros((8, 1024), F32)

    loads["rows1"].wait()
    tt[...] = jnp.transpose(rows1[...], (1, 0))
    both = chosen_both(p, tt, r1b, both_s.at[0], both_r.at[0])
    loads["dm"].wait()

    def cast(rows):
        gm[rows, :] = dm[rows, :].astype(BF)

    each_rows(128, T, cast)
    for name in ("wo", "mix", "r", "q", "k", "v"):
        loads[name].wait()
    lane = lax.broadcasted_iota(jnp.int32, (1, 128), 1)

    def attend_back(n):
        r, slot = order[n], n % 2
        cols_r = pl.ds(r * 256, 256)
        kt[...] = jnp.transpose(kv[r], (1, 0))
        mixt[...] = jnp.transpose(mix[:, cols_r], (1, 0))
        dmt_all[...] = dg(wov[cols_r, :], gm[...], 1, 1).astype(BF)
        if n >= 2:
            for c in [x_copies[n - 2]]:
                c.wait_send()

        def pair(j, carry):
            cols = lane_block(j * 128)
            kp = kv[r, :, cols]
            vp = vv[r, :, cols]
            qp = qv[r, :, cols] * BF(HD**-0.5)
            dk = jnp.zeros((2 * T, 128), F32)
            d_v = jnp.zeros((2 * T, 128), F32)
            for h in range(2):
                head = r * 4 + 2 * j + h
                feats = pl.ds(pl.multiple_of(j * 128 + h * 64, 64), 64)
                mine = (lane < 64) if h == 0 else (lane >= 64)
                dmt = (dmt_all[feats, :].astype(F32) * rv[head]).astype(BF)
                delta = jnp.sum(dmt.astype(F32) * mixt[feats, :].astype(F32), 0, keepdims=True)
                zero = jnp.zeros((64, T), BF)
                dmt2 = jnp.concatenate([dmt, zero] if h == 0 else [zero, dmt], 0)
                dma = jnp.transpose(dmt2, (1, 0))
                dp = dg(vp, dmt2, 1, 0)
                e_load(head, h).wait()
                ds = (eb[h].astype(F32) * (dp - delta)).astype(BF)
                qa = jnp.where(mine, qp, BF(0))
                d_v = d_v + dg(eb[h], dma, 1, 0)
                if n < 3:
                    nxt = jnp.where(j == 0, head + 2, order[n + 1] * 4 + h)
                    e_load(nxt, h).start()
                else:
                    @pl.when(j == 0)
                    def _():
                        e_load(head + 2, h).start()
                dk = dk + dg(ds, qa, 1, 0)
                dqt[feats, :] = (dg(kt[feats, :], ds, 1, 0) * HD**-0.5).astype(BF)
            xs[slot, T : 3 * T, cols] = dk.astype(BF)
            xs[slot, 3 * T : 5 * T, cols] = d_v.astype(BF)
            return carry

        lax.fori_loop(0, 2, pair, 0)
        xs[slot, 0:T, :] = jnp.transpose(dqt[...], (1, 0))
        if n >= 2:
            pl.semaphore_wait(credit, 1)
        c = remote(xs.at[slot], xr.at[slot], x_s.at[slot], x_r.at[slot], sibling)
        c.start()
        return c

    x_copies = []

    def gather_up(n):
        r, slot = order[n], n % 2
        x_copies[n].wait_recv()
        da[0:T, 0:256] = xs[slot, 0:T, :]
        da[T : 2 * T, 0:256] = xr[slot, 0:T, :]
        for k in range(2):
            base = T + 2 * T * k
            cols = pl.ds(256 * (k + 1), 256)
            da[0:T, cols] = (
                xs[slot, base : base + T, :].astype(F32) + xr[slot, base + T : base + 2 * T, :].astype(F32)
            ).astype(BF)
            da[T : 2 * T, cols] = (
                xs[slot, base + T : base + 2 * T, :].astype(F32) + xr[slot, base : base + T, :].astype(F32)
            ).astype(BF)
        if n < 2:
            pl.semaphore_signal(credit, inc=1, device_id=sibling, device_id_type=MESH)
        ga[r, 0] = dg(r1b[...], da[:, 0:512], 1, 0).astype(BF)
        ga[r, 1, :, 0:256] = dg(r1b[...], da[:, 512:768], 1, 0).astype(BF)
        cols_r = pl.ds(r * 256, 256)
        ga[r, 1, :, 256:512] = (dg(gmb[:, 0:T], mix[:, cols_r], 1, 0) + dg(gmb[:, T : 2 * T], mixs[:, cols_r], 1, 0)).astype(BF)
        wa_load(n).wait()
        if n + 1 < 4:
            wa_load(n + 1).start()
        new = dg(da[0:T, :], wav[slot], 1, 1)
        e1[...] = new if n == 0 else e1[...] + new
        late[2:3, r * 256 : (r + 1) * 256] = jnp.sum(da[0:T, 0:256].astype(F32), 0, keepdims=True)
        late[3:4, r * 256 : (r + 1) * 256] = jnp.sum(da[0:T, 512:768].astype(F32), 0, keepdims=True)

    for c in keep_loads:
        c.wait()
    for u in range(2):
        chains[u, 1].end(True)
    x_copies.append(attend_back(0))
    for c in both:
        c.wait_send()
    tt[...] = jnp.transpose(gm[...], (1, 0))
    both2 = chosen_both(p, tt, gmb, both_s.at[1], both_r.at[1])
    middle("f", 2)
    ev.take(0)
    ev.start(1)
    x_copies.append(attend_back(1))
    for c in both + both2:
        c.wait_recv()
    mix_copy.wait_recv()
    gather_up(0)
    middle("f", 3)
    start("a", 0)
    x_copies.append(attend_back(2))
    end("f", 2)
    ev.take(1)
    ev.start(2)
    gather_up(1)
    start("a", 1)
    end("f", 3)
    x_copies.append(attend_back(3))
    middle("a", 0)
    gather_up(2)
    start("a", 2)
    over("f", (2, 3))
    middle("a", 1)
    gather_up(3)
    start("a", 3)
    end("a", 0)
    ev.take(2)
    ev.z_start()

    loads["x"].wait()

    def first_back(i, carry):
        rows = pl.ds(pl.multiple_of(i * 128, 128), 128)
        unit, inverse = norm_stats(xv[rows, :].astype(F32))
        e = e1[rows, :]
        u = e * gain1[...]
        d = dm[rows, :] + inverse * (u - jnp.mean(u, -1, keepdims=True) - unit * jnp.mean(u * unit, -1, keepdims=True))
        gm[rows, :] = d.astype(BF)
        for k, v in enumerate((e * unit, e)):
            late[k : k + 1, :] += jnp.sum(v, 0, keepdims=True)
        return carry

    lax.fori_loop(0, T // 128, first_back, 0)
    return_copies(p, gm, gcl, gc_s, gc_r, here.at[1])
    lv = Vectors(p, late, lland, lzland, lv_s, lv_r, lz_s, lz_r)
    lv.start(0)
    end("a", 1)
    middle("a", 2)
    lv.take(0)
    lv.start(1)
    end("a", 2)
    over("a", (2,))
    middle("a", 3)
    lv.take(1)
    lv.start(2)

    def final(u, n, land):
        z_got(u, 0, land)
        z_got(u, 2, land)
        return chains[u, n].total() + land[0].astype(F32) + land[2].astype(F32)

    gup_out[...] = final(0, 0, land3.at[0])
    gdown_out[...] = final(1, 0, land3.at[1])
    lv.take(2)
    lv.z_start()
    ev.z_wait()
    shard = early[0:1, :]
    for r in (1, 2, 3):
        shard = shard + ezland[r - 1, r : r + 1, :]
    early_out[...] = early[...] + ezland[0] + ezland[1] + ezland[2]
    early_out[0:1, :] = shard
    end("a", 3)

    lv.z_wait()
    late_out[...] = late[...] + lzland[0] + lzland[1] + lzland[2]
    for k in (2, 3):
        shard = late[k : k + 1, 0:256]
        for r in (1, 2, 3):
            shard = shard + lzland[r - 1, k : k + 1, r * 256 : (r + 1) * 256]
        late_out[k : k + 1, 0:256] = shard
    total = final(2, 3, land3a.at[0])
    attn_out[:, 0:512] = total
    attn_out[:, 512:1024] = final(3, 3, land3a.at[1])
    return_wait(p, gcl, gc_r, here.at[1])

    for c in both2 + [mix_copy, x_copies[2], x_copies[3]]:
        c.wait_send()
    for (u, n), c in chains.items():
        c.sent(u < 2 and n < 2)
    return_sent(p, gm, gc_s)


def backward(*args):
    s = jax.ShapeDtypeStruct
    hbm, fast = pl.BlockSpec(memory_space=pltpu.HBM), pl.BlockSpec(memory_space=pltpu.VMEM)
    b, f, dma = (lambda *x: pltpu.VMEM(x, BF)), (lambda *x: pltpu.VMEM(x, F32)), (lambda *x: pltpu.SemaphoreType.DMA(x))
    return pl.pallas_call(
        backward_kernel,
        out_shape=[
            s((2, 256, 1024), BF), s((PART, 1024), F32), s((PART, 1024), F32), s((PART, 1024), F32),
            s((8, 1024), F32), s((8, 1024), F32),
        ],
        in_specs=[hbm] * 16 + [fast] * 3,
        out_specs=[hbm] + [fast] * 5,
        scratch_shapes=[
            b(8, 2, PART, 1024), b(8, PART, 1024), b(2, 3, PART, 1024), b(4, 2, 2, PART, 512), b(4, 2, PART, 512), b(2, 3, PART, 512),
            b(8, 2, PART, 1024), b(4, 2, 4 * PART, 512), b(2, 1024, 768),
            b(1024, 1024), b(4, T, 256), b(4, 2 * T, 256), b(4, 2 * T, 256), b(T, 1024), b(T, 1024), f(T, 1024), f(T, 1024),
            b(T, 2 * T), b(T, 2 * T), b(1024, T), b(T, 1024), b(T, 1024), b(T, 1024), b(2, 2 * T, T), f(16, 1, T),
            b(2, 5 * T, 256), b(2, 5 * T, 256), b(2 * T, 768),
            b(256, 2 * T), b(256, T), b(256, T), b(256, T), f(8, 1024), f(8, 1024), f(3, 8, 1024), f(3, 8, 1024), f(3, 8, 1024), f(3, 8, 1024),
            dma(16, 3), dma(16, 3), dma(4, 3), dma(4, 3), dma(2), dma(2), dma(2, 4), dma(2, 4), dma(2), dma(2),
            pltpu.SemaphoreType.DMA, pltpu.SemaphoreType.DMA, dma(3), dma(3), dma(3), dma(3), dma(3), dma(3), dma(3), dma(3),
            pltpu.SemaphoreType.REGULAR, dma(2), dma(31), dma(2),
        ],
        compiler_params=pltpu.CompilerParams(collective_id=1, has_side_effects=True, vmem_limit_bytes=63 * 2**20),
    )(*args)


def spread_kernel(
    out_in, cells_hbm, attn_hbm, up_hbm, down_hbm, early_hbm, late_hbm,
    out_cells, grad_cells, gq, gk, gv, bq, bv, go, bo, g1, s1, g2, s2, gup, bu, gdown, bd,
    cells_in, wide, attn, down, early, late, up, res, sems,
):
    p = Place()
    copies = [
        pltpu.make_async_copy(a, b, sems.at[k])
        for k, (a, b) in enumerate(
            (
                (cells_hbm, cells_in), (early_hbm, early), (late_hbm, late), (attn_hbm, attn), (down_hbm, down),
                (up_hbm, up), (out_in, res),
            )
        )
    ]
    for c in copies:
        c.start()
    copies[6].wait()
    backs = [pltpu.make_async_copy(res, out_cells, sems.at[8])]
    copies[0].wait()
    wide[...] = cells_in[...].astype(F32)
    backs.append(pltpu.make_async_copy(wide, grad_cells, sems.at[7]))
    for c in copies[1:6]:
        c.wait()
    backs.append(pltpu.make_async_copy(up, gup, sems.at[9]))
    for c in backs:
        c.start()
    gq[...] = attn[:, 0:256]
    gk[...] = attn[:, 256:512]
    gv[...] = attn[:, 512:768]
    go[...] = jnp.transpose(attn[:, 768:1024], (1, 0))
    gdown[...] = jnp.transpose(down[...], (1, 0))

    def cut(ref, k, block, part):
        row = ref[k : k + 1, lane_block(block * 128)]
        return pltpu.roll(row, lax.rem(128 - part * 32, 128), 1)[:, 0:32]

    for out, ref, k in ((bo, early, 4), (g1, late, 0), (s1, late, 1), (g2, early, 5), (s2, early, 6), (bd, early, 7)):
        out[...] = cut(ref, k, p.d, p.z)
    for out, k in ((bq, 2), (bv, 3)):
        out[...] = cut(late, k, p.d // 4, lax.rem(p.d, 4))
    bu[...] = early[0:1, lane_block(p.d * 128)]
    for c in backs:
        c.wait()


def spread(*args):
    s = jax.ShapeDtypeStruct
    hbm, fast = pl.BlockSpec(memory_space=pltpu.HBM), pl.BlockSpec(memory_space=pltpu.VMEM)
    v, w = s((1, 32), F32), s((PART, 256), F32)
    return pl.pallas_call(
        spread_kernel,
        out_shape=[
            s((2, 256, 1024), BF), s((2, 256, 1024), F32), w, w, w, v, v, s((256, PART), F32), v, v, v, v, v,
            s((PART, 1024), F32), s((1, PART), F32), s((1024, PART), F32), v,
        ],
        in_specs=[hbm] * 7,
        out_specs=[hbm, hbm] + [fast] * 11 + [hbm] + [fast] * 3,
        scratch_shapes=[
            pltpu.VMEM((2, 256, 1024), BF), pltpu.VMEM((2, 256, 1024), F32), pltpu.VMEM((PART, 1024), F32),
            pltpu.VMEM((PART, 1024), F32), pltpu.VMEM((8, 1024), F32), pltpu.VMEM((8, 1024), F32), pltpu.VMEM((PART, 1024), F32),
            pltpu.VMEM((2, 256, 1024), BF), pltpu.SemaphoreType.DMA((10,)),
        ],
        compiler_params=pltpu.CompilerParams(vmem_limit_bytes=62 * 2**20),
    )(*args)


def forward(*args):
    s = jax.ShapeDtypeStruct
    outs = [
        (T, 1024), (T, 1024), (4, T, 256), (4, 2 * T, 256), (4, 2 * T, 256), (T, 1024), (16, 2 * T, T), (16, 1, T),
        (4, 1024, 768), (1024, 1024), (3, 1024, 1024), (3, 1024, 1024), (2, 256, 1024), (T, 1024), (2, T, 1024), (2, T, 1024),
        (4, PART, 1024), (4, PART, 1024), (4, PART, 1024), (16, 1024), (4, 1, 1024),
    ]
    wide = (7, 13, 19, 20)
    hbm, fast = pl.BlockSpec(memory_space=pltpu.HBM), pl.BlockSpec(memory_space=pltpu.VMEM)
    b, f, dma = (lambda *x: pltpu.VMEM(x, BF)), (lambda *x: pltpu.VMEM(x, F32)), (lambda *x: pltpu.SemaphoreType.DMA(x))
    sems = []
    for parts in (3, 1, 1, 1):
        sems += [dma(6, parts), dma(3, parts), dma(3, 7), dma(3, 8)]
    return pl.pallas_call(
        forward_kernel,
        out_shape=[s(o, F32 if n in wide else BF) for n, o in enumerate(outs)],
        in_specs=[hbm, hbm, pl.BlockSpec(memory_space=pltpu.SMEM)] + [hbm] * 6 + [fast] * 7,
        out_specs=[hbm] * 19 + [fast] * 2,
        scratch_shapes=[
            b(T, 1024), b(T, 1024), b(T, 1024), b(4, 1024, 768), b(1024, 1024), b(4, T, 256), b(4, 2 * T, 256), b(4, 2 * T, 256),
            b(T, 1024), b(2, 2 * T, T), f(16, 1, T), b(2, 2 * T, 128), b(256, 2 * T), b(256, T), f(T, 1024), b(T, 1024),
            b(1024, T), b(T, 2 * T), b(T, 2 * T), f(T, 1024), f(T, 1024),
            b(2, 1024, 1024), b(2, 1024, 1024), b(2, T, 1024), b(2, T, 1024), b(2, T, 1024), b(2, T, 1024), f(T, 1024), b(3, 2, T, 1024), b(4, PART, 1024),
            f(8, 128), f(8, 128), f(4, 1, 1536),
        ]
        + sems
        + [dma(3, 2), dma(3, 2), dma(4), dma(4), dma(4, 2), dma(4, 2), dma(2, 4), dma(2, 4), dma(2, 2), dma(2, 2), dma(4, 3), dma(4, 3),
           pltpu.SemaphoreType.REGULAR, dma(7), dma(2, 2), dma(20)],
        compiler_params=pltpu.CompilerParams(collective_id=0, has_side_effects=True, vmem_limit_bytes=62 * 2**20),
    )(*args)


def body(*args):
    if lax.axis_size("dp") == 8 and lax.axis_size("mp") == 4:
        return fused_body(*args)
    return plain_body(*args)


def fused_body(
    cells,
    lengths,
    query_matrix,
    key_matrix,
    value_matrix,
    query_bias,
    value_bias,
    output_matrix,
    b_out,
    gain_one,
    shift_one,
    gain_two,
    shift_two,
    expand_weight,
    expand_bias,
    contract_weight,
    b_down,
    grad_out,
):
    slots = cells.shape[0]
    row = lambda v: v.reshape(1, -1)
    small = row(jnp.concatenate([query_bias, value_bias, expand_bias]))
    (x, rows_one, q_all, k_all, v_all, mixed_all, e_all, r_all, wa, wo, _, _, out_land, d_middle, gu, gd, keep, la, lc, vec, bup) = forward(
        cells, grad_out, lengths, query_matrix, key_matrix, value_matrix, output_matrix, expand_weight, contract_weight,
        small, row(b_out), row(gain_one), row(shift_one), row(gain_two), row(shift_two), row(b_down),
    )
    left = backward(
        x, rows_one, q_all, k_all, v_all, mixed_all, e_all, r_all, wa, wo, d_middle, gu, gd, keep, la, lc, vec, bup, row(gain_one)
    )
    return tuple(v.reshape(-1) if v.shape[0] == 1 else v for v in spread(out_land, *left))


def solution(mesh):
    return jax.shard_map(
        body,
        mesh=mesh,
        in_specs=(
            P("dp", "mp", None),
            P("dp"),
            P(None, "mp"),
            P(None, "mp"),
            P(None, "mp"),
            P("mp"),
            P("mp"),
            P("mp", None),
            P(),
            P(),
            P(),
            P(),
            P(),
            P(None, "mp"),
            P("mp"),
            P("mp", None),
            P(),
            P("dp", "mp", None),
        ),
        out_specs=(
            P("dp", "mp", None),
            P("dp", "mp", None),
            P("dp", "mp"),
            P("dp", "mp"),
            P("dp", "mp"),
            P(("mp", "dp")),
            P(("mp", "dp")),
            P("mp", "dp"),
            P(("dp", "mp")),
            P(("dp", "mp")),
            P(("dp", "mp")),
            P(("dp", "mp")),
            P(("dp", "mp")),
            P("dp", "mp"),
            P(("mp", "dp")),
            P("mp", "dp"),
            P(("dp", "mp")),
        ),
        check_vma=False,
    )
```
